32 devices in a mesh: fsdp: 2 (over core), context: 4 (over z), tensor: 4 (over y, x).
Axes of the slice: x: 2, y: 2, z: 4, core: 2. Of those that a mesh axis runs over, the one named last changes fastest.
Arguments:
- hidden_in: bfloat16 [2, 1024, 1536], P('fsdp', 'context'), may hold values from -6 to 6
- segment_ids: int32 [2, 1024], P('fsdp', 'context'), may hold values from 0 to 7, never falling along the last dimension, each value on 1 to 512 neighbouring positions
- w_query: bfloat16 [2, 1536, 1536], P(None, 'fsdp', 'tensor'), may hold values from -0.15625 to 0.15625
- w_key: bfloat16 [2, 1536, 1536], P(None, 'fsdp', 'tensor'), may hold values from -0.15625 to 0.15625
- w_value: bfloat16 [2, 1536, 1536], P(None, 'fsdp', 'tensor'), may hold values from -0.15625 to 0.15625
- w_gate_out: bfloat16 [2, 1536, 1536], P(None, 'fsdp', 'tensor'), may hold values from -0.15625 to 0.15625
- w_attn_out: bfloat16 [2, 1536, 1536], P(None, 'tensor', 'fsdp'), may hold values from -2.5 to 2.5
- w_forget: bfloat16 [2, 1536, 24], P(None, 'fsdp', 'tensor'), may hold values from -0.15625 to 0.15625
- b_forget: float32 [2, 24], P(None, 'tensor'), may hold values from 2 to 12
- gain_attn: bfloat16 [2, 1536], P(None, 'fsdp'), may hold values from 0.25 to 1.75
- gain_ffn: bfloat16 [2, 1536], P(None, 'fsdp'), may hold values from 0.25 to 1.75
- w_gate: bfloat16 [2, 1536, 4096], P(None, 'fsdp', 'tensor'), may hold values from -0.15625 to 0.15625
- w_up: bfloat16 [2, 1536, 4096], P(None, 'fsdp', 'tensor'), may hold values from -0.15625 to 0.15625
- w_down: bfloat16 [2, 4096, 1536], P(None, 'tensor', 'fsdp'), may hold values from -0.1875 to 0.1875
- cotangent: bfloat16 [2, 1024, 1536], P('fsdp', 'context'), may hold values from -6 to 6
Outputs:
- output: bfloat16 [2, 1024, 1536], P('fsdp', 'context')
- grad_input: bfloat16 [2, 1024, 1536], P('fsdp', 'context')
- grad_query: float32 [2, 1536, 1536], P(None, 'fsdp', 'tensor')
- grad_key: float32 [2, 1536, 1536], P(None, 'fsdp', 'tensor')
- grad_value: float32 [2, 1536, 1536], P(None, 'fsdp', 'tensor')
- grad_gate_out: float32 [2, 1536, 1536], P(None, 'fsdp', 'tensor')
- grad_attn_out: float32 [2, 1536, 1536], P(None, 'tensor', 'fsdp')
- grad_forget: float32 [2, 1536, 24], P(None, 'fsdp', 'tensor')
- grad_forget_bias: float32 [2, 24], P(None, 'tensor')
- grad_gain_attn: float32 [2, 1536], P(None, 'fsdp')
- grad_gain_ffn: float32 [2, 1536], P(None, 'fsdp')
- grad_gate: float32 [2, 1536, 4096], P(None, 'fsdp', 'tensor')
- grad_up: float32 [2, 1536, 4096], P(None, 'fsdp', 'tensor')
- grad_down: float32 [2, 4096, 1536], P(None, 'tensor', 'fsdp')
The draws below stay inside these ranges and needn't reach their ends.
Inputs may be any that keep to these rules, and one draw needn't show every extreme that they name: `segment_ids`: along each sequence the ids never fall; each of the 8 ids marks one document of 1 to 512 positions, and one document has exactly 512.
All inputs are finite; a program needn't handle non-finite values.
Results may differ from the reference program's by a relative error of at most 0.025.
Values may be sent and summed in bfloat16 or wider, within the bound.
No kernel may reach another device: no remote copies, remote signals or barrier semaphores. Data moves between devices by JAX's collectives and lax.ppermute only.
A program may use at most 256 MiB of HBM per device.

```python
import math
import jax
import jax.numpy as jnp
import numpy as np
from jax import lax

D = 1536
H = 24
HEAD = 64
FF = 4096
LAYERS = 2
DOCS = 8
SEQS = 2
LEN = 1024
DOC_MOST = 512


def draw_b_forget(key, part):
    spread = jax.random.uniform(key, (LAYERS, H), jnp.float32)
    longest = jnp.log(jnp.float32(LEN))
    shortest = jnp.log(jnp.float32(12.0))
    return longest - spread * (longest - shortest)


def levels(rng, extent, split, least, top_value):
    def one(dim, shards_of):
        draws = jax.random.uniform(jax.random.fold_in(jax.random.fold_in(rng, 6), dim), (shards_of,), jnp.float32, least / len(split), top_value / len(split))
        return jnp.repeat(jnp.exp(draws), extent[dim] // shards_of).reshape((-1,) + (1,) * (len(extent) - dim - 1))

    level = one(*split[0])
    for cut in split[1:]:
        level = level * one(*cut)
    return level


def length_profile(number_of, total, most, lean):
    loads = [(1 << 20) // math.isqrt(standing ** lean) + 1 for standing in range(2, number_of + 1)]
    spare, given = total - most - (number_of - 1), [1] * (number_of - 1)
    while spare > 0:
        free = [i for i in range(number_of - 1) if given[i] < most]
        pool, budget = sum([loads[i] for i in free]), spare
        for i in free:
            extra = min(most - given[i], max(1, budget * loads[i] // pool), spare)
            given[i] = given[i] + extra
            spare = spare - extra
    return np.array([most] + given)


def uneven_parts(rng, number_of, total, reach, slope):
    if number_of == 2:
        one = jax.random.randint(rng, (), max(1, total - reach), min(reach, total - 1) + 1)
        return jnp.stack([one, total - one])
    lengths = jnp.asarray(length_profile(number_of, total, reach, slope), jnp.int32)
    pairs = (number_of - 1) // 2
    source_of, receiver = lengths[1:1 + 2 * pairs:2], lengths[2:2 + 2 * pairs:2]
    room = jnp.minimum(source_of - 1, reach - receiver)
    shifted = jax.random.randint(jax.random.fold_in(rng, 1), (pairs,), 0, 1 << 20) % (room + 1)
    lengths = lengths.at[1:1 + 2 * pairs:2].set(source_of - shifted).at[2:2 + 2 * pairs:2].set(receiver + shifted)
    return lengths[jax.random.permutation(jax.random.fold_in(rng, 2), number_of)]


def gaussian(stream_key, extent, scale, reach, cuts=(), kind=jnp.bfloat16):
    array = jax.random.normal(stream_key, extent, jnp.float32) * scale
    if len(cuts) > 0:
        array = levels(stream_key, extent, cuts, -0.22, 0.18) * array
    return jnp.clip(array, min=-reach, max=reach).astype(kind)


def setup_inputs(seed: int = 0) -> dict:
    streams_of = jax.random.split(jax.random.key(seed), 16)
    hidden_in = gaussian(streams_of[0], (SEQS, LEN, D), 1.0, 6.0, ((0, 2), (1, 4)))
    segment_ids = jax.vmap(lambda own: jnp.searchsorted(jnp.cumsum(uneven_parts(own, DOCS, LEN, DOC_MOST, 2)), jnp.arange(LEN), side="right"))(jax.random.split(streams_of[1], SEQS)).reshape((SEQS, LEN)).astype(jnp.int32)
    w_query = gaussian(streams_of[2], (LAYERS, D, D), D ** -0.5, 0.15625, ((1, 2), (2, 4)))
    w_key = gaussian(streams_of[3], (LAYERS, D, D), D ** -0.5, 0.15625, ((1, 2), (2, 4)))
    w_value = gaussian(streams_of[4], (LAYERS, D, D), D ** -0.5, 0.15625, ((1, 2), (2, 4)))
    w_gate_out = gaussian(streams_of[5], (LAYERS, D, D), D ** -0.5, 0.15625, ((1, 2), (2, 4)))
    w_attn_out = gaussian(streams_of[6], (LAYERS, D, D), (max(D // 256, 4)) ** -0.5, 2.5, ((1, 4), (2, 2)))
    w_forget = gaussian(streams_of[7], (LAYERS, D, H), D ** -0.5, 0.15625, ((1, 2), (2, 4)))
    b_forget = draw_b_forget(jax.random.fold_in(streams_of[15], 71), 0)
    gain_attn = jnp.clip(1.0 + 0.15 * jax.random.normal(streams_of[9], (LAYERS, D), jnp.float32), 0.25, 1.75).astype(jnp.bfloat16)
    gain_ffn = jnp.clip(1.0 + 0.15 * jax.random.normal(streams_of[10], (LAYERS, D), jnp.float32), 0.25, 1.75).astype(jnp.bfloat16)
    w_gate = gaussian(streams_of[11], (LAYERS, D, FF), D ** -0.5, 0.15625, ((1, 2), (2, 4)))
    w_up = gaussian(streams_of[12], (LAYERS, D, FF), D ** -0.5, 0.15625, ((1, 2), (2, 4)))
    w_down = gaussian(streams_of[13], (LAYERS, FF, D), (FF // 4) ** -0.5, 0.1875, ((1, 4), (2, 2)))
    cotangent = gaussian(streams_of[14], (SEQS, LEN, D), 1.0, 6.0, ((0, 2), (1, 4)))
    return dict(hidden_in=hidden_in, segment_ids=segment_ids, w_query=w_query, w_key=w_key, w_value=w_value, w_gate_out=w_gate_out, w_attn_out=w_attn_out, w_forget=w_forget, b_forget=b_forget, gain_attn=gain_attn, gain_ffn=gain_ffn, w_gate=w_gate, w_up=w_up, w_down=w_down, cotangent=cotangent)


epsilon = 1e-06
masked_value = -1e+30

@jax.custom_vjp
def low(v):
    return lax.optimization_barrier(v.astype(jnp.bfloat16)).astype(jnp.float32)

@jax.custom_vjp
def low_back(v):
    return v

def low_keep(v):
    return (low(v), None)

def low_pass(kept, grad):
    return (grad,)

def back_keep(v):
    return (v, None)

def back_low(kept, grad):
    return (low(grad),)
low.defvjp(low_keep, low_pass)
low_back.defvjp(back_keep, back_low)

def product(left, right):
    return jnp.dot(left, right, preferred_element_type=jnp.float32, precision=lax.Precision.HIGHEST)

def norm_rows(hidden, gain):
    return hidden * lax.rsqrt(lax.optimization_barrier(jnp.mean(hidden * hidden, axis=-1, keepdims=True)) + epsilon) * gain

def attend_one(query_seq, key_seq, value_seq, decay_seq, segment_seq):
    raw_scores = jnp.einsum('qhe,khe->hqk', query_seq, key_seq, precision=lax.Precision.HIGHEST) * 0.125
    decay_heads = jnp.transpose(decay_seq)
    scores = low_back(raw_scores + (decay_heads[:, :, None] - decay_heads[:, None, :]))
    position = jnp.arange(LEN)
    live_pairs = (position[None, :] <= position[:, None]) & (segment_seq[:, None] == segment_seq[None, :])
    probability = jax.nn.softmax(jnp.where(live_pairs[None], scores, masked_value), axis=-1)
    return jnp.einsum('hqk,khe->qhe', low(probability), value_seq, precision=lax.Precision.HIGHEST)

def attend_all(queries, key_rows, value_rows, decay, segment_ids):

    def one_sequence(carried, members):
        return (carried, jax.checkpoint(attend_one)(members[0], members[1], members[2], members[3], members[4]))
    unused, attended = lax.scan(one_sequence, jnp.zeros((), jnp.float32), (queries, key_rows, value_rows, decay, segment_ids))
    return attended

def layer_forward(hidden, segment_ids, weight_query, weight_key, weight_value, weight_gate_out, weight_attn_out, weight_forget, bias_forget, gain_one, gain_two, weight_gate, weight_up, weight_down):
    heads_shape = (SEQS, LEN, H, HEAD)
    normed = low(norm_rows(hidden, gain_one))
    queries = low_back(low(product(normed, weight_query))).reshape(heads_shape)
    key_rows = low_back(low(product(normed, weight_key))).reshape(heads_shape)
    value_rows = low_back(low(product(normed, weight_value))).reshape(heads_shape)
    gate_pre = low_back(product(normed, weight_gate_out))
    forget_pre = low_back(product(normed, weight_forget) + bias_forget)
    decay = jnp.cumsum(jax.nn.log_sigmoid(forget_pre), axis=1)
    attended = low_back(attend_all(queries, key_rows, value_rows, decay, segment_ids).reshape(SEQS, LEN, D))
    gated = low(attended * jax.nn.sigmoid(gate_pre))
    mixed_rows = hidden + low_back(product(gated, weight_attn_out))
    normed_two = low(norm_rows(mixed_rows, gain_two))
    gate_ffn = low_back(product(normed_two, weight_gate))
    up_ffn = low_back(product(normed_two, weight_up))
    inner_low = low(jax.nn.silu(gate_ffn) * up_ffn)
    return mixed_rows + low_back(product(inner_low, weight_down))

def reference(hidden_in, segment_ids, w_query, w_key, w_value, w_gate_out, w_attn_out, w_forget, b_forget, gain_attn, gain_ffn, w_gate, w_up, w_down, cotangent):
    floats = tuple((member.astype(jnp.float32) for member in (hidden_in, w_query, w_key, w_value, w_gate_out, w_attn_out, w_forget, b_forget, gain_attn, gain_ffn, w_gate, w_up, w_down)))

    def forward(hidden, weight_query, weight_key, weight_value, weight_gate_out, weight_attn_out, weight_forget, bias_forget, gain_one, gain_two, weight_gate, weight_up, weight_down):
        hidden_now = hidden
        for layer_index in range(LAYERS):
            hidden_now = layer_forward(hidden_now, segment_ids, weight_query[layer_index], weight_key[layer_index], weight_value[layer_index], weight_gate_out[layer_index], weight_attn_out[layer_index], weight_forget[layer_index], bias_forget[layer_index], gain_one[layer_index], gain_two[layer_index], weight_gate[layer_index], weight_up[layer_index], weight_down[layer_index])
        return hidden_now
    result, pullback = jax.vjp(forward, *floats)
    gradients = pullback(cotangent.astype(jnp.float32))
    return (result.astype(jnp.bfloat16), gradients[0].astype(jnp.bfloat16), gradients[1], gradients[2], gradients[3], gradients[4], gradients[5], gradients[6], gradients[7], gradients[8], gradients[9], gradients[10], gradients[11], gradients[12])
```

```python
import functools

import jax
import jax.numpy as jnp
from jax import lax
from jax.experimental import pallas as pl
from jax.experimental.pallas import tpu as pltpu
from jax.sharding import PartitionSpec as P

epsilon = 1e-06
masked_value = -1e30
bf16 = jnp.bfloat16
f32 = jnp.float32


def query_rows(seq_len):
    return 256 if seq_len <= 2048 else 128


def swap(x, axis, k):
    n = lax.axis_size(axis)
    return lax.ppermute(x, axis, [(i, i ^ k) for i in range(n)])


def tensor_blocks(shard):
    return [shard] + [swap(shard, "tensor", k) for k in range(1, lax.axis_size("tensor"))]


def remote_blocks(shard):
    blocks = []
    for kz in range(1, lax.axis_size("context")):
        blocks += tensor_blocks(swap(shard, "context", kz))
    return blocks


def own_rows(shard):
    return jnp.concatenate(tensor_blocks(shard), axis=0)


def remote_rows(own, piece_index):
    count = lax.axis_size("context")
    rows, width = own.shape
    if count <= 4:
        block = rows // lax.axis_size("tensor")
        return jnp.concatenate(remote_blocks(own[:block]), axis=0)
    everything = lax.all_gather(own, "context")
    return jnp.concatenate(
        [lax.dynamic_index_in_dim(everything, piece_index ^ k, 0, False) for k in range(1, count)],
        axis=0,
    )


def scatter_sum(partial):
    count = lax.axis_size("tensor")
    block = partial.shape[0] // count
    total = partial[:block]
    for k in range(1, count):
        low = partial[k * block : (k + 1) * block].astype(bf16)
        total = total + swap(low, "tensor", k).astype(f32)
    return total


def sum_over(x, axis):
    total = x
    for k in range(1, lax.axis_size(axis)):
        total = total + swap(x, axis, k)
    return total


def block_place(j, place_ref, count_tensor, block):
    kz, kt = j // count_tensor, j % count_tensor
    at = ((kz ^ place_ref[0]) * count_tensor + (kt ^ place_ref[1])) * block
    return pl.multiple_of(at, block)


def shifted_sum(x, reverse):
    rows = x.shape[0]
    row = lax.broadcasted_iota(jnp.int32, x.shape, 0)
    step = 1
    while step < rows:
        if reverse:
            moved = jnp.where(row < rows - step, pltpu.roll(x, rows - step, 0), 0.0)
        else:
            moved = jnp.where(row >= step, pltpu.roll(x, step, 0), 0.0)
        x = x + moved
        step *= 2
    return x


def three_parts(x):
    high = x.astype(bf16)
    rest = x - high.astype(f32)
    middle = rest.astype(bf16)
    lowest = (rest - middle.astype(f32)).astype(bf16)
    return high.astype(f32), middle.astype(f32), lowest.astype(f32)


def head_column(table, head):
    lane = lax.broadcasted_iota(jnp.int32, table.shape, 1)
    return jnp.sum(jnp.where(lane == head, table, 0.0), axis=1, keepdims=True)


def key_windows(seq_len, rows):
    most = seq_len // 2
    found = []
    for start in range(0, seq_len, rows):
        first = max(0, start - (most // rows) * rows)
        found.append((start, first, start + rows))
    return found


def pair_setup(refs, scratch, place_ref, pair, count_tensor, block):
    q_ref, k_ref, v_ref = refs
    qa, qb, ka, kb, vv, decay = scratch
    seq_len = q_ref.shape[0]
    rows = query_rows(seq_len)

    def move(j, carry):
        at = block_place(j, place_ref, count_tensor, block)
        here = pl.ds(pl.multiple_of(j * block, block), block)
        qa[pl.ds(at, block), :] = q_ref[here, :]
        ka[pl.ds(at, block), :] = k_ref[here, :]
        vv[pl.ds(at, block), :] = v_ref[here, :]
        return carry

    lax.fori_loop(0, seq_len // block, move, 0)

    def mix(i, carry):
        here = pl.ds(pl.multiple_of(i * rows, rows), rows)
        lane = lax.broadcasted_iota(jnp.int32, (rows, 128), 1)
        table = decay[here, :]
        q = qa[here, :].astype(f32) * 0.125
        k = ka[here, :].astype(f32)
        for head, (q_out, k_out, first, mine) in enumerate(
            ((qa, ka, 64, lane < 64), (qb, kb, 0, lane >= 64))
        ):
            c = head_column(table, 2 * pair + head)
            high, middle, lowest = three_parts(c)
            spot = lane - first
            split = jnp.where(
                (spot == 0) | (spot == 3),
                high,
                jnp.where((spot == 1) | (spot == 4), middle, lowest),
            )
            low_spot = (spot >= 0) & (spot < 3)
            high_spot = (spot >= 3) & (spot < 6)
            key_side = jnp.where(low_spot, -split, jnp.where(high_spot, 1.0, 0.0))
            query_side = jnp.where(low_spot, 1.0, jnp.where(high_spot, split, 0.0))
            q_out[here, :] = jnp.where(mine, q, query_side).astype(bf16)
            k_out[here, :] = jnp.where(mine, k, key_side).astype(bf16)
        return carry

    lax.fori_loop(0, seq_len // rows, mix, 0)


def gather_decay(keep_ref, decay, place_ref, count_tensor, block):
    seq_len = keep_ref.shape[0]

    def move(j, carry):
        at = block_place(j, place_ref, count_tensor, block)
        decay[pl.ds(at, block), :] = keep_ref[pl.ds(pl.multiple_of(j * block, block), block), :]
        return carry

    lax.fori_loop(0, seq_len // block, move, 0)
    decay[...] = shifted_sum(decay[...], False)


def live_mask(start_ref, start, first, width, rows):
    key_pos = first + lax.broadcasted_iota(jnp.int32, (rows, width), 1)
    query_pos = start + lax.broadcasted_iota(jnp.int32, (rows, width), 0)
    doc_start = start_ref[pl.ds(start, rows), :]
    return (key_pos <= query_pos) & (key_pos >= doc_start)


def over_query_blocks(seq_len, rows, body):
    windows = key_windows(seq_len, rows)
    if len(windows) <= 4:
        for start, first, end in windows:
            body(start, first, end - first)
        return
    width = windows[-1][2] - windows[-1][1]

    def one(i, carry):
        start = pl.multiple_of(i * rows, rows)
        first = pl.multiple_of(jnp.maximum(start + rows - width, 0), rows)
        body(start, first, width)
        return carry

    lax.fori_loop(0, len(windows), one, 0)


nt_dims = (((1,), (1,)), ((), ()))
tn_dims = (((0,), (0,)), ((), ()))


def dot_nt(a, b):
    return lax.dot_general(a, b, nt_dims, preferred_element_type=f32)


def dot_tn(a, b):
    return lax.dot_general(a, b, tn_dims, preferred_element_type=f32)


def dot_nn(a, b):
    return jnp.dot(a, b, preferred_element_type=f32)


def probabilities(q_rows, k_rows, mask):
    s = jnp.where(mask, dot_nt(q_rows, k_rows), masked_value)
    e = jnp.exp(s - jnp.max(s, axis=1, keepdims=True))
    return e * (1.0 / jnp.sum(e, axis=1, keepdims=True))


def forward_kernel(
    count_tensor, block,
    place_ref, q_ref, k_ref, v_ref, gate_ref, keep_ref, start_ref,
    o_ref, u_ref,
    qa, qb, ka, kb, vv, decay, oo,
):
    pair = pl.program_id(0)
    seq_len, rows = q_ref.shape[0], query_rows(q_ref.shape[0])

    @pl.when(pair == 0)
    def _():
        gather_decay(keep_ref, decay, place_ref, count_tensor, block)

    pair_setup((q_ref, k_ref, v_ref), (qa, qb, ka, kb, vv, decay), place_ref, pair, count_tensor, block)
    lane = lax.broadcasted_iota(jnp.int32, (rows, 128), 1)

    def body(start, first, width):
        mask = live_mask(start_ref, start, first, width, rows)
        here, keys = pl.ds(start, rows), pl.ds(first, width)
        values = vv[keys, :]
        out = []
        for q_of, k_of in ((qa, ka), (qb, kb)):
            p = probabilities(q_of[here, :], k_of[keys, :], mask).astype(bf16)
            out.append(dot_nn(p, values))
        oo[here, :] = jnp.where(lane < 64, out[0], out[1])

    over_query_blocks(seq_len, rows, body)

    def move(j, carry):
        at = block_place(j, place_ref, count_tensor, block)
        here = pl.ds(pl.multiple_of(j * block, block), block)
        o = oo[pl.ds(at, block), :]
        o_ref[here, :] = o
        u_ref[here, :] = (o * jax.nn.sigmoid(gate_ref[here, :])).astype(bf16)
        return carry

    lax.fori_loop(0, seq_len // block, move, 0)


def backward_kernel(
    count_tensor, block,
    place_ref, q_ref, k_ref, v_ref, gate_ref, keep_ref, start_ref, o_ref, du_ref, forget_ref,
    dq_ref, dk_ref, dv_ref, dg_ref, dz_ref,
    qa, qb, ka, kb, vv, decay, dd, dqs, dka, dkb, dva, dcs,
):
    pair = pl.program_id(0)
    seq_len, rows = q_ref.shape[0], query_rows(q_ref.shape[0])
    blocks = seq_len // block

    @pl.when(pair == 0)
    def _():
        gather_decay(keep_ref, decay, place_ref, count_tensor, block)
        dcs[...] = jnp.zeros_like(dcs)

    pair_setup((q_ref, k_ref, v_ref), (qa, qb, ka, kb, vv, decay), place_ref, pair, count_tensor, block)

    def gates(j, carry):
        at = block_place(j, place_ref, count_tensor, block)
        here = pl.ds(pl.multiple_of(j * block, block), block)
        sig = jax.nn.sigmoid(gate_ref[here, :])
        du = du_ref[here, :]
        dd[pl.ds(at, block), :] = (du * sig).astype(bf16)
        dg_ref[here, :] = (du * o_ref[here, :] * sig * (1.0 - sig)).astype(bf16)
        return carry

    lax.fori_loop(0, blocks, gates, 0)
    dka[...] = jnp.zeros_like(dka)
    dkb[...] = jnp.zeros_like(dkb)
    dva[...] = jnp.zeros_like(dva)
    lane = lax.broadcasted_iota(jnp.int32, (rows, 128), 1)
    lane8 = lax.broadcasted_iota(jnp.int32, (rows, 8), 1)

    def pick(column_a, column_b):
        return jnp.where(lane8 == 2 * pair, column_a, jnp.where(lane8 == 2 * pair + 1, column_b, 0.0))

    def body(start, first, width):
        mask = live_mask(start_ref, start, first, width, rows)
        here, keys = pl.ds(start, rows), pl.ds(first, width)
        values = vv[keys, :]
        d_rows = dd[here, :]
        dq = []
        for head, (q_of, k_of, dk_of) in enumerate(((qa, ka, dka), (qb, kb, dkb))):
            mine = (lane < 64) if head == 0 else (lane >= 64)
            p = probabilities(q_of[here, :], k_of[keys, :], mask)
            d_mine = jnp.where(mine, d_rows, jnp.zeros_like(d_rows))
            dp = dot_nt(d_mine, values)
            delta = jnp.sum(p * dp, axis=1, keepdims=True)
            ds = (p * (dp - delta)).astype(bf16)
            dq.append(dot_nn(ds, k_of[keys, :]))
            dk_of[keys, :] += dot_tn(ds, q_of[here, :])
            dva[keys, :] += dot_tn(p.astype(bf16), d_mine)
        dqs[here, :] = jnp.where(lane < 64, dq[0], dq[1]) * 0.125
        dcs[here, :] += pick(dq[0][:, 67:68], dq[1][:, 3:4])

    over_query_blocks(seq_len, rows, body)

    def columns(i, carry):
        here = pl.ds(pl.multiple_of(i * rows, rows), rows)
        dcs[here, :] -= pick(dka[here, 64:65], dkb[here, 0:1])
        return carry

    lax.fori_loop(0, seq_len // rows, columns, 0)

    def move(j, carry):
        at = pl.ds(block_place(j, place_ref, count_tensor, block), block)
        here = pl.ds(pl.multiple_of(j * block, block), block)
        small = lax.broadcasted_iota(jnp.int32, (block, 128), 1)
        dq_ref[here, :] = dqs[at, :].astype(bf16)
        dk_ref[here, :] = jnp.where(small < 64, dka[at, :], dkb[at, :]).astype(bf16)
        dv_ref[here, :] = dva[at, :].astype(bf16)
        return carry

    lax.fori_loop(0, blocks, move, 0)

    @pl.when(pair == pl.num_programs(0) - 1)
    def _():
        dcs[...] = shifted_sum(dcs[...], True)

        def last(j, carry):
            at = pl.ds(block_place(j, place_ref, count_tensor, block), block)
            here = pl.ds(pl.multiple_of(j * block, block), block)
            dz_ref[here, :] = (dcs[at, :] * jax.nn.sigmoid(-forget_ref[here, :])).astype(bf16)
            return carry

        lax.fori_loop(0, blocks, last, 0)


def lanes(seq_len, at):
    return pl.BlockSpec((seq_len, 128), lambda p, place: (0, p + at))


def whole(seq_len, width):
    return pl.BlockSpec((seq_len, width), lambda p, place: (0, 0))


def attention_forward(place, qkv, gate, keep, doc_start, count_tensor, block):
    seq_len, width = gate.shape
    pairs = width // 128
    low = pltpu.VMEM((seq_len, 128), bf16)
    return pl.pallas_call(
        functools.partial(forward_kernel, count_tensor, block),
        grid_spec=pltpu.PrefetchScalarGridSpec(
            num_scalar_prefetch=1,
            grid=(pairs,),
            in_specs=[
                lanes(seq_len, 0), lanes(seq_len, pairs), lanes(seq_len, 2 * pairs), lanes(seq_len, 0),
                whole(seq_len, 8), whole(seq_len, 1),
            ],
            out_specs=[lanes(seq_len, 0), lanes(seq_len, 0)],
            scratch_shapes=[low] * 5 + [pltpu.VMEM((seq_len, 8), f32), pltpu.VMEM((seq_len, 128), f32)],
        ),
        out_shape=[
            jax.ShapeDtypeStruct((seq_len, width), f32),
            jax.ShapeDtypeStruct((seq_len, width), bf16),
        ],
        compiler_params=pltpu.CompilerParams(vmem_limit_bytes=48 << 20),
    )(place, qkv, qkv, qkv, gate, keep, doc_start)


def attention_backward(place, qkv, gate, keep, doc_start, o, du, forget, count_tensor, block):
    seq_len, width = gate.shape
    pairs = width // 128
    low, high = pltpu.VMEM((seq_len, 128), bf16), pltpu.VMEM((seq_len, 128), f32)
    small = pltpu.VMEM((seq_len, 8), f32)
    wide = jax.ShapeDtypeStruct((seq_len, width), bf16)
    return pl.pallas_call(
        functools.partial(backward_kernel, count_tensor, block),
        grid_spec=pltpu.PrefetchScalarGridSpec(
            num_scalar_prefetch=1,
            grid=(pairs,),
            in_specs=[
                lanes(seq_len, 0), lanes(seq_len, pairs), lanes(seq_len, 2 * pairs), lanes(seq_len, 0),
                whole(seq_len, 8), whole(seq_len, 1), lanes(seq_len, 0), lanes(seq_len, 0), whole(seq_len, 8),
            ],
            out_specs=[lanes(seq_len, 0)] * 4 + [whole(seq_len, 8)],
            scratch_shapes=[low] * 5 + [small] + [low] + [high] * 4 + [small],
        ),
        out_shape=[wide, wide, wide, wide, jax.ShapeDtypeStruct((seq_len, 8), bf16)],
        compiler_params=pltpu.CompilerParams(vmem_limit_bytes=56 << 20),
    )(place, qkv, qkv, qkv, gate, keep, doc_start, o, du, forget)


def inverse_rms(h):
    return lax.rsqrt(jnp.mean(h * h, axis=-1, keepdims=True) + epsilon)


def norm_back(grad_normed, hidden, inverse, gain):
    scaled = hidden * inverse
    weighted = grad_normed * gain
    grad_gain = jnp.sum(grad_normed * scaled, axis=0)
    mean = jnp.mean(weighted * scaled, axis=-1, keepdims=True)
    return inverse * (weighted - scaled * mean), grad_gain


def local(
    hidden_in, segment_ids, w_query, w_key, w_value, w_gate_out, w_attn_out, w_forget, b_forget,
    gain_attn, gain_ffn, w_gate, w_up, w_down, cotangent,
):
    seq_count, piece_len, width = hidden_in.shape
    count_z, count_t = lax.axis_size("context"), lax.axis_size("tensor")
    core, z, t = lax.axis_index("fsdp"), lax.axis_index("context"), lax.axis_index("tensor")
    layers, half, local_width = w_query.shape
    heads = w_forget.shape[2]
    block = piece_len // count_t
    seq_len = piece_len * count_z
    place = jnp.stack([z, t]).astype(jnp.int32)
    shared_rows = count_z <= 4

    def features(x):
        return jnp.where(core == 0, x, jnp.concatenate([x[..., half:], x[..., :half]], axis=-1))

    def rows_by_place(x):
        parts = x.reshape(count_t, block, x.shape[-1])
        return jnp.concatenate(
            [lax.dynamic_index_in_dim(parts, k ^ t, 0, False) for k in range(count_t)], axis=0
        )

    def full(w, axis):
        return jnp.concatenate([w, swap(w, "fsdp", 1)], axis=axis)

    segments = segment_ids.reshape(piece_len)
    if count_z <= 4:
        pieces = jnp.stack([segments] + [swap(segments, "context", k) for k in range(1, count_z)])
        seg_all = jnp.concatenate(
            [lax.dynamic_index_in_dim(pieces, k ^ z, 0, False) for k in range(count_z)]
        )
    else:
        seg_all = lax.all_gather(segments, "context", tiled=True)
    doc_start = jnp.sum((seg_all[None, :] < seg_all[:, None]).astype(jnp.int32), axis=1, keepdims=True)

    gains = jnp.concatenate([gain_attn, gain_ffn], axis=0)
    gains = full(gains, 1).astype(f32)
    w_forget_full = full(w_forget, 1)

    hidden_rows = rows_by_place(features(hidden_in.reshape(piece_len, width)).astype(f32))
    hidden = hidden_rows[:block]
    saved = []
    for layer in range(layers):
        w_qkvg = full(
            jnp.concatenate([w_query[layer], w_key[layer], w_value[layer], w_gate_out[layer]], axis=1), 0
        )
        w_out = full(w_attn_out[layer], 1)
        wg, wu, wd = full(w_gate[layer], 0), full(w_up[layer], 0), full(w_down[layer], 1)
        gain_one, gain_two = gains[layer], gains[layers + layer]
        inverse_one = inverse_rms(hidden)
        if layer == 0:
            own_a = (hidden_rows * inverse_rms(hidden_rows) * gain_one).astype(bf16)
        else:
            own_a = own_rows((hidden * inverse_one * gain_one).astype(bf16))
        a = jnp.concatenate([own_a, remote_rows(own_a, z)], axis=0)
        qkv = dot_nn(a, w_qkvg[:, : 3 * local_width]).astype(bf16)
        gate = dot_nn(a, w_qkvg[:, 3 * local_width :])
        forget = dot_nn(a, w_forget_full[layer]) + b_forget[layer]
        forget = jnp.pad(forget, ((0, 0), (0, 8 - heads)))
        keep = jax.nn.log_sigmoid(forget)
        o, u = attention_forward(place, qkv, gate, keep, doc_start, count_t, block)
        mixed = hidden + scatter_sum(dot_nn(u[:piece_len], w_out))
        inverse_two = inverse_rms(mixed)
        own_b = own_rows((mixed * inverse_two * gain_two).astype(bf16))
        gt, up = dot_nn(own_b, wg), dot_nn(own_b, wu)
        inner = (jax.nn.silu(gt) * up).astype(bf16)
        total = mixed + scatter_sum(dot_nn(inner, wd))
        saved.append(
            (w_qkvg, w_out, wg, wu, wd, gain_one, gain_two, hidden, inverse_one, a, qkv, gate, forget, keep,
             o, u, mixed, inverse_two, own_b, gt, up)
        )
        hidden = total

    def finish(x):
        return features(rows_by_place(own_rows(x.astype(bf16)))).reshape(1, piece_len, width)

    output = finish(hidden)

    cotangent_rows = rows_by_place(features(cotangent.reshape(piece_len, width)))
    grad = cotangent_rows[:block].astype(f32)
    results = [None] * layers
    gain_grads = [None] * (2 * layers)

    def exchange(mine, theirs):
        return mine + swap(theirs, "fsdp", 1).astype(f32)

    for layer in reversed(range(layers)):
        (w_qkvg, w_out, wg, wu, wd, gain_one, gain_two, hidden, inverse_one, a, qkv, gate, forget, keep,
         o, u, mixed, inverse_two, own_b, gt, up) = saved[layer]
        own_g = cotangent_rows if layer == layers - 1 else own_rows(grad.astype(bf16))

        def inner_grads(dm, gt, up):
            sig = jax.nn.sigmoid(gt)
            d_gate = (dm * up * sig * (1.0 + gt * (1.0 - sig))).astype(bf16)
            return d_gate, (dm * (gt * sig)).astype(bf16)

        d_gate, d_up = inner_grads(dot_nt(own_g, wd), gt, up)
        grad_b = scatter_sum(dot_nt(d_gate, wg) + dot_nt(d_up, wu))
        back, gain_grads[layers + layer] = norm_back(grad_b, mixed, inverse_two, gain_two)
        grad_mixed = grad + back
        own_y = own_rows(grad_mixed.astype(bf16))
        y = jnp.concatenate([own_y, remote_rows(own_y, z)], axis=0)
        du = dot_nt(y, w_out)
        dq, dk, dv, dg, dz = attention_backward(
            place, qkv, gate, keep, doc_start, o, du, forget, count_t, block
        )
        d_all = jnp.concatenate([dq, dk, dv, dg], axis=1)
        grad_a = scatter_sum(
            dot_nt(d_all[:piece_len], w_qkvg) + dot_nt(dz[:piece_len, :heads], w_forget_full[layer])
        )
        back, gain_grads[layer] = norm_back(grad_a, hidden, inverse_one, gain_one)
        grad = grad_mixed + back

        if shared_rows:
            b = jnp.concatenate([own_b, remote_rows(own_b, z)], axis=0)
            g = jnp.concatenate([own_g, remote_rows(own_g, z)], axis=0)
            gt_all, up_all = dot_nn(b, wg), dot_nn(b, wu)
            m_all = (jax.nn.silu(gt_all) * up_all).astype(bf16)
            d_gate_all, d_up_all = inner_grads(dot_nt(g, wd), gt_all, up_all)
        else:
            b, g, d_gate_all, d_up_all = own_b, own_g, d_gate, d_up
            m_all = (jax.nn.silu(gt) * up).astype(bf16)

        def by_rows(x, d):
            return exchange(dot_tn(x[:, :half], d), dot_tn(x[:, half:], d).astype(bf16))

        def by_columns(x, d):
            return exchange(dot_tn(x, d[:, :half]), dot_tn(x, d[:, half:]).astype(bf16))

        def pieces_sum(x):
            return x if shared_rows else lax.psum(x, "context")

        dzr = dz[:, :heads]
        bias = jnp.sum(dzr.astype(f32), axis=0)
        forget_theirs = dot_tn(a[:, half:], dzr)
        results[layer] = (
            by_rows(a, dq), by_rows(a, dk), by_rows(a, dv), by_rows(a, dg), by_columns(u, y),
            dot_tn(a[:, :half], dzr) + swap(forget_theirs, "fsdp", 1),
            bias + swap(bias, "fsdp", 1),
            *(pieces_sum(x) for x in (by_rows(b, d_gate_all), by_rows(b, d_up_all), by_columns(m_all, g))),
        )
    grad_input = finish(grad)
    gain_total = sum_over(sum_over(jnp.stack(gain_grads), "tensor"), "context")
    gain_total = gain_total[:, :half] + swap(gain_total[:, half:], "fsdp", 1)
    s = [jnp.stack([results[layer][k] for layer in range(layers)]) for k in range(10)]
    return (
        output, grad_input, s[0], s[1], s[2], s[3], s[4], s[5], s[6],
        gain_total[:layers], gain_total[layers:], s[7], s[8], s[9],
    )


def solution(mesh):
    rows = P("fsdp", "context", None)
    wide, tall = P(None, "fsdp", "tensor"), P(None, "tensor", "fsdp")
    heads, gain = P(None, "tensor"), P(None, "fsdp")
    return jax.shard_map(
        local,
        mesh=mesh,
        in_specs=(
            rows, P("fsdp", "context"), wide, wide, wide, wide, tall, wide, heads, gain, gain, wide, wide, tall, rows,
        ),
        out_specs=(rows, rows, wide, wide, wide, wide, tall, wide, heads, gain, gain, wide, wide, tall),
        check_vma=False,
    )
```

```python
import functools

import jax
import jax.numpy as jnp
from jax import lax
from jax.experimental import pallas as pl
from jax.experimental.pallas import tpu as pltpu
from jax.sharding import PartitionSpec as P

epsilon = 1e-06
masked_value = -1e30
bf16 = jnp.bfloat16
f32 = jnp.float32
pair_lanes = 128
hidden_block = 256
chunk_rows = 256


def query_rows(seq_len):
    return 256 if seq_len <= 2048 else 128


def swap(x, axis, k):
    n = lax.axis_size(axis)
    return lax.ppermute(x, axis, [(i, i ^ k) for i in range(n)])


def own_rows(shard):
    blocks = [shard] + [swap(shard, "tensor", k) for k in range(1, lax.axis_size("tensor"))]
    return jnp.concatenate(blocks, axis=0)


def after(x, token):
    return x + (token[:1, :1].astype(f32) * 0.0).astype(x.dtype)


def all_rows(own, token=None):
    count_z, count_t = lax.axis_size("context"), lax.axis_size("tensor")
    block = own.shape[0] // count_t
    shard = own[:block]
    if token is not None:
        shard = after(shard, token)
        own_sent = after(own, token)
    else:
        own_sent = own
    if count_z != 4:
        return (lax.all_gather(own_sent, "context", tiled=True),)
    far = [swap(shard, "context", 2), swap(shard, "context", 3)]
    near = swap(own_sent, "context", 1)
    far = jnp.concatenate(far, axis=0)
    return (own, near, far) + tuple(swap(far, "tensor", k) for k in range(1, count_t))


def row_places():
    count_z, count_t = lax.axis_size("context"), lax.axis_size("tensor")
    z, t = lax.axis_index("context"), lax.axis_index("tensor")
    own = [(z, k) for k in range(count_t)]
    if count_z != 4:
        parts = [(p, k) for p in range(count_z) for k in range(count_t)]
    else:
        parts = [(z ^ kz, k) for kz in (0, 1) for k in range(count_t)]
        parts += [(z ^ kz, k) for k in range(count_t) for kz in (2, 3)]
    return jnp.stack([(p * count_t + (t ^ k)).astype(jnp.int32) for p, k in own + parts])


def received_sum(own, sends):
    total = own
    for k, part in enumerate(sends, 1):
        total = total + swap(part, "tensor", k).astype(f32)
    return total


def sum_over(x, axis):
    total = x
    for k in range(1, lax.axis_size(axis)):
        total = total + swap(x, axis, k)
    return total


def dot_nt(a, b):
    return lax.dot_general(a, b, (((1,), (1,)), ((), ())), preferred_element_type=f32)


def dot_tn(a, b):
    return lax.dot_general(a, b, (((0,), (0,)), ((), ())), preferred_element_type=f32)


def dot_nn(a, b):
    return jnp.dot(a, b, preferred_element_type=f32)


def each(count, body):
    if count <= 4:
        for i in range(count):
            body(i)
        return

    def one(i, carry):
        body(i)
        return carry

    lax.fori_loop(0, count, one, 0)


def rows_at(i, rows):
    start = i * rows
    return pl.ds(start if isinstance(start, int) else pl.multiple_of(start, rows), rows)


def assemble(parts, whole_ref, place_ref, count_t, block):
    j = 0
    for part in parts:
        for r in range(part.shape[0] // block):
            at = j * block if place_ref is None else pl.multiple_of(place_ref[count_t + j] * block, block)
            whole_ref[pl.ds(at, block), :] = part[r * block : (r + 1) * block, :]
            j += 1


def own_of(ref, place_ref, count_t, block):
    return jnp.concatenate(
        [ref[pl.ds(pl.multiple_of(place_ref[k] * block, block), block), :] for k in range(count_t)], axis=0
    )


def hand_out(total, own_ref, send_refs):
    block = own_ref.shape[0]
    own_ref[...] = total[:block, :]
    for k, ref in enumerate(send_refs, 1):
        ref[...] = total[k * block : (k + 1) * block, :].astype(bf16)


def shifted_sum(x, reverse):
    rows = x.shape[0]
    row = lax.broadcasted_iota(jnp.int32, x.shape, 0)
    step = 1
    while step < rows:
        if reverse:
            moved = jnp.where(row < rows - step, pltpu.roll(x, rows - step, 0), 0.0)
        else:
            moved = jnp.where(row >= step, pltpu.roll(x, step, 0), 0.0)
        x = x + moved
        step *= 2
    return x


def log_sigmoid(z):
    e = jnp.exp(-jnp.abs(z))
    small = e * (1.0 - e * (1 / 2 - e * (1 / 3 - e * (1 / 4 - e * (1 / 5 - e * (1 / 6 - e * (1 / 7)))))))
    return jnp.minimum(z, 0.0) - jnp.where(e < 0.0625, small, jnp.log(1.0 + e))


def three_parts(x):
    high = x.astype(bf16).astype(f32)
    middle = (x - high).astype(bf16).astype(f32)
    lowest = (x - high - middle).astype(bf16).astype(f32)
    return high, middle, lowest


def head_column(table, head):
    lane = lax.broadcasted_iota(jnp.int32, table.shape, 1)
    return jnp.sum(jnp.where(lane == head, table, 0.0), axis=1, keepdims=True)


def mix_decay(q_ref, k_ref, decay_ref, pair, qa, qb, ka, kb):
    rows = chunk_rows

    def mix(i):
        here = rows_at(i, rows)
        lane = lax.broadcasted_iota(jnp.int32, (rows, pair_lanes), 1)
        table = decay_ref[here, :]
        q = q_ref[here, :].astype(f32) * 0.125
        k = k_ref[here, :].astype(f32)
        for head, (q_out, k_out, first, mine) in enumerate(
            ((qa, ka, 64, lane < 64), (qb, kb, 0, lane >= 64))
        ):
            high, middle, lowest = three_parts(head_column(table, 2 * pair + head))
            spot = lane - first
            split = jnp.where(
                (spot == 0) | (spot == 3), high, jnp.where((spot == 1) | (spot == 4), middle, lowest)
            )
            low_spot = (spot >= 0) & (spot < 3)
            high_spot = (spot >= 3) & (spot < 6)
            key_side = jnp.where(low_spot, -split, jnp.where(high_spot, 1.0, 0.0))
            query_side = jnp.where(low_spot, 1.0, jnp.where(high_spot, split, 0.0))
            q_out[here, :] = jnp.where(mine, q, query_side).astype(bf16)
            k_out[here, :] = jnp.where(mine, k, key_side).astype(bf16)

    each(q_ref.shape[0] // rows, mix)


def live_mask(start_ref, start, first, width, rows):
    key_pos = first + lax.broadcasted_iota(jnp.int32, (rows, width), 1)
    query_pos = start + lax.broadcasted_iota(jnp.int32, (rows, width), 0)
    doc_start = start_ref[pl.ds(start, rows), :]
    return (key_pos <= query_pos) & (key_pos >= doc_start)


def over_query_blocks(seq_len, rows, body):
    before = seq_len // 2
    if seq_len // rows <= 4:
        for start in range(0, seq_len, rows):
            first = max(0, start - before)
            body(start, first, start + rows - first)
        return
    width = before + rows

    def one(i, carry):
        start = pl.multiple_of(i * rows, rows)
        first = pl.multiple_of(jnp.maximum(start - before, 0), rows)
        body(start, first, width)
        return carry

    lax.fori_loop(0, seq_len // rows, one, 0)


def probabilities(q_rows, k_rows, mask):
    s = jnp.where(mask, dot_nt(q_rows, k_rows), masked_value)
    e = jnp.exp(s - jnp.max(s, axis=1, keepdims=True))
    return e * (1.0 / jnp.sum(e, axis=1, keepdims=True))


def lane_blocks(refs):
    return jnp.concatenate([r[0] for r in refs], axis=1)


def forward_kernel(count_parts, count_t, block, join, *refs):
    place_ref, parts, refs = refs[0], refs[1 : 1 + count_parts], list(refs[1 + count_parts :])
    mine, theirs, (wo, to, wf, bias, start_ref) = refs[:4], refs[4:8], refs[8:13]
    refs = refs[13:]
    a_ref = refs.pop(0) if join else parts[0]
    q_ref, k_ref, v_ref, gate_ref, o_ref, u_ref, z_ref, decay_ref, own_ref = refs[:9]
    sends, (qa, qb, ka, kb, acc) = refs[9:-5], refs[-5:]
    pair = pl.program_id(0)
    seq_len, half = a_ref.shape[0], a_ref.shape[1] // 2
    rows = query_rows(seq_len)

    @pl.when(pair == 0)
    def _():
        if join:
            assemble(parts, a_ref, place_ref, count_t, block)
        acc[...] = jnp.zeros_like(acc)

        def gates(i):
            here = rows_at(i, chunk_rows)
            z = (dot_nn(a_ref[here, :], wf[...]) + bias[...])[:, :8]
            z_ref[here, :] = z
            decay_ref[here, :] = log_sigmoid(z)

        each(seq_len // chunk_rows, gates)
        decay_ref[...] = shifted_sum(decay_ref[...], False)

    w_mine, w_theirs = lane_blocks(mine), lane_blocks(theirs)

    def project(i):
        here = rows_at(i, chunk_rows)
        out = dot_nn(a_ref[here, :half], w_mine) + dot_nn(a_ref[here, half:], w_theirs)
        q_ref[here, :] = out[:, :128].astype(bf16)
        k_ref[here, :] = out[:, 128:256].astype(bf16)
        v_ref[here, :] = out[:, 256:384].astype(bf16)
        gate_ref[here, :] = out[:, 384:]

    each(seq_len // chunk_rows, project)
    mix_decay(q_ref, k_ref, decay_ref, pair, qa, qb, ka, kb)
    lane = lax.broadcasted_iota(jnp.int32, (rows, pair_lanes), 1)

    def body(start, first, width):
        mask = live_mask(start_ref, start, first, width, rows)
        here, keys = pl.ds(start, rows), pl.ds(first, width)
        values = v_ref[keys, :]
        out = []
        for q_of, k_of in ((qa, ka), (qb, kb)):
            p = probabilities(q_of[here, :], k_of[keys, :], mask).astype(bf16)
            out.append(dot_nn(p, values))
        o = jnp.where(lane < 64, out[0], out[1])
        o_ref[here, :] = o
        u_ref[here, :] = (o * jax.nn.sigmoid(gate_ref[here, :])).astype(bf16)

    over_query_blocks(seq_len, rows, body)
    u_own = own_of(u_ref, place_ref, count_t, block)
    acc[:, :half] += dot_nn(u_own, wo[0])
    acc[:, half:] += dot_nn(u_own, to[0])

    @pl.when(pair == pl.num_programs(0) - 1)
    def _():
        hand_out(acc, own_ref, sends)


def backward_kernel(count_parts, count_t, block, join, *refs):
    place_ref, parts, refs = refs[0], refs[1 : 1 + count_parts], list(refs[1 + count_parts :])
    mine, theirs, (wo, to, wf) = refs[:4], refs[4:8], refs[8:11]
    q_ref, k_ref, v_ref, gate_ref, o_ref, z_ref, decay_ref, start_ref = refs[11:19]
    refs = refs[19:]
    y_ref = refs.pop(0) if join else parts[0]
    dq_ref, dk_ref, dv_ref, dg_ref, dz_ref, own_ref = refs[:6]
    sends, (qa, qb, ka, kb, dd, dka, dkb, dva, dcs, acc) = refs[6:-10], refs[-10:]
    pair = pl.program_id(0)
    seq_len, half = y_ref.shape[0], y_ref.shape[1] // 2
    rows = query_rows(seq_len)

    @pl.when(pair == 0)
    def _():
        if join:
            assemble(parts, y_ref, place_ref, count_t, block)
        acc[...] = jnp.zeros_like(acc)
        dcs[...] = jnp.zeros_like(dcs)

    def gates(i):
        here = rows_at(i, chunk_rows)
        du = dot_nt(y_ref[here, :half], wo[0]) + dot_nt(y_ref[here, half:], to[0])
        sig = jax.nn.sigmoid(gate_ref[here, :])
        dd[here, :] = (du * sig).astype(bf16)
        dg_ref[here, :] = (du * o_ref[here, :] * sig * (1.0 - sig)).astype(bf16)

    each(seq_len // chunk_rows, gates)
    mix_decay(q_ref, k_ref, decay_ref, pair, qa, qb, ka, kb)
    dka[...] = jnp.zeros_like(dka)
    dkb[...] = jnp.zeros_like(dkb)
    dva[...] = jnp.zeros_like(dva)
    lane = lax.broadcasted_iota(jnp.int32, (rows, pair_lanes), 1)

    def pick(column_a, column_b):
        at = lax.broadcasted_iota(jnp.int32, (column_a.shape[0], pair_lanes), 1)
        return jnp.where(at == 2 * pair, column_a, jnp.where(at == 2 * pair + 1, column_b, 0.0))

    def body(start, first, width):
        mask = live_mask(start_ref, start, first, width, rows)
        here, keys = pl.ds(start, rows), pl.ds(first, width)
        values = v_ref[keys, :]
        d_rows = dd[here, :]
        dq = []
        for head, (q_of, k_of, dk_of) in enumerate(((qa, ka, dka), (qb, kb, dkb))):
            own_lanes = (lane < 64) if head == 0 else (lane >= 64)
            p = probabilities(q_of[here, :], k_of[keys, :], mask)
            d_mine = jnp.where(own_lanes, d_rows, jnp.zeros_like(d_rows))
            dp = dot_nt(d_mine, values)
            delta = jnp.sum(p * dp, axis=1, keepdims=True)
            ds = (p * (dp - delta)).astype(bf16)
            dq.append(dot_nn(ds, k_of[keys, :]))
            dk_of[keys, :] += dot_tn(ds, q_of[here, :])
            dva[keys, :] += dot_tn(p.astype(bf16), d_mine)
        dq_ref[here, :] = (jnp.where(lane < 64, dq[0], dq[1]) * 0.125).astype(bf16)
        dcs[here, :] += pick(dq[0][:, 67:68], dq[1][:, 3:4])

    over_query_blocks(seq_len, rows, body)

    def finish(i):
        here = rows_at(i, chunk_rows)
        lanes_now = lax.broadcasted_iota(jnp.int32, (chunk_rows, pair_lanes), 1)
        ka_rows, kb_rows = dka[here, :], dkb[here, :]
        dk_ref[here, :] = jnp.where(lanes_now < 64, ka_rows, kb_rows).astype(bf16)
        dv_ref[here, :] = dva[here, :].astype(bf16)
        dcs[here, :] -= pick(ka_rows[:, 64:65], kb_rows[:, 0:1])

    each(seq_len // chunk_rows, finish)
    d_own = jnp.concatenate(
        [own_of(r, place_ref, count_t, block) for r in (dq_ref, dk_ref, dv_ref, dg_ref)], axis=1
    )
    acc[:, :half] += dot_nt(d_own, lane_blocks(mine))
    acc[:, half:] += dot_nt(d_own, lane_blocks(theirs))

    @pl.when(pair == pl.num_programs(0) - 1)
    def _():
        dcs[...] = shifted_sum(dcs[...], True)

        def last(i):
            here = rows_at(i, chunk_rows)
            dz_ref[here, :] = (dcs[here, :8] * jax.nn.sigmoid(-z_ref[here, :])).astype(bf16)

        each(seq_len // chunk_rows, last)
        dz_own = own_of(dz_ref, place_ref, count_t, block)
        acc[...] += dot_nt(dz_own, wf[:, :8])
        hand_out(acc, own_ref, sends)


def ffn_forward_kernel(b_ref, wg, wu, wd, tg, tu, td, gt_ref, up_ref, own_ref, *rest):
    sends, acc = rest[:-1], rest[-1]
    half = b_ref.shape[1] // 2
    low, high = b_ref[:, :half], b_ref[:, half:]
    gt = dot_nn(low, wg[0]) + dot_nn(high, tg[0])
    up = dot_nn(low, wu[0]) + dot_nn(high, tu[0])
    gt_ref[...] = gt
    up_ref[...] = up
    m = (gt * jax.nn.sigmoid(gt) * up).astype(bf16)

    @pl.when(pl.program_id(0) == 0)
    def _():
        acc[...] = jnp.zeros_like(acc)

    acc[:, :half] += dot_nn(m, wd[0])
    acc[:, half:] += dot_nn(m, td[0])

    @pl.when(pl.program_id(0) == pl.num_programs(0) - 1)
    def _():
        hand_out(acc, own_ref, sends)


def inner_grads(dm, gt, up):
    sig = jax.nn.sigmoid(gt)
    d_gate = (dm * up * sig * (1.0 + gt * (1.0 - sig))).astype(bf16)
    return d_gate, (dm * (gt * sig)).astype(bf16)


def ffn_backward_kernel(g_ref, gt_ref, up_ref, wg, wu, wd, tg, tu, td, own_ref, *rest):
    sends, acc = rest[:-1], rest[-1]
    half = g_ref.shape[1] // 2
    dm = dot_nt(g_ref[:, :half], wd[0]) + dot_nt(g_ref[:, half:], td[0])
    d_gate, d_up = inner_grads(dm, gt_ref[...], up_ref[...])

    @pl.when(pl.program_id(0) == 0)
    def _():
        acc[...] = jnp.zeros_like(acc)

    acc[:, :half] += dot_nt(d_gate, wg[0]) + dot_nt(d_up, wu[0])
    acc[:, half:] += dot_nt(d_gate, tg[0]) + dot_nt(d_up, tu[0])

    @pl.when(pl.program_id(0) == pl.num_programs(0) - 1)
    def _():
        hand_out(acc, own_ref, sends)


def ffn_inner_kernel(count_parts, block, *refs):
    b_parts, g_parts = refs[:count_parts], refs[count_parts : 2 * count_parts]
    wg, wu, wd, tg, tu, td, b_ref, g_ref, m_ref, dgate_ref, dup_ref = refs[2 * count_parts :]
    half = b_ref.shape[1] // 2

    @pl.when(pl.program_id(0) == 0)
    def _():
        assemble(b_parts, b_ref, None, 0, block)
        assemble(g_parts, g_ref, None, 0, block)

    def chunk(i):
        here = rows_at(i, chunk_rows)
        low, high = b_ref[here, :half], b_ref[here, half:]
        gt = dot_nn(low, wg[0]) + dot_nn(high, tg[0])
        up = dot_nn(low, wu[0]) + dot_nn(high, tu[0])
        dm = dot_nt(g_ref[here, :half], wd[0]) + dot_nt(g_ref[here, half:], td[0])
        m_ref[here, :] = (gt * jax.nn.sigmoid(gt) * up).astype(bf16)
        dgate_ref[here, :], dup_ref[here, :] = inner_grads(dm, gt, up)

    each(b_ref.shape[0] // chunk_rows, chunk)


def fixed(shape, single=True):
    zeros = (0,) * len(shape)
    if single:
        return pl.BlockSpec(shape, lambda *_: zeros, pipeline_mode=pl.Buffered(1))
    return pl.BlockSpec(shape, lambda *_: zeros)


def lanes(seq_len):
    return pl.BlockSpec((seq_len, pair_lanes), lambda p, *_: (0, p))


def lanes_read(seq_len):
    if seq_len <= 2048:
        return lanes(seq_len)
    return pl.BlockSpec((seq_len, pair_lanes), lambda p, *_: (0, p), pipeline_mode=pl.Buffered(1))


def columns_of(w, layer, width):
    return pl.BlockSpec((1, w.shape[1], width), lambda p, *_: (layer, 0, p))


def rows_of(w, layer, height):
    return pl.BlockSpec((1, height, w.shape[2]), lambda p, *_: (layer, p, 0))


def shape(dims, dtype):
    return jax.ShapeDtypeStruct(dims, dtype)


def share_outs(block, width, count_t):
    out = [shape((block, width), f32)] + [shape((block, width), bf16)] * (count_t - 1)
    return out, [fixed((block, width), False)] * count_t


def attention_specs(parts, layer, w4, t4, wo, to, seq_len, join):
    specs = [fixed(p.shape) for p in parts]
    specs += [columns_of(w, layer, pair_lanes) for w in (*w4, *t4)]
    specs += [rows_of(wo, layer, pair_lanes), rows_of(to, layer, pair_lanes)]
    return specs


def attention_forward(places, parts, layer, w4, t4, wo, to, wf, bias, doc_start, count_t, piece_len):
    seq_len, width = doc_start.shape[0], parts[0].shape[1]
    local_width = wo.shape[1]
    block = piece_len // count_t
    join = len(parts) > 1
    low, high = lambda: shape((seq_len, local_width), bf16), lambda: shape((seq_len, local_width), f32)
    shared, shared_specs = share_outs(block, width, count_t)
    outs = [low(), low(), low(), high(), high(), low(), shape((seq_len, 8), f32), shape((seq_len, 8), f32)]
    specs = [lanes(seq_len)] * 6 + [fixed((seq_len, 8), False)] * 2
    if join:
        outs, specs = [shape((seq_len, width), bf16)] + outs, [fixed((seq_len, width))] + specs
    got = pl.pallas_call(
        functools.partial(forward_kernel, len(parts), count_t, block, join),
        grid_spec=pltpu.PrefetchScalarGridSpec(
            num_scalar_prefetch=1,
            grid=(local_width // pair_lanes,),
            in_specs=attention_specs(parts, layer, w4, t4, wo, to, seq_len, join)
            + [fixed(wf.shape), fixed(bias.shape), fixed(doc_start.shape)],
            out_specs=specs + shared_specs,
            scratch_shapes=[pltpu.VMEM((seq_len, pair_lanes), bf16)] * 4 + [pltpu.VMEM((piece_len, width), f32)],
        ),
        out_shape=outs + shared,
        compiler_params=pltpu.CompilerParams(vmem_limit_bytes=60 << 20),
    )(places, *parts, *w4, *t4, wo, to, wf, bias, doc_start)
    got = list(got)
    a = got.pop(0) if join else parts[0]
    return a, got[:8], got[8], got[9:]


def attention_backward(places, parts, layer, w4, t4, wo, to, wf, saved, doc_start, count_t, piece_len):
    q, k, v, gate, o, u, z, decay = saved
    seq_len, width = doc_start.shape[0], parts[0].shape[1]
    local_width = wo.shape[1]
    block = piece_len // count_t
    join = len(parts) > 1
    shared, shared_specs = share_outs(block, width, count_t)
    outs = [shape((seq_len, local_width), bf16)] * 4 + [shape((seq_len, 8), bf16)]
    specs = [lanes(seq_len)] * 4 + [fixed((seq_len, 8), False)]
    if join:
        outs, specs = [shape((seq_len, width), bf16)] + outs, [fixed((seq_len, width))] + specs
    low, high = pltpu.VMEM((seq_len, pair_lanes), bf16), pltpu.VMEM((seq_len, pair_lanes), f32)
    got = pl.pallas_call(
        functools.partial(backward_kernel, len(parts), count_t, block, join),
        grid_spec=pltpu.PrefetchScalarGridSpec(
            num_scalar_prefetch=1,
            grid=(local_width // pair_lanes,),
            in_specs=attention_specs(parts, layer, w4, t4, wo, to, seq_len, join)
            + [fixed(wf.shape)]
            + [lanes_read(seq_len)] * 5
            + [fixed((seq_len, 8)), fixed((seq_len, 8)), fixed(doc_start.shape)],
            out_specs=specs + shared_specs,
            scratch_shapes=[low] * 5 + [high] * 4 + [pltpu.VMEM((piece_len, width), f32)],
        ),
        out_shape=outs + shared,
        compiler_params=pltpu.CompilerParams(vmem_limit_bytes=60 << 20),
    )(places, *parts, *w4, *t4, wo, to, wf, q, k, v, gate, o, z, decay, doc_start)
    got = list(got)
    y = got.pop(0) if join else parts[0]
    return y, got[:5], got[5], got[6:]


def ffn_weights(layer, w3, t3):
    specs = []
    for wg, wu, wd in (w3, t3):
        specs += [
            columns_of(wg, layer, hidden_block), columns_of(wu, layer, hidden_block), rows_of(wd, layer, hidden_block),
        ]
    return specs


def blocks_of(rows):
    return pl.BlockSpec((rows, hidden_block), lambda p, *_: (0, p))


def ffn_forward(b, layer, w3, t3, count_t):
    rows, width = b.shape
    inner = w3[2].shape[1]
    shared, shared_specs = share_outs(rows // count_t, width, count_t)
    got = pl.pallas_call(
        ffn_forward_kernel,
        grid=(inner // hidden_block,),
        in_specs=[fixed(b.shape)] + ffn_weights(layer, w3, t3),
        out_specs=[blocks_of(rows)] * 2 + shared_specs,
        scratch_shapes=[pltpu.VMEM((rows, width), f32)],
        out_shape=[shape((rows, inner), f32)] * 2 + shared,
        compiler_params=pltpu.CompilerParams(vmem_limit_bytes=40 << 20),
    )(b, *w3, *t3)
    return got[0], got[1], got[2], got[3:]


def ffn_backward(g, gt, up, layer, w3, t3, count_t):
    rows, width = g.shape
    shared, shared_specs = share_outs(rows // count_t, width, count_t)
    got = pl.pallas_call(
        ffn_backward_kernel,
        grid=(gt.shape[1] // hidden_block,),
        in_specs=[fixed(g.shape)] + [blocks_of(rows)] * 2 + ffn_weights(layer, w3, t3),
        out_specs=shared_specs,
        scratch_shapes=[pltpu.VMEM((rows, width), f32)],
        out_shape=shared,
        compiler_params=pltpu.CompilerParams(vmem_limit_bytes=40 << 20),
    )(g, gt, up, *w3, *t3)
    return got[0], got[1:]


def ffn_inner(b_parts, g_parts, layer, w3, t3, block):
    rows, width = sum(p.shape[0] for p in b_parts), b_parts[0].shape[1]
    inner = w3[2].shape[1]
    return pl.pallas_call(
        functools.partial(ffn_inner_kernel, len(b_parts), block),
        grid=(inner // hidden_block,),
        in_specs=[fixed(p.shape) for p in (*b_parts, *g_parts)] + ffn_weights(layer, w3, t3),
        out_specs=[fixed((rows, width))] * 2 + [blocks_of(rows)] * 3,
        out_shape=[shape((rows, width), bf16)] * 2 + [shape((rows, inner), bf16)] * 3,
        compiler_params=pltpu.CompilerParams(vmem_limit_bytes=56 << 20),
    )(*b_parts, *g_parts, *w3, *t3)


def inverse_rms(h):
    return lax.rsqrt(jnp.mean(h * h, axis=-1, keepdims=True) + epsilon)


def norm_back(grad_normed, hidden, inverse, gain):
    scaled = hidden * inverse
    weighted = grad_normed * gain
    grad_gain = jnp.sum(grad_normed * scaled, axis=0)
    mean = jnp.mean(weighted * scaled, axis=-1, keepdims=True)
    return inverse * (weighted - scaled * mean), grad_gain


def local(
    hidden_in, segment_ids, w_query, w_key, w_value, w_gate_out, w_attn_out, w_forget, b_forget,
    gain_attn, gain_ffn, w_gate, w_up, w_down, cotangent,
):
    seq_count, piece_len, width = hidden_in.shape
    count_z, count_t = lax.axis_size("context"), lax.axis_size("tensor")
    core, z, t = lax.axis_index("fsdp"), lax.axis_index("context"), lax.axis_index("tensor")
    layers, half, local_width = w_query.shape
    heads = w_forget.shape[2]
    block = piece_len // count_t
    seq_len = piece_len * count_z
    places = row_places()
    shared_rows = count_z == 4

    def features(x):
        return jnp.where(core == 0, x, jnp.concatenate([x[..., half:], x[..., :half]], axis=-1))

    def rows_by_place(x):
        parts = x.reshape(count_t, block, x.shape[-1])
        return jnp.concatenate(
            [lax.dynamic_index_in_dim(parts, k ^ t, 0, False) for k in range(count_t)], axis=0
        )

    def other(w):
        return swap(w, "fsdp", 1)

    def full(w, axis):
        return jnp.concatenate([w, other(w)], axis=axis)

    gains = full(jnp.concatenate([gain_attn, gain_ffn], axis=0), 1).astype(f32)
    hidden_rows = rows_by_place(features(hidden_in.reshape(piece_len, width)).astype(f32))
    first_a = (hidden_rows * inverse_rms(hidden_rows) * gains[0]).astype(bf16)
    a_parts = all_rows(first_a)

    w_forget_full = jnp.pad(full(w_forget, 1), ((0, 0), (0, 0), (0, pair_lanes - heads)))
    bias = jnp.pad(b_forget, ((0, 0), (0, pair_lanes - heads)))
    w4 = (w_query, w_key, w_value, w_gate_out)
    t4 = tuple(other(w) for w in w4)
    to = other(w_attn_out)
    w3 = (w_gate, w_up, w_down)
    t3 = tuple(other(w) for w in w3)

    segments = segment_ids.reshape(piece_len)
    if count_z == 4:
        pieces = jnp.stack([segments] + [swap(segments, "context", k) for k in range(1, count_z)])
        seg_all = jnp.concatenate(
            [lax.dynamic_index_in_dim(pieces, k ^ z, 0, False) for k in range(count_z)]
        )
    else:
        seg_all = lax.all_gather(segments, "context", tiled=True)
    doc_start = jnp.sum((seg_all[None, :] < seg_all[:, None]).astype(jnp.int32), axis=1, keepdims=True)

    def in_order(parts):
        if len(parts) > 1:
            return parts
        stacked = parts[0].reshape(count_z, count_t, block, width)
        return (
            jnp.concatenate(
                [lax.dynamic_index_in_dim(stacked, k ^ t, 1, True) for k in range(count_t)], axis=1
            ).reshape(seq_len, width),
        )

    hidden = hidden_rows[:block]
    saved = []
    cotangent_rows = rows_by_place(features(cotangent.reshape(piece_len, width)))
    for layer in range(layers):
        gain_one, gain_two = gains[layer], gains[layers + layer]
        inverse_one = inverse_rms(hidden)
        if layer > 0:
            a_parts = all_rows(own_rows((hidden * inverse_one * gain_one).astype(bf16)))
        a, kept, own, sends = attention_forward(
            places, in_order(a_parts), layer, w4, t4, w_attn_out, to, w_forget_full[layer],
            bias[layer : layer + 1], doc_start, count_t, piece_len,
        )
        if shared_rows:
            if layer == 0:
                g_last = all_rows(cotangent_rows, a_parts[-1])
            else:
                saved[-1]["b_parts"] = all_rows(saved[-1]["b"], a_parts[-1])
        mixed = hidden + received_sum(own, sends)
        inverse_two = inverse_rms(mixed)
        b = own_rows((mixed * inverse_two * gain_two).astype(bf16))
        gt, up, own, sends = ffn_forward(b, layer, w3, t3, count_t)
        saved.append(
            dict(hidden=hidden, inverse_one=inverse_one, a=a, kept=kept, mixed=mixed, inverse_two=inverse_two,
                 b=b, gt=gt, up=up)
        )
        hidden = mixed + received_sum(own, sends)

    def finish(x):
        return features(rows_by_place(own_rows(x.astype(bf16)))).reshape(1, piece_len, width)

    output = finish(hidden)

    grad = cotangent_rows[:block].astype(f32)
    results = [None] * layers
    gain_grads = [None] * (2 * layers)

    def exchange(mine, theirs):
        return mine + other(theirs).astype(f32)

    for layer in reversed(range(layers)):
        s = saved[layer]
        gain_one, gain_two = gains[layer], gains[layers + layer]
        g = cotangent_rows if layer == layers - 1 else own_rows(grad.astype(bf16))
        own, sends = ffn_backward(g, s["gt"], s["up"], layer, w3, t3, count_t)
        back, gain_grads[layers + layer] = norm_back(received_sum(own, sends), s["mixed"], s["inverse_two"], gain_two)
        grad_mixed = grad + back
        y_parts = all_rows(own_rows(grad_mixed.astype(bf16)))
        y, (dq, dk, dv, dg, dz), own, sends = attention_backward(
            places, in_order(y_parts), layer, w4, t4, w_attn_out, to, w_forget_full[layer], s["kept"],
            doc_start, count_t, piece_len,
        )
        if not shared_rows:
            b_parts, g_parts = (s["b"],), (g,)
        elif layer == layers - 1:
            b_parts, g_parts = all_rows(s["b"], y_parts[-1]), g_last
        else:
            b_parts, g_parts = s["b_parts"], all_rows(g, y_parts[-1])
        back, gain_grads[layer] = norm_back(received_sum(own, sends), s["hidden"], s["inverse_one"], gain_one)
        grad = grad_mixed + back

        b, g, m, d_gate, d_up = ffn_inner(b_parts, g_parts, layer, w3, t3, block)

        def by_rows(x, d):
            return exchange(dot_tn(x[:, :half], d), dot_tn(x[:, half:], d).astype(bf16))

        def by_columns(x, d):
            return exchange(dot_tn(x, d[:, :half]), dot_tn(x, d[:, half:]).astype(bf16))

        def pieces_sum(x):
            return x if shared_rows else lax.psum(x, "context")

        a, u = s["a"], s["kept"][5]
        dzr = dz[:, :heads]
        bias_grad = jnp.sum(dzr.astype(f32), axis=0)
        results[layer] = (
            by_rows(a, dq), by_rows(a, dk), by_rows(a, dv), by_rows(a, dg), by_columns(u, y),
            dot_tn(a[:, :half], dzr) + other(dot_tn(a[:, half:], dzr)),
            bias_grad + other(bias_grad),
            *(pieces_sum(x) for x in (by_rows(b, d_gate), by_rows(b, d_up), by_columns(m, g))),
        )
    grad_input = finish(grad)
    gain_total = sum_over(sum_over(jnp.stack(gain_grads), "tensor"), "context")
    gain_total = gain_total[:, :half] + other(gain_total[:, half:])
    s = [jnp.stack([results[layer][k] for layer in range(layers)]) for k in range(10)]
    return (
        output, grad_input, s[0], s[1], s[2], s[3], s[4], s[5], s[6],
        gain_total[:layers], gain_total[layers:], s[7], s[8], s[9],
    )


def solution(mesh):
    rows = P("fsdp", "context", None)
    wide, tall = P(None, "fsdp", "tensor"), P(None, "tensor", "fsdp")
    heads, gain = P(None, "tensor"), P(None, "fsdp")
    return jax.shard_map(
        local,
        mesh=mesh,
        in_specs=(
            rows, P("fsdp", "context"), wide, wide, wide, wide, tall, wide, heads, gain, gain, wide, wide, tall, rows,
        ),
        out_specs=(rows, rows, wide, wide, wide, wide, tall, wide, heads, gain, gain, wide, wide, tall),
        check_vma=False,
    )
```

```python
import functools

import jax
import jax.numpy as jnp
from jax import lax
from jax.experimental import pallas as pl
from jax.experimental.pallas import tpu as pltpu
from jax.sharding import PartitionSpec as P

epsilon = 1e-06
masked_value = -1e30
bf16 = jnp.bfloat16
f32 = jnp.float32
pair_lanes = 128
hidden_block = 256
chunk_rows = 256


def query_rows(seq_len):
    return 256 if seq_len <= 2048 else 128


def swap(x, axis, k):
    n = lax.axis_size(axis)
    return lax.ppermute(x, axis, [(i, i ^ k) for i in range(n)])


def own_rows(shard):
    blocks = [shard] + [swap(shard, "tensor", k) for k in range(1, lax.axis_size("tensor"))]
    return jnp.concatenate(blocks, axis=0)


def after(x, token):
    return x if token is None else x + (token[:1, :1].astype(f32) * 0.0).astype(x.dtype)


def all_rows(own, first=None, second=None, shard=None):
    count_z, count_t = lax.axis_size("context"), lax.axis_size("tensor")
    if count_z != 4:
        return (lax.all_gather(own, "context", tiled=True),)
    if shard is None:
        shard = own[: own.shape[0] // count_t]
    shard = after(shard, first)
    parts = [own, None]
    for kz in (2, 3):
        far = after(swap(shard, "context", kz), second)
        parts += [far] + [swap(far, "tensor", k) for k in range(1, count_t)]
    parts[1] = swap(after(own, first), "context", 1)
    return tuple(parts)


def row_places():
    count_z, count_t = lax.axis_size("context"), lax.axis_size("tensor")
    z, t = lax.axis_index("context"), lax.axis_index("tensor")
    parts = [((z ^ p) if count_z == 4 else p, k) for p in range(count_z) for k in range(count_t)]
    own = [(z, k) for k in range(count_t)]
    return jnp.stack([(p * count_t + (t ^ k)).astype(jnp.int32) for p, k in own + parts])


def received_sum(own, sends):
    total = own
    for k, part in enumerate(sends, 1):
        total = total + swap(part, "tensor", k).astype(f32)
    return total


def sum_over(x, axis):
    total = x
    for k in range(1, lax.axis_size(axis)):
        total = total + swap(x, axis, k)
    return total


def dot_nt(a, b):
    return lax.dot_general(a, b, (((1,), (1,)), ((), ())), preferred_element_type=f32)


def dot_tn(a, b):
    return lax.dot_general(a, b, (((0,), (0,)), ((), ())), preferred_element_type=f32)


def dot_nn(a, b):
    return jnp.dot(a, b, preferred_element_type=f32)


def each(count, body):
    if count <= 4:
        for i in range(count):
            body(i)
        return

    def one(i, carry):
        body(i)
        return carry

    lax.fori_loop(0, count, one, 0)


def rows_at(i, rows):
    start = i * rows
    return pl.ds(start if isinstance(start, int) else pl.multiple_of(start, rows), rows)


def assemble(parts, whole_ref, place_ref, count_t, block):
    j = 0
    for part in parts:
        for r in range(part.shape[0] // block):
            at = j * block if place_ref is None else pl.multiple_of(place_ref[count_t + j] * block, block)
            whole_ref[pl.ds(at, block), :] = part[r * block : (r + 1) * block, :]
            j += 1


def own_of(ref, place_ref, count_t, block):
    return jnp.concatenate(
        [ref[pl.ds(pl.multiple_of(place_ref[k] * block, block), block), :] for k in range(count_t)], axis=0
    )


def hand_out(total, own_ref, send_refs):
    block = own_ref.shape[0]
    own_ref[...] = total[:block, :]
    for k, ref in enumerate(send_refs, 1):
        ref[...] = total[k * block : (k + 1) * block, :].astype(bf16)


def shifted_sum(x, reverse):
    rows = x.shape[0]
    row = lax.broadcasted_iota(jnp.int32, x.shape, 0)
    step = 1
    while step < rows:
        if reverse:
            moved = jnp.where(row < rows - step, pltpu.roll(x, rows - step, 0), 0.0)
        else:
            moved = jnp.where(row >= step, pltpu.roll(x, step, 0), 0.0)
        x = x + moved
        step *= 2
    return x


def log_sigmoid(z):
    e = jnp.exp(-jnp.abs(z))
    small = e * (1.0 - e * (1 / 2 - e * (1 / 3 - e * (1 / 4 - e * (1 / 5 - e * (1 / 6 - e * (1 / 7)))))))
    return jnp.minimum(z, 0.0) - jnp.where(e < 0.0625, small, jnp.log(1.0 + e))


def three_parts(x):
    high = x.astype(bf16).astype(f32)
    middle = (x - high).astype(bf16).astype(f32)
    lowest = (x - high - middle).astype(bf16).astype(f32)
    return high, middle, lowest


def head_column(table, head):
    lane = lax.broadcasted_iota(jnp.int32, table.shape, 1)
    return jnp.sum(jnp.where(lane == head, table, 0.0), axis=1, keepdims=True)


def decay_terms(table, pair, head, lane):
    mine, first = (lane < 64, 64) if head == 0 else (lane >= 64, 0)
    high, middle, lowest = three_parts(head_column(table, 2 * pair + head))
    spot = lane - first
    split = jnp.where((spot == 0) | (spot == 3), high, jnp.where((spot == 1) | (spot == 4), middle, lowest))
    low_spot, high_spot = (spot >= 0) & (spot < 3), (spot >= 3) & (spot < 6)
    return mine, split, low_spot, high_spot


def mix_keys(k_ref, decay_ref, pair, ka, kb):
    def mix(i):
        here = rows_at(i, chunk_rows)
        lane = lax.broadcasted_iota(jnp.int32, (chunk_rows, pair_lanes), 1)
        k = k_ref[here, :].astype(f32)
        for head, out in enumerate((ka, kb)):
            mine, split, low_spot, high_spot = decay_terms(decay_ref[here, :], pair, head, lane)
            side = jnp.where(low_spot, -split, jnp.where(high_spot, 1.0, 0.0))
            out[here, :] = jnp.where(mine, k, side).astype(bf16)

    each(k_ref.shape[0] // chunk_rows, mix)


def mix_queries(q_ref, decay_ref, start, pair, qa, qb):
    def mix(i):
        here = rows_at(i, chunk_rows)
        lane = lax.broadcasted_iota(jnp.int32, (chunk_rows, pair_lanes), 1)
        q = q_ref[here, :].astype(f32) * 0.125
        table = decay_ref[pl.ds(pl.multiple_of(start + i * chunk_rows, chunk_rows), chunk_rows), :]
        for head, out in enumerate((qa, qb)):
            mine, split, low_spot, high_spot = decay_terms(table, pair, head, lane)
            side = jnp.where(low_spot, 1.0, jnp.where(high_spot, split, 0.0))
            out[here, :] = jnp.where(mine, q, side).astype(bf16)

    each(q_ref.shape[0] // chunk_rows, mix)


def live_mask(start_ref, start, first, width, rows):
    key_pos = first + lax.broadcasted_iota(jnp.int32, (rows, width), 1)
    query_pos = start + lax.broadcasted_iota(jnp.int32, (rows, width), 0)
    doc_start = start_ref[pl.ds(start, rows), :]
    return (key_pos <= query_pos) & (key_pos >= doc_start)


def over_query_blocks(seq_len, rows, body):
    before = seq_len // 2
    if seq_len // rows <= 4:
        for start in range(0, seq_len, rows):
            first = max(0, start - before)
            body(start, first, start + rows - first)
        return
    width = before + rows

    def one(i, carry):
        start = pl.multiple_of(i * rows, rows)
        first = pl.multiple_of(jnp.maximum(start - before, 0), rows)
        body(start, first, width)
        return carry

    lax.fori_loop(0, seq_len // rows, one, 0)


def probabilities(q_rows, k_rows, mask):
    s = jnp.where(mask, dot_nt(q_rows, k_rows), masked_value)
    e = jnp.exp(s - jnp.max(s, axis=1, keepdims=True))
    return e * (1.0 / jnp.sum(e, axis=1, keepdims=True))


def lane_blocks(refs):
    return jnp.concatenate([r[0] for r in refs], axis=1)


def forward_own_kernel(count_parts, count_t, block, join, *refs):
    place_ref, parts, refs = refs[0], refs[1 : 1 + count_parts], list(refs[1 + count_parts :])
    (wq, wk, wv, wg), (tq, tk, tv, tg) = refs[:4], refs[4:8]
    wo, to, wf, bias, start_ref = refs[8:13]
    refs = refs[13:]
    a_ref = refs.pop(0) if join else parts[0]
    k_ref, v_ref, z_ref, decay_ref, own_ref = refs[:5]
    sends, (q_own, qa, qb, ka, kb, acc) = refs[5:-6], refs[-6:]
    pair = pl.program_id(0)
    seq_len, half = a_ref.shape[0], a_ref.shape[1] // 2
    piece_len = count_t * block
    piece_start = pl.multiple_of(place_ref[0] // count_t * piece_len, piece_len)

    @pl.when(pair == 0)
    def _():
        if join:
            assemble(parts, a_ref, place_ref, count_t, block)
        acc[...] = jnp.zeros_like(acc)

        def gates(i):
            here = rows_at(i, chunk_rows)
            z = (dot_nn(a_ref[here, :], wf[...]) + bias[...])[:, :8]
            z_ref[here, :] = z
            decay_ref[here, :] = log_sigmoid(z)

        each(seq_len // chunk_rows, gates)
        decay_ref[...] = shifted_sum(decay_ref[...], False)

    w_mine, w_theirs = lane_blocks((wk, wv)), lane_blocks((tk, tv))

    def project(i):
        here = rows_at(i, chunk_rows)
        out = dot_nn(a_ref[here, :half], w_mine) + dot_nn(a_ref[here, half:], w_theirs)
        k_ref[here, :] = out[:, :128].astype(bf16)
        v_ref[here, :] = out[:, 128:].astype(bf16)

    each(seq_len // chunk_rows, project)
    piece = pl.ds(piece_start, piece_len)
    out = dot_nn(a_ref[piece, :half], lane_blocks((wq, wg))) + dot_nn(a_ref[piece, half:], lane_blocks((tq, tg)))
    q_own[...] = out[:, :128].astype(bf16)
    gate = jax.nn.sigmoid(out[:, 128:])
    mix_keys(k_ref, decay_ref, pair, ka, kb)
    mix_queries(q_own, decay_ref, piece_start, pair, qa, qb)
    before = seq_len // 2
    for s in range(0, piece_len, query_rows(seq_len)):
        rows = query_rows(seq_len)
        width = before + rows
        start = pl.multiple_of(piece_start + s, rows)
        first = pl.multiple_of(jnp.maximum(start - before, 0), rows)
        mask = live_mask(start_ref, start, first, width, rows)
        keys = pl.ds(first, width)
        out = []
        for q_of, k_of in ((qa, ka), (qb, kb)):
            p = probabilities(q_of[s : s + rows, :], k_of[keys, :], mask).astype(bf16)
            out.append(dot_nn(p, v_ref[keys, :]))
        lane = lax.broadcasted_iota(jnp.int32, (rows, pair_lanes), 1)
        u = (jnp.where(lane < 64, out[0], out[1]) * gate[s : s + rows, :]).astype(bf16)
        acc[s : s + rows, :half] += dot_nn(u, wo[0])
        acc[s : s + rows, half:] += dot_nn(u, to[0])

    @pl.when(pair == pl.num_programs(0) - 1)
    def _():
        for k, ref in enumerate((own_ref, *sends)):
            at = pl.multiple_of(place_ref[k] % count_t * block, block)
            ref[...] = acc[pl.ds(at, block), :].astype(ref.dtype)


def forward_rest_kernel(*refs):
    a_ref, wq, wg, tq, tg, k_ref, v_ref, decay_ref, start_ref = refs[:9]
    q_ref, gate_ref, o_ref, u_ref, qa, qb, ka, kb = refs[-8:]
    pair = pl.program_id(0)
    seq_len, half = a_ref.shape[0], a_ref.shape[1] // 2
    rows = query_rows(seq_len)
    w_mine, w_theirs = lane_blocks((wq, wg)), lane_blocks((tq, tg))

    def project(i):
        here = rows_at(i, chunk_rows)
        out = dot_nn(a_ref[here, :half], w_mine) + dot_nn(a_ref[here, half:], w_theirs)
        q_ref[here, :] = out[:, :128].astype(bf16)
        gate_ref[here, :] = out[:, 128:]

    each(seq_len // chunk_rows, project)
    mix_keys(k_ref, decay_ref, pair, ka, kb)
    mix_queries(q_ref, decay_ref, 0, pair, qa, qb)
    lane = lax.broadcasted_iota(jnp.int32, (rows, pair_lanes), 1)

    def body(start, first, width):
        mask = live_mask(start_ref, start, first, width, rows)
        here, keys = pl.ds(start, rows), pl.ds(first, width)
        values = v_ref[keys, :]
        out = []
        for q_of, k_of in ((qa, ka), (qb, kb)):
            p = probabilities(q_of[here, :], k_of[keys, :], mask).astype(bf16)
            out.append(dot_nn(p, values))
        o = jnp.where(lane < 64, out[0], out[1])
        o_ref[here, :] = o
        u_ref[here, :] = (o * jax.nn.sigmoid(gate_ref[here, :])).astype(bf16)

    over_query_blocks(seq_len, rows, body)


def backward_kernel(count_parts, count_t, block, join, *refs):
    place_ref, parts, refs = refs[0], refs[1 : 1 + count_parts], list(refs[1 + count_parts :])
    mine, theirs, (wo, to, wf) = refs[:4], refs[4:8], refs[8:11]
    q_ref, k_ref, v_ref, gate_ref, o_ref, z_ref, decay_ref, start_ref = refs[11:19]
    refs = refs[19:]
    y_ref = refs.pop(0) if join else parts[0]
    dq_ref, dk_ref, dv_ref, dg_ref, dz_ref, own_ref = refs[:6]
    sends, (qa, qb, ka, kb, dd, dka, dkb, dva, dcs, acc) = refs[6:-10], refs[-10:]
    pair = pl.program_id(0)
    seq_len, half = y_ref.shape[0], y_ref.shape[1] // 2
    rows = query_rows(seq_len)

    @pl.when(pair == 0)
    def _():
        if join:
            assemble(parts, y_ref, place_ref, count_t, block)
        acc[...] = jnp.zeros_like(acc)
        dcs[...] = jnp.zeros_like(dcs)

    def gates(i):
        here = rows_at(i, chunk_rows)
        du = dot_nt(y_ref[here, :half], wo[0]) + dot_nt(y_ref[here, half:], to[0])
        sig = jax.nn.sigmoid(gate_ref[here, :])
        dd[here, :] = (du * sig).astype(bf16)
        dg_ref[here, :] = (du * o_ref[here, :] * sig * (1.0 - sig)).astype(bf16)

    each(seq_len // chunk_rows, gates)
    mix_keys(k_ref, decay_ref, pair, ka, kb)
    mix_queries(q_ref, decay_ref, 0, pair, qa, qb)
    dka[...] = jnp.zeros_like(dka)
    dkb[...] = jnp.zeros_like(dkb)
    dva[...] = jnp.zeros_like(dva)
    lane = lax.broadcasted_iota(jnp.int32, (rows, pair_lanes), 1)

    def pick(column_a, column_b):
        at = lax.broadcasted_iota(jnp.int32, (column_a.shape[0], pair_lanes), 1)
        return jnp.where(at == 2 * pair, column_a, jnp.where(at == 2 * pair + 1, column_b, 0.0))

    def body(start, first, width):
        mask = live_mask(start_ref, start, first, width, rows)
        here, keys = pl.ds(start, rows), pl.ds(first, width)
        values = v_ref[keys, :]
        d_rows = dd[here, :]
        dq = []
        for head, (q_of, k_of, dk_of) in enumerate(((qa, ka, dka), (qb, kb, dkb))):
            own_lanes = (lane < 64) if head == 0 else (lane >= 64)
            p = probabilities(q_of[here, :], k_of[keys, :], mask)
            d_mine = jnp.where(own_lanes, d_rows, jnp.zeros_like(d_rows))
            dp = dot_nt(d_mine, values)
            delta = jnp.sum(p * dp, axis=1, keepdims=True)
            ds = (p * (dp - delta)).astype(bf16)
            dq.append(dot_nn(ds, k_of[keys, :]))
            dk_of[keys, :] += dot_tn(ds, q_of[here, :])
            dva[keys, :] += dot_tn(p.astype(bf16), d_mine)
        dq_ref[here, :] = (jnp.where(lane < 64, dq[0], dq[1]) * 0.125).astype(bf16)
        dcs[here, :] += pick(dq[0][:, 67:68], dq[1][:, 3:4])

    over_query_blocks(seq_len, rows, body)

    def finish(i):
        here = rows_at(i, chunk_rows)
        lanes_now = lax.broadcasted_iota(jnp.int32, (chunk_rows, pair_lanes), 1)
        ka_rows, kb_rows = dka[here, :], dkb[here, :]
        dk_ref[here, :] = jnp.where(lanes_now < 64, ka_rows, kb_rows).astype(bf16)
        dv_ref[here, :] = dva[here, :].astype(bf16)
        dcs[here, :] -= pick(ka_rows[:, 64:65], kb_rows[:, 0:1])

    each(seq_len // chunk_rows, finish)
    d_own = jnp.concatenate(
        [own_of(r, place_ref, count_t, block) for r in (dq_ref, dk_ref, dv_ref, dg_ref)], axis=1
    )
    acc[:, :half] += dot_nt(d_own, lane_blocks(mine))
    acc[:, half:] += dot_nt(d_own, lane_blocks(theirs))

    @pl.when(pair == pl.num_programs(0) - 1)
    def _():
        dcs[...] = shifted_sum(dcs[...], True)

        def last(i):
            here = rows_at(i, chunk_rows)
            dz_ref[here, :] = (dcs[here, :8] * jax.nn.sigmoid(-z_ref[here, :])).astype(bf16)

        each(seq_len // chunk_rows, last)
        dz_own = own_of(dz_ref, place_ref, count_t, block)
        acc[...] += dot_nt(dz_own, wf[:, :8])
        hand_out(acc, own_ref, sends)


def ffn_forward_kernel(b_ref, wg, wu, wd, tg, tu, td, gt_ref, up_ref, own_ref, *rest):
    sends, acc = rest[:-1], rest[-1]
    half = b_ref.shape[1] // 2
    low, high = b_ref[:, :half], b_ref[:, half:]
    gt = dot_nn(low, wg[0]) + dot_nn(high, tg[0])
    up = dot_nn(low, wu[0]) + dot_nn(high, tu[0])
    gt_ref[...] = gt
    up_ref[...] = up
    m = (gt * jax.nn.sigmoid(gt) * up).astype(bf16)

    @pl.when(pl.program_id(0) == 0)
    def _():
        acc[...] = jnp.zeros_like(acc)

    acc[:, :half] += dot_nn(m, wd[0])
    acc[:, half:] += dot_nn(m, td[0])

    @pl.when(pl.program_id(0) == pl.num_programs(0) - 1)
    def _():
        hand_out(acc, own_ref, sends)


def inner_grads(dm, gt, up):
    sig = jax.nn.sigmoid(gt)
    d_gate = (dm * up * sig * (1.0 + gt * (1.0 - sig))).astype(bf16)
    return d_gate, (dm * (gt * sig)).astype(bf16)


def ffn_backward_kernel(g_ref, gt_ref, up_ref, wg, wu, wd, tg, tu, td, own_ref, *rest):
    sends, acc = rest[:-1], rest[-1]
    half = g_ref.shape[1] // 2
    dm = dot_nt(g_ref[:, :half], wd[0]) + dot_nt(g_ref[:, half:], td[0])
    d_gate, d_up = inner_grads(dm, gt_ref[...], up_ref[...])

    @pl.when(pl.program_id(0) == 0)
    def _():
        acc[...] = jnp.zeros_like(acc)

    acc[:, :half] += dot_nt(d_gate, wg[0]) + dot_nt(d_up, wu[0])
    acc[:, half:] += dot_nt(d_gate, tg[0]) + dot_nt(d_up, tu[0])

    @pl.when(pl.program_id(0) == pl.num_programs(0) - 1)
    def _():
        hand_out(acc, own_ref, sends)


def ffn_inner_kernel(count_parts, block, *refs):
    b_parts, g_parts = refs[:count_parts], refs[count_parts : 2 * count_parts]
    wg, wu, wd, tg, tu, td = refs[2 * count_parts : 2 * count_parts + 6]
    b_ref, g_ref, m_ref, dgate_ref, dup_ref = refs[-5:]
    half = b_ref.shape[1] // 2

    @pl.when(pl.program_id(0) == 0)
    def _():
        assemble(b_parts, b_ref, None, 0, block)
        assemble(g_parts, g_ref, None, 0, block)

    def chunk(i):
        here = rows_at(i, chunk_rows)
        low, high = b_ref[here, :half], b_ref[here, half:]
        gt = dot_nn(low, wg[0]) + dot_nn(high, tg[0])
        up = dot_nn(low, wu[0]) + dot_nn(high, tu[0])
        dm = dot_nt(g_ref[here, :half], wd[0]) + dot_nt(g_ref[here, half:], td[0])
        m_ref[here, :] = (gt * jax.nn.sigmoid(gt) * up).astype(bf16)
        dgate_ref[here, :], dup_ref[here, :] = inner_grads(dm, gt, up)

    each(b_ref.shape[0] // chunk_rows, chunk)


def fixed(shape, single=True):
    zeros = (0,) * len(shape)
    if single:
        return pl.BlockSpec(shape, lambda *_: zeros, pipeline_mode=pl.Buffered(1))
    return pl.BlockSpec(shape, lambda *_: zeros)


def lanes(seq_len):
    return pl.BlockSpec((seq_len, pair_lanes), lambda p, *_: (0, p))


def lanes_read(seq_len):
    if seq_len <= 2048:
        return lanes(seq_len)
    return pl.BlockSpec((seq_len, pair_lanes), lambda p, *_: (0, p), pipeline_mode=pl.Buffered(1))


def columns_of(w, layer, width):
    return pl.BlockSpec((1, w.shape[1], width), lambda p, *_: (layer, 0, p))


def rows_of(w, layer, height):
    return pl.BlockSpec((1, height, w.shape[2]), lambda p, *_: (layer, p, 0))


def shape(dims, dtype):
    return jax.ShapeDtypeStruct(dims, dtype)


def share_outs(block, width, count_t):
    out = [shape((block, width), f32)] + [shape((block, width), bf16)] * (count_t - 1)
    return out, [fixed((block, width), False)] * count_t


def attention_specs(parts, layer, w4, t4, wo, to, seq_len, join):
    specs = [fixed(p.shape) for p in parts]
    specs += [columns_of(w, layer, pair_lanes) for w in (*w4, *t4)]
    specs += [rows_of(wo, layer, pair_lanes), rows_of(to, layer, pair_lanes)]
    return specs


def cost(microseconds):
    return pl.CostEstimate(flops=int(microseconds * 1.1e9), bytes_accessed=0, transcendentals=0)


def token_specs(tokens):
    return [pl.BlockSpec((16, 128), lambda *_: (0, 0)) for _ in tokens]


def forward_own(places, parts, layer, w4, t4, wo, to, wf, bias, doc_start, count_t, piece_len):
    seq_len, width = doc_start.shape[0], parts[0].shape[1]
    local_width = wo.shape[1]
    block = piece_len // count_t
    join = len(parts) > 1
    shared, shared_specs = share_outs(block, width, count_t)
    outs = [shape((seq_len, local_width), bf16)] * 2 + [shape((seq_len, 8), f32)] * 2
    specs = [lanes(seq_len)] * 2 + [fixed((seq_len, 8), False)] * 2
    if join:
        outs, specs = [shape((seq_len, width), bf16)] + outs, [fixed((seq_len, width))] + specs
    low, piece = pltpu.VMEM((seq_len, pair_lanes), bf16), pltpu.VMEM((piece_len, pair_lanes), bf16)
    got = pl.pallas_call(
        functools.partial(forward_own_kernel, len(parts), count_t, block, join),
        grid_spec=pltpu.PrefetchScalarGridSpec(
            num_scalar_prefetch=1,
            grid=(local_width // pair_lanes,),
            in_specs=attention_specs(parts, layer, w4, t4, wo, to, seq_len, join)
            + [fixed(wf.shape), fixed(bias.shape), fixed(doc_start.shape)],
            out_specs=specs + shared_specs,
            scratch_shapes=[piece] * 3 + [low] * 2 + [pltpu.VMEM((piece_len, width), f32)],
        ),
        out_shape=outs + shared,
        cost_estimate=cost(14),
        compiler_params=pltpu.CompilerParams(vmem_limit_bytes=60 << 20),
    )(places, *parts, *w4, *t4, wo, to, wf, bias, doc_start)
    got = list(got)
    a = got.pop(0) if join else parts[0]
    return a, got[:4], got[4], got[5:]


def forward_rest(a, layer, w4, t4, k, v, decay, doc_start, *tokens):
    seq_len = a.shape[0]
    local_width = k.shape[1]
    low, high = shape((seq_len, local_width), bf16), shape((seq_len, local_width), f32)
    weights = (w4[0], w4[3], t4[0], t4[3])
    return pl.pallas_call(
        forward_rest_kernel,
        grid=(local_width // pair_lanes,),
        in_specs=[fixed(a.shape)]
        + [columns_of(w, layer, pair_lanes) for w in weights]
        + [lanes_read(seq_len)] * 2
        + [fixed(decay.shape), fixed(doc_start.shape)]
        + token_specs(tokens),
        out_specs=[lanes(seq_len)] * 4,
        scratch_shapes=[pltpu.VMEM((seq_len, pair_lanes), bf16)] * 4,
        out_shape=[low, high, high, low],
        cost_estimate=cost(20),
        compiler_params=pltpu.CompilerParams(vmem_limit_bytes=60 << 20),
    )(a, *weights, k, v, decay, doc_start, *tokens)


def attention_backward(places, parts, layer, w4, t4, wo, to, wf, saved, doc_start, count_t, piece_len):
    q, k, v, gate, o, u, z, decay = saved
    seq_len, width = doc_start.shape[0], parts[0].shape[1]
    local_width = wo.shape[1]
    block = piece_len // count_t
    join = len(parts) > 1
    shared, shared_specs = share_outs(block, width, count_t)
    outs = [shape((seq_len, local_width), bf16)] * 4 + [shape((seq_len, 8), bf16)]
    specs = [lanes(seq_len)] * 4 + [fixed((seq_len, 8), False)]
    if join:
        outs, specs = [shape((seq_len, width), bf16)] + outs, [fixed((seq_len, width))] + specs
    low, high = pltpu.VMEM((seq_len, pair_lanes), bf16), pltpu.VMEM((seq_len, pair_lanes), f32)
    got = pl.pallas_call(
        functools.partial(backward_kernel, len(parts), count_t, block, join),
        grid_spec=pltpu.PrefetchScalarGridSpec(
            num_scalar_prefetch=1,
            grid=(local_width // pair_lanes,),
            in_specs=attention_specs(parts, layer, w4, t4, wo, to, seq_len, join)
            + [fixed(wf.shape)]
            + [lanes_read(seq_len)] * 5
            + [fixed((seq_len, 8)), fixed((seq_len, 8)), fixed(doc_start.shape)],
            out_specs=specs + shared_specs,
            scratch_shapes=[low] * 5 + [high] * 4 + [pltpu.VMEM((piece_len, width), f32)],
        ),
        out_shape=outs + shared,
        cost_estimate=cost(32),
        compiler_params=pltpu.CompilerParams(vmem_limit_bytes=60 << 20),
    )(places, *parts, *w4, *t4, wo, to, wf, q, k, v, gate, o, z, decay, doc_start)
    got = list(got)
    y = got.pop(0) if join else parts[0]
    return y, got[:5], got[5], got[6:]


def ffn_weights(layer, w3, t3):
    specs = []
    for wg, wu, wd in (w3, t3):
        specs += [
            columns_of(wg, layer, hidden_block), columns_of(wu, layer, hidden_block), rows_of(wd, layer, hidden_block),
        ]
    return specs


def blocks_of(rows):
    return pl.BlockSpec((rows, hidden_block), lambda p, *_: (0, p))


def ffn_forward(b, layer, w3, t3, count_t):
    rows, width = b.shape
    inner = w3[2].shape[1]
    shared, shared_specs = share_outs(rows // count_t, width, count_t)
    got = pl.pallas_call(
        ffn_forward_kernel,
        grid=(inner // hidden_block,),
        in_specs=[fixed(b.shape)] + ffn_weights(layer, w3, t3),
        out_specs=[blocks_of(rows)] * 2 + shared_specs,
        scratch_shapes=[pltpu.VMEM((rows, width), f32)],
        out_shape=[shape((rows, inner), f32)] * 2 + shared,
        cost_estimate=cost(7),
        compiler_params=pltpu.CompilerParams(vmem_limit_bytes=40 << 20),
    )(b, *w3, *t3)
    return got[0], got[1], got[2], got[3:]


def ffn_backward(g, gt, up, layer, w3, t3, count_t):
    rows, width = g.shape
    shared, shared_specs = share_outs(rows // count_t, width, count_t)
    got = pl.pallas_call(
        ffn_backward_kernel,
        grid=(gt.shape[1] // hidden_block,),
        in_specs=[fixed(g.shape)] + [blocks_of(rows)] * 2 + ffn_weights(layer, w3, t3),
        out_specs=shared_specs,
        scratch_shapes=[pltpu.VMEM((rows, width), f32)],
        out_shape=shared,
        cost_estimate=cost(8),
        compiler_params=pltpu.CompilerParams(vmem_limit_bytes=40 << 20),
    )(g, gt, up, *w3, *t3)
    return got[0], got[1:]


def ffn_inner(b_parts, g_parts, layer, w3, t3, block, *tokens):
    rows, width = sum(p.shape[0] for p in b_parts), b_parts[0].shape[1]
    inner = w3[2].shape[1]
    return pl.pallas_call(
        functools.partial(ffn_inner_kernel, len(b_parts), block),
        grid=(inner // hidden_block,),
        in_specs=[fixed(p.shape) for p in (*b_parts, *g_parts)] + ffn_weights(layer, w3, t3) + token_specs(tokens),
        out_specs=[fixed((rows, width))] * 2 + [blocks_of(rows)] * 3,
        out_shape=[shape((rows, width), bf16)] * 2 + [shape((rows, inner), bf16)] * 3,
        cost_estimate=cost(16),
        compiler_params=pltpu.CompilerParams(vmem_limit_bytes=56 << 20),
    )(*b_parts, *g_parts, *w3, *t3, *tokens)


def unset_kernel(*refs):
    pass


def unset(*like):
    return pl.pallas_call(
        unset_kernel,
        out_specs=[pl.BlockSpec(memory_space=pl.ANY) for _ in like],
        out_shape=list(like),
    )()


def inverse_rms(h):
    return lax.rsqrt(jnp.mean(h * h, axis=-1, keepdims=True) + epsilon)


def norm_back(grad_normed, hidden, inverse, gain):
    scaled = hidden * inverse
    weighted = grad_normed * gain
    grad_gain = jnp.sum(grad_normed * scaled, axis=0)
    mean = jnp.mean(weighted * scaled, axis=-1, keepdims=True)
    return inverse * (weighted - scaled * mean), grad_gain


def local(
    hidden_in, segment_ids, w_query, w_key, w_value, w_gate_out, w_attn_out, w_forget, b_forget,
    gain_attn, gain_ffn, w_gate, w_up, w_down, cotangent,
):
    seq_count, piece_len, width = hidden_in.shape
    count_z, count_t = lax.axis_size("context"), lax.axis_size("tensor")
    core, z, t = lax.axis_index("fsdp"), lax.axis_index("context"), lax.axis_index("tensor")
    layers, half, local_width = w_query.shape
    heads = w_forget.shape[2]
    block = piece_len // count_t
    seq_len = piece_len * count_z
    places = row_places()
    shared_rows = count_z == 4

    def features(x):
        return jnp.where(core == 0, x, jnp.concatenate([x[..., half:], x[..., :half]], axis=-1))

    def rows_by_place(x):
        parts = x.reshape(count_t, block, x.shape[-1])
        return jnp.concatenate(
            [lax.dynamic_index_in_dim(parts, k ^ t, 0, False) for k in range(count_t)], axis=0
        )

    def other(w):
        return swap(w, "fsdp", 1)

    def full(w, axis):
        return jnp.concatenate([w, other(w)], axis=axis)

    segments = segment_ids.reshape(piece_len)
    if count_z == 4:
        pieces = jnp.stack([segments] + [swap(segments, "context", k) for k in range(1, count_z)])
        seg_all = jnp.concatenate(
            [lax.dynamic_index_in_dim(pieces, k ^ z, 0, False) for k in range(count_z)]
        )
    else:
        seg_all = lax.all_gather(segments, "context", tiled=True)
    doc_start = jnp.sum((seg_all[None, :] < seg_all[:, None]).astype(jnp.int32), axis=1, keepdims=True)

    gains = full(jnp.concatenate([gain_attn, gain_ffn], axis=0), 1).astype(f32)
    hidden_rows = rows_by_place(features(hidden_in.reshape(piece_len, width)).astype(f32))
    first_a = (hidden_rows * inverse_rms(hidden_rows) * gains[0]).astype(bf16)
    a_parts = all_rows(first_a)

    w_forget_full = jnp.pad(full(w_forget, 1), ((0, 0), (0, 0), (0, pair_lanes - heads)))
    bias = jnp.pad(b_forget, ((0, 0), (0, pair_lanes - heads)))
    w4 = (w_query, w_key, w_value, w_gate_out)
    t4 = tuple(other(w) for w in w4)
    to = other(w_attn_out)
    w3 = (w_gate, w_up, w_down)
    t3 = tuple(other(w) for w in w3)

    def in_order(parts):
        if len(parts) > 1:
            return parts
        stacked = parts[0].reshape(count_z, count_t, block, width)
        return (
            jnp.concatenate(
                [lax.dynamic_index_in_dim(stacked, k ^ t, 1, True) for k in range(count_t)], axis=1
            ).reshape(seq_len, width),
        )

    hidden = hidden_rows[:block]
    saved = []
    cotangent_rows = rows_by_place(features(cotangent.reshape(piece_len, width)))
    for layer in range(layers):
        gain_one, gain_two = gains[layer], gains[layers + layer]
        inverse_one = inverse_rms(hidden)
        if layer > 0:
            shard = (hidden * inverse_one * gain_one).astype(bf16)
            saved[-1]["rest"] = shard
            a_parts = all_rows(own_rows(shard), shard=shard)
        a, (k, v, forget, decay), own, sends = forward_own(
            places, in_order(a_parts), layer, w4, t4, w_attn_out, to, w_forget_full[layer],
            bias[layer : layer + 1], doc_start, count_t, piece_len,
        )
        if shared_rows:
            if layer == 0:
                g_last = all_rows(cotangent_rows, a_parts[-1], a_parts[-1])
            else:
                before = saved[-1]
                before["b_parts"] = all_rows(before["b"], None, a_parts[-1], before["b_shard"])
        mixed = hidden + received_sum(own, sends)
        inverse_two = inverse_rms(mixed)
        b_shard = (mixed * inverse_two * gain_two).astype(bf16)
        b = own_rows(b_shard)
        gt, up, own, sends = ffn_forward(b, layer, w3, t3, count_t)
        saved.append(
            dict(hidden=hidden, inverse_one=inverse_one, a=a, k=k, v=v, forget=forget, decay=decay, mixed=mixed,
                 inverse_two=inverse_two, b=b, b_shard=b_shard, gt=gt, up=up)
        )
        if layer < layers - 1:
            hidden = mixed + received_sum(own, sends)

    def finish(x):
        return features(rows_by_place(own_rows(x.astype(bf16)))).reshape(1, piece_len, width)

    last_own, last_sends = own, sends
    grad = cotangent_rows[:block].astype(f32)
    wide = shape((layers, half, local_width), f32)
    inner = shape((layers, half, w_gate.shape[2]), f32)
    results = list(
        unset(
            wide, wide, wide, wide, shape((layers, local_width, half), f32),
            inner, inner, shape((layers, w_down.shape[1], half), f32),
        )
    )
    small = [[None] * layers for _ in range(2)]
    gain_grads = [None] * (2 * layers)

    for layer in reversed(range(layers)):
        s = saved[layer]
        gain_one, gain_two = gains[layer], gains[layers + layer]
        if layer == layers - 1:
            g = g_shard = cotangent_rows
            if shared_rows:
                s["b_parts"], g_parts = all_rows(s["b"], shard=s["b_shard"]), g_last
        else:
            g_shard = grad.astype(bf16)
            g = own_rows(g_shard)
            if shared_rows:
                g_parts = all_rows(g, shard=g_shard)
        own, sends = ffn_backward(g, s["gt"], s["up"], layer, w3, t3, count_t)
        back, gain_grads[layers + layer] = norm_back(received_sum(own, sends), s["mixed"], s["inverse_two"], gain_two)
        grad_mixed = grad + back
        y_shard = grad_mixed.astype(bf16)
        y_parts = all_rows(own_rows(y_shard), shard=y_shard)
        q, gate, o, u = forward_rest(
            s["a"], layer, w4, t4, s["k"], s["v"], s["decay"], doc_start, s.get("rest", y_shard)
        )
        kept = (q, s["k"], s["v"], gate, o, u, s["forget"], s["decay"])
        y, (dq, dk, dv, dg, dz), own, sends = attention_backward(
            places, in_order(y_parts), layer, w4, t4, w_attn_out, to, w_forget_full[layer], kept,
            doc_start, count_t, piece_len,
        )
        if layer == layers - 1:
            output = finish(s["mixed"] + received_sum(last_own, [after(x, y_parts[-1]) for x in last_sends]))
        back, gain_grads[layer] = norm_back(received_sum(own, sends), s["hidden"], s["inverse_one"], gain_one)
        grad = grad_mixed + back

        if not shared_rows:
            s["b_parts"], g_parts = (s["b"],), (g,)
        token = grad.astype(bf16) if layer > 0 else y_shard
        b, g, m, d_gate, d_up = ffn_inner(s["b_parts"], g_parts, layer, w3, t3, block, token)

        def put(k, mine, theirs):
            total = mine + other(theirs).astype(f32)
            if k >= 5 and not shared_rows:
                total = lax.psum(total, "context")
            results[k] = lax.dynamic_update_slice_in_dim(results[k], total[None], layer, 0)

        def by_rows(k, x, d):
            put(k, dot_tn(x[:, :half], d), dot_tn(x[:, half:], d).astype(bf16))

        def by_columns(k, x, d):
            put(k, dot_tn(x, d[:, :half]), dot_tn(x, d[:, half:]).astype(bf16))

        a = s["a"]
        for k, d in enumerate((dq, dk, dv, dg)):
            by_rows(k, a, d)
        by_columns(4, u, y)
        by_rows(5, b, d_gate)
        by_rows(6, b, d_up)
        by_columns(7, m, g)
        dzr = dz[:, :heads]
        bias_grad = jnp.sum(dzr.astype(f32), axis=0)
        small[0][layer] = dot_tn(a[:, :half], dzr) + other(dot_tn(a[:, half:], dzr))
        small[1][layer] = bias_grad + other(bias_grad)
    grad_input = finish(grad)
    gain_total = sum_over(sum_over(jnp.stack(gain_grads), "tensor"), "context")
    gain_total = gain_total[:, :half] + other(gain_total[:, half:])
    return (
        output, grad_input, *results[:5], jnp.stack(small[0]), jnp.stack(small[1]),
        gain_total[:layers], gain_total[layers:], *results[5:],
    )


def solution(mesh):
    rows = P("fsdp", "context", None)
    wide, tall = P(None, "fsdp", "tensor"), P(None, "tensor", "fsdp")
    heads, gain = P(None, "tensor"), P(None, "fsdp")
    return jax.shard_map(
        local,
        mesh=mesh,
        in_specs=(
            rows, P("fsdp", "context"), wide, wide, wide, wide, tall, wide, heads, gain, gain, wide, wide, tall, rows,
        ),
        out_specs=(rows, rows, wide, wide, wide, wide, tall, wide, heads, gain, gain, wide, wide, tall),
        check_vma=False,
    )
```

```python
import functools

import jax
import jax.numpy as jnp
from jax import lax
from jax.experimental import pallas as pl
from jax.experimental.pallas import tpu as pltpu
from jax.sharding import PartitionSpec as P

epsilon = 1e-06
masked_value = -1e30
bf16 = jnp.bfloat16
f32 = jnp.float32
pair_lanes = 128
hidden_block = 256
chunk_rows = 256


def query_rows(seq_len):
    return 256 if seq_len <= 2048 else 128


def swap(x, axis, k):
    n = lax.axis_size(axis)
    return lax.ppermute(x, axis, [(i, i ^ k) for i in range(n)])


def after(x, token):
    return x if token is None else x + (token[:1, :1].astype(f32) * 0.0).astype(x.dtype)


def gathered(block, axis):
    count = lax.axis_size(axis)
    copies = jnp.broadcast_to(block[None], (count,) + block.shape)
    return lax.all_to_all(copies, axis, 0, 0, tiled=True).reshape((-1,) + block.shape[1:])


def all_rows(shard, own=None, token=None):
    shard = after(shard, token)
    if own is None:
        own = sent = gathered(shard, "tensor")
    else:
        sent = after(own, token)
    if lax.axis_size("context") != 4:
        return (lax.all_gather(sent, "context", tiled=True),)
    far = [swap(shard, "context", k) for k in (2, 3)]
    if token is None:
        far = [gathered(x, "tensor") for x in far]
    else:
        block, width = shard.shape
        both = gathered(jnp.concatenate(far, axis=0), "tensor").reshape(-1, 2, block, width)
        far = [both]
    return (own, swap(sent, "context", 1), *far)


def received_sum(sends):
    count = lax.axis_size("tensor")
    got = lax.all_to_all(sends.reshape(count, -1, sends.shape[1]), "tensor", 0, 0, tiled=True)
    return jnp.sum(got.astype(f32), axis=0)


def sum_over(x, axis):
    total = x
    for k in range(1, lax.axis_size(axis)):
        total = total + swap(x, axis, k)
    return total


def dot_nt(a, b):
    return lax.dot_general(a, b, (((1,), (1,)), ((), ())), preferred_element_type=f32)


def dot_tn(a, b):
    return lax.dot_general(a, b, (((0,), (0,)), ((), ())), preferred_element_type=f32)


def dot_nn(a, b):
    return jnp.dot(a, b, preferred_element_type=f32)


def each(count, body):
    if count <= 4:
        for i in range(count):
            body(i)
        return

    def one(i, carry):
        body(i)
        return carry

    lax.fori_loop(0, count, one, 0)


def rows_at(i, rows):
    start = i * rows
    return pl.ds(start if isinstance(start, int) else pl.multiple_of(start, rows), rows)


def assemble(parts, whole_ref, z):
    first, piece_len = 0, parts[0].shape[0]
    for part in parts:
        if len(part.shape) == 2:
            at = pl.multiple_of((z ^ first) * piece_len, piece_len)
            whole_ref[pl.ds(at, piece_len), :] = part[...]
            first += 1
            continue
        blocks, pieces, block = part.shape[:3]
        for p in range(pieces):
            for b in range(blocks):
                at = pl.multiple_of((z ^ (first + p)) * piece_len + b * block, block)
                whole_ref[pl.ds(at, block), :] = part[b, p]
        first += pieces


def triangle(rows, reverse):
    row = lax.broadcasted_iota(jnp.int32, (rows, rows), 0)
    column = lax.broadcasted_iota(jnp.int32, (rows, rows), 1)
    return jnp.where((column >= row) if reverse else (column <= row), 1.0, 0.0).astype(bf16)


def running_sum(ref, reverse):
    rows = chunk_rows
    ones = triangle(rows, reverse)
    count = ref.shape[0] // rows
    edge = 0 if reverse else rows - 1

    def chunk(i, carry):
        here = pl.ds(pl.multiple_of((count - 1 - i if reverse else i) * rows, rows), rows)
        high, middle, lowest = three_parts(ref[here, :])
        total = dot_nn(ones, high) + dot_nn(ones, middle) + dot_nn(ones, lowest) + carry
        ref[here, :] = total
        return total[edge : edge + 1, :]

    lax.fori_loop(0, count, chunk, jnp.zeros((1, ref.shape[1]), f32), unroll=count <= 4)


def log_sigmoid(z):
    e = jnp.exp(-jnp.abs(z))
    small = e * (1.0 - e * (1 / 2 - e * (1 / 3 - e * (1 / 4 - e * (1 / 5 - e * (1 / 6 - e * (1 / 7)))))))
    return jnp.minimum(z, 0.0) - jnp.where(e < 0.0625, small, jnp.log(1.0 + e))


def three_parts(x):
    high = x.astype(bf16)
    middle = (x - high.astype(f32)).astype(bf16)
    return high, middle, (x - high.astype(f32) - middle.astype(f32)).astype(bf16)


def decay_side(terms, pair, key_side):
    row = lax.broadcasted_iota(jnp.int32, (pair_lanes, pair_lanes), 0)
    lane = lax.broadcasted_iota(jnp.int32, (pair_lanes, pair_lanes), 1)
    spot = lane & 63
    term = spot if key_side else spot - 3
    head = jnp.where(lane >= 64, 2 * pair, 2 * pair + 1)
    chosen = (term >= 0) & (term < 3) & (row == 8 * term + head)
    pick = jnp.where(chosen, -1.0 if key_side else 1.0, 0.0).astype(bf16)
    lanes_now = lax.broadcasted_iota(jnp.int32, (1, pair_lanes), 1) & 63
    other = lanes_now - 3 if key_side else lanes_now
    ones = jnp.where((other >= 0) & (other < 3), 1.0, 0.0)
    return (dot_nn(terms, pick) + ones).astype(bf16)


def mix_keys(k_ref, terms_ref, pair, ka, kb):
    def mix(i):
        here = rows_at(i, chunk_rows)
        lane = lax.broadcasted_iota(jnp.int32, (chunk_rows, pair_lanes), 1)
        k, side = k_ref[here, :], decay_side(terms_ref[here, :], pair, True)
        ka[here, :] = jnp.where(lane < 64, k, side)
        kb[here, :] = jnp.where(lane < 64, side, k)

    each(k_ref.shape[0] // chunk_rows, mix)


def mix_queries(q_ref, terms_ref, start, pair, qa, qb):
    def mix(i):
        here = rows_at(i, chunk_rows)
        lane = lax.broadcasted_iota(jnp.int32, (chunk_rows, pair_lanes), 1)
        q = (q_ref[here, :].astype(f32) * 0.125).astype(bf16)
        terms = terms_ref[pl.ds(pl.multiple_of(start + i * chunk_rows, chunk_rows), chunk_rows), :]
        side = decay_side(terms, pair, False)
        qa[here, :] = jnp.where(lane < 64, q, side)
        qb[here, :] = jnp.where(lane < 64, side, q)

    each(q_ref.shape[0] // chunk_rows, mix)


def live_mask(start_ref, start, first, width, rows):
    key_pos = first + lax.broadcasted_iota(jnp.int32, (rows, width), 1)
    query_pos = start + lax.broadcasted_iota(jnp.int32, (rows, width), 0)
    doc_start = start_ref[pl.ds(start, rows), :]
    return (key_pos <= query_pos) & (key_pos >= doc_start)


def over_query_blocks(seq_len, rows, body):
    before = seq_len // 2
    if seq_len // rows <= 4:
        for start in range(0, seq_len, rows):
            first = max(0, start - before)
            body(start, first, start + rows - first)
        return
    width = before + rows

    def one(i, carry):
        start = pl.multiple_of(i * rows, rows)
        first = pl.multiple_of(jnp.maximum(start - before, 0), rows)
        body(start, first, width)
        return carry

    lax.fori_loop(0, seq_len // rows, one, 0)


def probabilities(q_rows, k_rows, mask):
    s = jnp.where(mask, dot_nt(q_rows, k_rows), masked_value)
    e = jnp.exp(s - jnp.max(s, axis=1, keepdims=True))
    return e * (1.0 / jnp.sum(e, axis=1, keepdims=True))


def lane_blocks(refs):
    return jnp.concatenate([r[0] for r in refs], axis=1)


def forward_own_kernel(count_parts, piece_len, join, *refs):
    place_ref, parts, refs = refs[0], refs[1 : 1 + count_parts], list(refs[1 + count_parts :])
    (wq, wk, wv, wg), (tq, tk, tv, tg) = refs[:4], refs[4:8]
    wo, to, wf, bias, start_ref = refs[8:13]
    refs = refs[13:]
    a_ref = refs.pop(0) if join else parts[0]
    k_ref, v_ref, z_ref, terms_ref, send_ref, q_own, qa, qb, ka, kb, decay, acc = refs
    pair = pl.program_id(0)
    seq_len, half = a_ref.shape[0], a_ref.shape[1] // 2
    piece_start = pl.multiple_of(place_ref[0] * piece_len, piece_len)

    @pl.when(pair == 0)
    def _():
        if join:
            assemble(parts, a_ref, place_ref[0])
        acc[...] = jnp.zeros_like(acc)

        def gates(i):
            here = rows_at(i, chunk_rows)
            z = dot_nn(a_ref[here, :], wf[...]) + bias[...]
            z_ref[here, :] = z
            decay[here, :] = log_sigmoid(z)

        each(seq_len // chunk_rows, gates)
        running_sum(decay, False)

        def split(i):
            here = rows_at(i, chunk_rows)
            lane = lax.broadcasted_iota(jnp.int32, (chunk_rows, pair_lanes), 1)
            high, middle, lowest = (x.astype(f32) for x in three_parts(decay[here, :]))
            later = jnp.where(lane < 16, pltpu.roll(middle, 8, 1), pltpu.roll(lowest, 16, 1))
            terms = jnp.where(lane < 8, high, later)
            terms_ref[here, :] = jnp.where(lane < 24, terms, 0.0).astype(bf16)

        each(seq_len // chunk_rows, split)

    w_mine, w_theirs = lane_blocks((wk, wv)), lane_blocks((tk, tv))

    def project(i):
        here = rows_at(i, chunk_rows)
        out = dot_nn(a_ref[here, :half], w_mine) + dot_nn(a_ref[here, half:], w_theirs)
        k_ref[here, :] = out[:, :128].astype(bf16)
        v_ref[here, :] = out[:, 128:].astype(bf16)

    each(seq_len // chunk_rows, project)
    piece = pl.ds(piece_start, piece_len)
    out = dot_nn(a_ref[piece, :half], lane_blocks((wq, wg))) + dot_nn(a_ref[piece, half:], lane_blocks((tq, tg)))
    q_own[...] = out[:, :128].astype(bf16)
    gate = jax.nn.sigmoid(out[:, 128:])
    mix_keys(k_ref, terms_ref, pair, ka, kb)
    mix_queries(q_own, terms_ref, piece_start, pair, qa, qb)
    before = seq_len // 2
    for s in range(0, piece_len, query_rows(seq_len)):
        rows = query_rows(seq_len)
        width = before + rows
        start = pl.multiple_of(piece_start + s, rows)
        first = pl.multiple_of(jnp.maximum(start - before, 0), rows)
        mask = live_mask(start_ref, start, first, width, rows)
        keys = pl.ds(first, width)
        out = []
        for q_of, k_of in ((qa, ka), (qb, kb)):
            p = probabilities(q_of[s : s + rows, :], k_of[keys, :], mask).astype(bf16)
            out.append(dot_nn(p, v_ref[keys, :]))
        lane = lax.broadcasted_iota(jnp.int32, (rows, pair_lanes), 1)
        u = (jnp.where(lane < 64, out[0], out[1]) * gate[s : s + rows, :]).astype(bf16)
        acc[s : s + rows, :half] += dot_nn(u, wo[0])
        acc[s : s + rows, half:] += dot_nn(u, to[0])

    @pl.when(pair == pl.num_programs(0) - 1)
    def _():
        send_ref[...] = acc[...].astype(bf16)


def forward_rest_kernel(*refs):
    a_ref, wq, wg, tq, tg, k_ref, v_ref, terms_ref, start_ref = refs[:9]
    q_ref, gate_ref, o_ref, u_ref, qa, qb, ka, kb = refs[-8:]
    pair = pl.program_id(0)
    seq_len, half = a_ref.shape[0], a_ref.shape[1] // 2
    rows = query_rows(seq_len)
    w_mine, w_theirs = lane_blocks((wq, wg)), lane_blocks((tq, tg))

    def project(i):
        here = rows_at(i, chunk_rows)
        out = dot_nn(a_ref[here, :half], w_mine) + dot_nn(a_ref[here, half:], w_theirs)
        q_ref[here, :] = out[:, :128].astype(bf16)
        gate_ref[here, :] = out[:, 128:]

    each(seq_len // chunk_rows, project)
    mix_keys(k_ref, terms_ref, pair, ka, kb)
    mix_queries(q_ref, terms_ref, 0, pair, qa, qb)
    lane = lax.broadcasted_iota(jnp.int32, (rows, pair_lanes), 1)

    def body(start, first, width):
        mask = live_mask(start_ref, start, first, width, rows)
        here, keys = pl.ds(start, rows), pl.ds(first, width)
        values = v_ref[keys, :]
        out = []
        for q_of, k_of in ((qa, ka), (qb, kb)):
            p = probabilities(q_of[here, :], k_of[keys, :], mask).astype(bf16)
            out.append(dot_nn(p, values))
        o = jnp.where(lane < 64, out[0], out[1])
        o_ref[here, :] = o
        u_ref[here, :] = (o * jax.nn.sigmoid(gate_ref[here, :])).astype(bf16)

    over_query_blocks(seq_len, rows, body)


def backward_kernel(count_parts, piece_len, join, *refs):
    place_ref, parts, refs = refs[0], refs[1 : 1 + count_parts], list(refs[1 + count_parts :])
    mine, theirs, (wo, to, wf) = refs[:4], refs[4:8], refs[8:11]
    q_ref, k_ref, v_ref, gate_ref, o_ref, z_ref, terms_ref, start_ref = refs[11:19]
    refs = refs[19:]
    y_ref = refs.pop(0) if join else parts[0]
    dq_ref, dk_ref, dv_ref, dg_ref, dz_ref, send_ref = refs[:6]
    qa, qb, ka, kb, dd, dka, dkb, dva, dcs, acc = refs[6:]
    pair = pl.program_id(0)
    seq_len, half = y_ref.shape[0], y_ref.shape[1] // 2
    rows = query_rows(seq_len)
    piece = pl.ds(pl.multiple_of(place_ref[0] * piece_len, piece_len), piece_len)

    @pl.when(pair == 0)
    def _():
        if join:
            assemble(parts, y_ref, place_ref[0])
        acc[...] = jnp.zeros_like(acc)
        dcs[...] = jnp.zeros_like(dcs)

    def gates(i):
        here = rows_at(i, chunk_rows)
        du = dot_nt(y_ref[here, :half], wo[0]) + dot_nt(y_ref[here, half:], to[0])
        sig = jax.nn.sigmoid(gate_ref[here, :])
        dd[here, :] = (du * sig).astype(bf16)
        dg_ref[here, :] = (du * o_ref[here, :] * sig * (1.0 - sig)).astype(bf16)

    each(seq_len // chunk_rows, gates)
    mix_keys(k_ref, terms_ref, pair, ka, kb)
    mix_queries(q_ref, terms_ref, 0, pair, qa, qb)
    dka[...] = jnp.zeros_like(dka)
    dkb[...] = jnp.zeros_like(dkb)
    dva[...] = jnp.zeros_like(dva)
    lane = lax.broadcasted_iota(jnp.int32, (rows, pair_lanes), 1)

    def pick(column_a, column_b):
        at = lax.broadcasted_iota(jnp.int32, (column_a.shape[0], pair_lanes), 1)
        return jnp.where(at == 2 * pair, column_a, jnp.where(at == 2 * pair + 1, column_b, 0.0))

    def body(start, first, width):
        mask = live_mask(start_ref, start, first, width, rows)
        here, keys = pl.ds(start, rows), pl.ds(first, width)
        values = v_ref[keys, :]
        d_rows = dd[here, :]
        dq = []
        for head, (q_of, k_of, dk_of) in enumerate(((qa, ka, dka), (qb, kb, dkb))):
            own_lanes = (lane < 64) if head == 0 else (lane >= 64)
            p = probabilities(q_of[here, :], k_of[keys, :], mask)
            d_mine = jnp.where(own_lanes, d_rows, jnp.zeros_like(d_rows))
            dp = dot_nt(d_mine, values)
            delta = jnp.sum(p * dp, axis=1, keepdims=True)
            ds = (p * (dp - delta)).astype(bf16)
            dq.append(dot_nn(ds, k_of[keys, :]))
            dk_of[keys, :] += dot_tn(ds, q_of[here, :])
            dva[keys, :] += dot_tn(p.astype(bf16), d_mine)
        dq_ref[here, :] = (jnp.where(lane < 64, dq[0], dq[1]) * 0.125).astype(bf16)
        dcs[here, :] += pick(dq[0][:, 67:68], dq[1][:, 3:4])

    over_query_blocks(seq_len, rows, body)

    def finish(i):
        here = rows_at(i, chunk_rows)
        lanes_now = lax.broadcasted_iota(jnp.int32, (chunk_rows, pair_lanes), 1)
        ka_rows, kb_rows = dka[here, :], dkb[here, :]
        dk_ref[here, :] = jnp.where(lanes_now < 64, ka_rows, kb_rows).astype(bf16)
        dv_ref[here, :] = dva[here, :].astype(bf16)
        dcs[here, :] -= pick(ka_rows[:, 64:65], kb_rows[:, 0:1])

    each(seq_len // chunk_rows, finish)
    d_own = jnp.concatenate([r[piece, :] for r in (dq_ref, dk_ref, dv_ref, dg_ref)], axis=1)
    acc[:, :half] += dot_nt(d_own, lane_blocks(mine))
    acc[:, half:] += dot_nt(d_own, lane_blocks(theirs))

    @pl.when(pair == pl.num_programs(0) - 1)
    def _():
        running_sum(dcs, True)

        def last(i):
            here = rows_at(i, chunk_rows)
            dz_ref[here, :] = (dcs[here, :] * jax.nn.sigmoid(-z_ref[here, :])).astype(bf16)

        each(seq_len // chunk_rows, last)
        send_ref[...] = (acc[...] + dot_nt(dz_ref[piece, :], wf[...])).astype(bf16)


def ffn_forward_kernel(b_ref, wg, wu, wd, tg, tu, td, gt_ref, up_ref, send_ref, acc):
    half = b_ref.shape[1] // 2
    low, high = b_ref[:, :half], b_ref[:, half:]
    gt = dot_nn(low, wg[0]) + dot_nn(high, tg[0])
    up = dot_nn(low, wu[0]) + dot_nn(high, tu[0])
    gt_ref[...] = gt
    up_ref[...] = up
    m = (gt * jax.nn.sigmoid(gt) * up).astype(bf16)

    @pl.when(pl.program_id(0) == 0)
    def _():
        acc[...] = jnp.zeros_like(acc)

    acc[:, :half] += dot_nn(m, wd[0])
    acc[:, half:] += dot_nn(m, td[0])

    @pl.when(pl.program_id(0) == pl.num_programs(0) - 1)
    def _():
        send_ref[...] = acc[...].astype(bf16)


def inner_grads(dm, gt, up):
    sig = jax.nn.sigmoid(gt)
    d_gate = (dm * up * sig * (1.0 + gt * (1.0 - sig))).astype(bf16)
    return d_gate, (dm * (gt * sig)).astype(bf16)


def ffn_backward_kernel(g_ref, gt_ref, up_ref, wg, wu, wd, tg, tu, td, send_ref, acc):
    half = g_ref.shape[1] // 2
    dm = dot_nt(g_ref[:, :half], wd[0]) + dot_nt(g_ref[:, half:], td[0])
    d_gate, d_up = inner_grads(dm, gt_ref[...], up_ref[...])

    @pl.when(pl.program_id(0) == 0)
    def _():
        acc[...] = jnp.zeros_like(acc)

    acc[:, :half] += dot_nt(d_gate, wg[0]) + dot_nt(d_up, wu[0])
    acc[:, half:] += dot_nt(d_gate, tg[0]) + dot_nt(d_up, tu[0])

    @pl.when(pl.program_id(0) == pl.num_programs(0) - 1)
    def _():
        send_ref[...] = acc[...].astype(bf16)


def ffn_inner_kernel(count_parts, *refs):
    place_ref, refs = refs[0], refs[1:]
    b_parts, g_parts = refs[:count_parts], refs[count_parts : 2 * count_parts]
    wg, wu, wd, tg, tu, td = refs[2 * count_parts : 2 * count_parts + 6]
    b_ref, g_ref, m_ref, dgate_ref, dup_ref = refs[-5:]
    half = b_ref.shape[1] // 2

    @pl.when(pl.program_id(0) == 0)
    def _():
        assemble(b_parts, b_ref, place_ref[0])
        assemble(g_parts, g_ref, place_ref[0])

    def chunk(i):
        here = rows_at(i, chunk_rows)
        low, high = b_ref[here, :half], b_ref[here, half:]
        gt = dot_nn(low, wg[0]) + dot_nn(high, tg[0])
        up = dot_nn(low, wu[0]) + dot_nn(high, tu[0])
        dm = dot_nt(g_ref[here, :half], wd[0]) + dot_nt(g_ref[here, half:], td[0])
        m_ref[here, :] = (gt * jax.nn.sigmoid(gt) * up).astype(bf16)
        dgate_ref[here, :], dup_ref[here, :] = inner_grads(dm, gt, up)

    each(b_ref.shape[0] // chunk_rows, chunk)


def fixed(shape, single=True):
    zeros = (0,) * len(shape)
    if single:
        return pl.BlockSpec(shape, lambda *_: zeros, pipeline_mode=pl.Buffered(1))
    return pl.BlockSpec(shape, lambda *_: zeros)


def lanes(seq_len):
    return pl.BlockSpec((seq_len, pair_lanes), lambda p, *_: (0, p))


def lanes_read(seq_len):
    if seq_len <= 2048:
        return lanes(seq_len)
    return pl.BlockSpec((seq_len, pair_lanes), lambda p, *_: (0, p), pipeline_mode=pl.Buffered(1))


def columns_of(w, layer, width):
    return pl.BlockSpec((1, w.shape[1], width), lambda p, *_: (layer, 0, p))


def rows_of(w, layer, height):
    return pl.BlockSpec((1, height, w.shape[2]), lambda p, *_: (layer, p, 0))


def shape(dims, dtype):
    return jax.ShapeDtypeStruct(dims, dtype)


def attention_specs(parts, layer, w4, t4, wo, to, seq_len, join):
    specs = [fixed(p.shape) for p in parts]
    specs += [columns_of(w, layer, pair_lanes) for w in (*w4, *t4)]
    specs += [rows_of(wo, layer, pair_lanes), rows_of(to, layer, pair_lanes)]
    return specs


def cost(microseconds):
    return pl.CostEstimate(flops=int(microseconds * 1.1e9), bytes_accessed=0, transcendentals=0)


def token_specs(tokens):
    return [pl.BlockSpec((16, 128), lambda *_: (0, 0)) for _ in tokens]


def forward_own(place, parts, layer, w4, t4, wo, to, wf, bias, doc_start, piece_len):
    seq_len, width = doc_start.shape[0], parts[0].shape[1]
    local_width = wo.shape[1]
    join = len(parts) > 1
    terms = (seq_len, pair_lanes)
    outs = [shape((seq_len, local_width), bf16)] * 2 + [shape(terms, f32), shape(terms, bf16)]
    outs += [shape((piece_len, width), bf16)]
    specs = [lanes(seq_len)] * 2 + [fixed(terms, False)] * 2 + [fixed((piece_len, width), False)]
    if join:
        outs, specs = [shape((seq_len, width), bf16)] + outs, [fixed((seq_len, width))] + specs
    low, piece = pltpu.VMEM((seq_len, pair_lanes), bf16), pltpu.VMEM((piece_len, pair_lanes), bf16)
    got = pl.pallas_call(
        functools.partial(forward_own_kernel, len(parts), piece_len, join),
        grid_spec=pltpu.PrefetchScalarGridSpec(
            num_scalar_prefetch=1,
            grid=(local_width // pair_lanes,),
            in_specs=attention_specs(parts, layer, w4, t4, wo, to, seq_len, join)
            + [fixed(wf.shape), fixed(bias.shape), fixed(doc_start.shape)],
            out_specs=specs,
            scratch_shapes=[piece] * 3 + [low] * 2 + [pltpu.VMEM(terms, f32), pltpu.VMEM((piece_len, width), f32)],
        ),
        out_shape=outs,
        cost_estimate=cost(14),
        compiler_params=pltpu.CompilerParams(vmem_limit_bytes=60 << 20),
    )(place, *parts, *w4, *t4, wo, to, wf, bias, doc_start)
    got = list(got)
    a = got.pop(0) if join else parts[0]
    return a, got[:4], got[4]


def forward_rest(a, layer, w4, t4, k, v, terms, doc_start, *tokens):
    seq_len = a.shape[0]
    local_width = k.shape[1]
    low, high = shape((seq_len, local_width), bf16), shape((seq_len, local_width), f32)
    weights = (w4[0], w4[3], t4[0], t4[3])
    return pl.pallas_call(
        forward_rest_kernel,
        grid=(local_width // pair_lanes,),
        in_specs=[fixed(a.shape)]
        + [columns_of(w, layer, pair_lanes) for w in weights]
        + [lanes_read(seq_len)] * 2
        + [fixed(terms.shape), fixed(doc_start.shape)]
        + token_specs(tokens),
        out_specs=[lanes(seq_len)] * 4,
        scratch_shapes=[pltpu.VMEM((seq_len, pair_lanes), bf16)] * 4,
        out_shape=[low, high, high, low],
        cost_estimate=cost(20),
        compiler_params=pltpu.CompilerParams(vmem_limit_bytes=60 << 20),
    )(a, *weights, k, v, terms, doc_start, *tokens)


def attention_backward(place, parts, layer, w4, t4, wo, to, wf, saved, doc_start, piece_len):
    q, k, v, gate, o, z, terms = saved
    seq_len, width = doc_start.shape[0], parts[0].shape[1]
    local_width = wo.shape[1]
    join = len(parts) > 1
    outs = [shape((seq_len, local_width), bf16)] * 4 + [shape((seq_len, pair_lanes), bf16)]
    outs += [shape((piece_len, width), bf16)]
    specs = [lanes(seq_len)] * 4 + [fixed((seq_len, pair_lanes), False), fixed((piece_len, width), False)]
    if join:
        outs, specs = [shape((seq_len, width), bf16)] + outs, [fixed((seq_len, width))] + specs
    low, high = pltpu.VMEM((seq_len, pair_lanes), bf16), pltpu.VMEM((seq_len, pair_lanes), f32)
    got = pl.pallas_call(
        functools.partial(backward_kernel, len(parts), piece_len, join),
        grid_spec=pltpu.PrefetchScalarGridSpec(
            num_scalar_prefetch=1,
            grid=(local_width // pair_lanes,),
            in_specs=attention_specs(parts, layer, w4, t4, wo, to, seq_len, join)
            + [fixed(wf.shape)]
            + [lanes_read(seq_len)] * 5
            + [fixed(z.shape), fixed(terms.shape), fixed(doc_start.shape)],
            out_specs=specs,
            scratch_shapes=[low] * 5 + [high] * 4 + [pltpu.VMEM((piece_len, width), f32)],
        ),
        out_shape=outs,
        cost_estimate=cost(32),
        compiler_params=pltpu.CompilerParams(vmem_limit_bytes=60 << 20),
    )(place, *parts, *w4, *t4, wo, to, wf, q, k, v, gate, o, z, terms, doc_start)
    got = list(got)
    y = got.pop(0) if join else parts[0]
    return y, got[:5], got[5]


def ffn_weights(layer, w3, t3):
    specs = []
    for wg, wu, wd in (w3, t3):
        specs += [
            columns_of(wg, layer, hidden_block), columns_of(wu, layer, hidden_block), rows_of(wd, layer, hidden_block),
        ]
    return specs


def blocks_of(rows):
    return pl.BlockSpec((rows, hidden_block), lambda p, *_: (0, p))


def ffn_forward(b, layer, w3, t3):
    rows, width = b.shape
    inner = w3[2].shape[1]
    return pl.pallas_call(
        ffn_forward_kernel,
        grid=(inner // hidden_block,),
        in_specs=[fixed(b.shape)] + ffn_weights(layer, w3, t3),
        out_specs=[blocks_of(rows)] * 2 + [fixed((rows, width), False)],
        scratch_shapes=[pltpu.VMEM((rows, width), f32)],
        out_shape=[shape((rows, inner), f32)] * 2 + [shape((rows, width), bf16)],
        cost_estimate=cost(7),
        compiler_params=pltpu.CompilerParams(vmem_limit_bytes=40 << 20),
    )(b, *w3, *t3)


def ffn_backward(g, gt, up, layer, w3, t3):
    rows, width = g.shape
    return pl.pallas_call(
        ffn_backward_kernel,
        grid=(gt.shape[1] // hidden_block,),
        in_specs=[fixed(g.shape)] + [blocks_of(rows)] * 2 + ffn_weights(layer, w3, t3),
        out_specs=fixed((rows, width), False),
        scratch_shapes=[pltpu.VMEM((rows, width), f32)],
        out_shape=shape((rows, width), bf16),
        cost_estimate=cost(8),
        compiler_params=pltpu.CompilerParams(vmem_limit_bytes=40 << 20),
    )(g, gt, up, *w3, *t3)


def ffn_inner(place, b_parts, g_parts, layer, w3, t3, *tokens):
    width = b_parts[0].shape[1]
    rows = sum(p.size for p in b_parts) // width
    inner = w3[2].shape[1]
    return pl.pallas_call(
        functools.partial(ffn_inner_kernel, len(b_parts)),
        grid_spec=pltpu.PrefetchScalarGridSpec(
            num_scalar_prefetch=1,
            grid=(inner // hidden_block,),
            in_specs=[fixed(p.shape) for p in (*b_parts, *g_parts)]
            + ffn_weights(layer, w3, t3)
            + token_specs(tokens),
            out_specs=[fixed((rows, width))] * 2 + [blocks_of(rows)] * 3,
        ),
        out_shape=[shape((rows, width), bf16)] * 2 + [shape((rows, inner), bf16)] * 3,
        cost_estimate=cost(16),
        compiler_params=pltpu.CompilerParams(vmem_limit_bytes=56 << 20),
    )(place, *b_parts, *g_parts, *w3, *t3, *tokens)


def unset_kernel(*refs):
    pass


def unset(*like):
    return pl.pallas_call(
        unset_kernel,
        out_specs=[pl.BlockSpec(memory_space=pl.ANY) for _ in like],
        out_shape=list(like),
    )()


def inverse_rms(h):
    return lax.rsqrt(jnp.mean(h * h, axis=-1, keepdims=True) + epsilon)


def norm_back(grad_normed, hidden, inverse, gain):
    scaled = hidden * inverse
    weighted = grad_normed * gain
    grad_gain = jnp.sum(grad_normed * scaled, axis=0)
    mean = jnp.mean(weighted * scaled, axis=-1, keepdims=True)
    return inverse * (weighted - scaled * mean), grad_gain


def local(
    hidden_in, segment_ids, w_query, w_key, w_value, w_gate_out, w_attn_out, w_forget, b_forget,
    gain_attn, gain_ffn, w_gate, w_up, w_down, cotangent,
):
    seq_count, piece_len, width = hidden_in.shape
    count_z, count_t = lax.axis_size("context"), lax.axis_size("tensor")
    core, z, t = lax.axis_index("fsdp"), lax.axis_index("context"), lax.axis_index("tensor")
    layers, half, local_width = w_query.shape
    heads = w_forget.shape[2]
    block = piece_len // count_t
    seq_len = piece_len * count_z
    shared_rows = count_z == 4
    place = z.reshape(1).astype(jnp.int32)
    own_place = place if shared_rows else jnp.zeros((1,), jnp.int32)

    def features(x):
        return jnp.where(core == 0, x, jnp.concatenate([x[..., half:], x[..., :half]], axis=-1))

    def own_block(x):
        return lax.dynamic_slice_in_dim(x, t * block, block, 0)

    def other(w):
        return swap(w, "fsdp", 1)

    def full(w, axis):
        return jnp.concatenate([w, other(w)], axis=axis)

    seg_all = gathered(segment_ids.reshape(1, piece_len), "context").reshape(seq_len)
    doc_start = jnp.sum((seg_all[None, :] < seg_all[:, None]).astype(jnp.int32), axis=1, keepdims=True)

    gains = full(jnp.concatenate([gain_attn, gain_ffn], axis=0), 1).astype(f32)
    hidden_rows = features(hidden_in.reshape(piece_len, width)).astype(f32)
    first_a = (hidden_rows * inverse_rms(hidden_rows) * gains[0]).astype(bf16)
    first_a = after(first_a, seg_all.reshape(1, seq_len))
    a_parts = all_rows(own_block(first_a), first_a)

    w_forget_full = jnp.pad(full(w_forget, 1), ((0, 0), (0, 0), (0, pair_lanes - heads)))
    bias = jnp.pad(b_forget, ((0, 0), (0, pair_lanes - heads)))
    w4 = (w_query, w_key, w_value, w_gate_out)
    t4 = tuple(other(w) for w in w4)
    to = other(w_attn_out)
    w3 = (w_gate, w_up, w_down)
    t3 = tuple(other(w) for w in w3)

    hidden = own_block(hidden_rows)
    saved = []
    cotangent_rows = features(cotangent.reshape(piece_len, width))
    for layer in range(layers):
        gain_one, gain_two = gains[layer], gains[layers + layer]
        inverse_one = inverse_rms(hidden)
        if layer > 0:
            a_parts = all_rows((hidden * inverse_one * gain_one).astype(bf16))
        a, (k, v, forget, terms), sends = forward_own(
            place, a_parts, layer, w4, t4, w_attn_out, to, w_forget_full[layer],
            bias[layer : layer + 1], doc_start, piece_len,
        )
        if shared_rows:
            if layer == 0:
                g_last = all_rows(own_block(cotangent_rows), cotangent_rows, a_parts[-1])
            else:
                before = saved[-1]
                before["b_parts"] = all_rows(before["b_shard"], before["b"], a_parts[-1])
        mixed = hidden + received_sum(sends)
        inverse_two = inverse_rms(mixed)
        b_shard = (mixed * inverse_two * gain_two).astype(bf16)
        b = gathered(b_shard, "tensor")
        gt, up, sends = ffn_forward(b, layer, w3, t3)
        saved.append(
            dict(hidden=hidden, inverse_one=inverse_one, a=a, k=k, v=v, forget=forget, terms=terms, mixed=mixed,
                 inverse_two=inverse_two, b=b, b_shard=b_shard, gt=gt, up=up)
        )
        if layer < layers - 1:
            hidden = mixed + received_sum(sends)

    def finish(x):
        return features(gathered(x.astype(bf16), "tensor")).reshape(1, piece_len, width)

    last_sends = sends
    grad = own_block(cotangent_rows).astype(f32)
    wide = shape((layers, half, local_width), f32)
    inner = shape((layers, half, w_gate.shape[2]), f32)
    results = list(
        unset(
            wide, wide, wide, wide, shape((layers, local_width, half), f32),
            inner, inner, shape((layers, w_down.shape[1], half), f32),
        )
    )
    small = [[None] * layers for _ in range(2)]
    gain_grads = [None] * (2 * layers)

    for layer in reversed(range(layers)):
        s = saved[layer]
        gain_one, gain_two = gains[layer], gains[layers + layer]
        g_shard = grad.astype(bf16)
        g = cotangent_rows if layer == layers - 1 else gathered(g_shard, "tensor")
        sends = ffn_backward(g, s["gt"], s["up"], layer, w3, t3)
        back, gain_grads[layers + layer] = norm_back(received_sum(sends), s["mixed"], s["inverse_two"], gain_two)
        grad_mixed = grad + back
        y_shard = grad_mixed.astype(bf16)
        if layer == layers - 1:
            rest_token = y_shard
        y_parts = all_rows(y_shard)
        q, gate, o, u = forward_rest(s["a"], layer, w4, t4, s["k"], s["v"], s["terms"], doc_start, rest_token)
        y, (dq, dk, dv, dg, dz), sends = attention_backward(
            place, y_parts, layer, w4, t4, w_attn_out, to, w_forget_full[layer],
            (q, s["k"], s["v"], gate, o, s["forget"], s["terms"]), doc_start, piece_len,
        )
        if not shared_rows:
            b_parts, g_parts = (s["b"],), (g,)
        elif layer == layers - 1:
            b_parts, g_parts = all_rows(s["b_shard"], s["b"], y_parts[-1]), g_last
        else:
            b_parts, g_parts = s["b_parts"], all_rows(g_shard, g, y_parts[-1])
        if layer == layers - 1:
            output = finish(s["mixed"] + received_sum(after(last_sends, y_parts[-1])))
        back, gain_grads[layer] = norm_back(received_sum(sends), s["hidden"], s["inverse_one"], gain_one)
        grad = grad_mixed + back
        s.update(u=u, y=y, d=(dq, dk, dv, dg), dz=dz, b_parts=b_parts, g_parts=g_parts, y_shard=y_shard)

    def weight_grads(layer, token):
        s = saved[layer]
        b, g, m, d_gate, d_up = ffn_inner(own_place, s["b_parts"], s["g_parts"], layer, w3, t3, token)

        def put(k, mine, theirs):
            total = mine + other(theirs).astype(f32)
            if k >= 5 and not shared_rows:
                total = lax.psum(total, "context")
            results[k] = lax.dynamic_update_slice_in_dim(results[k], total[None], layer, 0)

        def by_rows(k, x, d):
            put(k, dot_tn(x[:, :half], d), dot_tn(x[:, half:], d).astype(bf16))

        def by_columns(k, x, d):
            put(k, dot_tn(x, d[:, :half]), dot_tn(x, d[:, half:]).astype(bf16))

        a = s["a"]
        for k, d in enumerate(s["d"]):
            by_rows(k, a, d)
        by_columns(4, s["u"], s["y"])
        by_rows(5, b, d_gate)
        by_rows(6, b, d_up)
        by_columns(7, m, g)
        dzr = s["dz"][:, :heads]
        bias_grad = jnp.sum(dzr.astype(f32), axis=0)
        small[0][layer] = dot_tn(a[:, :half], dzr) + other(dot_tn(a[:, half:], dzr))
        small[1][layer] = bias_grad + other(bias_grad)

    for layer in reversed(range(layers)):
        weight_grads(layer, saved[max(layer - 1, 0)]["y_shard"])
    grad_input = finish(grad)
    gain_total = sum_over(sum_over(jnp.stack(gain_grads), "tensor"), "context")
    gain_total = gain_total[:, :half] + other(gain_total[:, half:])
    return (
        output, grad_input, *results[:5], jnp.stack(small[0]), jnp.stack(small[1]),
        gain_total[:layers], gain_total[layers:], *results[5:],
    )


def solution(mesh):
    rows = P("fsdp", "context", None)
    wide, tall = P(None, "fsdp", "tensor"), P(None, "tensor", "fsdp")
    heads, gain = P(None, "tensor"), P(None, "fsdp")
    return jax.shard_map(
        local,
        mesh=mesh,
        in_specs=(
            rows, P("fsdp", "context"), wide, wide, wide, wide, tall, wide, heads, gain, gain, wide, wide, tall, rows,
        ),
        out_specs=(rows, rows, wide, wide, wide, wide, tall, wide, heads, gain, gain, wide, wide, tall),
        check_vma=False,
    )
```

```python
import functools

import jax
import jax.numpy as jnp
from jax import lax
from jax.experimental import pallas as pl
from jax.experimental.pallas import tpu as pltpu
from jax.sharding import PartitionSpec as P

epsilon = 1e-06
masked_value = -1e30
bf16 = jnp.bfloat16
f32 = jnp.float32
pair_lanes = 128
hidden_block = 256
chunk_rows = 256


def query_rows(seq_len):
    return 256 if seq_len <= 2048 else 128


def swap(x, axis, k):
    n = lax.axis_size(axis)
    return lax.ppermute(x, axis, [(i, i ^ k) for i in range(n)])


def after(x, *tokens):
    for token in tokens:
        if token is not None:
            first = lax.slice(token, (0,) * token.ndim, (1,) * token.ndim).reshape(1, 1)
            x = x + (first.astype(f32) * 0.0).astype(x.dtype)
    return x


def gathered(block, axis):
    count = lax.axis_size(axis)
    copies = jnp.broadcast_to(block[None], (count,) + block.shape)
    return lax.all_to_all(copies, axis, 0, 0, tiled=True).reshape((-1,) + block.shape[1:])


def over_context(shard, own):
    if lax.axis_size("context") != 4:
        return (lax.all_gather(own, "context", tiled=True),)
    return swap(own, "context", 1), swap(shard, "context", 2), swap(shard, "context", 3)


def all_rows(shard, own=None, token=None, together=False):
    if own is None:
        own = gathered(shard, "tensor")
    if lax.axis_size("context") != 4:
        return over_context(shard, own)
    near, second, third = over_context(shard, own)
    if together:
        return all_rows_later(own, (near, second, third), token)
    second, third = after(second, token), after(third, second)
    blocks = [second] + [swap(second, "tensor", k) for k in range(1, lax.axis_size("tensor"))]
    return (own, near, *blocks, gathered(third, "tensor"))


def all_rows_later(own, sent, token):
    near, second, third = sent
    block, width = second.shape
    both = gathered(after(jnp.concatenate([second, third], axis=0), token), "tensor")
    return own, near, both.reshape(-1, 2, block, width)


def received_sum(sends):
    count = lax.axis_size("tensor")
    got = lax.all_to_all(sends.reshape(count, -1, sends.shape[1]), "tensor", 0, 0, tiled=True)
    return jnp.sum(got.astype(f32), axis=0)


def sum_over(x, axis):
    total = x
    for k in range(1, lax.axis_size(axis)):
        total = total + swap(x, axis, k)
    return total


def dot_nt(a, b):
    return lax.dot_general(a, b, (((1,), (1,)), ((), ())), preferred_element_type=f32)


def dot_tn(a, b):
    return lax.dot_general(a, b, (((0,), (0,)), ((), ())), preferred_element_type=f32)


def dot_nn(a, b):
    return jnp.dot(a, b, preferred_element_type=f32)


def each(count, body):
    if count <= 4:
        for i in range(count):
            body(i)
        return

    def one(i, carry):
        body(i)
        return carry

    lax.fori_loop(0, count, one, 0)


def rows_at(i, rows):
    start = i * rows
    return pl.ds(start if isinstance(start, int) else pl.multiple_of(start, rows), rows)


def assemble(parts, whole_ref, place_ref):
    z, t = place_ref[0], place_ref[1]
    piece, blocks_seen, piece_len = 0, 0, parts[0].shape[0]
    for part in parts:
        if len(part.shape) == 4:
            blocks, pieces, block = part.shape[:3]
            for p in range(pieces):
                for b in range(blocks):
                    at = pl.multiple_of((z ^ (piece + p)) * piece_len + b * block, block)
                    whole_ref[pl.ds(at, block), :] = part[b, p]
            piece += pieces
            continue
        rows = part.shape[0]
        if rows == piece_len:
            at = pl.multiple_of((z ^ piece) * piece_len, piece_len)
            piece += 1
        else:
            at = pl.multiple_of((z ^ piece) * piece_len + (t ^ blocks_seen) * rows, rows)
            blocks_seen += 1
            if blocks_seen * rows == piece_len:
                piece, blocks_seen = piece + 1, 0
        whole_ref[pl.ds(at, rows), :] = part[...]


def triangle(rows, reverse):
    row = lax.broadcasted_iota(jnp.int32, (rows, rows), 0)
    column = lax.broadcasted_iota(jnp.int32, (rows, rows), 1)
    return jnp.where((column >= row) if reverse else (column <= row), 1.0, 0.0).astype(bf16)


def running_sum(ref, reverse):
    rows = chunk_rows
    ones = triangle(rows, reverse)
    count = ref.shape[0] // rows
    edge = 0 if reverse else rows - 1

    def chunk(i, carry):
        here = pl.ds(pl.multiple_of((count - 1 - i if reverse else i) * rows, rows), rows)
        high, middle, lowest = three_parts(ref[here, :])
        total = dot_nn(ones, high) + dot_nn(ones, middle) + dot_nn(ones, lowest) + carry
        ref[here, :] = total
        return total[edge : edge + 1, :]

    lax.fori_loop(0, count, chunk, jnp.zeros((1, ref.shape[1]), f32), unroll=count <= 4)


def log_sigmoid(z):
    e = jnp.exp(-jnp.abs(z))
    small = e * (1.0 - e * (1 / 2 - e * (1 / 3 - e * (1 / 4 - e * (1 / 5 - e * (1 / 6 - e * (1 / 7)))))))
    return jnp.minimum(z, 0.0) - jnp.where(e < 0.0625, small, jnp.log(1.0 + e))


def three_parts(x):
    high = x.astype(bf16)
    middle = (x - high.astype(f32)).astype(bf16)
    return high, middle, (x - high.astype(f32) - middle.astype(f32)).astype(bf16)


def decay_side(terms, pair, key_side):
    row = lax.broadcasted_iota(jnp.int32, (pair_lanes, pair_lanes), 0)
    lane = lax.broadcasted_iota(jnp.int32, (pair_lanes, pair_lanes), 1)
    spot = lane & 63
    term = spot if key_side else spot - 3
    head = jnp.where(lane >= 64, 2 * pair, 2 * pair + 1)
    chosen = (term >= 0) & (term < 3) & (row == 8 * term + head)
    pick = jnp.where(chosen, -1.0 if key_side else 1.0, 0.0).astype(bf16)
    lanes_now = lax.broadcasted_iota(jnp.int32, (1, pair_lanes), 1) & 63
    other = lanes_now - 3 if key_side else lanes_now
    ones = jnp.where((other >= 0) & (other < 3), 1.0, 0.0)
    return (dot_nn(terms, pick) + ones).astype(bf16)


def mix_keys(k_ref, terms_ref, pair, ka, kb):
    def mix(i):
        here = rows_at(i, chunk_rows)
        lane = lax.broadcasted_iota(jnp.int32, (chunk_rows, pair_lanes), 1)
        k, side = k_ref[here, :], decay_side(terms_ref[here, :], pair, True)
        ka[here, :] = jnp.where(lane < 64, k, side)
        kb[here, :] = jnp.where(lane < 64, side, k)

    each(k_ref.shape[0] // chunk_rows, mix)


def mix_queries(q_ref, terms_ref, start, pair, qa, qb):
    def mix(i):
        here = rows_at(i, chunk_rows)
        lane = lax.broadcasted_iota(jnp.int32, (chunk_rows, pair_lanes), 1)
        q = (q_ref[here, :].astype(f32) * 0.125).astype(bf16)
        terms = terms_ref[pl.ds(pl.multiple_of(start + i * chunk_rows, chunk_rows), chunk_rows), :]
        side = decay_side(terms, pair, False)
        qa[here, :] = jnp.where(lane < 64, q, side)
        qb[here, :] = jnp.where(lane < 64, side, q)

    each(q_ref.shape[0] // chunk_rows, mix)


def live_mask(start_ref, start, first, width, rows):
    key_pos = first + lax.broadcasted_iota(jnp.int32, (rows, width), 1)
    query_pos = start + lax.broadcasted_iota(jnp.int32, (rows, width), 0)
    doc_start = start_ref[pl.ds(start, rows), :]
    return (key_pos <= query_pos) & (key_pos >= doc_start)


def over_query_blocks(seq_len, rows, body):
    before = seq_len // 2
    if seq_len // rows <= 4:
        for start in range(0, seq_len, rows):
            first = max(0, start - before)
            body(start, first, start + rows - first)
        return
    width = before + rows

    def one(i, carry):
        start = pl.multiple_of(i * rows, rows)
        first = pl.multiple_of(jnp.maximum(start - before, 0), rows)
        body(start, first, width)
        return carry

    lax.fori_loop(0, seq_len // rows, one, 0)


def probabilities(q_rows, k_rows, mask):
    s = jnp.where(mask, dot_nt(q_rows, k_rows), masked_value)
    e = jnp.exp(s - jnp.max(s, axis=1, keepdims=True))
    return e * (1.0 / jnp.sum(e, axis=1, keepdims=True))


def lane_blocks(refs):
    return jnp.concatenate([r[0] for r in refs], axis=1)


def forward_own_kernel(count_parts, piece_len, join, *refs):
    place_ref, parts, refs = refs[0], refs[1 : 1 + count_parts], list(refs[1 + count_parts :])
    (wq, wk, wv, wg), (tq, tk, tv, tg) = refs[:4], refs[4:8]
    wo, to, wf, bias, start_ref = refs[8:13]
    refs = refs[13:]
    a_ref = refs.pop(0) if join else parts[0]
    q_ref, k_ref, v_ref, gate_ref, z_ref, terms_ref, send_ref, qa, qb, ka, kb, decay, acc = refs
    pair = pl.program_id(0)
    seq_len, half = a_ref.shape[0], a_ref.shape[1] // 2
    piece_start = pl.multiple_of(place_ref[0] * piece_len, piece_len)

    @pl.when(pair == 0)
    def _():
        if join:
            assemble(parts, a_ref, place_ref)
        acc[...] = jnp.zeros_like(acc)

        def gates(i):
            here = rows_at(i, chunk_rows)
            z = dot_nn(a_ref[here, :], wf[...]) + bias[...]
            z_ref[here, :] = z
            decay[here, :] = log_sigmoid(z)

        each(seq_len // chunk_rows, gates)
        running_sum(decay, False)

        def split(i):
            here = rows_at(i, chunk_rows)
            lane = lax.broadcasted_iota(jnp.int32, (chunk_rows, pair_lanes), 1)
            high, middle, lowest = (x.astype(f32) for x in three_parts(decay[here, :]))
            later = jnp.where(lane < 16, pltpu.roll(middle, 8, 1), pltpu.roll(lowest, 16, 1))
            terms = jnp.where(lane < 8, high, later)
            terms_ref[here, :] = jnp.where(lane < 24, terms, 0.0).astype(bf16)

        each(seq_len // chunk_rows, split)

    w_mine, w_theirs = lane_blocks((wq, wk, wv, wg)), lane_blocks((tq, tk, tv, tg))

    def project(i):
        here = rows_at(i, chunk_rows)
        out = dot_nn(a_ref[here, :half], w_mine) + dot_nn(a_ref[here, half:], w_theirs)
        q_ref[here, :] = out[:, :128].astype(bf16)
        k_ref[here, :] = out[:, 128:256].astype(bf16)
        v_ref[here, :] = out[:, 256:384].astype(bf16)
        gate_ref[here, :] = out[:, 384:]

    each(seq_len // chunk_rows, project)
    piece = pl.ds(piece_start, piece_len)
    gate = jax.nn.sigmoid(gate_ref[piece, :])
    mix_keys(k_ref, terms_ref, pair, ka, kb)
    mix_queries(q_ref.at[piece, :], terms_ref, piece_start, pair, qa, qb)
    before = seq_len // 2
    for s in range(0, piece_len, query_rows(seq_len)):
        rows = query_rows(seq_len)
        width = before + rows
        start = pl.multiple_of(piece_start + s, rows)
        first = pl.multiple_of(jnp.maximum(start - before, 0), rows)
        mask = live_mask(start_ref, start, first, width, rows)
        keys = pl.ds(first, width)
        out = []
        for q_of, k_of in ((qa, ka), (qb, kb)):
            p = probabilities(q_of[s : s + rows, :], k_of[keys, :], mask).astype(bf16)
            out.append(dot_nn(p, v_ref[keys, :]))
        lane = lax.broadcasted_iota(jnp.int32, (rows, pair_lanes), 1)
        u = (jnp.where(lane < 64, out[0], out[1]) * gate[s : s + rows, :]).astype(bf16)
        acc[s : s + rows, :half] += dot_nn(u, wo[0])
        acc[s : s + rows, half:] += dot_nn(u, to[0])

    @pl.when(pair == pl.num_programs(0) - 1)
    def _():
        send_ref[...] = acc[...].astype(bf16)


def backward_kernel(count_parts, piece_len, join, *refs):
    place_ref, parts, refs = refs[0], refs[1 : 1 + count_parts], list(refs[1 + count_parts :])
    mine, theirs, (wo, to, wf) = refs[:4], refs[4:8], refs[8:11]
    q_ref, k_ref, v_ref, gate_ref, z_ref, terms_ref, start_ref = refs[11:18]
    refs = refs[18:]
    y_ref = refs.pop(0) if join else parts[0]
    dq_ref, dk_ref, dv_ref, dg_ref, u_ref, dz_ref, send_ref = refs[:7]
    qa, qb, ka, kb, dd, dus, dka, dkb, dva, dcs, acc = refs[7:]
    pair = pl.program_id(0)
    seq_len, half = y_ref.shape[0], y_ref.shape[1] // 2
    rows = query_rows(seq_len)
    piece = pl.ds(pl.multiple_of(place_ref[0] * piece_len, piece_len), piece_len)

    @pl.when(pair == 0)
    def _():
        if join:
            assemble(parts, y_ref, place_ref)
        acc[...] = jnp.zeros_like(acc)
        dcs[...] = jnp.zeros_like(dcs)

    def gates(i):
        here = rows_at(i, chunk_rows)
        du = dot_nt(y_ref[here, :half], wo[0]) + dot_nt(y_ref[here, half:], to[0])
        sig = jax.nn.sigmoid(gate_ref[here, :])
        dd[here, :] = (du * sig).astype(bf16)
        dus[here, :] = du * sig * (1.0 - sig)

    each(seq_len // chunk_rows, gates)
    mix_keys(k_ref, terms_ref, pair, ka, kb)
    mix_queries(q_ref, terms_ref, 0, pair, qa, qb)
    dka[...] = jnp.zeros_like(dka)
    dkb[...] = jnp.zeros_like(dkb)
    dva[...] = jnp.zeros_like(dva)
    lane = lax.broadcasted_iota(jnp.int32, (rows, pair_lanes), 1)

    def pick(column_a, column_b):
        at = lax.broadcasted_iota(jnp.int32, (column_a.shape[0], pair_lanes), 1)
        return jnp.where(at == 2 * pair, column_a, jnp.where(at == 2 * pair + 1, column_b, 0.0))

    def body(start, first, width):
        mask = live_mask(start_ref, start, first, width, rows)
        here, keys = pl.ds(start, rows), pl.ds(first, width)
        values = v_ref[keys, :]
        d_rows = dd[here, :]
        dq, o = [], []
        for head, (q_of, k_of, dk_of) in enumerate(((qa, ka, dka), (qb, kb, dkb))):
            own_lanes = (lane < 64) if head == 0 else (lane >= 64)
            p = probabilities(q_of[here, :], k_of[keys, :], mask)
            d_mine = jnp.where(own_lanes, d_rows, jnp.zeros_like(d_rows))
            dp = dot_nt(d_mine, values)
            delta = jnp.sum(p * dp, axis=1, keepdims=True)
            ds = (p * (dp - delta)).astype(bf16)
            dq.append(dot_nn(ds, k_of[keys, :]))
            dk_of[keys, :] += dot_tn(ds, q_of[here, :])
            low = p.astype(bf16)
            dva[keys, :] += dot_tn(low, d_mine)
            o.append(dot_nn(low, values))
        o = jnp.where(lane < 64, o[0], o[1])
        dg_ref[here, :] = (dus[here, :] * o).astype(bf16)
        u_ref[here, :] = (o * jax.nn.sigmoid(gate_ref[here, :])).astype(bf16)
        dq_ref[here, :] = (jnp.where(lane < 64, dq[0], dq[1]) * 0.125).astype(bf16)
        dcs[here, :] += pick(dq[0][:, 67:68], dq[1][:, 3:4])

    over_query_blocks(seq_len, rows, body)

    def finish(i):
        here = rows_at(i, chunk_rows)
        lanes_now = lax.broadcasted_iota(jnp.int32, (chunk_rows, pair_lanes), 1)
        ka_rows, kb_rows = dka[here, :], dkb[here, :]
        dk_ref[here, :] = jnp.where(lanes_now < 64, ka_rows, kb_rows).astype(bf16)
        dv_ref[here, :] = dva[here, :].astype(bf16)
        dcs[here, :] -= pick(ka_rows[:, 64:65], kb_rows[:, 0:1])

    each(seq_len // chunk_rows, finish)
    d_own = jnp.concatenate([r[piece, :] for r in (dq_ref, dk_ref, dv_ref, dg_ref)], axis=1)
    acc[:, :half] += dot_nt(d_own, lane_blocks(mine))
    acc[:, half:] += dot_nt(d_own, lane_blocks(theirs))

    @pl.when(pair == pl.num_programs(0) - 1)
    def _():
        running_sum(dcs, True)

        def last(i):
            here = rows_at(i, chunk_rows)
            dz_ref[here, :] = (dcs[here, :] * jax.nn.sigmoid(-z_ref[here, :])).astype(bf16)

        each(seq_len // chunk_rows, last)
        send_ref[...] = (acc[...] + dot_nt(dz_ref[piece, :], wf[...])).astype(bf16)


def ffn_forward_kernel(b_ref, wg, wu, wd, tg, tu, td, gt_ref, up_ref, send_ref, acc):
    half = b_ref.shape[1] // 2
    low, high = b_ref[:, :half], b_ref[:, half:]
    gt = dot_nn(low, wg[0]) + dot_nn(high, tg[0])
    up = dot_nn(low, wu[0]) + dot_nn(high, tu[0])
    gt_ref[...] = gt
    up_ref[...] = up
    m = (gt * jax.nn.sigmoid(gt) * up).astype(bf16)

    @pl.when(pl.program_id(0) == 0)
    def _():
        acc[...] = jnp.zeros_like(acc)

    acc[:, :half] += dot_nn(m, wd[0])
    acc[:, half:] += dot_nn(m, td[0])

    @pl.when(pl.program_id(0) == pl.num_programs(0) - 1)
    def _():
        send_ref[...] = acc[...].astype(bf16)


def inner_grads(dm, gt, up):
    sig = jax.nn.sigmoid(gt)
    d_gate = (dm * up * sig * (1.0 + gt * (1.0 - sig))).astype(bf16)
    return d_gate, (dm * (gt * sig)).astype(bf16)


def ffn_backward_kernel(g_ref, gt_ref, up_ref, wg, wu, wd, tg, tu, td, *refs):
    send_ref, acc = refs[-2:]
    half = g_ref.shape[1] // 2
    dm = dot_nt(g_ref[:, :half], wd[0]) + dot_nt(g_ref[:, half:], td[0])
    d_gate, d_up = inner_grads(dm, gt_ref[...], up_ref[...])

    @pl.when(pl.program_id(0) == 0)
    def _():
        acc[...] = jnp.zeros_like(acc)

    acc[:, :half] += dot_nt(d_gate, wg[0]) + dot_nt(d_up, wu[0])
    acc[:, half:] += dot_nt(d_gate, tg[0]) + dot_nt(d_up, tu[0])

    @pl.when(pl.program_id(0) == pl.num_programs(0) - 1)
    def _():
        send_ref[...] = acc[...].astype(bf16)


def ffn_theirs_kernel(count_parts, *refs):
    place_ref, refs = refs[0], refs[1:]
    b_parts, g_parts = refs[:count_parts], refs[count_parts : 2 * count_parts]
    wg, wu, wd, tg, tu, td = refs[2 * count_parts : 2 * count_parts + 6]
    b_ref, g_ref, m_ref, dgate_ref, dup_ref, gate_out, up_out, down_out, turned = refs[-9:]
    half = b_ref.shape[1] // 2

    @pl.when(pl.program_id(0) == 0)
    def _():
        assemble(b_parts, b_ref, place_ref)
        assemble(g_parts, g_ref, place_ref)
        turned[...] = b_ref[:, half:].T

    def chunk(i):
        here = rows_at(i, chunk_rows)
        low, high = b_ref[here, :half], b_ref[here, half:]
        gt = dot_nn(low, wg[0]) + dot_nn(high, tg[0])
        up = dot_nn(low, wu[0]) + dot_nn(high, tu[0])
        dm = dot_nt(g_ref[here, :half], wd[0]) + dot_nt(g_ref[here, half:], td[0])
        m_ref[here, :] = (gt * jax.nn.sigmoid(gt) * up).astype(bf16)
        dgate_ref[here, :], dup_ref[here, :] = inner_grads(dm, gt, up)

    each(b_ref.shape[0] // chunk_rows, chunk)
    gate_out[...] = dot_nn(turned[...], dgate_ref[...]).astype(bf16)
    up_out[...] = dot_nn(turned[...], dup_ref[...]).astype(bf16)
    down_out[...] = dot_tn(m_ref[...], g_ref[:, half:]).astype(bf16)


def ffn_mine_kernel(b_ref, g_ref, m_ref, dgate_ref, dup_ref, gate_in, up_in, down_in, *refs):
    gate_out, up_out, down_out, turned = refs[-4:]

    @pl.when(pl.program_id(0) == 0)
    def _():
        turned[...] = b_ref[...].T

    gate_out[0] = dot_nn(turned[...], dgate_ref[...]) + gate_in[...].astype(f32)
    up_out[0] = dot_nn(turned[...], dup_ref[...]) + up_in[...].astype(f32)
    down_out[0] = dot_tn(m_ref[...], g_ref[...]) + down_in[...].astype(f32)


def attention_grads_kernel(steps, mine, *refs):
    a_ref, dq, dk, dv, dg, dz, u_ref, y_ref = refs[:8]
    received = refs[8:14] if mine else [None] * 6
    acc, acc_out = refs[-2:]
    outs = refs[-8:-2]
    turned = a_ref[...].T
    width = dq.shape[1]
    parts = [dot_nn(turned, d[...]) for d in (dq, dk, dv, dg, dz)]
    out = dot_tn(u_ref[...], y_ref[...])

    def give(values):
        for ref, value, more in zip(outs, values, received):
            total = value if more is None else value + more[...].astype(f32)
            if len(ref.shape) == 3:
                ref[0] = total.astype(ref.dtype)
            else:
                ref[...] = total.astype(ref.dtype)

    if steps == 1:
        give([*parts, out])
        return
    step = pl.program_id(0)

    @pl.when(step == 0)
    def _():
        acc[...] = jnp.zeros_like(acc)
        acc_out[...] = jnp.zeros_like(acc_out)

    for k, part in enumerate(parts):
        acc[:, k * width : k * width + part.shape[1]] += part
    acc_out[...] += out

    @pl.when(step == steps - 1)
    def _():
        found = [acc[:, k * width : k * width + p.shape[1]] for k, p in enumerate(parts)]
        give([*found, acc_out[...]])


def fixed(shape, single=True):
    zeros = (0,) * len(shape)
    if single:
        return pl.BlockSpec(shape, lambda *_: zeros, pipeline_mode=pl.Buffered(1))
    return pl.BlockSpec(shape, lambda *_: zeros)


def lanes(seq_len):
    return pl.BlockSpec((seq_len, pair_lanes), lambda p, *_: (0, p))


def lanes_read(seq_len):
    if seq_len <= 2048:
        return lanes(seq_len)
    return pl.BlockSpec((seq_len, pair_lanes), lambda p, *_: (0, p), pipeline_mode=pl.Buffered(1))


def columns_of(w, layer, width):
    return pl.BlockSpec((1, w.shape[1], width), lambda p, *_: (layer, 0, p))


def rows_of(w, layer, height):
    return pl.BlockSpec((1, height, w.shape[2]), lambda p, *_: (layer, p, 0))


def shape(dims, dtype):
    return jax.ShapeDtypeStruct(dims, dtype)


def attention_specs(parts, layer, w4, t4, wo, to, seq_len, join):
    specs = [fixed(p.shape) for p in parts]
    specs += [columns_of(w, layer, pair_lanes) for w in (*w4, *t4)]
    specs += [rows_of(wo, layer, pair_lanes), rows_of(to, layer, pair_lanes)]
    return specs


def cost(microseconds):
    return pl.CostEstimate(flops=int(microseconds * 1.1e9), bytes_accessed=0, transcendentals=0)


def token_specs(tokens):
    return [pl.BlockSpec((16, 128), lambda *_: (0, 0)) for _ in tokens]


def forward_own(place, parts, layer, w4, t4, wo, to, wf, bias, doc_start, piece_len):
    seq_len, width = doc_start.shape[0], parts[0].shape[1]
    local_width = wo.shape[1]
    join = len(parts) > 1
    terms = (seq_len, pair_lanes)
    outs = [shape((seq_len, local_width), bf16)] * 3 + [shape((seq_len, local_width), f32)]
    outs += [shape(terms, f32), shape(terms, bf16), shape((piece_len, width), bf16)]
    specs = [lanes(seq_len)] * 4 + [fixed(terms, False)] * 2 + [fixed((piece_len, width), False)]
    if join:
        outs, specs = [shape((seq_len, width), bf16)] + outs, [fixed((seq_len, width))] + specs
    low, piece = pltpu.VMEM((seq_len, pair_lanes), bf16), pltpu.VMEM((piece_len, pair_lanes), bf16)
    got = pl.pallas_call(
        functools.partial(forward_own_kernel, len(parts), piece_len, join),
        grid_spec=pltpu.PrefetchScalarGridSpec(
            num_scalar_prefetch=1,
            grid=(local_width // pair_lanes,),
            in_specs=attention_specs(parts, layer, w4, t4, wo, to, seq_len, join)
            + [fixed(wf.shape), fixed(bias.shape), fixed(doc_start.shape)],
            out_specs=specs,
            scratch_shapes=[piece] * 2 + [low] * 2 + [pltpu.VMEM(terms, f32), pltpu.VMEM((piece_len, width), f32)],
        ),
        out_shape=outs,
        cost_estimate=cost(19),
        compiler_params=pltpu.CompilerParams(vmem_limit_bytes=60 << 20),
    )(place, *parts, *w4, *t4, wo, to, wf, bias, doc_start)
    got = list(got)
    a = got.pop(0) if join else parts[0]
    return a, got[:6], got[6]


def attention_backward(place, parts, layer, w4, t4, wo, to, wf, saved, doc_start, piece_len):
    q, k, v, gate, z, terms = saved
    seq_len, width = doc_start.shape[0], parts[0].shape[1]
    local_width = wo.shape[1]
    join = len(parts) > 1
    outs = [shape((seq_len, local_width), bf16)] * 5 + [shape((seq_len, pair_lanes), bf16)]
    outs += [shape((piece_len, width), bf16)]
    specs = [lanes(seq_len)] * 5 + [fixed((seq_len, pair_lanes), False), fixed((piece_len, width), False)]
    if join:
        outs, specs = [shape((seq_len, width), bf16)] + outs, [fixed((seq_len, width))] + specs
    low, high = pltpu.VMEM((seq_len, pair_lanes), bf16), pltpu.VMEM((seq_len, pair_lanes), f32)
    got = pl.pallas_call(
        functools.partial(backward_kernel, len(parts), piece_len, join),
        grid_spec=pltpu.PrefetchScalarGridSpec(
            num_scalar_prefetch=1,
            grid=(local_width // pair_lanes,),
            in_specs=attention_specs(parts, layer, w4, t4, wo, to, seq_len, join)
            + [fixed(wf.shape)]
            + [lanes_read(seq_len)] * 4
            + [fixed(z.shape), fixed(terms.shape), fixed(doc_start.shape)],
            out_specs=specs,
            scratch_shapes=[low] * 5 + [high] * 5 + [pltpu.VMEM((piece_len, width), f32)],
        ),
        out_shape=outs,
        cost_estimate=cost(33),
        compiler_params=pltpu.CompilerParams(vmem_limit_bytes=60 << 20),
    )(place, *parts, *w4, *t4, wo, to, wf, q, k, v, gate, z, terms, doc_start)
    got = list(got)
    y = got.pop(0) if join else parts[0]
    return y, got[:6], got[6]


def ffn_weights(layer, w3, t3):
    specs = []
    for wg, wu, wd in (w3, t3):
        specs += [
            columns_of(wg, layer, hidden_block), columns_of(wu, layer, hidden_block), rows_of(wd, layer, hidden_block),
        ]
    return specs


def blocks_of(rows):
    return pl.BlockSpec((rows, hidden_block), lambda p, *_: (0, p))


def ffn_forward(b, layer, w3, t3):
    rows, width = b.shape
    inner = w3[2].shape[1]
    return pl.pallas_call(
        ffn_forward_kernel,
        grid=(inner // hidden_block,),
        in_specs=[fixed(b.shape)] + ffn_weights(layer, w3, t3),
        out_specs=[blocks_of(rows)] * 2 + [fixed((rows, width), False)],
        scratch_shapes=[pltpu.VMEM((rows, width), f32)],
        out_shape=[shape((rows, inner), f32)] * 2 + [shape((rows, width), bf16)],
        cost_estimate=cost(7),
        compiler_params=pltpu.CompilerParams(vmem_limit_bytes=40 << 20),
    )(b, *w3, *t3)


def ffn_backward(g, gt, up, layer, w3, t3, *tokens):
    rows, width = g.shape
    return pl.pallas_call(
        ffn_backward_kernel,
        grid=(gt.shape[1] // hidden_block,),
        in_specs=[fixed(g.shape)] + [blocks_of(rows)] * 2 + ffn_weights(layer, w3, t3) + token_specs(tokens),
        out_specs=fixed((rows, width), False),
        scratch_shapes=[pltpu.VMEM((rows, width), f32)],
        out_shape=shape((rows, width), bf16),
        cost_estimate=cost(8),
        compiler_params=pltpu.CompilerParams(vmem_limit_bytes=40 << 20),
    )(g, gt, up, *w3, *t3, *tokens)


def ffn_theirs(place, b_parts, g_parts, layer, w3, t3, *tokens):
    width = b_parts[0].shape[1]
    half = width // 2
    rows = sum(p.size for p in b_parts) // width
    inner = w3[2].shape[1]
    wide = pl.BlockSpec((half, hidden_block), lambda p, *_: (0, p))
    return pl.pallas_call(
        functools.partial(ffn_theirs_kernel, len(b_parts)),
        grid_spec=pltpu.PrefetchScalarGridSpec(
            num_scalar_prefetch=1,
            grid=(inner // hidden_block,),
            in_specs=[fixed(p.shape) for p in (*b_parts, *g_parts)]
            + ffn_weights(layer, w3, t3)
            + token_specs(tokens),
            out_specs=[fixed((rows, width))] * 2
            + [blocks_of(rows)] * 3
            + [wide, wide, pl.BlockSpec((hidden_block, half), lambda p, *_: (p, 0))],
            scratch_shapes=[pltpu.VMEM((half, rows), bf16)],
        ),
        out_shape=[shape((rows, width), bf16)] * 2
        + [shape((rows, inner), bf16)] * 3
        + [shape((half, inner), bf16)] * 2
        + [shape((inner, half), bf16)],
        cost_estimate=cost(24),
        compiler_params=pltpu.CompilerParams(vmem_limit_bytes=60 << 20),
    )(place, *b_parts, *g_parts, *w3, *t3, *tokens)


def anywhere():
    return pl.BlockSpec(memory_space=pl.ANY)


def ffn_mine(layer, b, g, values, received, totals, *tokens):
    rows, width = b.shape
    half, inner = width // 2, values[0].shape[1]
    wide = pl.BlockSpec((half, hidden_block), lambda p: (0, p))
    tall = pl.BlockSpec((hidden_block, half), lambda p: (p, 0))
    wide_out = pl.BlockSpec((1, half, hidden_block), lambda p: (layer, 0, p))
    tall_out = pl.BlockSpec((1, hidden_block, half), lambda p: (layer, p, 0))
    return pl.pallas_call(
        ffn_mine_kernel,
        grid=(inner // hidden_block,),
        in_specs=[fixed((rows, half))] * 2
        + [blocks_of(rows)] * 3
        + [wide, wide, tall]
        + [anywhere()] * 3
        + token_specs(tokens),
        out_specs=[wide_out, wide_out, tall_out],
        out_shape=[shape(x.shape, x.dtype) for x in totals],
        scratch_shapes=[pltpu.VMEM((half, rows), bf16)],
        input_output_aliases={8: 0, 9: 1, 10: 2},
        cost_estimate=cost(9),
        compiler_params=pltpu.CompilerParams(vmem_limit_bytes=40 << 20),
    )(b, g, *values, *received, *totals, *tokens)


def attention_grads(layer, a, ds, dz, u, y, received=None, totals=None, tokens=()):
    rows, width = a.shape
    half, local_width = width // 2, u.shape[1]
    part = min(rows, 1024)
    steps = rows // part
    mine = received is not None
    side = 0 if mine else 1
    features = pl.BlockSpec((part, half), lambda p: (p, side))
    across = [pl.BlockSpec((part, x.shape[1]), lambda p: (p, 0)) for x in (*ds, dz, u)]
    specs = [features, *across, features]
    operands = [a, *ds, dz, u, y]
    flat = [(half, local_width)] * 4 + [(half, pair_lanes), (local_width, half)]
    if mine:
        specs += [fixed(x) for x in flat] + [anywhere()] * 5
        operands += [*received, *totals]
        outs = [shape(x.shape, f32) for x in totals[:4]] + [shape(flat[4], f32), shape(totals[4].shape, f32)]
        layered = pl.BlockSpec((1, half, local_width), lambda p: (layer, 0, 0))
        out_specs = [layered] * 4 + [fixed(flat[4], False)]
        out_specs += [pl.BlockSpec((1, local_width, half), lambda p: (layer, 0, 0))]
        aliases = {14: 0, 15: 1, 16: 2, 17: 3, 18: 5}
    else:
        outs, out_specs, aliases = [shape(x, bf16) for x in flat], [fixed(x, False) for x in flat], {}
    sizes = [(half, 4 * local_width + pair_lanes), (local_width, half)] if steps > 1 else [(8, 128)] * 2
    return pl.pallas_call(
        functools.partial(attention_grads_kernel, steps, mine),
        grid=(steps,),
        in_specs=specs + token_specs(tokens),
        out_specs=out_specs,
        out_shape=outs,
        scratch_shapes=[pltpu.VMEM(x, f32) for x in sizes],
        input_output_aliases=aliases,
        cost_estimate=cost(7),
        compiler_params=pltpu.CompilerParams(vmem_limit_bytes=60 << 20),
    )(*operands, *tokens)


def unset_kernel(*refs):
    pass


def unset(*like):
    return pl.pallas_call(
        unset_kernel,
        out_specs=[pl.BlockSpec(memory_space=pl.ANY) for _ in like],
        out_shape=list(like),
    )()


def inverse_rms(h):
    return lax.rsqrt(jnp.mean(h * h, axis=-1, keepdims=True) + epsilon)


def norm_back(grad_normed, hidden, inverse, gain):
    scaled = hidden * inverse
    weighted = grad_normed * gain
    grad_gain = jnp.sum(grad_normed * scaled, axis=0)
    mean = jnp.mean(weighted * scaled, axis=-1, keepdims=True)
    return inverse * (weighted - scaled * mean), grad_gain


def local(
    hidden_in, segment_ids, w_query, w_key, w_value, w_gate_out, w_attn_out, w_forget, b_forget,
    gain_attn, gain_ffn, w_gate, w_up, w_down, cotangent,
):
    seq_count, piece_len, width = hidden_in.shape
    count_z, count_t = lax.axis_size("context"), lax.axis_size("tensor")
    core, z, t = lax.axis_index("fsdp"), lax.axis_index("context"), lax.axis_index("tensor")
    layers, half, local_width = w_query.shape
    heads = w_forget.shape[2]
    block = piece_len // count_t
    seq_len = piece_len * count_z
    shared_rows = count_z == 4
    place = jnp.stack([z, t]).astype(jnp.int32)
    own_place = place if shared_rows else jnp.zeros((2,), jnp.int32)

    def features(x):
        return jnp.where(core == 0, x, jnp.concatenate([x[..., half:], x[..., :half]], axis=-1))

    def own_block(x):
        return lax.dynamic_slice_in_dim(x, t * block, block, 0)

    def other(w):
        return swap(w, "fsdp", 1)

    def full(w, axis):
        return jnp.concatenate([w, other(w)], axis=axis)

    seg_all = gathered(segment_ids.reshape(1, piece_len), "context").reshape(seq_len)
    doc_start = jnp.sum((seg_all[None, :] < seg_all[:, None]).astype(jnp.int32), axis=1, keepdims=True)

    gains = full(jnp.concatenate([gain_attn, gain_ffn], axis=0), 1).astype(f32)
    hidden_rows = features(hidden_in.reshape(piece_len, width)).astype(f32)
    first_a = (hidden_rows * inverse_rms(hidden_rows) * gains[0]).astype(bf16)
    a_parts = all_rows(own_block(first_a), first_a, seg_all)

    w_forget_full = jnp.pad(full(w_forget, 1), ((0, 0), (0, 0), (0, pair_lanes - heads)))
    bias = jnp.pad(b_forget, ((0, 0), (0, pair_lanes - heads)))
    w4 = (w_query, w_key, w_value, w_gate_out)
    t4 = tuple(other(w) for w in w4)
    to = other(w_attn_out)
    w3 = (w_gate, w_up, w_down)
    t3 = tuple(other(w) for w in w3)

    hidden = own_block(hidden_rows)
    saved = []
    cotangent_rows = features(cotangent.reshape(piece_len, width))
    last = layers - 1
    grad = own_block(cotangent_rows).astype(f32)
    far = {}
    for layer in range(layers):
        gain_one, gain_two = gains[layer], gains[layers + layer]
        inverse_one = inverse_rms(hidden)
        if layer > 0:
            a_shard = (hidden * inverse_one * gain_one).astype(bf16)
            a_parts = all_rows(after(a_shard, *far.get("b", ())))
        a, (q, k, v, gate, forget, terms), sends = forward_own(
            place, a_parts, layer, w4, t4, w_attn_out, to, w_forget_full[layer],
            bias[layer : layer + 1], doc_start, piece_len,
        )
        if shared_rows and layer == 0:
            token = a_parts[-1]
            far["g"] = over_context(after(own_block(cotangent_rows), token), after(cotangent_rows, token))
        if shared_rows and layer == last:
            g_last = all_rows_later(cotangent_rows, far["g"], a_parts[-1])
            sends = after(sends, *g_last[1:])
        mixed = hidden + received_sum(sends)
        inverse_two = inverse_rms(mixed)
        b_shard = (mixed * inverse_two * gain_two).astype(bf16)
        b = gathered(b_shard, "tensor")
        if shared_rows:
            if layer > 0:
                before = saved[-1]
                before["b_parts"] = all_rows_later(before["b"], far["b"], b)
            far["b"] = over_context(b_shard, b)
        gt, up, sends = ffn_forward(b, layer, w3, t3)
        saved.append(
            dict(hidden=hidden, inverse_one=inverse_one, a=a, kept=(q, k, v, gate, forget, terms), mixed=mixed,
                 inverse_two=inverse_two, b=b, gt=gt, up=up)
        )
        if layer < last:
            hidden = mixed + received_sum(after(sends, *far.get("b", ())[1:]))

    def finish(x):
        return features(gathered(x.astype(bf16), "tensor")).reshape(1, piece_len, width)

    last_sends = sends
    wide = shape((layers, half, local_width), f32)
    inner = shape((layers, half, w_gate.shape[2]), f32)
    results = list(
        unset(
            wide, wide, wide, wide, shape((layers, local_width, half), f32),
            inner, inner, shape((layers, w_down.shape[1], half), f32),
        )
    )
    small = [[None] * layers for _ in range(2)]
    gain_grads = [None] * (2 * layers)

    for layer in reversed(range(layers)):
        s = saved[layer]
        gain_one, gain_two = gains[layer], gains[layers + layer]
        if layer == last:
            g = cotangent_rows
        else:
            g_shard = grad.astype(bf16)
            g = gathered(g_shard, "tensor")
            if shared_rows:
                far["g"] = over_context(g_shard, g)
        if not shared_rows:
            sends = ffn_backward(g, s["gt"], s["up"], layer, w3, t3)
        elif layer == last:
            sends = ffn_backward(g, s["gt"], s["up"], layer, w3, t3, *far["b"][1:])
            sends = after(sends, *[x["b_parts"][-1] for x in saved[:-1]])
        else:
            sends = ffn_backward(g, s["gt"], s["up"], layer, w3, t3)
            sends = after(sends, *far["g"][1:])
        back, gain_grads[layers + layer] = norm_back(received_sum(sends), s["mixed"], s["inverse_two"], gain_two)
        grad_mixed = grad + back
        y_shard = grad_mixed.astype(bf16)
        sent_before = far["b" if layer == last else "g"] if shared_rows else ()
        y_parts = all_rows(after(y_shard, *sent_before), together=layer < last)
        y, (dq, dk, dv, dg, u, dz), sends = attention_backward(
            place, y_parts, layer, w4, t4, w_attn_out, to, w_forget_full[layer], s["kept"], doc_start, piece_len,
        )
        token = y_parts[-1]
        if not shared_rows:
            s["b_parts"], g_parts = (s["b"],), (g,)
        elif layer == last:
            s["b_parts"], g_parts = all_rows_later(s["b"], far["b"], token), g_last
            sends = after(sends, s["b_parts"][-1])
        else:
            g_parts = all_rows_later(g, far["g"], token)
            sends = after(sends, g_parts[-1])
        back, gain_grads[layer] = norm_back(received_sum(sends), s["hidden"], s["inverse_one"], gain_one)
        grad = grad_mixed + back
        s.update(u=u, y=y, d=(dq, dk, dv, dg), dz=dz, g_parts=g_parts, y_shard=y_shard)

    def ffn_theirs_of(layer, *tokens):
        s = saved[layer]
        b, g, *values = ffn_theirs(own_place, s["b_parts"], s["g_parts"], layer, w3, t3, *tokens)
        s.update(ffn=(b, g, values[:3]), ffn_received=[other(x) for x in values[3:]])

    def ffn_mine_of(layer, *tokens):
        s = saved[layer]
        results[5:] = ffn_mine(layer, *s["ffn"], s["ffn_received"], results[5:], *tokens)

    def attention_grads_of(layer, tokens=(), mine_tokens=()):
        s = saved[layer]
        parts = (s["a"], s["d"], s["dz"], s["u"], s["y"])
        theirs = attention_grads(layer, *parts, tokens=tokens)
        found = attention_grads(layer, *parts, [other(x) for x in theirs], results[:5], mine_tokens)
        results[:5] = [*found[:4], found[5]]
        bias_grad = jnp.sum(s["dz"].astype(f32), axis=0)[:heads]
        small[0][layer] = found[4][:, :heads]
        small[1][layer] = bias_grad + other(bias_grad)

    for layer in reversed(range(1, layers)):
        attention_grads_of(layer)
        ffn_theirs_of(layer, saved[layer - 1]["y_shard"])
    ffn_theirs_of(0)
    token = saved[0]["ffn"][0]
    for layer in reversed(range(1, layers)):
        ffn_mine_of(layer, token)
    attention_grads_of(0, (token,), saved[0]["ffn_received"])
    ffn_mine_of(0)
    if not shared_rows:
        results[5:] = [lax.psum(x, "context") for x in results[5:]]
    output = finish(saved[last]["mixed"] + received_sum(after(last_sends, grad)))
    grad_input = finish(grad)
    gain_total = sum_over(sum_over(jnp.stack(gain_grads), "tensor"), "context")
    gain_total = gain_total[:, :half] + other(gain_total[:, half:])
    return (
        output, grad_input, *results[:5], jnp.stack(small[0]), jnp.stack(small[1]),
        gain_total[:layers], gain_total[layers:], *results[5:],
    )


def solution(mesh):
    rows = P("fsdp", "context", None)
    wide, tall = P(None, "fsdp", "tensor"), P(None, "tensor", "fsdp")
    heads, gain = P(None, "tensor"), P(None, "fsdp")
    return jax.shard_map(
        local,
        mesh=mesh,
        in_specs=(
            rows, P("fsdp", "context"), wide, wide, wide, wide, tall, wide, heads, gain, gain, wide, wide, tall, rows,
        ),
        out_specs=(rows, rows, wide, wide, wide, wide, tall, wide, heads, gain, gain, wide, wide, tall),
        check_vma=False,
    )
```

```python
import functools

import jax
import jax.numpy as jnp
from jax import lax
from jax.experimental import pallas as pl
from jax.experimental.pallas import tpu as pltpu
from jax.sharding import PartitionSpec as P

epsilon = 1e-06
masked_value = -1e30
bf16 = jnp.bfloat16
f32 = jnp.float32
pair_lanes = 128
hidden_block = 256
chunk_rows = 256


def query_rows(seq_len):
    return 256 if seq_len <= 2048 else 128


def swap(x, axis, k):
    n = lax.axis_size(axis)
    return lax.ppermute(x, axis, [(i, i ^ k) for i in range(n)])


def pass_kernel(*refs):
    pass


def after(x, *tokens):
    if not tokens:
        return x
    anywhere = pl.BlockSpec(memory_space=pl.ANY)
    return pl.pallas_call(
        pass_kernel,
        in_specs=[anywhere] * (1 + len(tokens)),
        out_specs=anywhere,
        out_shape=jax.ShapeDtypeStruct(x.shape, x.dtype),
        input_output_aliases={0: 0},
    )(x, *tokens)


def gathered(block, axis):
    count = lax.axis_size(axis)
    copies = jnp.broadcast_to(block[None], (count,) + block.shape)
    return lax.all_to_all(copies, axis, 0, 0, tiled=True).reshape((-1,) + block.shape[1:])


def near_rows(own):
    return swap(own, "context", 1)


def far_blocks(shard):
    return swap(shard, "context", 2), swap(shard, "context", 3)


def far_rows(blocks, *tokens):
    block, width = blocks[0].shape
    return gathered(after(jnp.concatenate(blocks, axis=0), *tokens), "tensor").reshape(-1, 2, block, width)


def all_rows(shard, own=None, token=None, together=False):
    if own is None:
        own = gathered(shard, "tensor")
    if lax.axis_size("context") != 4:
        return (lax.all_gather(own, "context", tiled=True),), ()
    second, third = far_blocks(shard)
    near = near_rows(own)
    if together:
        return (own, near, far_rows((second, third))), (second, third)
    if token is not None:
        second = after(second, token)
    third = after(third, second)
    blocks = [second] + [swap(second, "tensor", k) for k in range(1, lax.axis_size("tensor"))]
    return (own, near, *blocks, gathered(third, "tensor")), (second, third)


def received_sum(sends):
    count = lax.axis_size("tensor")
    got = lax.all_to_all(sends.reshape(count, -1, sends.shape[1]), "tensor", 0, 0, tiled=True)
    return jnp.sum(got.astype(f32), axis=0)


def dot_nt(a, b):
    return lax.dot_general(a, b, (((1,), (1,)), ((), ())), preferred_element_type=f32)


def dot_tn(a, b):
    return lax.dot_general(a, b, (((0,), (0,)), ((), ())), preferred_element_type=f32)


def dot_nn(a, b):
    return jnp.dot(a, b, preferred_element_type=f32)


def each(count, body):
    if count <= 4:
        for i in range(count):
            body(i)
        return

    def one(i, carry):
        body(i)
        return carry

    lax.fori_loop(0, count, one, 0)


def rows_at(i, rows):
    start = i * rows
    return pl.ds(start if isinstance(start, int) else pl.multiple_of(start, rows), rows)


def assemble(parts, whole_ref, place_ref):
    z, t = place_ref[0], place_ref[1]
    piece, blocks_seen, piece_len = 0, 0, parts[0].shape[0]
    for part in parts:
        if len(part.shape) == 4:
            blocks, pieces, block = part.shape[:3]
            for p in range(pieces):
                for b in range(blocks):
                    at = pl.multiple_of((z ^ (piece + p)) * piece_len + b * block, block)
                    whole_ref[pl.ds(at, block), :] = part[b, p]
            piece += pieces
            continue
        rows = part.shape[0]
        if rows == piece_len:
            at = pl.multiple_of((z ^ piece) * piece_len, piece_len)
            piece += 1
        else:
            at = pl.multiple_of((z ^ piece) * piece_len + (t ^ blocks_seen) * rows, rows)
            blocks_seen += 1
            if blocks_seen * rows == piece_len:
                piece, blocks_seen = piece + 1, 0
        whole_ref[pl.ds(at, rows), :] = part[...]


def triangle(rows, reverse):
    row = lax.broadcasted_iota(jnp.int32, (rows, rows), 0)
    column = lax.broadcasted_iota(jnp.int32, (rows, rows), 1)
    return jnp.where((column >= row) if reverse else (column <= row), 1.0, 0.0).astype(bf16)


def running_sum(ref, reverse):
    rows = chunk_rows
    ones = triangle(rows, reverse)
    count = ref.shape[0] // rows
    edge = 0 if reverse else rows - 1

    def chunk(i, carry):
        here = pl.ds(pl.multiple_of((count - 1 - i if reverse else i) * rows, rows), rows)
        high, middle, lowest = three_parts(ref[here, :])
        total = dot_nn(ones, high) + dot_nn(ones, middle) + dot_nn(ones, lowest) + carry
        ref[here, :] = total
        return total[edge : edge + 1, :]

    lax.fori_loop(0, count, chunk, jnp.zeros((1, ref.shape[1]), f32), unroll=count <= 4)


def log_sigmoid(z):
    e = jnp.exp(-jnp.abs(z))
    small = e * (1.0 - e * (1 / 2 - e * (1 / 3 - e * (1 / 4 - e * (1 / 5 - e * (1 / 6 - e * (1 / 7)))))))
    return jnp.minimum(z, 0.0) - jnp.where(e < 0.0625, small, jnp.log(1.0 + e))


def three_parts(x):
    high = x.astype(bf16)
    middle = (x - high.astype(f32)).astype(bf16)
    return high, middle, (x - high.astype(f32) - middle.astype(f32)).astype(bf16)


def decay_side(terms, pair, key_side):
    row = lax.broadcasted_iota(jnp.int32, (pair_lanes, pair_lanes), 0)
    lane = lax.broadcasted_iota(jnp.int32, (pair_lanes, pair_lanes), 1)
    spot = lane & 63
    term = spot if key_side else spot - 3
    head = jnp.where(lane >= 64, 2 * pair, 2 * pair + 1)
    chosen = (term >= 0) & (term < 3) & (row == 8 * term + head)
    pick = jnp.where(chosen, -1.0 if key_side else 1.0, 0.0).astype(bf16)
    lanes_now = lax.broadcasted_iota(jnp.int32, (1, pair_lanes), 1) & 63
    other = lanes_now - 3 if key_side else lanes_now
    ones = jnp.where((other >= 0) & (other < 3), 1.0, 0.0)
    return (dot_nn(terms, pick) + ones).astype(bf16)


def mix_keys(k_ref, terms_ref, pair, ka, kb):
    def mix(i):
        here = rows_at(i, chunk_rows)
        lane = lax.broadcasted_iota(jnp.int32, (chunk_rows, pair_lanes), 1)
        k, side = k_ref[here, :], decay_side(terms_ref[here, :], pair, True)
        ka[here, :] = jnp.where(lane < 64, k, side)
        kb[here, :] = jnp.where(lane < 64, side, k)

    each(k_ref.shape[0] // chunk_rows, mix)


def mix_queries(q_ref, terms_ref, start, pair, qa, qb):
    def mix(i):
        here = rows_at(i, chunk_rows)
        lane = lax.broadcasted_iota(jnp.int32, (chunk_rows, pair_lanes), 1)
        q = (q_ref[here, :].astype(f32) * 0.125).astype(bf16)
        terms = terms_ref[pl.ds(pl.multiple_of(start + i * chunk_rows, chunk_rows), chunk_rows), :]
        side = decay_side(terms, pair, False)
        qa[here, :] = jnp.where(lane < 64, q, side)
        qb[here, :] = jnp.where(lane < 64, side, q)

    each(q_ref.shape[0] // chunk_rows, mix)


def live_mask(start_ref, start, first, width, rows):
    key_pos = first + lax.broadcasted_iota(jnp.int32, (rows, width), 1)
    query_pos = start + lax.broadcasted_iota(jnp.int32, (rows, width), 0)
    doc_start = start_ref[pl.ds(start, rows), :]
    return (key_pos <= query_pos) & (key_pos >= doc_start)


def over_query_blocks(seq_len, rows, body):
    before = seq_len // 2
    if seq_len // rows <= 4:
        for start in range(0, seq_len, rows):
            first = max(0, start - before)
            body(start, first, start + rows - first)
        return
    width = before + rows

    def one(i, carry):
        start = pl.multiple_of(i * rows, rows)
        first = pl.multiple_of(jnp.maximum(start - before, 0), rows)
        body(start, first, width)
        return carry

    lax.fori_loop(0, seq_len // rows, one, 0)


def probabilities(q_rows, k_rows, mask):
    s = jnp.where(mask, dot_nt(q_rows, k_rows), masked_value)
    e = jnp.exp(s - jnp.max(s, axis=1, keepdims=True))
    return e * (1.0 / jnp.sum(e, axis=1, keepdims=True))


def lane_blocks(refs):
    return jnp.concatenate([r[0] for r in refs], axis=1)


def forward_own_kernel(count_parts, piece_len, join, *refs):
    place_ref, parts, refs = refs[0], refs[1 : 1 + count_parts], list(refs[1 + count_parts :])
    (wq, wk, wv, wg), (tq, tk, tv, tg) = refs[:4], refs[4:8]
    wo, to, wf, bias, start_ref = refs[8:13]
    refs = refs[13:]
    a_ref = refs.pop(0) if join else parts[0]
    q_ref, k_ref, v_ref, gate_ref, z_ref, terms_ref, send_ref, qa, qb, ka, kb, decay, acc = refs
    pair = pl.program_id(0)
    seq_len, half = a_ref.shape[0], a_ref.shape[1] // 2
    piece_start = pl.multiple_of(place_ref[0] * piece_len, piece_len)

    @pl.when(pair == 0)
    def _():
        if join:
            assemble(parts, a_ref, place_ref)
        acc[...] = jnp.zeros_like(acc)

        def gates(i):
            here = rows_at(i, chunk_rows)
            z = dot_nn(a_ref[here, :], wf[...]) + bias[...]
            z_ref[here, :] = z
            decay[here, :] = log_sigmoid(z)

        each(seq_len // chunk_rows, gates)
        running_sum(decay, False)

        def split(i):
            here = rows_at(i, chunk_rows)
            lane = lax.broadcasted_iota(jnp.int32, (chunk_rows, pair_lanes), 1)
            high, middle, lowest = (x.astype(f32) for x in three_parts(decay[here, :]))
            later = jnp.where(lane < 16, pltpu.roll(middle, 8, 1), pltpu.roll(lowest, 16, 1))
            terms = jnp.where(lane < 8, high, later)
            terms_ref[here, :] = jnp.where(lane < 24, terms, 0.0).astype(bf16)

        each(seq_len // chunk_rows, split)

    w_mine, w_theirs = lane_blocks((wq, wk, wv, wg)), lane_blocks((tq, tk, tv, tg))

    def project(i):
        here = rows_at(i, chunk_rows)
        out = dot_nn(a_ref[here, :half], w_mine) + dot_nn(a_ref[here, half:], w_theirs)
        q_ref[here, :] = out[:, :128].astype(bf16)
        k_ref[here, :] = out[:, 128:256].astype(bf16)
        v_ref[here, :] = out[:, 256:384].astype(bf16)
        gate_ref[here, :] = out[:, 384:]

    each(seq_len // chunk_rows, project)
    piece = pl.ds(piece_start, piece_len)
    gate = jax.nn.sigmoid(gate_ref[piece, :])
    mix_keys(k_ref, terms_ref, pair, ka, kb)
    mix_queries(q_ref.at[piece, :], terms_ref, piece_start, pair, qa, qb)
    before = seq_len // 2
    for s in range(0, piece_len, query_rows(seq_len)):
        rows = query_rows(seq_len)
        width = before + rows
        start = pl.multiple_of(piece_start + s, rows)
        first = pl.multiple_of(jnp.maximum(start - before, 0), rows)
        mask = live_mask(start_ref, start, first, width, rows)
        keys = pl.ds(first, width)
        out = []
        for q_of, k_of in ((qa, ka), (qb, kb)):
            p = probabilities(q_of[s : s + rows, :], k_of[keys, :], mask).astype(bf16)
            out.append(dot_nn(p, v_ref[keys, :]))
        lane = lax.broadcasted_iota(jnp.int32, (rows, pair_lanes), 1)
        u = (jnp.where(lane < 64, out[0], out[1]) * gate[s : s + rows, :]).astype(bf16)
        acc[s : s + rows, :half] += dot_nn(u, wo[0])
        acc[s : s + rows, half:] += dot_nn(u, to[0])

    @pl.when(pair == pl.num_programs(0) - 1)
    def _():
        send_ref[...] = acc[...].astype(bf16)


def backward_kernel(count_parts, piece_len, join, *refs):
    place_ref, parts, refs = refs[0], refs[1 : 1 + count_parts], list(refs[1 + count_parts :])
    mine, theirs, (wo, to, wf) = refs[:4], refs[4:8], refs[8:11]
    q_ref, k_ref, v_ref, gate_ref, z_ref, terms_ref, start_ref = refs[11:18]
    refs = refs[18:]
    y_ref = refs.pop(0) if join else parts[0]
    dq_ref, dk_ref, dv_ref, dg_ref, u_ref, dz_ref, send_ref = refs[:7]
    qa, qb, ka, kb, dd, dus, dka, dkb, dva, dcs, acc = refs[7:]
    pair = pl.program_id(0)
    seq_len, half = y_ref.shape[0], y_ref.shape[1] // 2
    rows = query_rows(seq_len)
    piece = pl.ds(pl.multiple_of(place_ref[0] * piece_len, piece_len), piece_len)

    @pl.when(pair == 0)
    def _():
        if join:
            assemble(parts, y_ref, place_ref)
        acc[...] = jnp.zeros_like(acc)
        dcs[...] = jnp.zeros_like(dcs)

    def gates(i):
        here = rows_at(i, chunk_rows)
        du = dot_nt(y_ref[here, :half], wo[0]) + dot_nt(y_ref[here, half:], to[0])
        sig = jax.nn.sigmoid(gate_ref[here, :])
        dd[here, :] = (du * sig).astype(bf16)
        dus[here, :] = du * sig * (1.0 - sig)

    each(seq_len // chunk_rows, gates)
    mix_keys(k_ref, terms_ref, pair, ka, kb)
    mix_queries(q_ref, terms_ref, 0, pair, qa, qb)
    dka[...] = jnp.zeros_like(dka)
    dkb[...] = jnp.zeros_like(dkb)
    dva[...] = jnp.zeros_like(dva)
    lane = lax.broadcasted_iota(jnp.int32, (rows, pair_lanes), 1)

    def pick(column_a, column_b):
        at = lax.broadcasted_iota(jnp.int32, (column_a.shape[0], pair_lanes), 1)
        return jnp.where(at == 2 * pair, column_a, jnp.where(at == 2 * pair + 1, column_b, 0.0))

    def body(start, first, width):
        mask = live_mask(start_ref, start, first, width, rows)
        here, keys = pl.ds(start, rows), pl.ds(first, width)
        values = v_ref[keys, :]
        d_rows = dd[here, :]
        dq, o = [], []
        for head, (q_of, k_of, dk_of) in enumerate(((qa, ka, dka), (qb, kb, dkb))):
            own_lanes = (lane < 64) if head == 0 else (lane >= 64)
            p = probabilities(q_of[here, :], k_of[keys, :], mask)
            d_mine = jnp.where(own_lanes, d_rows, jnp.zeros_like(d_rows))
            dp = dot_nt(d_mine, values)
            delta = jnp.sum(p * dp, axis=1, keepdims=True)
            ds = (p * (dp - delta)).astype(bf16)
            dq.append(dot_nn(ds, k_of[keys, :]))
            dk_of[keys, :] += dot_tn(ds, q_of[here, :])
            low = p.astype(bf16)
            dva[keys, :] += dot_tn(low, d_mine)
            o.append(dot_nn(low, values))
        o = jnp.where(lane < 64, o[0], o[1])
        dg_ref[here, :] = (dus[here, :] * o).astype(bf16)
        u_ref[here, :] = (o * jax.nn.sigmoid(gate_ref[here, :])).astype(bf16)
        dq_ref[here, :] = (jnp.where(lane < 64, dq[0], dq[1]) * 0.125).astype(bf16)
        dcs[here, :] += pick(dq[0][:, 67:68], dq[1][:, 3:4])

    over_query_blocks(seq_len, rows, body)

    def finish(i):
        here = rows_at(i, chunk_rows)
        lanes_now = lax.broadcasted_iota(jnp.int32, (chunk_rows, pair_lanes), 1)
        ka_rows, kb_rows = dka[here, :], dkb[here, :]
        dk_ref[here, :] = jnp.where(lanes_now < 64, ka_rows, kb_rows).astype(bf16)
        dv_ref[here, :] = dva[here, :].astype(bf16)
        dcs[here, :] -= pick(ka_rows[:, 64:65], kb_rows[:, 0:1])

    each(seq_len // chunk_rows, finish)
    d_own = jnp.concatenate([r[piece, :] for r in (dq_ref, dk_ref, dv_ref, dg_ref)], axis=1)
    acc[:, :half] += dot_nt(d_own, lane_blocks(mine))
    acc[:, half:] += dot_nt(d_own, lane_blocks(theirs))

    @pl.when(pair == pl.num_programs(0) - 1)
    def _():
        running_sum(dcs, True)

        def last(i):
            here = rows_at(i, chunk_rows)
            dz_ref[here, :] = (dcs[here, :] * jax.nn.sigmoid(-z_ref[here, :])).astype(bf16)

        each(seq_len // chunk_rows, last)
        send_ref[...] = (acc[...] + dot_nt(dz_ref[piece, :], wf[...])).astype(bf16)


def ffn_forward_kernel(b_ref, wg, wu, wd, tg, tu, td, gt_ref, up_ref, send_ref, acc):
    half = b_ref.shape[1] // 2
    low, high = b_ref[:, :half], b_ref[:, half:]
    gt = dot_nn(low, wg[0]) + dot_nn(high, tg[0])
    up = dot_nn(low, wu[0]) + dot_nn(high, tu[0])
    gt_ref[...] = gt
    up_ref[...] = up
    m = (gt * jax.nn.sigmoid(gt) * up).astype(bf16)

    @pl.when(pl.program_id(0) == 0)
    def _():
        acc[...] = jnp.zeros_like(acc)

    acc[:, :half] += dot_nn(m, wd[0])
    acc[:, half:] += dot_nn(m, td[0])

    @pl.when(pl.program_id(0) == pl.num_programs(0) - 1)
    def _():
        send_ref[...] = acc[...].astype(bf16)


def inner_grads(dm, gt, up):
    sig = jax.nn.sigmoid(gt)
    d_gate = (dm * up * sig * (1.0 + gt * (1.0 - sig))).astype(bf16)
    return d_gate, (dm * (gt * sig)).astype(bf16)


def ffn_backward_kernel(g_ref, gt_ref, up_ref, wg, wu, wd, tg, tu, td, *refs):
    send_ref, acc = refs[-2:]
    half = g_ref.shape[1] // 2
    dm = dot_nt(g_ref[:, :half], wd[0]) + dot_nt(g_ref[:, half:], td[0])
    d_gate, d_up = inner_grads(dm, gt_ref[...], up_ref[...])

    @pl.when(pl.program_id(0) == 0)
    def _():
        acc[...] = jnp.zeros_like(acc)

    acc[:, :half] += dot_nt(d_gate, wg[0]) + dot_nt(d_up, wu[0])
    acc[:, half:] += dot_nt(d_gate, tg[0]) + dot_nt(d_up, tu[0])

    @pl.when(pl.program_id(0) == pl.num_programs(0) - 1)
    def _():
        send_ref[...] = acc[...].astype(bf16)


def ffn_theirs_kernel(count_parts, *refs):
    place_ref, refs = refs[0], refs[1:]
    b_parts, g_parts = refs[:count_parts], refs[count_parts : 2 * count_parts]
    wg, wu, wd, tg, tu, td = refs[2 * count_parts : 2 * count_parts + 6]
    b_ref, g_ref, m_ref, dgate_ref, dup_ref, gate_out, up_out, down_out, turned = refs[-9:]
    half = b_ref.shape[1] // 2

    @pl.when(pl.program_id(0) == 0)
    def _():
        assemble(b_parts, b_ref, place_ref)
        assemble(g_parts, g_ref, place_ref)
        turned[...] = b_ref[:, half:].T

    def chunk(i):
        here = rows_at(i, chunk_rows)
        low, high = b_ref[here, :half], b_ref[here, half:]
        gt = dot_nn(low, wg[0]) + dot_nn(high, tg[0])
        up = dot_nn(low, wu[0]) + dot_nn(high, tu[0])
        dm = dot_nt(g_ref[here, :half], wd[0]) + dot_nt(g_ref[here, half:], td[0])
        m_ref[here, :] = (gt * jax.nn.sigmoid(gt) * up).astype(bf16)
        dgate_ref[here, :], dup_ref[here, :] = inner_grads(dm, gt, up)

    each(b_ref.shape[0] // chunk_rows, chunk)
    gate_out[...] = dot_nn(turned[...], dgate_ref[...]).astype(bf16)
    up_out[...] = dot_nn(turned[...], dup_ref[...]).astype(bf16)
    down_out[...] = dot_tn(m_ref[...], g_ref[:, half:]).astype(bf16)


def ffn_mine_kernel(b_ref, g_ref, m_ref, dgate_ref, dup_ref, gate_in, up_in, down_in, *refs):
    gate_out, up_out, down_out, turned = refs[-4:]

    @pl.when(pl.program_id(0) == 0)
    def _():
        turned[...] = b_ref[...].T

    gate_out[0] = dot_nn(turned[...], dgate_ref[...]) + gate_in[...].astype(f32)
    up_out[0] = dot_nn(turned[...], dup_ref[...]) + up_in[...].astype(f32)
    down_out[0] = dot_tn(m_ref[...], g_ref[...]) + down_in[...].astype(f32)


def attention_grads_kernel(steps, mine, *refs):
    a_ref, dq, dk, dv, dg, dz, u_ref, y_ref = refs[:8]
    received = refs[8:14] if mine else [None] * 6
    acc, acc_out = refs[-2:]
    outs = refs[-8:-2]
    turned = a_ref[...].T
    width = dq.shape[1]
    parts = [dot_nn(turned, d[...]) for d in (dq, dk, dv, dg, dz)]
    out = dot_tn(u_ref[...], y_ref[...])

    def give(values):
        for ref, value, more in zip(outs, values, received):
            total = value if more is None else value + more[...].astype(f32)
            if len(ref.shape) == 3:
                ref[0] = total.astype(ref.dtype)
            else:
                ref[...] = total.astype(ref.dtype)

    if steps == 1:
        give([*parts, out])
        return
    step = pl.program_id(0)

    @pl.when(step == 0)
    def _():
        acc[...] = jnp.zeros_like(acc)
        acc_out[...] = jnp.zeros_like(acc_out)

    for k, part in enumerate(parts):
        acc[:, k * width : k * width + part.shape[1]] += part
    acc_out[...] += out

    @pl.when(step == steps - 1)
    def _():
        found = [acc[:, k * width : k * width + p.shape[1]] for k, p in enumerate(parts)]
        give([*found, acc_out[...]])


def fixed(shape, single=True):
    zeros = (0,) * len(shape)
    if single:
        return pl.BlockSpec(shape, lambda *_: zeros, pipeline_mode=pl.Buffered(1))
    return pl.BlockSpec(shape, lambda *_: zeros)


def lanes(seq_len):
    return pl.BlockSpec((seq_len, pair_lanes), lambda p, *_: (0, p))


def lanes_read(seq_len):
    if seq_len <= 2048:
        return lanes(seq_len)
    return pl.BlockSpec((seq_len, pair_lanes), lambda p, *_: (0, p), pipeline_mode=pl.Buffered(1))


def columns_of(w, layer, width):
    return pl.BlockSpec((1, w.shape[1], width), lambda p, *_: (layer, 0, p))


def rows_of(w, layer, height):
    return pl.BlockSpec((1, height, w.shape[2]), lambda p, *_: (layer, p, 0))


def shape(dims, dtype):
    return jax.ShapeDtypeStruct(dims, dtype)


def attention_specs(parts, layer, w4, t4, wo, to, seq_len, join):
    specs = [fixed(p.shape) for p in parts]
    specs += [columns_of(w, layer, pair_lanes) for w in (*w4, *t4)]
    specs += [rows_of(wo, layer, pair_lanes), rows_of(to, layer, pair_lanes)]
    return specs


def cost(microseconds):
    return pl.CostEstimate(flops=int(microseconds * 1.1e9), bytes_accessed=0, transcendentals=0)


def token_specs(tokens):
    return [pl.BlockSpec((16, 128), lambda *_: (0, 0)) for _ in tokens]


def forward_own(place, parts, layer, w4, t4, wo, to, wf, bias, doc_start, piece_len):
    seq_len, width = doc_start.shape[0], parts[0].shape[1]
    local_width = wo.shape[1]
    join = len(parts) > 1
    terms = (seq_len, pair_lanes)
    outs = [shape((seq_len, local_width), bf16)] * 3 + [shape((seq_len, local_width), f32)]
    outs += [shape(terms, f32), shape(terms, bf16), shape((piece_len, width), bf16)]
    specs = [lanes(seq_len)] * 4 + [fixed(terms, False)] * 2 + [fixed((piece_len, width), False)]
    if join:
        outs, specs = [shape((seq_len, width), bf16)] + outs, [fixed((seq_len, width))] + specs
    low, piece = pltpu.VMEM((seq_len, pair_lanes), bf16), pltpu.VMEM((piece_len, pair_lanes), bf16)
    got = pl.pallas_call(
        functools.partial(forward_own_kernel, len(parts), piece_len, join),
        grid_spec=pltpu.PrefetchScalarGridSpec(
            num_scalar_prefetch=1,
            grid=(local_width // pair_lanes,),
            in_specs=attention_specs(parts, layer, w4, t4, wo, to, seq_len, join)
            + [fixed(wf.shape), fixed(bias.shape), fixed(doc_start.shape)],
            out_specs=specs,
            scratch_shapes=[piece] * 2 + [low] * 2 + [pltpu.VMEM(terms, f32), pltpu.VMEM((piece_len, width), f32)],
        ),
        out_shape=outs,
        cost_estimate=cost(19),
        compiler_params=pltpu.CompilerParams(vmem_limit_bytes=60 << 20),
    )(place, *parts, *w4, *t4, wo, to, wf, bias, doc_start)
    got = list(got)
    a = got.pop(0) if join else parts[0]
    return a, got[:6], got[6]


def attention_backward(place, parts, layer, w4, t4, wo, to, wf, saved, doc_start, piece_len):
    q, k, v, gate, z, terms = saved
    seq_len, width = doc_start.shape[0], parts[0].shape[1]
    local_width = wo.shape[1]
    join = len(parts) > 1
    outs = [shape((seq_len, local_width), bf16)] * 5 + [shape((seq_len, pair_lanes), bf16)]
    outs += [shape((piece_len, width), bf16)]
    specs = [lanes(seq_len)] * 5 + [fixed((seq_len, pair_lanes), False), fixed((piece_len, width), False)]
    if join:
        outs, specs = [shape((seq_len, width), bf16)] + outs, [fixed((seq_len, width))] + specs
    low, high = pltpu.VMEM((seq_len, pair_lanes), bf16), pltpu.VMEM((seq_len, pair_lanes), f32)
    got = pl.pallas_call(
        functools.partial(backward_kernel, len(parts), piece_len, join),
        grid_spec=pltpu.PrefetchScalarGridSpec(
            num_scalar_prefetch=1,
            grid=(local_width // pair_lanes,),
            in_specs=attention_specs(parts, layer, w4, t4, wo, to, seq_len, join)
            + [fixed(wf.shape)]
            + [lanes_read(seq_len)] * 4
            + [fixed(z.shape), fixed(terms.shape), fixed(doc_start.shape)],
            out_specs=specs,
            scratch_shapes=[low] * 5 + [high] * 5 + [pltpu.VMEM((piece_len, width), f32)],
        ),
        out_shape=outs,
        cost_estimate=cost(33),
        compiler_params=pltpu.CompilerParams(vmem_limit_bytes=60 << 20),
    )(place, *parts, *w4, *t4, wo, to, wf, q, k, v, gate, z, terms, doc_start)
    got = list(got)
    y = got.pop(0) if join else parts[0]
    return y, got[:6], got[6]


def ffn_weights(layer, w3, t3):
    specs = []
    for wg, wu, wd in (w3, t3):
        specs += [
            columns_of(wg, layer, hidden_block), columns_of(wu, layer, hidden_block), rows_of(wd, layer, hidden_block),
        ]
    return specs


def blocks_of(rows):
    return pl.BlockSpec((rows, hidden_block), lambda p, *_: (0, p))


def ffn_forward(b, layer, w3, t3):
    rows, width = b.shape
    inner = w3[2].shape[1]
    return pl.pallas_call(
        ffn_forward_kernel,
        grid=(inner // hidden_block,),
        in_specs=[fixed(b.shape)] + ffn_weights(layer, w3, t3),
        out_specs=[blocks_of(rows)] * 2 + [fixed((rows, width), False)],
        scratch_shapes=[pltpu.VMEM((rows, width), f32)],
        out_shape=[shape((rows, inner), f32)] * 2 + [shape((rows, width), bf16)],
        cost_estimate=cost(7),
        compiler_params=pltpu.CompilerParams(vmem_limit_bytes=40 << 20),
    )(b, *w3, *t3)


def ffn_backward(g, gt, up, layer, w3, t3, *tokens):
    rows, width = g.shape
    return pl.pallas_call(
        ffn_backward_kernel,
        grid=(gt.shape[1] // hidden_block,),
        in_specs=[fixed(g.shape)] + [blocks_of(rows)] * 2 + ffn_weights(layer, w3, t3) + token_specs(tokens),
        out_specs=fixed((rows, width), False),
        scratch_shapes=[pltpu.VMEM((rows, width), f32)],
        out_shape=shape((rows, width), bf16),
        cost_estimate=cost(8),
        compiler_params=pltpu.CompilerParams(vmem_limit_bytes=40 << 20),
    )(g, gt, up, *w3, *t3, *tokens)


def ffn_theirs(place, b_parts, g_parts, layer, w3, t3, *tokens):
    width = b_parts[0].shape[1]
    half = width // 2
    rows = sum(p.size for p in b_parts) // width
    inner = w3[2].shape[1]
    wide = pl.BlockSpec((half, hidden_block), lambda p, *_: (0, p))
    return pl.pallas_call(
        functools.partial(ffn_theirs_kernel, len(b_parts)),
        grid_spec=pltpu.PrefetchScalarGridSpec(
            num_scalar_prefetch=1,
            grid=(inner // hidden_block,),
            in_specs=[fixed(p.shape) for p in (*b_parts, *g_parts)]
            + ffn_weights(layer, w3, t3)
            + token_specs(tokens),
            out_specs=[fixed((rows, width))] * 2
            + [blocks_of(rows)] * 3
            + [wide, wide, pl.BlockSpec((hidden_block, half), lambda p, *_: (p, 0))],
            scratch_shapes=[pltpu.VMEM((half, rows), bf16)],
        ),
        out_shape=[shape((rows, width), bf16)] * 2
        + [shape((rows, inner), bf16)] * 3
        + [shape((half, inner), bf16)] * 2
        + [shape((inner, half), bf16)],
        cost_estimate=cost(24),
        compiler_params=pltpu.CompilerParams(vmem_limit_bytes=60 << 20),
    )(place, *b_parts, *g_parts, *w3, *t3, *tokens)


def anywhere():
    return pl.BlockSpec(memory_space=pl.ANY)


def ffn_mine(layer, b, g, values, received, totals, *tokens):
    rows, width = b.shape
    half, inner = width // 2, values[0].shape[1]
    wide = pl.BlockSpec((half, hidden_block), lambda p: (0, p))
    tall = pl.BlockSpec((hidden_block, half), lambda p: (p, 0))
    wide_out = pl.BlockSpec((1, half, hidden_block), lambda p: (layer, 0, p))
    tall_out = pl.BlockSpec((1, hidden_block, half), lambda p: (layer, p, 0))
    return pl.pallas_call(
        ffn_mine_kernel,
        grid=(inner // hidden_block,),
        in_specs=[fixed((rows, half))] * 2
        + [blocks_of(rows)] * 3
        + [wide, wide, tall]
        + [anywhere()] * 3
        + token_specs(tokens),
        out_specs=[wide_out, wide_out, tall_out],
        out_shape=[shape(x.shape, x.dtype) for x in totals],
        scratch_shapes=[pltpu.VMEM((half, rows), bf16)],
        input_output_aliases={8: 0, 9: 1, 10: 2},
        cost_estimate=cost(9),
        compiler_params=pltpu.CompilerParams(vmem_limit_bytes=40 << 20),
    )(b, g, *values, *received, *totals, *tokens)


def attention_grads(layer, a, ds, dz, u, y, received=None, totals=None, tokens=()):
    rows, width = a.shape
    half, local_width = width // 2, u.shape[1]
    part = min(rows, 1024)
    steps = rows // part
    mine = received is not None
    side = 0 if mine else 1
    features = pl.BlockSpec((part, half), lambda p: (p, side))
    across = [pl.BlockSpec((part, x.shape[1]), lambda p: (p, 0)) for x in (*ds, dz, u)]
    specs = [features, *across, features]
    operands = [a, *ds, dz, u, y]
    flat = [(half, local_width)] * 4 + [(half, pair_lanes), (local_width, half)]
    if mine:
        specs += [fixed(x) for x in flat] + [anywhere()] * 5
        operands += [*received, *totals]
        outs = [shape(x.shape, f32) for x in totals[:4]] + [shape(flat[4], f32), shape(totals[4].shape, f32)]
        layered = pl.BlockSpec((1, half, local_width), lambda p: (layer, 0, 0))
        out_specs = [layered] * 4 + [fixed(flat[4], False)]
        out_specs += [pl.BlockSpec((1, local_width, half), lambda p: (layer, 0, 0))]
        aliases = {14: 0, 15: 1, 16: 2, 17: 3, 18: 5}
    else:
        outs, out_specs, aliases = [shape(x, bf16) for x in flat], [fixed(x, False) for x in flat], {}
    sizes = [(half, 4 * local_width + pair_lanes), (local_width, half)] if steps > 1 else [(8, 128)] * 2
    return pl.pallas_call(
        functools.partial(attention_grads_kernel, steps, mine),
        grid=(steps,),
        in_specs=specs + token_specs(tokens),
        out_specs=out_specs,
        out_shape=outs,
        scratch_shapes=[pltpu.VMEM(x, f32) for x in sizes],
        input_output_aliases=aliases,
        cost_estimate=cost(7),
        compiler_params=pltpu.CompilerParams(vmem_limit_bytes=60 << 20),
    )(*operands, *tokens)


def unset(*like):
    return pl.pallas_call(
        pass_kernel,
        out_specs=[pl.BlockSpec(memory_space=pl.ANY) for _ in like],
        out_shape=list(like),
    )()


def inverse_rms(h):
    return lax.rsqrt(jnp.mean(h * h, axis=-1, keepdims=True) + epsilon)


def norm_back(grad_normed, hidden, inverse, gain):
    scaled = hidden * inverse
    weighted = grad_normed * gain
    grad_gain = jnp.sum(grad_normed * scaled, axis=0)
    mean = jnp.mean(weighted * scaled, axis=-1, keepdims=True)
    return inverse * (weighted - scaled * mean), grad_gain


def local(
    hidden_in, segment_ids, w_query, w_key, w_value, w_gate_out, w_attn_out, w_forget, b_forget,
    gain_attn, gain_ffn, w_gate, w_up, w_down, cotangent,
):
    seq_count, piece_len, width = hidden_in.shape
    count_z, count_t = lax.axis_size("context"), lax.axis_size("tensor")
    core, z, t = lax.axis_index("fsdp"), lax.axis_index("context"), lax.axis_index("tensor")
    layers, half, local_width = w_query.shape
    heads = w_forget.shape[2]
    block = piece_len // count_t
    seq_len = piece_len * count_z
    shared_rows = count_z == 4
    place = jnp.stack([z, t]).astype(jnp.int32)
    own_place = place if shared_rows else jnp.zeros((2,), jnp.int32)

    def features(x):
        return jnp.where(core == 0, x, jnp.concatenate([x[..., half:], x[..., :half]], axis=-1))

    def own_block(x):
        return lax.dynamic_slice_in_dim(x, t * block, block, 0)

    def other(w):
        return swap(w, "fsdp", 1)

    def full(w, axis):
        return jnp.concatenate([w, other(w)], axis=axis)

    seg_all = gathered(segment_ids.reshape(1, piece_len), "context").reshape(seq_len)
    doc_start = jnp.sum((seg_all[None, :] < seg_all[:, None]).astype(jnp.int32), axis=1, keepdims=True)

    gains = full(jnp.concatenate([gain_attn, gain_ffn], axis=0), 1).astype(f32)
    hidden_rows = features(hidden_in.reshape(piece_len, width)).astype(f32)
    first_a = (hidden_rows * inverse_rms(hidden_rows) * gains[0]).astype(bf16)
    a_parts, _ = all_rows(own_block(first_a), first_a, seg_all)

    w_forget_full = jnp.pad(full(w_forget, 1), ((0, 0), (0, 0), (0, pair_lanes - heads)))
    bias = jnp.pad(b_forget, ((0, 0), (0, pair_lanes - heads)))
    w4 = (w_query, w_key, w_value, w_gate_out)
    t4 = tuple(other(w) for w in w4)
    to = other(w_attn_out)
    w3 = (w_gate, w_up, w_down)
    t3 = tuple(other(w) for w in w3)

    hidden = own_block(hidden_rows)
    saved = []
    cotangent_rows = features(cotangent.reshape(piece_len, width))
    last = layers - 1
    grad = own_block(cotangent_rows).astype(f32)
    for layer in range(layers):
        gain_one, gain_two = gains[layer], gains[layers + layer]
        inverse_one = inverse_rms(hidden)
        if layer > 0:
            a_parts, _ = all_rows((hidden * inverse_one * gain_one).astype(bf16))
        a, (q, k, v, gate, forget, terms), sends = forward_own(
            place, a_parts, layer, w4, t4, w_attn_out, to, w_forget_full[layer],
            bias[layer : layer + 1], doc_start, piece_len,
        )
        token = a_parts[-1]
        if shared_rows and layer == 0:
            g_far = far_blocks(after(own_block(cotangent_rows), token))
            sends = after(sends, *g_far)
        if shared_rows and layer == last:
            g_last = far_rows(g_far, token)
            tokens = [g_last]
            for s in saved:
                s["b_far"] = far_blocks(after(s["b_shard"], token))
                tokens += s["b_far"]
            sends = after(sends, *tokens)
        mixed = hidden + received_sum(sends)
        inverse_two = inverse_rms(mixed)
        b_shard = (mixed * inverse_two * gain_two).astype(bf16)
        b = gathered(b_shard, "tensor")
        if shared_rows and layer == last:
            for s in saved:
                s["b_rows"] = far_rows(s["b_far"], b)
        gt, up, sends = ffn_forward(b, layer, w3, t3)
        saved.append(
            dict(hidden=hidden, inverse_one=inverse_one, a=a, kept=(q, k, v, gate, forget, terms), mixed=mixed,
                 inverse_two=inverse_two, b=b, b_shard=b_shard, gt=gt, up=up)
        )
        if layer < last:
            hidden = mixed + received_sum(sends)

    def finish(x):
        return features(gathered(x.astype(bf16), "tensor")).reshape(1, piece_len, width)

    last_sends = sends
    wide = shape((layers, half, local_width), f32)
    inner = shape((layers, half, w_gate.shape[2]), f32)
    results = list(
        unset(
            wide, wide, wide, wide, shape((layers, local_width, half), f32),
            inner, inner, shape((layers, w_down.shape[1], half), f32),
        )
    )
    small = [[None] * layers for _ in range(2)]
    gain_grads = [None] * (2 * layers)

    for layer in reversed(range(layers)):
        s = saved[layer]
        gain_one, gain_two = gains[layer], gains[layers + layer]
        before_y, tokens = (), ()
        if layer == last:
            g = cotangent_rows
            if shared_rows:
                tokens = s["b_far"] = far_blocks(s["b_shard"])
        else:
            g_shard = grad.astype(bf16)
            g = gathered(g_shard, "tensor")
            if shared_rows:
                before_y = g_far = far_blocks(g_shard)
        sends = ffn_backward(g, s["gt"], s["up"], layer, w3, t3, *tokens)
        if shared_rows and layer == last:
            sends = after(sends, *[x["b_rows"] for x in saved[:-1]])
        back, gain_grads[layers + layer] = norm_back(received_sum(sends), s["mixed"], s["inverse_two"], gain_two)
        grad_mixed = grad + back
        y_parts, y_far = all_rows(after(grad_mixed.astype(bf16), *before_y), together=layer < last)
        y, (dq, dk, dv, dg, u, dz), sends = attention_backward(
            place, y_parts, layer, w4, t4, w_attn_out, to, w_forget_full[layer], s["kept"], doc_start, piece_len,
        )
        token = y_parts[-1]
        if layer == last:
            block_sum = own_block(last_sends).astype(f32) + s["mixed"]
            with_rows = lax.dynamic_update_slice_in_dim(last_sends, block_sum.astype(bf16), t * block, 0)
            output = lax.psum(after(with_rows, token), "tensor")
        if not shared_rows:
            s["b_parts"], s["g_parts"] = (s["b"],), (g,)
        elif layer == last:
            s["b_rows"] = far_rows(s["b_far"], token)
            g_near = near_rows(after(g, token))
            s["g_parts"] = (g, g_near, g_last)
            tokens = [s["b_rows"], g_near]
            for x in saved:
                x["b_near"] = near_rows(after(x["b"], token))
                tokens.append(x["b_near"])
            sends = after(sends, *tokens)
        else:
            s["g_parts"] = (g, near_rows(after(g, token)), far_rows(g_far, token))
            sends = after(sends, *s["g_parts"][1:])
        if shared_rows:
            s["b_parts"] = (s["b"], s["b_near"], s["b_rows"])
        back, gain_grads[layer] = norm_back(received_sum(sends), s["hidden"], s["inverse_one"], gain_one)
        grad = grad_mixed + back
        s.update(u=u, y=y, d=(dq, dk, dv, dg), dz=dz, y_far=y_far)

    def ffn_theirs_of(layer, *tokens):
        s = saved[layer]
        b, g, *values = ffn_theirs(own_place, s["b_parts"], s["g_parts"], layer, w3, t3, *tokens)
        s.update(ffn=(b, g, values[:3]), ffn_received=[other(x) for x in values[3:]])

    def ffn_mine_of(layer, *tokens):
        s = saved[layer]
        results[5:] = ffn_mine(layer, *s["ffn"], s["ffn_received"], results[5:], *tokens)

    def attention_grads_of(layer, tokens=(), mine_tokens=()):
        s = saved[layer]
        parts = (s["a"], s["d"], s["dz"], s["u"], s["y"])
        theirs = attention_grads(layer, *parts, tokens=tokens)
        found = attention_grads(layer, *parts, [other(x) for x in theirs], results[:5], mine_tokens)
        results[:5] = [*found[:4], found[5]]
        bias_grad = jnp.sum(s["dz"].astype(f32), axis=0)[:heads]
        small[0][layer] = found[4][:, :heads]
        small[1][layer] = bias_grad + other(bias_grad)

    for layer in reversed(range(layers)):
        ffn_theirs_of(layer, *(saved[layer - 1]["y_far"] if layer > 0 else ()))
    tokens = (saved[0]["ffn"][0], grad)
    for layer in reversed(range(1, layers)):
        attention_grads_of(layer, (), tokens)
        ffn_mine_of(layer, *tokens)
    attention_grads_of(0, tokens, saved[0]["ffn_received"])
    ffn_mine_of(0)
    if not shared_rows:
        results[5:] = [lax.psum(x, "context") for x in results[5:]]
    output = features(output).reshape(1, piece_len, width)
    grad_input = finish(grad)
    gain_total = lax.psum(features(jnp.stack(gain_grads)), ("fsdp", "context", "tensor"))
    gain_total = lax.dynamic_slice_in_dim(gain_total, core * half, half, 1)
    return (
        output, grad_input, *results[:5], jnp.stack(small[0]), jnp.stack(small[1]),
        gain_total[:layers], gain_total[layers:], *results[5:],
    )


def solution(mesh):
    rows = P("fsdp", "context", None)
    wide, tall = P(None, "fsdp", "tensor"), P(None, "tensor", "fsdp")
    heads, gain = P(None, "tensor"), P(None, "fsdp")
    return jax.shard_map(
        local,
        mesh=mesh,
        in_specs=(
            rows, P("fsdp", "context"), wide, wide, wide, wide, tall, wide, heads, gain, gain, wide, wide, tall, rows,
        ),
        out_specs=(rows, rows, wide, wide, wide, wide, tall, wide, heads, gain, gain, wide, wide, tall),
        check_vma=False,
    )
```

```python
import functools

import jax
import jax.numpy as jnp
from jax import lax
from jax.experimental import pallas as pl
from jax.experimental.pallas import tpu as pltpu
from jax.sharding import PartitionSpec as P

epsilon = 1e-06
masked_value = -1e30
bf16 = jnp.bfloat16
f32 = jnp.float32
pair_lanes = 128
hidden_block = 256
chunk_rows = 256


def query_rows(seq_len):
    return 256 if seq_len <= 2048 else 128


def swap(x, axis, k):
    n = lax.axis_size(axis)
    return lax.ppermute(x, axis, [(i, i ^ k) for i in range(n)])


def pass_kernel(*refs):
    pass


def after(x, *tokens):
    if not tokens:
        return x
    anywhere = pl.BlockSpec(memory_space=pl.ANY)
    return pl.pallas_call(
        pass_kernel,
        in_specs=[anywhere] * (1 + len(tokens)),
        out_specs=anywhere,
        out_shape=jax.ShapeDtypeStruct(x.shape, x.dtype),
        input_output_aliases={0: 0},
    )(x, *tokens)


def gathered(block, axis):
    count = lax.axis_size(axis)
    copies = jnp.broadcast_to(block[None], (count,) + block.shape)
    return lax.all_to_all(copies, axis, 0, 0, tiled=True).reshape((-1,) + block.shape[1:])


def sequence_rows(shard):
    return lax.all_gather(shard, ("context", "tensor"), tiled=True)


def near_rows(own):
    return swap(own, "context", 1)


def far_blocks(shard):
    return swap(shard, "context", 2), swap(shard, "context", 3)


def all_rows(shard, own=None, token=None, together=False):
    if own is None:
        own = gathered(shard, "tensor")
    if lax.axis_size("context") != 4:
        return (lax.all_gather(own, "context", tiled=True),), ()
    second, third = far_blocks(shard)
    near = near_rows(own)
    if together:
        block, width = shard.shape
        far = gathered(jnp.concatenate([second, third], axis=0), "tensor")
        return (own, near, far.reshape(-1, 2, block, width)), (second, third)
    if token is not None:
        second = after(second, token)
    third = after(third, second)
    blocks = [second] + [swap(second, "tensor", k) for k in range(1, lax.axis_size("tensor"))]
    return (own, near, *blocks, gathered(third, "tensor")), (second, third)


def received_sum(sends):
    count = lax.axis_size("tensor")
    got = lax.all_to_all(sends.reshape(count, -1, sends.shape[1]), "tensor", 0, 0, tiled=True)
    return jnp.sum(got.astype(f32), axis=0)


def dot_nt(a, b):
    return lax.dot_general(a, b, (((1,), (1,)), ((), ())), preferred_element_type=f32)


def dot_tn(a, b):
    return lax.dot_general(a, b, (((0,), (0,)), ((), ())), preferred_element_type=f32)


def dot_nn(a, b):
    return jnp.dot(a, b, preferred_element_type=f32)


def each(count, body):
    if count <= 4:
        for i in range(count):
            body(i)
        return

    def one(i, carry):
        body(i)
        return carry

    lax.fori_loop(0, count, one, 0)


def rows_at(i, rows):
    start = i * rows
    return pl.ds(start if isinstance(start, int) else pl.multiple_of(start, rows), rows)


def assemble(parts, whole_ref, place_ref):
    z, t = place_ref[0], place_ref[1]
    piece, blocks_seen, piece_len = 0, 0, parts[0].shape[0]
    for part in parts:
        if len(part.shape) == 4:
            blocks, pieces, block = part.shape[:3]
            for p in range(pieces):
                for b in range(blocks):
                    at = pl.multiple_of((z ^ (piece + p)) * piece_len + b * block, block)
                    whole_ref[pl.ds(at, block), :] = part[b, p]
            piece += pieces
            continue
        rows = part.shape[0]
        if rows == piece_len:
            at = pl.multiple_of((z ^ piece) * piece_len, piece_len)
            piece += 1
        else:
            at = pl.multiple_of((z ^ piece) * piece_len + (t ^ blocks_seen) * rows, rows)
            blocks_seen += 1
            if blocks_seen * rows == piece_len:
                piece, blocks_seen = piece + 1, 0
        whole_ref[pl.ds(at, rows), :] = part[...]


def triangle(rows, reverse):
    row = lax.broadcasted_iota(jnp.int32, (rows, rows), 0)
    column = lax.broadcasted_iota(jnp.int32, (rows, rows), 1)
    return jnp.where((column >= row) if reverse else (column <= row), 1.0, 0.0).astype(bf16)


def running_sum(ref, reverse):
    rows = chunk_rows
    ones = triangle(rows, reverse)
    count = ref.shape[0] // rows
    edge = 0 if reverse else rows - 1

    def chunk(i, carry):
        here = pl.ds(pl.multiple_of((count - 1 - i if reverse else i) * rows, rows), rows)
        high, middle, lowest = three_parts(ref[here, :])
        total = dot_nn(ones, high) + dot_nn(ones, middle) + dot_nn(ones, lowest) + carry
        ref[here, :] = total
        return total[edge : edge + 1, :]

    lax.fori_loop(0, count, chunk, jnp.zeros((1, ref.shape[1]), f32), unroll=count <= 4)


def log_sigmoid(z):
    e = jnp.exp(-jnp.abs(z))
    small = e * (1.0 - e * (1 / 2 - e * (1 / 3 - e * (1 / 4 - e * (1 / 5 - e * (1 / 6 - e * (1 / 7)))))))
    return jnp.minimum(z, 0.0) - jnp.where(e < 0.0625, small, jnp.log(1.0 + e))


def three_parts(x):
    high = x.astype(bf16)
    middle = (x - high.astype(f32)).astype(bf16)
    return high, middle, (x - high.astype(f32) - middle.astype(f32)).astype(bf16)


def decay_side(terms, pair, key_side):
    row = lax.broadcasted_iota(jnp.int32, (pair_lanes, pair_lanes), 0)
    lane = lax.broadcasted_iota(jnp.int32, (pair_lanes, pair_lanes), 1)
    spot = lane & 63
    term = spot if key_side else spot - 3
    head = jnp.where(lane >= 64, 2 * pair, 2 * pair + 1)
    chosen = (term >= 0) & (term < 3) & (row == 8 * term + head)
    pick = jnp.where(chosen, -1.0 if key_side else 1.0, 0.0).astype(bf16)
    lanes_now = lax.broadcasted_iota(jnp.int32, (1, pair_lanes), 1) & 63
    other = lanes_now - 3 if key_side else lanes_now
    ones = jnp.where((other >= 0) & (other < 3), 1.0, 0.0)
    return (dot_nn(terms, pick) + ones).astype(bf16)


def mix_keys(k_ref, terms_ref, pair, ka, kb):
    def mix(i):
        here = rows_at(i, chunk_rows)
        lane = lax.broadcasted_iota(jnp.int32, (chunk_rows, pair_lanes), 1)
        k, side = k_ref[here, :], decay_side(terms_ref[here, :], pair, True)
        ka[here, :] = jnp.where(lane < 64, k, side)
        kb[here, :] = jnp.where(lane < 64, side, k)

    each(k_ref.shape[0] // chunk_rows, mix)


def mix_queries(q_ref, terms_ref, start, pair, qa, qb):
    def mix(i):
        here = rows_at(i, chunk_rows)
        lane = lax.broadcasted_iota(jnp.int32, (chunk_rows, pair_lanes), 1)
        q = (q_ref[here, :].astype(f32) * 0.125).astype(bf16)
        terms = terms_ref[pl.ds(pl.multiple_of(start + i * chunk_rows, chunk_rows), chunk_rows), :]
        side = decay_side(terms, pair, False)
        qa[here, :] = jnp.where(lane < 64, q, side)
        qb[here, :] = jnp.where(lane < 64, side, q)

    each(q_ref.shape[0] // chunk_rows, mix)


def live_mask(start_ref, start, first, width, rows):
    key_pos = first + lax.broadcasted_iota(jnp.int32, (rows, width), 1)
    query_pos = start + lax.broadcasted_iota(jnp.int32, (rows, width), 0)
    doc_start = start_ref[pl.ds(start, rows), :]
    return (key_pos <= query_pos) & (key_pos >= doc_start)


def over_query_blocks(seq_len, rows, body):
    before = seq_len // 2
    if seq_len // rows <= 4:
        for start in range(0, seq_len, rows):
            first = max(0, start - before)
            body(start, first, start + rows - first)
        return
    width = before + rows

    def one(i, carry):
        start = pl.multiple_of(i * rows, rows)
        first = pl.multiple_of(jnp.maximum(start - before, 0), rows)
        body(start, first, width)
        return carry

    lax.fori_loop(0, seq_len // rows, one, 0)


def probabilities(q_rows, k_rows, mask):
    s = jnp.where(mask, dot_nt(q_rows, k_rows), masked_value)
    e = jnp.exp(s - jnp.max(s, axis=1, keepdims=True))
    return e * (1.0 / jnp.sum(e, axis=1, keepdims=True))


def lane_blocks(refs):
    return jnp.concatenate([r[0] for r in refs], axis=1)


def forward_own_kernel(count_parts, piece_len, join, *refs):
    place_ref, parts, refs = refs[0], refs[1 : 1 + count_parts], list(refs[1 + count_parts :])
    (wq, wk, wv, wg), (tq, tk, tv, tg) = refs[:4], refs[4:8]
    wo, to, wf, bias, start_ref = refs[8:13]
    refs = refs[13:]
    a_ref = refs.pop(0) if join else parts[0]
    q_ref, k_ref, v_ref, gate_ref, z_ref, terms_ref, send_ref, qa, qb, ka, kb, decay, acc = refs
    pair = pl.program_id(0)
    seq_len, half = a_ref.shape[0], a_ref.shape[1] // 2
    piece_start = pl.multiple_of(place_ref[0] * piece_len, piece_len)

    @pl.when(pair == 0)
    def _():
        if join:
            assemble(parts, a_ref, place_ref)
        acc[...] = jnp.zeros_like(acc)

        def gates(i):
            here = rows_at(i, chunk_rows)
            z = dot_nn(a_ref[here, :], wf[...]) + bias[...]
            z_ref[here, :] = z
            decay[here, :] = log_sigmoid(z)

        each(seq_len // chunk_rows, gates)
        running_sum(decay, False)

        def split(i):
            here = rows_at(i, chunk_rows)
            lane = lax.broadcasted_iota(jnp.int32, (chunk_rows, pair_lanes), 1)
            high, middle, lowest = (x.astype(f32) for x in three_parts(decay[here, :]))
            later = jnp.where(lane < 16, pltpu.roll(middle, 8, 1), pltpu.roll(lowest, 16, 1))
            terms = jnp.where(lane < 8, high, later)
            terms_ref[here, :] = jnp.where(lane < 24, terms, 0.0).astype(bf16)

        each(seq_len // chunk_rows, split)

    w_mine, w_theirs = lane_blocks((wq, wk, wv, wg)), lane_blocks((tq, tk, tv, tg))

    def project(i):
        here = rows_at(i, chunk_rows)
        out = dot_nn(a_ref[here, :half], w_mine) + dot_nn(a_ref[here, half:], w_theirs)
        q_ref[here, :] = out[:, :128].astype(bf16)
        k_ref[here, :] = out[:, 128:256].astype(bf16)
        v_ref[here, :] = out[:, 256:384].astype(bf16)
        gate_ref[here, :] = out[:, 384:]

    each(seq_len // chunk_rows, project)
    piece = pl.ds(piece_start, piece_len)
    gate = jax.nn.sigmoid(gate_ref[piece, :])
    mix_keys(k_ref, terms_ref, pair, ka, kb)
    mix_queries(q_ref.at[piece, :], terms_ref, piece_start, pair, qa, qb)
    before = seq_len // 2
    for s in range(0, piece_len, query_rows(seq_len)):
        rows = query_rows(seq_len)
        width = before + rows
        start = pl.multiple_of(piece_start + s, rows)
        first = pl.multiple_of(jnp.maximum(start - before, 0), rows)
        mask = live_mask(start_ref, start, first, width, rows)
        keys = pl.ds(first, width)
        out = []
        for q_of, k_of in ((qa, ka), (qb, kb)):
            p = probabilities(q_of[s : s + rows, :], k_of[keys, :], mask).astype(bf16)
            out.append(dot_nn(p, v_ref[keys, :]))
        lane = lax.broadcasted_iota(jnp.int32, (rows, pair_lanes), 1)
        u = (jnp.where(lane < 64, out[0], out[1]) * gate[s : s + rows, :]).astype(bf16)
        acc[s : s + rows, :half] += dot_nn(u, wo[0])
        acc[s : s + rows, half:] += dot_nn(u, to[0])

    @pl.when(pair == pl.num_programs(0) - 1)
    def _():
        send_ref[...] = acc[...].astype(bf16)


def backward_kernel(count_parts, piece_len, join, *refs):
    place_ref, parts, refs = refs[0], refs[1 : 1 + count_parts], list(refs[1 + count_parts :])
    mine, theirs, (wo, to, wf) = refs[:4], refs[4:8], refs[8:11]
    q_ref, k_ref, v_ref, gate_ref, z_ref, terms_ref, start_ref = refs[11:18]
    refs = refs[18:]
    y_ref = refs.pop(0) if join else parts[0]
    dq_ref, dk_ref, dv_ref, dg_ref, u_ref, dz_ref, send_ref = refs[:7]
    qa, qb, ka, kb, dd, dus, dka, dkb, dva, dcs, acc = refs[7:]
    pair = pl.program_id(0)
    seq_len, half = y_ref.shape[0], y_ref.shape[1] // 2
    rows = query_rows(seq_len)
    piece = pl.ds(pl.multiple_of(place_ref[0] * piece_len, piece_len), piece_len)

    @pl.when(pair == 0)
    def _():
        if join:
            assemble(parts, y_ref, place_ref)
        acc[...] = jnp.zeros_like(acc)
        dcs[...] = jnp.zeros_like(dcs)

    def gates(i):
        here = rows_at(i, chunk_rows)
        du = dot_nt(y_ref[here, :half], wo[0]) + dot_nt(y_ref[here, half:], to[0])
        sig = jax.nn.sigmoid(gate_ref[here, :])
        dd[here, :] = (du * sig).astype(bf16)
        dus[here, :] = du * sig * (1.0 - sig)

    each(seq_len // chunk_rows, gates)
    mix_keys(k_ref, terms_ref, pair, ka, kb)
    mix_queries(q_ref, terms_ref, 0, pair, qa, qb)
    dka[...] = jnp.zeros_like(dka)
    dkb[...] = jnp.zeros_like(dkb)
    dva[...] = jnp.zeros_like(dva)
    lane = lax.broadcasted_iota(jnp.int32, (rows, pair_lanes), 1)

    def pick(column_a, column_b):
        at = lax.broadcasted_iota(jnp.int32, (column_a.shape[0], pair_lanes), 1)
        return jnp.where(at == 2 * pair, column_a, jnp.where(at == 2 * pair + 1, column_b, 0.0))

    def body(start, first, width):
        mask = live_mask(start_ref, start, first, width, rows)
        here, keys = pl.ds(start, rows), pl.ds(first, width)
        values = v_ref[keys, :]
        d_rows = dd[here, :]
        dq, o = [], []
        for head, (q_of, k_of, dk_of) in enumerate(((qa, ka, dka), (qb, kb, dkb))):
            own_lanes = (lane < 64) if head == 0 else (lane >= 64)
            p = probabilities(q_of[here, :], k_of[keys, :], mask)
            d_mine = jnp.where(own_lanes, d_rows, jnp.zeros_like(d_rows))
            dp = dot_nt(d_mine, values)
            delta = jnp.sum(p * dp, axis=1, keepdims=True)
            ds = (p * (dp - delta)).astype(bf16)
            dq.append(dot_nn(ds, k_of[keys, :]))
            dk_of[keys, :] += dot_tn(ds, q_of[here, :])
            low = p.astype(bf16)
            dva[keys, :] += dot_tn(low, d_mine)
            o.append(dot_nn(low, values))
        o = jnp.where(lane < 64, o[0], o[1])
        dg_ref[here, :] = (dus[here, :] * o).astype(bf16)
        u_ref[here, :] = (o * jax.nn.sigmoid(gate_ref[here, :])).astype(bf16)
        dq_ref[here, :] = (jnp.where(lane < 64, dq[0], dq[1]) * 0.125).astype(bf16)
        dcs[here, :] += pick(dq[0][:, 67:68], dq[1][:, 3:4])

    over_query_blocks(seq_len, rows, body)

    def finish(i):
        here = rows_at(i, chunk_rows)
        lanes_now = lax.broadcasted_iota(jnp.int32, (chunk_rows, pair_lanes), 1)
        ka_rows, kb_rows = dka[here, :], dkb[here, :]
        dk_ref[here, :] = jnp.where(lanes_now < 64, ka_rows, kb_rows).astype(bf16)
        dv_ref[here, :] = dva[here, :].astype(bf16)
        dcs[here, :] -= pick(ka_rows[:, 64:65], kb_rows[:, 0:1])

    each(seq_len // chunk_rows, finish)
    d_own = jnp.concatenate([r[piece, :] for r in (dq_ref, dk_ref, dv_ref, dg_ref)], axis=1)
    acc[:, :half] += dot_nt(d_own, lane_blocks(mine))
    acc[:, half:] += dot_nt(d_own, lane_blocks(theirs))

    @pl.when(pair == pl.num_programs(0) - 1)
    def _():
        running_sum(dcs, True)

        def last(i):
            here = rows_at(i, chunk_rows)
            dz_ref[here, :] = (dcs[here, :] * jax.nn.sigmoid(-z_ref[here, :])).astype(bf16)

        each(seq_len // chunk_rows, last)
        send_ref[...] = (acc[...] + dot_nt(dz_ref[piece, :], wf[...])).astype(bf16)


def ffn_forward_kernel(b_ref, wg, wu, wd, tg, tu, td, gt_ref, up_ref, send_ref, acc):
    half = b_ref.shape[1] // 2
    low, high = b_ref[:, :half], b_ref[:, half:]
    gt = dot_nn(low, wg[0]) + dot_nn(high, tg[0])
    up = dot_nn(low, wu[0]) + dot_nn(high, tu[0])
    gt_ref[...] = gt
    up_ref[...] = up
    m = (gt * jax.nn.sigmoid(gt) * up).astype(bf16)

    @pl.when(pl.program_id(0) == 0)
    def _():
        acc[...] = jnp.zeros_like(acc)

    acc[:, :half] += dot_nn(m, wd[0])
    acc[:, half:] += dot_nn(m, td[0])

    @pl.when(pl.program_id(0) == pl.num_programs(0) - 1)
    def _():
        send_ref[...] = acc[...].astype(bf16)


def inner_grads(dm, gt, up):
    sig = jax.nn.sigmoid(gt)
    d_gate = (dm * up * sig * (1.0 + gt * (1.0 - sig))).astype(bf16)
    return d_gate, (dm * (gt * sig)).astype(bf16)


def ffn_backward_kernel(g_ref, gt_ref, up_ref, wg, wu, wd, tg, tu, td, *refs):
    send_ref, acc = refs[-2:]
    half = g_ref.shape[1] // 2
    dm = dot_nt(g_ref[:, :half], wd[0]) + dot_nt(g_ref[:, half:], td[0])
    d_gate, d_up = inner_grads(dm, gt_ref[...], up_ref[...])

    @pl.when(pl.program_id(0) == 0)
    def _():
        acc[...] = jnp.zeros_like(acc)

    acc[:, :half] += dot_nt(d_gate, wg[0]) + dot_nt(d_up, wu[0])
    acc[:, half:] += dot_nt(d_gate, tg[0]) + dot_nt(d_up, tu[0])

    @pl.when(pl.program_id(0) == pl.num_programs(0) - 1)
    def _():
        send_ref[...] = acc[...].astype(bf16)


def ffn_theirs_kernel(b_ref, g_ref, wg, wu, wd, tg, tu, td, *refs):
    m_ref, dgate_ref, dup_ref, gate_out, up_out, down_out, turned = refs[-7:]
    half = b_ref.shape[1] // 2

    @pl.when(pl.program_id(0) == 0)
    def _():
        turned[...] = b_ref[:, half:].T

    def chunk(i):
        here = rows_at(i, chunk_rows)
        low, high = b_ref[here, :half], b_ref[here, half:]
        gt = dot_nn(low, wg[0]) + dot_nn(high, tg[0])
        up = dot_nn(low, wu[0]) + dot_nn(high, tu[0])
        dm = dot_nt(g_ref[here, :half], wd[0]) + dot_nt(g_ref[here, half:], td[0])
        m_ref[here, :] = (gt * jax.nn.sigmoid(gt) * up).astype(bf16)
        dgate_ref[here, :], dup_ref[here, :] = inner_grads(dm, gt, up)

    each(b_ref.shape[0] // chunk_rows, chunk)
    gate_out[...] = dot_nn(turned[...], dgate_ref[...]).astype(bf16)
    up_out[...] = dot_nn(turned[...], dup_ref[...]).astype(bf16)
    down_out[...] = dot_tn(m_ref[...], g_ref[:, half:]).astype(bf16)


def ffn_mine_kernel(b_ref, g_ref, m_ref, dgate_ref, dup_ref, gate_in, up_in, down_in, *refs):
    gate_out, up_out, down_out, turned = refs[-4:]

    @pl.when(pl.program_id(0) == 0)
    def _():
        turned[...] = b_ref[...].T

    gate_out[0] = dot_nn(turned[...], dgate_ref[...]) + gate_in[...].astype(f32)
    up_out[0] = dot_nn(turned[...], dup_ref[...]) + up_in[...].astype(f32)
    down_out[0] = dot_tn(m_ref[...], g_ref[...]) + down_in[...].astype(f32)


def attention_grads_kernel(steps, mine, *refs):
    a_ref, dq, dk, dv, dg, dz, u_ref, y_ref = refs[:8]
    received = refs[8:14] if mine else [None] * 6
    acc, acc_out = refs[-2:]
    outs = refs[-8:-2]
    turned = a_ref[...].T
    width = dq.shape[1]
    parts = [dot_nn(turned, d[...]) for d in (dq, dk, dv, dg, dz)]
    out = dot_tn(u_ref[...], y_ref[...])

    def give(values):
        for ref, value, more in zip(outs, values, received):
            total = value if more is None else value + more[...].astype(f32)
            if len(ref.shape) == 3:
                ref[0] = total.astype(ref.dtype)
            else:
                ref[...] = total.astype(ref.dtype)

    if steps == 1:
        give([*parts, out])
        return
    step = pl.program_id(0)

    @pl.when(step == 0)
    def _():
        acc[...] = jnp.zeros_like(acc)
        acc_out[...] = jnp.zeros_like(acc_out)

    for k, part in enumerate(parts):
        acc[:, k * width : k * width + part.shape[1]] += part
    acc_out[...] += out

    @pl.when(step == steps - 1)
    def _():
        found = [acc[:, k * width : k * width + p.shape[1]] for k, p in enumerate(parts)]
        give([*found, acc_out[...]])


def fixed(shape, single=True):
    zeros = (0,) * len(shape)
    if single:
        return pl.BlockSpec(shape, lambda *_: zeros, pipeline_mode=pl.Buffered(1))
    return pl.BlockSpec(shape, lambda *_: zeros)


def lanes(seq_len):
    return pl.BlockSpec((seq_len, pair_lanes), lambda p, *_: (0, p))


def lanes_read(seq_len):
    if seq_len <= 2048:
        return lanes(seq_len)
    return pl.BlockSpec((seq_len, pair_lanes), lambda p, *_: (0, p), pipeline_mode=pl.Buffered(1))


def columns_of(w, layer, width):
    return pl.BlockSpec((1, w.shape[1], width), lambda p, *_: (layer, 0, p))


def rows_of(w, layer, height):
    return pl.BlockSpec((1, height, w.shape[2]), lambda p, *_: (layer, p, 0))


def shape(dims, dtype):
    return jax.ShapeDtypeStruct(dims, dtype)


def attention_specs(parts, layer, w4, t4, wo, to, seq_len, join):
    specs = [fixed(p.shape) for p in parts]
    specs += [columns_of(w, layer, pair_lanes) for w in (*w4, *t4)]
    specs += [rows_of(wo, layer, pair_lanes), rows_of(to, layer, pair_lanes)]
    return specs


def cost(microseconds):
    return pl.CostEstimate(flops=int(microseconds * 1.1e9), bytes_accessed=0, transcendentals=0)


def token_specs(tokens):
    return [pl.BlockSpec((16, 128), lambda *_: (0, 0)) for _ in tokens]


def forward_own(place, parts, layer, w4, t4, wo, to, wf, bias, doc_start, piece_len):
    seq_len, width = doc_start.shape[0], parts[0].shape[1]
    local_width = wo.shape[1]
    join = len(parts) > 1
    terms = (seq_len, pair_lanes)
    outs = [shape((seq_len, local_width), bf16)] * 3 + [shape((seq_len, local_width), f32)]
    outs += [shape(terms, f32), shape(terms, bf16), shape((piece_len, width), bf16)]
    specs = [lanes(seq_len)] * 4 + [fixed(terms, False)] * 2 + [fixed((piece_len, width), False)]
    if join:
        outs, specs = [shape((seq_len, width), bf16)] + outs, [fixed((seq_len, width))] + specs
    low, piece = pltpu.VMEM((seq_len, pair_lanes), bf16), pltpu.VMEM((piece_len, pair_lanes), bf16)
    got = pl.pallas_call(
        functools.partial(forward_own_kernel, len(parts), piece_len, join),
        grid_spec=pltpu.PrefetchScalarGridSpec(
            num_scalar_prefetch=1,
            grid=(local_width // pair_lanes,),
            in_specs=attention_specs(parts, layer, w4, t4, wo, to, seq_len, join)
            + [fixed(wf.shape), fixed(bias.shape), fixed(doc_start.shape)],
            out_specs=specs,
            scratch_shapes=[piece] * 2 + [low] * 2 + [pltpu.VMEM(terms, f32), pltpu.VMEM((piece_len, width), f32)],
        ),
        out_shape=outs,
        cost_estimate=cost(19),
        compiler_params=pltpu.CompilerParams(vmem_limit_bytes=60 << 20),
    )(place, *parts, *w4, *t4, wo, to, wf, bias, doc_start)
    got = list(got)
    a = got.pop(0) if join else parts[0]
    return a, got[:6], got[6]


def attention_backward(place, parts, layer, w4, t4, wo, to, wf, saved, doc_start, piece_len):
    q, k, v, gate, z, terms = saved
    seq_len, width = doc_start.shape[0], parts[0].shape[1]
    local_width = wo.shape[1]
    join = len(parts) > 1
    outs = [shape((seq_len, local_width), bf16)] * 5 + [shape((seq_len, pair_lanes), bf16)]
    outs += [shape((piece_len, width), bf16)]
    specs = [lanes(seq_len)] * 5 + [fixed((seq_len, pair_lanes), False), fixed((piece_len, width), False)]
    if join:
        outs, specs = [shape((seq_len, width), bf16)] + outs, [fixed((seq_len, width))] + specs
    low, high = pltpu.VMEM((seq_len, pair_lanes), bf16), pltpu.VMEM((seq_len, pair_lanes), f32)
    got = pl.pallas_call(
        functools.partial(backward_kernel, len(parts), piece_len, join),
        grid_spec=pltpu.PrefetchScalarGridSpec(
            num_scalar_prefetch=1,
            grid=(local_width // pair_lanes,),
            in_specs=attention_specs(parts, layer, w4, t4, wo, to, seq_len, join)
            + [fixed(wf.shape)]
            + [lanes_read(seq_len)] * 4
            + [fixed(z.shape), fixed(terms.shape), fixed(doc_start.shape)],
            out_specs=specs,
            scratch_shapes=[low] * 5 + [high] * 5 + [pltpu.VMEM((piece_len, width), f32)],
        ),
        out_shape=outs,
        cost_estimate=cost(33),
        compiler_params=pltpu.CompilerParams(vmem_limit_bytes=60 << 20),
    )(place, *parts, *w4, *t4, wo, to, wf, q, k, v, gate, z, terms, doc_start)
    got = list(got)
    y = got.pop(0) if join else parts[0]
    return y, got[:6], got[6]


def ffn_weights(layer, w3, t3):
    specs = []
    for wg, wu, wd in (w3, t3):
        specs += [
            columns_of(wg, layer, hidden_block), columns_of(wu, layer, hidden_block), rows_of(wd, layer, hidden_block),
        ]
    return specs


def blocks_of(rows):
    return pl.BlockSpec((rows, hidden_block), lambda p, *_: (0, p))


def ffn_forward(b, layer, w3, t3):
    rows, width = b.shape
    inner = w3[2].shape[1]
    return pl.pallas_call(
        ffn_forward_kernel,
        grid=(inner // hidden_block,),
        in_specs=[fixed(b.shape)] + ffn_weights(layer, w3, t3),
        out_specs=[blocks_of(rows)] * 2 + [fixed((rows, width), False)],
        scratch_shapes=[pltpu.VMEM((rows, width), f32)],
        out_shape=[shape((rows, inner), f32)] * 2 + [shape((rows, width), bf16)],
        cost_estimate=cost(7),
        compiler_params=pltpu.CompilerParams(vmem_limit_bytes=60 << 20),
    )(b, *w3, *t3)


def ffn_backward(g, gt, up, layer, w3, t3, *tokens):
    rows, width = g.shape
    return pl.pallas_call(
        ffn_backward_kernel,
        grid=(gt.shape[1] // hidden_block,),
        in_specs=[fixed(g.shape)] + [blocks_of(rows)] * 2 + ffn_weights(layer, w3, t3) + token_specs(tokens),
        out_specs=fixed((rows, width), False),
        scratch_shapes=[pltpu.VMEM((rows, width), f32)],
        out_shape=shape((rows, width), bf16),
        cost_estimate=cost(8),
        compiler_params=pltpu.CompilerParams(vmem_limit_bytes=60 << 20),
    )(g, gt, up, *w3, *t3, *tokens)


def ffn_theirs(b, g, layer, w3, t3, *tokens):
    rows, width = b.shape
    half = width // 2
    inner = w3[2].shape[1]
    wide = pl.BlockSpec((half, hidden_block), lambda p: (0, p))
    return pl.pallas_call(
        ffn_theirs_kernel,
        grid=(inner // hidden_block,),
        in_specs=[fixed(b.shape), fixed(g.shape)] + ffn_weights(layer, w3, t3) + token_specs(tokens),
        out_specs=[blocks_of(rows)] * 3 + [wide, wide, pl.BlockSpec((hidden_block, half), lambda p: (p, 0))],
        scratch_shapes=[pltpu.VMEM((half, rows), bf16)],
        out_shape=[shape((rows, inner), bf16)] * 3
        + [shape((half, inner), bf16)] * 2
        + [shape((inner, half), bf16)],
        cost_estimate=cost(24),
        compiler_params=pltpu.CompilerParams(vmem_limit_bytes=60 << 20),
    )(b, g, *w3, *t3, *tokens)


def anywhere():
    return pl.BlockSpec(memory_space=pl.ANY)


def ffn_mine(layer, b, g, values, received, totals, *tokens):
    rows, width = b.shape
    half, inner = width // 2, values[0].shape[1]
    wide = pl.BlockSpec((half, hidden_block), lambda p: (0, p))
    tall = pl.BlockSpec((hidden_block, half), lambda p: (p, 0))
    wide_out = pl.BlockSpec((1, half, hidden_block), lambda p: (layer, 0, p))
    tall_out = pl.BlockSpec((1, hidden_block, half), lambda p: (layer, p, 0))
    return pl.pallas_call(
        ffn_mine_kernel,
        grid=(inner // hidden_block,),
        in_specs=[fixed((rows, half))] * 2
        + [blocks_of(rows)] * 3
        + [wide, wide, tall]
        + [anywhere()] * 3
        + token_specs(tokens),
        out_specs=[wide_out, wide_out, tall_out],
        out_shape=[shape(x.shape, x.dtype) for x in totals],
        scratch_shapes=[pltpu.VMEM((half, rows), bf16)],
        input_output_aliases={8: 0, 9: 1, 10: 2},
        cost_estimate=cost(9),
        compiler_params=pltpu.CompilerParams(vmem_limit_bytes=60 << 20),
    )(b, g, *values, *received, *totals, *tokens)


def attention_grads(layer, a, ds, dz, u, y, received=None, totals=None, tokens=()):
    rows, width = a.shape
    half, local_width = width // 2, u.shape[1]
    part = min(rows, 1024)
    steps = rows // part
    mine = received is not None
    side = 0 if mine else 1
    features = pl.BlockSpec((part, half), lambda p: (p, side))
    across = [pl.BlockSpec((part, x.shape[1]), lambda p: (p, 0)) for x in (*ds, dz, u)]
    specs = [features, *across, features]
    operands = [a, *ds, dz, u, y]
    flat = [(half, local_width)] * 4 + [(half, pair_lanes), (local_width, half)]
    if mine:
        specs += [fixed(x) for x in flat] + [anywhere()] * 5
        operands += [*received, *totals]
        outs = [shape(x.shape, f32) for x in totals[:4]] + [shape(flat[4], f32), shape(totals[4].shape, f32)]
        layered = pl.BlockSpec((1, half, local_width), lambda p: (layer, 0, 0))
        out_specs = [layered] * 4 + [fixed(flat[4], False)]
        out_specs += [pl.BlockSpec((1, local_width, half), lambda p: (layer, 0, 0))]
        aliases = {14: 0, 15: 1, 16: 2, 17: 3, 18: 5}
    else:
        outs, out_specs, aliases = [shape(x, bf16) for x in flat], [fixed(x, False) for x in flat], {}
    sizes = [(half, 4 * local_width + pair_lanes), (local_width, half)] if steps > 1 else [(8, 128)] * 2
    return pl.pallas_call(
        functools.partial(attention_grads_kernel, steps, mine),
        grid=(steps,),
        in_specs=specs + token_specs(tokens),
        out_specs=out_specs,
        out_shape=outs,
        scratch_shapes=[pltpu.VMEM(x, f32) for x in sizes],
        input_output_aliases=aliases,
        cost_estimate=cost(7),
        compiler_params=pltpu.CompilerParams(vmem_limit_bytes=60 << 20),
    )(*operands, *tokens)


def unset(*like):
    return pl.pallas_call(
        pass_kernel,
        out_specs=[pl.BlockSpec(memory_space=pl.ANY) for _ in like],
        out_shape=list(like),
    )()


def inverse_rms(h):
    return lax.rsqrt(jnp.mean(h * h, axis=-1, keepdims=True) + epsilon)


def norm_back(grad_normed, hidden, inverse, gain):
    scaled = hidden * inverse
    weighted = grad_normed * gain
    grad_gain = jnp.sum(grad_normed * scaled, axis=0)
    mean = jnp.mean(weighted * scaled, axis=-1, keepdims=True)
    return inverse * (weighted - scaled * mean), grad_gain


def local(
    hidden_in, segment_ids, w_query, w_key, w_value, w_gate_out, w_attn_out, w_forget, b_forget,
    gain_attn, gain_ffn, w_gate, w_up, w_down, cotangent,
):
    seq_count, piece_len, width = hidden_in.shape
    count_z, count_t = lax.axis_size("context"), lax.axis_size("tensor")
    core, z, t = lax.axis_index("fsdp"), lax.axis_index("context"), lax.axis_index("tensor")
    layers, half, local_width = w_query.shape
    heads = w_forget.shape[2]
    block = piece_len // count_t
    seq_len = piece_len * count_z
    shared_rows = count_z == 4
    place = jnp.stack([z, t]).astype(jnp.int32)

    def features(x):
        return jnp.where(core == 0, x, jnp.concatenate([x[..., half:], x[..., :half]], axis=-1))

    def own_block(x):
        return lax.dynamic_slice_in_dim(x, t * block, block, 0)

    def other(w):
        return swap(w, "fsdp", 1)

    def full(w, axis):
        return jnp.concatenate([w, other(w)], axis=axis)

    seg_all = gathered(segment_ids.reshape(1, piece_len), "context").reshape(seq_len)
    doc_start = jnp.sum((seg_all[None, :] < seg_all[:, None]).astype(jnp.int32), axis=1, keepdims=True)

    gains = full(jnp.concatenate([gain_attn, gain_ffn], axis=0), 1).astype(f32)
    hidden_rows = features(hidden_in.reshape(piece_len, width)).astype(f32)
    first_a = (hidden_rows * inverse_rms(hidden_rows) * gains[0]).astype(bf16)
    a_parts, _ = all_rows(own_block(first_a), first_a, seg_all)

    w_forget_full = jnp.pad(full(w_forget, 1), ((0, 0), (0, 0), (0, pair_lanes - heads)))
    bias = jnp.pad(b_forget, ((0, 0), (0, pair_lanes - heads)))
    w4 = (w_query, w_key, w_value, w_gate_out)
    t4 = tuple(other(w) for w in w4)
    to = other(w_attn_out)
    w3 = (w_gate, w_up, w_down)
    t3 = tuple(other(w) for w in w3)

    hidden = own_block(hidden_rows)
    saved = []
    cotangent_rows = features(cotangent.reshape(piece_len, width))
    last = layers - 1
    grad = own_block(cotangent_rows).astype(f32)
    for layer in range(layers):
        gain_one, gain_two = gains[layer], gains[layers + layer]
        inverse_one = inverse_rms(hidden)
        if layer > 0:
            a_parts, _ = all_rows((hidden * inverse_one * gain_one).astype(bf16))
        forget_weights = w_forget_full[layer]
        if shared_rows and layer == 1:
            forget_weights = after(forget_weights, g_last)
        a, (q, k, v, gate, forget, terms), sends = forward_own(
            place, a_parts, layer, w4, t4, w_attn_out, to, forget_weights,
            bias[layer : layer + 1], doc_start, piece_len,
        )
        if shared_rows:
            token = a_parts[-1]
            if layer == 0:
                g_last = sequence_rows(after(own_block(cotangent_rows), token))
            else:
                saved[-1]["b_rows"] = sequence_rows(after(saved[-1]["b_shard"], token))
        mixed = hidden + received_sum(sends)
        inverse_two = inverse_rms(mixed)
        b_shard = (mixed * inverse_two * gain_two).astype(bf16)
        b = gathered(b_shard, "tensor")
        gt, up, sends = ffn_forward(b, layer, w3, t3)
        saved.append(
            dict(hidden=hidden, inverse_one=inverse_one, a=a, kept=(q, k, v, gate, forget, terms), mixed=mixed,
                 inverse_two=inverse_two, b=b, b_shard=b_shard, gt=gt, up=up)
        )
        if layer < last:
            hidden = mixed + received_sum(sends)

    def finish(x):
        return features(gathered(x.astype(bf16), "tensor")).reshape(1, piece_len, width)

    last_sends = sends
    wide = shape((layers, half, local_width), f32)
    inner = shape((layers, half, w_gate.shape[2]), f32)
    results = list(
        unset(
            wide, wide, wide, wide, shape((layers, local_width, half), f32),
            inner, inner, shape((layers, w_down.shape[1], half), f32),
        )
    )
    small = [[None] * layers for _ in range(2)]
    gain_grads = [None] * (2 * layers)

    def ffn_theirs_of(layer, *tokens):
        s = saved[layer]
        values = ffn_theirs(s["b_rows"], s["g_rows"], layer, w3, t3, *tokens)
        s.update(values=values[:3], ffn_received=[other(x) for x in values[3:]])

    for layer in reversed(range(layers)):
        s = saved[layer]
        gain_one, gain_two = gains[layer], gains[layers + layer]
        if layer == last:
            g = cotangent_rows
        else:
            g_shard = grad.astype(bf16)
            g = gathered(g_shard, "tensor")
            if shared_rows:
                s["g_rows"] = sequence_rows(g_shard)
        sends = ffn_backward(g, s["gt"], s["up"], layer, w3, t3)
        back, gain_grads[layers + layer] = norm_back(received_sum(sends), s["mixed"], s["inverse_two"], gain_two)
        grad_mixed = grad + back
        y_parts, y_far = all_rows(grad_mixed.astype(bf16), together=layer < last)
        kept = s["kept"]
        if layer == last and shared_rows:
            kept = (*kept[:-1], after(kept[-1], *[x["b_rows"] for x in saved[:-1]]))
        if layer < last:
            ffn_theirs_of(layer + 1, *y_far)
            kept = (*kept[:-1], after(kept[-1], saved[layer + 1]["values"][0]))
        y, (dq, dk, dv, dg, u, dz), sends = attention_backward(
            place, y_parts, layer, w4, t4, w_attn_out, to, w_forget_full[layer], kept, doc_start, piece_len,
        )
        token = y_parts[-1]
        if layer == last:
            block_sum = own_block(last_sends).astype(f32) + s["mixed"]
            with_rows = lax.dynamic_update_slice_in_dim(last_sends, block_sum.astype(bf16), t * block, 0)
            output = lax.psum(after(with_rows, token), "tensor")
        if not shared_rows:
            s.update(b_rows=s["b"], g_rows=g)
        elif layer == last:
            s.update(b_rows=sequence_rows(after(s["b_shard"], token)), g_rows=g_last)
        back, gain_grads[layer] = norm_back(received_sum(sends), s["hidden"], s["inverse_one"], gain_one)
        grad = grad_mixed + back
        s.update(u=u, y=y, d=(dq, dk, dv, dg), dz=dz, y_far=y_far)

    def ffn_mine_of(layer, *tokens):
        s = saved[layer]
        received = s["ffn_received"]
        results[5:] = ffn_mine(layer, s["b_rows"], s["g_rows"], s["values"], received, results[5:], *tokens)

    def attention_grads_of(layer, tokens=(), mine_tokens=()):
        s = saved[layer]
        parts = (s["a"], s["d"], s["dz"], s["u"], s["y"])
        theirs = attention_grads(layer, *parts, tokens=tokens)
        found = attention_grads(layer, *parts, [other(x) for x in theirs], results[:5], mine_tokens)
        results[:5] = [*found[:4], found[5]]
        bias_grad = jnp.sum(s["dz"].astype(f32), axis=0)[:heads]
        small[0][layer] = found[4][:, :heads]
        small[1][layer] = bias_grad + other(bias_grad)

    ffn_theirs_of(0)
    tokens = (saved[0]["values"][0], grad)
    for layer in reversed(range(1, layers)):
        attention_grads_of(layer, (), tokens)
        ffn_mine_of(layer, *tokens)
    attention_grads_of(0, tokens, saved[0]["ffn_received"])
    ffn_mine_of(0)
    if not shared_rows:
        results[5:] = [lax.psum(x, "context") for x in results[5:]]
    output = features(after(output, saved[0]["values"][0])).reshape(1, piece_len, width)
    grad_input = finish(grad)
    gain_total = jnp.stack(gain_grads).reshape(1, -1)
    for axis in (("context", "tensor"),) if shared_rows else ("context", "tensor"):
        gain_total = jnp.sum(gathered(gain_total, axis), axis=0, keepdims=True)
    gain_total = gain_total.reshape(2 * layers, width)
    gain_total = gain_total[:, :half] + other(gain_total[:, half:])
    return (
        output, grad_input, *results[:5], jnp.stack(small[0]), jnp.stack(small[1]),
        gain_total[:layers], gain_total[layers:], *results[5:],
    )


def solution(mesh):
    rows = P("fsdp", "context", None)
    wide, tall = P(None, "fsdp", "tensor"), P(None, "tensor", "fsdp")
    heads, gain = P(None, "tensor"), P(None, "fsdp")
    return jax.shard_map(
        local,
        mesh=mesh,
        in_specs=(
            rows, P("fsdp", "context"), wide, wide, wide, wide, tall, wide, heads, gain, gain, wide, wide, tall, rows,
        ),
        out_specs=(rows, rows, wide, wide, wide, wide, tall, wide, heads, gain, gain, wide, wide, tall),
        check_vma=False,
    )
```

```python
import functools

import jax
import jax.numpy as jnp
from jax import lax
from jax.experimental import pallas as pl
from jax.experimental.pallas import tpu as pltpu
from jax.sharding import PartitionSpec as P

epsilon = 1e-06
masked_value = -1e30
bf16 = jnp.bfloat16
f32 = jnp.float32
pair_lanes = 128
hidden_block = 256
chunk_rows = 256


def query_rows(seq_len):
    return 256 if seq_len <= 2048 else 128


def swap(x, axis, k):
    n = lax.axis_size(axis)
    return lax.ppermute(x, axis, [(i, i ^ k) for i in range(n)])


def pass_kernel(*refs):
    pass


def after(x, *tokens):
    if not tokens:
        return x
    anywhere = pl.BlockSpec(memory_space=pl.ANY)
    return pl.pallas_call(
        pass_kernel,
        in_specs=[anywhere] * (1 + len(tokens)),
        out_specs=anywhere,
        out_shape=jax.ShapeDtypeStruct(x.shape, x.dtype),
        input_output_aliases={0: 0},
    )(x, *tokens)


def gathered(block, axis):
    count = lax.axis_size(axis)
    copies = jnp.broadcast_to(block[None], (count,) + block.shape)
    return lax.all_to_all(copies, axis, 0, 0, tiled=True).reshape((-1,) + block.shape[1:])


def sequence_rows(shard):
    return lax.all_gather(shard, ("context", "tensor"), tiled=True)


def near_rows(own):
    return swap(own, "context", 1)


def far_blocks(shard):
    return swap(shard, "context", 2), swap(shard, "context", 3)


def all_rows(shard, own=None, token=None, together=False):
    if own is None:
        own = gathered(shard, "tensor")
    if lax.axis_size("context") != 4:
        return (lax.all_gather(own, "context", tiled=True),), ()
    second, third = far_blocks(shard)
    near = near_rows(own)
    if together:
        block, width = shard.shape
        far = gathered(jnp.concatenate([second, third], axis=0), "tensor")
        return (own, near, far.reshape(-1, 2, block, width)), (second, third)
    if token is not None:
        second = after(second, token)
    third = after(third, second)
    blocks = [second] + [swap(second, "tensor", k) for k in range(1, lax.axis_size("tensor"))]
    return (own, near, *blocks, gathered(third, "tensor")), (second, third)


def received_sum(sends):
    count = lax.axis_size("tensor")
    got = lax.all_to_all(sends.reshape(count, -1, sends.shape[1]), "tensor", 0, 0, tiled=True)
    return jnp.sum(got.astype(f32), axis=0)


def dot_nt(a, b):
    return lax.dot_general(a, b, (((1,), (1,)), ((), ())), preferred_element_type=f32)


def dot_tn(a, b):
    return lax.dot_general(a, b, (((0,), (0,)), ((), ())), preferred_element_type=f32)


def dot_nn(a, b):
    return jnp.dot(a, b, preferred_element_type=f32)


def each(count, body):
    if count <= 4:
        for i in range(count):
            body(i)
        return

    def one(i, carry):
        body(i)
        return carry

    lax.fori_loop(0, count, one, 0)


def rows_at(i, rows):
    start = i * rows
    return pl.ds(start if isinstance(start, int) else pl.multiple_of(start, rows), rows)


def assemble(parts, whole_ref, place_ref):
    z, t = place_ref[0], place_ref[1]
    piece, blocks_seen, piece_len = 0, 0, parts[0].shape[0]
    for part in parts:
        if len(part.shape) == 4:
            blocks, pieces, block = part.shape[:3]
            for p in range(pieces):
                for b in range(blocks):
                    at = pl.multiple_of((z ^ (piece + p)) * piece_len + b * block, block)
                    whole_ref[pl.ds(at, block), :] = part[b, p]
            piece += pieces
            continue
        rows = part.shape[0]
        if rows == piece_len:
            at = pl.multiple_of((z ^ piece) * piece_len, piece_len)
            piece += 1
        else:
            at = pl.multiple_of((z ^ piece) * piece_len + (t ^ blocks_seen) * rows, rows)
            blocks_seen += 1
            if blocks_seen * rows == piece_len:
                piece, blocks_seen = piece + 1, 0
        whole_ref[pl.ds(at, rows), :] = part[...]


def triangle(rows, reverse):
    row = lax.broadcasted_iota(jnp.int32, (rows, rows), 0)
    column = lax.broadcasted_iota(jnp.int32, (rows, rows), 1)
    return jnp.where((column >= row) if reverse else (column <= row), 1.0, 0.0).astype(bf16)


def running_sum(ref, reverse):
    rows = chunk_rows
    ones = triangle(rows, reverse)
    count = ref.shape[0] // rows
    edge = 0 if reverse else rows - 1

    def chunk(i, carry):
        here = pl.ds(pl.multiple_of((count - 1 - i if reverse else i) * rows, rows), rows)
        high, middle, lowest = three_parts(ref[here, :])
        total = dot_nn(ones, high) + dot_nn(ones, middle) + dot_nn(ones, lowest) + carry
        ref[here, :] = total
        return total[edge : edge + 1, :]

    lax.fori_loop(0, count, chunk, jnp.zeros((1, ref.shape[1]), f32), unroll=count <= 4)


def log_sigmoid(z):
    e = jnp.exp(-jnp.abs(z))
    small = e * (1.0 - e * (1 / 2 - e * (1 / 3 - e * (1 / 4 - e * (1 / 5 - e * (1 / 6 - e * (1 / 7)))))))
    return jnp.minimum(z, 0.0) - jnp.where(e < 0.0625, small, jnp.log(1.0 + e))


def three_parts(x):
    high = x.astype(bf16)
    middle = (x - high.astype(f32)).astype(bf16)
    return high, middle, (x - high.astype(f32) - middle.astype(f32)).astype(bf16)


def decay_side(terms, pair, key_side):
    row = lax.broadcasted_iota(jnp.int32, (pair_lanes, pair_lanes), 0)
    lane = lax.broadcasted_iota(jnp.int32, (pair_lanes, pair_lanes), 1)
    spot = lane & 63
    term = spot if key_side else spot - 3
    head = jnp.where(lane >= 64, 2 * pair, 2 * pair + 1)
    chosen = (term >= 0) & (term < 3) & (row == 8 * term + head)
    pick = jnp.where(chosen, -1.0 if key_side else 1.0, 0.0).astype(bf16)
    lanes_now = lax.broadcasted_iota(jnp.int32, (1, pair_lanes), 1) & 63
    other = lanes_now - 3 if key_side else lanes_now
    ones = jnp.where((other >= 0) & (other < 3), 1.0, 0.0)
    return (dot_nn(terms, pick) + ones).astype(bf16)


def mix_keys(k_ref, terms_ref, pair, ka, kb):
    def mix(i):
        here = rows_at(i, chunk_rows)
        lane = lax.broadcasted_iota(jnp.int32, (chunk_rows, pair_lanes), 1)
        k, side = k_ref[here, :], decay_side(terms_ref[here, :], pair, True)
        ka[here, :] = jnp.where(lane < 64, k, side)
        kb[here, :] = jnp.where(lane < 64, side, k)

    each(k_ref.shape[0] // chunk_rows, mix)


def mix_queries(q_ref, terms_ref, start, pair, qa, qb):
    def mix(i):
        here = rows_at(i, chunk_rows)
        lane = lax.broadcasted_iota(jnp.int32, (chunk_rows, pair_lanes), 1)
        q = (q_ref[here, :].astype(f32) * 0.125).astype(bf16)
        terms = terms_ref[pl.ds(pl.multiple_of(start + i * chunk_rows, chunk_rows), chunk_rows), :]
        side = decay_side(terms, pair, False)
        qa[here, :] = jnp.where(lane < 64, q, side)
        qb[here, :] = jnp.where(lane < 64, side, q)

    each(q_ref.shape[0] // chunk_rows, mix)


def live_mask(start_ref, start, first, width, rows):
    key_pos = first + lax.broadcasted_iota(jnp.int32, (rows, width), 1)
    query_pos = start + lax.broadcasted_iota(jnp.int32, (rows, width), 0)
    doc_start = start_ref[pl.ds(start, rows), :]
    return (key_pos <= query_pos) & (key_pos >= doc_start)


def over_query_blocks(seq_len, rows, body):
    before = seq_len // 2
    if seq_len // rows <= 4:
        for start in range(0, seq_len, rows):
            first = max(0, start - before)
            body(start, first, start + rows - first)
        return
    width = before + rows

    def one(i, carry):
        start = pl.multiple_of(i * rows, rows)
        first = pl.multiple_of(jnp.maximum(start - before, 0), rows)
        body(start, first, width)
        return carry

    lax.fori_loop(0, seq_len // rows, one, 0)


def probabilities(q_rows, k_rows, mask):
    s = jnp.where(mask, dot_nt(q_rows, k_rows), masked_value)
    e = jnp.exp(s - jnp.max(s, axis=1, keepdims=True))
    return e * (1.0 / jnp.sum(e, axis=1, keepdims=True))


def lane_blocks(refs):
    return jnp.concatenate([r[0] for r in refs], axis=1)


def forward_own_kernel(count_parts, piece_len, join, *refs):
    place_ref, parts, refs = refs[0], refs[1 : 1 + count_parts], list(refs[1 + count_parts :])
    (wq, wk, wv, wg), (tq, tk, tv, tg) = refs[:4], refs[4:8]
    wo, to, wf, bias, start_ref = refs[8:13]
    refs = refs[13:]
    a_ref = refs.pop(0) if join else parts[0]
    q_ref, k_ref, v_ref, gate_ref, z_ref, terms_ref, send_ref, qa, qb, ka, kb, decay, acc = refs
    pair = pl.program_id(0)
    seq_len, half = a_ref.shape[0], a_ref.shape[1] // 2
    piece_start = pl.multiple_of(place_ref[0] * piece_len, piece_len)

    @pl.when(pair == 0)
    def _():
        if join:
            assemble(parts, a_ref, place_ref)
        acc[...] = jnp.zeros_like(acc)

        def gates(i):
            here = rows_at(i, chunk_rows)
            z = dot_nn(a_ref[here, :], wf[...]) + bias[...]
            z_ref[here, :] = z
            decay[here, :] = log_sigmoid(z)

        each(seq_len // chunk_rows, gates)
        running_sum(decay, False)

        def split(i):
            here = rows_at(i, chunk_rows)
            lane = lax.broadcasted_iota(jnp.int32, (chunk_rows, pair_lanes), 1)
            high, middle, lowest = (x.astype(f32) for x in three_parts(decay[here, :]))
            later = jnp.where(lane < 16, pltpu.roll(middle, 8, 1), pltpu.roll(lowest, 16, 1))
            terms = jnp.where(lane < 8, high, later)
            terms_ref[here, :] = jnp.where(lane < 24, terms, 0.0).astype(bf16)

        each(seq_len // chunk_rows, split)

    w_mine, w_theirs = lane_blocks((wq, wk, wv, wg)), lane_blocks((tq, tk, tv, tg))

    def project(i):
        here = rows_at(i, chunk_rows)
        out = dot_nn(a_ref[here, :half], w_mine) + dot_nn(a_ref[here, half:], w_theirs)
        q_ref[here, :] = out[:, :128].astype(bf16)
        k_ref[here, :] = out[:, 128:256].astype(bf16)
        v_ref[here, :] = out[:, 256:384].astype(bf16)
        gate_ref[here, :] = out[:, 384:]

    each(seq_len // chunk_rows, project)
    piece = pl.ds(piece_start, piece_len)
    gate = jax.nn.sigmoid(gate_ref[piece, :])
    mix_keys(k_ref, terms_ref, pair, ka, kb)
    mix_queries(q_ref.at[piece, :], terms_ref, piece_start, pair, qa, qb)
    before = seq_len // 2
    for s in range(0, piece_len, query_rows(seq_len)):
        rows = query_rows(seq_len)
        width = before + rows
        start = pl.multiple_of(piece_start + s, rows)
        first = pl.multiple_of(jnp.maximum(start - before, 0), rows)
        mask = live_mask(start_ref, start, first, width, rows)
        keys = pl.ds(first, width)
        out = []
        for q_of, k_of in ((qa, ka), (qb, kb)):
            p = probabilities(q_of[s : s + rows, :], k_of[keys, :], mask).astype(bf16)
            out.append(dot_nn(p, v_ref[keys, :]))
        lane = lax.broadcasted_iota(jnp.int32, (rows, pair_lanes), 1)
        u = (jnp.where(lane < 64, out[0], out[1]) * gate[s : s + rows, :]).astype(bf16)
        acc[s : s + rows, :half] += dot_nn(u, wo[0])
        acc[s : s + rows, half:] += dot_nn(u, to[0])

    @pl.when(pair == pl.num_programs(0) - 1)
    def _():
        send_ref[...] = acc[...].astype(bf16)


def backward_kernel(count_parts, piece_len, join, *refs):
    place_ref, parts, refs = refs[0], refs[1 : 1 + count_parts], list(refs[1 + count_parts :])
    mine, theirs, (wo, to, wf) = refs[:4], refs[4:8], refs[8:11]
    q_ref, k_ref, v_ref, gate_ref, z_ref, terms_ref, start_ref = refs[11:18]
    refs = refs[18:]
    y_ref = refs.pop(0) if join else parts[0]
    dq_ref, dk_ref, dv_ref, dg_ref, u_ref, dz_ref, send_ref = refs[:7]
    qa, qb, ka, kb, dd, dus, dka, dkb, dva, dcs, acc = refs[7:]
    pair = pl.program_id(0)
    seq_len, half = y_ref.shape[0], y_ref.shape[1] // 2
    rows = query_rows(seq_len)
    piece = pl.ds(pl.multiple_of(place_ref[0] * piece_len, piece_len), piece_len)

    @pl.when(pair == 0)
    def _():
        if join:
            assemble(parts, y_ref, place_ref)
        acc[...] = jnp.zeros_like(acc)
        dcs[...] = jnp.zeros_like(dcs)

    def gates(i):
        here = rows_at(i, chunk_rows)
        du = dot_nt(y_ref[here, :half], wo[0]) + dot_nt(y_ref[here, half:], to[0])
        sig = jax.nn.sigmoid(gate_ref[here, :])
        dd[here, :] = (du * sig).astype(bf16)
        dus[here, :] = du * sig * (1.0 - sig)

    each(seq_len // chunk_rows, gates)
    mix_keys(k_ref, terms_ref, pair, ka, kb)
    mix_queries(q_ref, terms_ref, 0, pair, qa, qb)
    dka[...] = jnp.zeros_like(dka)
    dkb[...] = jnp.zeros_like(dkb)
    dva[...] = jnp.zeros_like(dva)
    lane = lax.broadcasted_iota(jnp.int32, (rows, pair_lanes), 1)

    def pick(column_a, column_b):
        at = lax.broadcasted_iota(jnp.int32, (column_a.shape[0], pair_lanes), 1)
        return jnp.where(at == 2 * pair, column_a, jnp.where(at == 2 * pair + 1, column_b, 0.0))

    def body(start, first, width):
        mask = live_mask(start_ref, start, first, width, rows)
        here, keys = pl.ds(start, rows), pl.ds(first, width)
        values = v_ref[keys, :]
        d_rows = dd[here, :]
        dq, o = [], []
        for head, (q_of, k_of, dk_of) in enumerate(((qa, ka, dka), (qb, kb, dkb))):
            own_lanes = (lane < 64) if head == 0 else (lane >= 64)
            p = probabilities(q_of[here, :], k_of[keys, :], mask)
            d_mine = jnp.where(own_lanes, d_rows, jnp.zeros_like(d_rows))
            dp = dot_nt(d_mine, values)
            delta = jnp.sum(p * dp, axis=1, keepdims=True)
            ds = (p * (dp - delta)).astype(bf16)
            dq.append(dot_nn(ds, k_of[keys, :]))
            dk_of[keys, :] += dot_tn(ds, q_of[here, :])
            low = p.astype(bf16)
            dva[keys, :] += dot_tn(low, d_mine)
            o.append(dot_nn(low, values))
        o = jnp.where(lane < 64, o[0], o[1])
        dg_ref[here, :] = (dus[here, :] * o).astype(bf16)
        u_ref[here, :] = (o * jax.nn.sigmoid(gate_ref[here, :])).astype(bf16)
        dq_ref[here, :] = (jnp.where(lane < 64, dq[0], dq[1]) * 0.125).astype(bf16)
        dcs[here, :] += pick(dq[0][:, 67:68], dq[1][:, 3:4])

    over_query_blocks(seq_len, rows, body)

    def finish(i):
        here = rows_at(i, chunk_rows)
        lanes_now = lax.broadcasted_iota(jnp.int32, (chunk_rows, pair_lanes), 1)
        ka_rows, kb_rows = dka[here, :], dkb[here, :]
        dk_ref[here, :] = jnp.where(lanes_now < 64, ka_rows, kb_rows).astype(bf16)
        dv_ref[here, :] = dva[here, :].astype(bf16)
        dcs[here, :] -= pick(ka_rows[:, 64:65], kb_rows[:, 0:1])

    each(seq_len // chunk_rows, finish)
    d_own = jnp.concatenate([r[piece, :] for r in (dq_ref, dk_ref, dv_ref, dg_ref)], axis=1)
    acc[:, :half] += dot_nt(d_own, lane_blocks(mine))
    acc[:, half:] += dot_nt(d_own, lane_blocks(theirs))

    @pl.when(pair == pl.num_programs(0) - 1)
    def _():
        running_sum(dcs, True)

        def last(i):
            here = rows_at(i, chunk_rows)
            dz_ref[here, :] = (dcs[here, :] * jax.nn.sigmoid(-z_ref[here, :])).astype(bf16)

        each(seq_len // chunk_rows, last)
        send_ref[...] = (acc[...] + dot_nt(dz_ref[piece, :], wf[...])).astype(bf16)


def ffn_forward_kernel(b_ref, wg, wu, wd, tg, tu, td, gt_ref, up_ref, send_ref, acc):
    half = b_ref.shape[1] // 2
    low, high = b_ref[:, :half], b_ref[:, half:]
    gt = dot_nn(low, wg[0]) + dot_nn(high, tg[0])
    up = dot_nn(low, wu[0]) + dot_nn(high, tu[0])
    gt_ref[...] = gt
    up_ref[...] = up
    m = (gt * jax.nn.sigmoid(gt) * up).astype(bf16)

    @pl.when(pl.program_id(0) == 0)
    def _():
        acc[...] = jnp.zeros_like(acc)

    acc[:, :half] += dot_nn(m, wd[0])
    acc[:, half:] += dot_nn(m, td[0])

    @pl.when(pl.program_id(0) == pl.num_programs(0) - 1)
    def _():
        send_ref[...] = acc[...].astype(bf16)


def inner_grads(dm, gt, up):
    sig = jax.nn.sigmoid(gt)
    d_gate = (dm * up * sig * (1.0 + gt * (1.0 - sig))).astype(bf16)
    return d_gate, (dm * (gt * sig)).astype(bf16)


def ffn_backward_kernel(g_ref, gt_ref, up_ref, wg, wu, wd, tg, tu, td, *refs):
    send_ref, acc = refs[-2:]
    half = g_ref.shape[1] // 2
    dm = dot_nt(g_ref[:, :half], wd[0]) + dot_nt(g_ref[:, half:], td[0])
    d_gate, d_up = inner_grads(dm, gt_ref[...], up_ref[...])

    @pl.when(pl.program_id(0) == 0)
    def _():
        acc[...] = jnp.zeros_like(acc)

    acc[:, :half] += dot_nt(d_gate, wg[0]) + dot_nt(d_up, wu[0])
    acc[:, half:] += dot_nt(d_gate, tg[0]) + dot_nt(d_up, tu[0])

    @pl.when(pl.program_id(0) == pl.num_programs(0) - 1)
    def _():
        send_ref[...] = acc[...].astype(bf16)


def ffn_theirs_kernel(b_ref, g_ref, wg, wu, wd, tg, tu, td, *refs):
    m_ref, dgate_ref, dup_ref, gate_out, up_out, down_out, turned = refs[-7:]
    half = b_ref.shape[1] // 2

    @pl.when(pl.program_id(0) == 0)
    def _():
        turned[...] = b_ref[:, half:].T

    def chunk(i):
        here = rows_at(i, chunk_rows)
        low, high = b_ref[here, :half], b_ref[here, half:]
        gt = dot_nn(low, wg[0]) + dot_nn(high, tg[0])
        up = dot_nn(low, wu[0]) + dot_nn(high, tu[0])
        dm = dot_nt(g_ref[here, :half], wd[0]) + dot_nt(g_ref[here, half:], td[0])
        m_ref[here, :] = (gt * jax.nn.sigmoid(gt) * up).astype(bf16)
        dgate_ref[here, :], dup_ref[here, :] = inner_grads(dm, gt, up)

    each(b_ref.shape[0] // chunk_rows, chunk)
    gate_out[...] = dot_nn(turned[...], dgate_ref[...]).astype(bf16)
    up_out[...] = dot_nn(turned[...], dup_ref[...]).astype(bf16)
    down_out[...] = dot_tn(m_ref[...], g_ref[:, half:]).astype(bf16)


def ffn_mine_kernel(b_ref, g_ref, m_ref, dgate_ref, dup_ref, gate_in, up_in, down_in, *refs):
    gate_out, up_out, down_out, turned = refs[-4:]

    @pl.when(pl.program_id(0) == 0)
    def _():
        turned[...] = b_ref[...].T

    gate_out[0] = dot_nn(turned[...], dgate_ref[...]) + gate_in[...].astype(f32)
    up_out[0] = dot_nn(turned[...], dup_ref[...]) + up_in[...].astype(f32)
    down_out[0] = dot_tn(m_ref[...], g_ref[...]) + down_in[...].astype(f32)


def attention_grads_kernel(steps, mine, *refs):
    a_ref, dq, dk, dv, dg, dz, u_ref, y_ref = refs[:8]
    received = refs[8:14] if mine else [None] * 6
    acc, acc_out = refs[-2:]
    outs = refs[-8:-2]
    turned = a_ref[...].T
    width = dq.shape[1]
    parts = [dot_nn(turned, d[...]) for d in (dq, dk, dv, dg, dz)]
    out = dot_tn(u_ref[...], y_ref[...])

    def give(values):
        for ref, value, more in zip(outs, values, received):
            total = value if more is None else value + more[...].astype(f32)
            if len(ref.shape) == 3:
                ref[0] = total.astype(ref.dtype)
            else:
                ref[...] = total.astype(ref.dtype)

    if steps == 1:
        give([*parts, out])
        return
    step = pl.program_id(0)

    @pl.when(step == 0)
    def _():
        acc[...] = jnp.zeros_like(acc)
        acc_out[...] = jnp.zeros_like(acc_out)

    for k, part in enumerate(parts):
        acc[:, k * width : k * width + part.shape[1]] += part
    acc_out[...] += out

    @pl.when(step == steps - 1)
    def _():
        found = [acc[:, k * width : k * width + p.shape[1]] for k, p in enumerate(parts)]
        give([*found, acc_out[...]])


def fixed(shape, single=True):
    zeros = (0,) * len(shape)
    if single:
        return pl.BlockSpec(shape, lambda *_: zeros, pipeline_mode=pl.Buffered(1))
    return pl.BlockSpec(shape, lambda *_: zeros)


def lanes(seq_len):
    return pl.BlockSpec((seq_len, pair_lanes), lambda p, *_: (0, p))


def lanes_read(seq_len):
    if seq_len <= 2048:
        return lanes(seq_len)
    return pl.BlockSpec((seq_len, pair_lanes), lambda p, *_: (0, p), pipeline_mode=pl.Buffered(1))


def columns_of(w, layer, width):
    return pl.BlockSpec((1, w.shape[1], width), lambda p, *_: (layer, 0, p))


def rows_of(w, layer, height):
    return pl.BlockSpec((1, height, w.shape[2]), lambda p, *_: (layer, p, 0))


def shape(dims, dtype):
    return jax.ShapeDtypeStruct(dims, dtype)


def attention_specs(parts, layer, w4, t4, wo, to, seq_len, join):
    specs = [fixed(p.shape) for p in parts]
    specs += [columns_of(w, layer, pair_lanes) for w in (*w4, *t4)]
    specs += [rows_of(wo, layer, pair_lanes), rows_of(to, layer, pair_lanes)]
    return specs


def cost(microseconds):
    return pl.CostEstimate(flops=int(microseconds * 1.1e9), bytes_accessed=0, transcendentals=0)


def token_specs(tokens):
    return [pl.BlockSpec((16, 128), lambda *_: (0, 0)) for _ in tokens]


def forward_own(place, parts, layer, w4, t4, wo, to, wf, bias, doc_start, piece_len):
    seq_len, width = doc_start.shape[0], parts[0].shape[1]
    local_width = wo.shape[1]
    join = len(parts) > 1
    terms = (seq_len, pair_lanes)
    outs = [shape((seq_len, local_width), bf16)] * 3 + [shape((seq_len, local_width), f32)]
    outs += [shape(terms, f32), shape(terms, bf16), shape((piece_len, width), bf16)]
    specs = [lanes(seq_len)] * 4 + [fixed(terms, False)] * 2 + [fixed((piece_len, width), False)]
    if join:
        outs, specs = [shape((seq_len, width), bf16)] + outs, [fixed((seq_len, width))] + specs
    low, piece = pltpu.VMEM((seq_len, pair_lanes), bf16), pltpu.VMEM((piece_len, pair_lanes), bf16)
    got = pl.pallas_call(
        functools.partial(forward_own_kernel, len(parts), piece_len, join),
        grid_spec=pltpu.PrefetchScalarGridSpec(
            num_scalar_prefetch=1,
            grid=(local_width // pair_lanes,),
            in_specs=attention_specs(parts, layer, w4, t4, wo, to, seq_len, join)
            + [fixed(wf.shape), fixed(bias.shape), fixed(doc_start.shape)],
            out_specs=specs,
            scratch_shapes=[piece] * 2 + [low] * 2 + [pltpu.VMEM(terms, f32), pltpu.VMEM((piece_len, width), f32)],
        ),
        out_shape=outs,
        cost_estimate=cost(19),
        compiler_params=pltpu.CompilerParams(vmem_limit_bytes=60 << 20),
    )(place, *parts, *w4, *t4, wo, to, wf, bias, doc_start)
    got = list(got)
    a = got.pop(0) if join else parts[0]
    return a, got[:6], got[6]


def attention_backward(place, parts, layer, w4, t4, wo, to, wf, saved, doc_start, piece_len):
    q, k, v, gate, z, terms = saved
    seq_len, width = doc_start.shape[0], parts[0].shape[1]
    local_width = wo.shape[1]
    join = len(parts) > 1
    outs = [shape((seq_len, local_width), bf16)] * 5 + [shape((seq_len, pair_lanes), bf16)]
    outs += [shape((piece_len, width), bf16)]
    specs = [lanes(seq_len)] * 5 + [fixed((seq_len, pair_lanes), False), fixed((piece_len, width), False)]
    if join:
        outs, specs = [shape((seq_len, width), bf16)] + outs, [fixed((seq_len, width))] + specs
    low, high = pltpu.VMEM((seq_len, pair_lanes), bf16), pltpu.VMEM((seq_len, pair_lanes), f32)
    got = pl.pallas_call(
        functools.partial(backward_kernel, len(parts), piece_len, join),
        grid_spec=pltpu.PrefetchScalarGridSpec(
            num_scalar_prefetch=1,
            grid=(local_width // pair_lanes,),
            in_specs=attention_specs(parts, layer, w4, t4, wo, to, seq_len, join)
            + [fixed(wf.shape)]
            + [lanes_read(seq_len)] * 4
            + [fixed(z.shape), fixed(terms.shape), fixed(doc_start.shape)],
            out_specs=specs,
            scratch_shapes=[low] * 5 + [high] * 5 + [pltpu.VMEM((piece_len, width), f32)],
        ),
        out_shape=outs,
        cost_estimate=cost(33),
        compiler_params=pltpu.CompilerParams(vmem_limit_bytes=60 << 20),
    )(place, *parts, *w4, *t4, wo, to, wf, q, k, v, gate, z, terms, doc_start)
    got = list(got)
    y = got.pop(0) if join else parts[0]
    return y, got[:6], got[6]


def ffn_weights(layer, w3, t3):
    specs = []
    for wg, wu, wd in (w3, t3):
        specs += [
            columns_of(wg, layer, hidden_block), columns_of(wu, layer, hidden_block), rows_of(wd, layer, hidden_block),
        ]
    return specs


def blocks_of(rows):
    return pl.BlockSpec((rows, hidden_block), lambda p, *_: (0, p))


def ffn_forward(b, layer, w3, t3):
    rows, width = b.shape
    inner = w3[2].shape[1]
    return pl.pallas_call(
        ffn_forward_kernel,
        grid=(inner // hidden_block,),
        in_specs=[fixed(b.shape)] + ffn_weights(layer, w3, t3),
        out_specs=[blocks_of(rows)] * 2 + [fixed((rows, width), False)],
        scratch_shapes=[pltpu.VMEM((rows, width), f32)],
        out_shape=[shape((rows, inner), f32)] * 2 + [shape((rows, width), bf16)],
        cost_estimate=cost(7),
        compiler_params=pltpu.CompilerParams(vmem_limit_bytes=60 << 20),
    )(b, *w3, *t3)


def ffn_backward(g, gt, up, layer, w3, t3, *tokens):
    rows, width = g.shape
    return pl.pallas_call(
        ffn_backward_kernel,
        grid=(gt.shape[1] // hidden_block,),
        in_specs=[fixed(g.shape)] + [blocks_of(rows)] * 2 + ffn_weights(layer, w3, t3) + token_specs(tokens),
        out_specs=fixed((rows, width), False),
        scratch_shapes=[pltpu.VMEM((rows, width), f32)],
        out_shape=shape((rows, width), bf16),
        cost_estimate=cost(8),
        compiler_params=pltpu.CompilerParams(vmem_limit_bytes=60 << 20),
    )(g, gt, up, *w3, *t3, *tokens)


def ffn_theirs(b, g, layer, w3, t3, *tokens):
    rows, width = b.shape
    half = width // 2
    inner = w3[2].shape[1]
    wide = pl.BlockSpec((half, hidden_block), lambda p: (0, p))
    return pl.pallas_call(
        ffn_theirs_kernel,
        grid=(inner // hidden_block,),
        in_specs=[fixed(b.shape), fixed(g.shape)] + ffn_weights(layer, w3, t3) + token_specs(tokens),
        out_specs=[blocks_of(rows)] * 3 + [wide, wide, pl.BlockSpec((hidden_block, half), lambda p: (p, 0))],
        scratch_shapes=[pltpu.VMEM((half, rows), bf16)],
        out_shape=[shape((rows, inner), bf16)] * 3
        + [shape((half, inner), bf16)] * 2
        + [shape((inner, half), bf16)],
        cost_estimate=cost(24),
        compiler_params=pltpu.CompilerParams(vmem_limit_bytes=60 << 20),
    )(b, g, *w3, *t3, *tokens)


def anywhere():
    return pl.BlockSpec(memory_space=pl.ANY)


def ffn_mine(layer, b, g, values, received, totals, *tokens):
    rows, width = b.shape
    half, inner = width // 2, values[0].shape[1]
    wide = pl.BlockSpec((half, hidden_block), lambda p: (0, p))
    tall = pl.BlockSpec((hidden_block, half), lambda p: (p, 0))
    wide_out = pl.BlockSpec((1, half, hidden_block), lambda p: (layer, 0, p))
    tall_out = pl.BlockSpec((1, hidden_block, half), lambda p: (layer, p, 0))
    return pl.pallas_call(
        ffn_mine_kernel,
        grid=(inner // hidden_block,),
        in_specs=[fixed((rows, half))] * 2
        + [blocks_of(rows)] * 3
        + [wide, wide, tall]
        + [anywhere()] * 3
        + token_specs(tokens),
        out_specs=[wide_out, wide_out, tall_out],
        out_shape=[shape(x.shape, x.dtype) for x in totals],
        scratch_shapes=[pltpu.VMEM((half, rows), bf16)],
        input_output_aliases={8: 0, 9: 1, 10: 2},
        cost_estimate=cost(9),
        compiler_params=pltpu.CompilerParams(vmem_limit_bytes=60 << 20),
    )(b, g, *values, *received, *totals, *tokens)


def attention_grads(layer, a, ds, dz, u, y, received=None, totals=None, tokens=()):
    rows, width = a.shape
    half, local_width = width // 2, u.shape[1]
    part = min(rows, 1024)
    steps = rows // part
    mine = received is not None
    side = 0 if mine else 1
    features = pl.BlockSpec((part, half), lambda p: (p, side))
    across = [pl.BlockSpec((part, x.shape[1]), lambda p: (p, 0)) for x in (*ds, dz, u)]
    specs = [features, *across, features]
    operands = [a, *ds, dz, u, y]
    flat = [(half, local_width)] * 4 + [(half, pair_lanes), (local_width, half)]
    if mine:
        specs += [fixed(x) for x in flat] + [anywhere()] * 5
        operands += [*received, *totals]
        outs = [shape(x.shape, f32) for x in totals[:4]] + [shape(flat[4], f32), shape(totals[4].shape, f32)]
        layered = pl.BlockSpec((1, half, local_width), lambda p: (layer, 0, 0))
        out_specs = [layered] * 4 + [fixed(flat[4], False)]
        out_specs += [pl.BlockSpec((1, local_width, half), lambda p: (layer, 0, 0))]
        aliases = {14: 0, 15: 1, 16: 2, 17: 3, 18: 5}
    else:
        outs, out_specs, aliases = [shape(x, bf16) for x in flat], [fixed(x, False) for x in flat], {}
    sizes = [(half, 4 * local_width + pair_lanes), (local_width, half)] if steps > 1 else [(8, 128)] * 2
    return pl.pallas_call(
        functools.partial(attention_grads_kernel, steps, mine),
        grid=(steps,),
        in_specs=specs + token_specs(tokens),
        out_specs=out_specs,
        out_shape=outs,
        scratch_shapes=[pltpu.VMEM(x, f32) for x in sizes],
        input_output_aliases=aliases,
        cost_estimate=cost(7),
        compiler_params=pltpu.CompilerParams(vmem_limit_bytes=60 << 20),
    )(*operands, *tokens)


def unset(*like):
    return pl.pallas_call(
        pass_kernel,
        out_specs=[pl.BlockSpec(memory_space=pl.ANY) for _ in like],
        out_shape=list(like),
    )()


def inverse_rms(h):
    return lax.rsqrt(jnp.mean(h * h, axis=-1, keepdims=True) + epsilon)


def norm_back(grad_normed, hidden, inverse, gain):
    scaled = hidden * inverse
    weighted = grad_normed * gain
    grad_gain = jnp.sum(grad_normed * scaled, axis=0)
    mean = jnp.mean(weighted * scaled, axis=-1, keepdims=True)
    return inverse * (weighted - scaled * mean), grad_gain


def local(
    hidden_in, segment_ids, w_query, w_key, w_value, w_gate_out, w_attn_out, w_forget, b_forget,
    gain_attn, gain_ffn, w_gate, w_up, w_down, cotangent,
):
    seq_count, piece_len, width = hidden_in.shape
    count_z, count_t = lax.axis_size("context"), lax.axis_size("tensor")
    core, z, t = lax.axis_index("fsdp"), lax.axis_index("context"), lax.axis_index("tensor")
    layers, half, local_width = w_query.shape
    heads = w_forget.shape[2]
    block = piece_len // count_t
    seq_len = piece_len * count_z
    shared_rows = count_z == 4
    place = jnp.stack([z, t]).astype(jnp.int32)

    def features(x):
        return jnp.where(core == 0, x, jnp.concatenate([x[..., half:], x[..., :half]], axis=-1))

    def own_block(x):
        return lax.dynamic_slice_in_dim(x, t * block, block, 0)

    def other(w):
        return swap(w, "fsdp", 1)

    def full(w, axis):
        return jnp.concatenate([w, other(w)], axis=axis)

    seg_all = gathered(segment_ids.reshape(1, piece_len), "context").reshape(seq_len)
    doc_start = jnp.sum((seg_all[None, :] < seg_all[:, None]).astype(jnp.int32), axis=1, keepdims=True)

    gains = full(jnp.concatenate([gain_attn, gain_ffn], axis=0), 1).astype(f32)
    hidden_rows = features(hidden_in.reshape(piece_len, width)).astype(f32)
    first_a = (hidden_rows * inverse_rms(hidden_rows) * gains[0]).astype(bf16)
    a_parts, _ = all_rows(own_block(first_a), first_a, seg_all)

    w_forget_full = jnp.pad(full(w_forget, 1), ((0, 0), (0, 0), (0, pair_lanes - heads)))
    bias = jnp.pad(b_forget, ((0, 0), (0, pair_lanes - heads)))
    w4 = (w_query, w_key, w_value, w_gate_out)
    t4 = tuple(other(w) for w in w4)
    to = other(w_attn_out)
    w3 = (w_gate, w_up, w_down)
    t3 = tuple(other(w) for w in w3)

    hidden = own_block(hidden_rows)
    saved = []
    cotangent_rows = features(cotangent.reshape(piece_len, width))
    last = layers - 1
    grad = own_block(cotangent_rows).astype(f32)
    for layer in range(layers):
        gain_one, gain_two = gains[layer], gains[layers + layer]
        inverse_one = inverse_rms(hidden)
        if layer > 0:
            a_parts, _ = all_rows((hidden * inverse_one * gain_one).astype(bf16))
        forget_weights = w_forget_full[layer]
        if shared_rows and layer == 1:
            forget_weights = after(forget_weights, g_last)
        a, (q, k, v, gate, forget, terms), sends = forward_own(
            place, a_parts, layer, w4, t4, w_attn_out, to, forget_weights,
            bias[layer : layer + 1], doc_start, piece_len,
        )
        if shared_rows and layer == 0:
            g_last = sequence_rows(after(own_block(cotangent_rows), a_parts[-1]))
        mixed = hidden + received_sum(sends)
        inverse_two = inverse_rms(mixed)
        b_shard = (mixed * inverse_two * gain_two).astype(bf16)
        b = gathered(b_shard, "tensor")
        gt, up, sends = ffn_forward(b, layer, w3, t3)
        saved.append(
            dict(hidden=hidden, inverse_one=inverse_one, a=a, kept=(q, k, v, gate, forget, terms), mixed=mixed,
                 inverse_two=inverse_two, b=b, b_shard=b_shard, gt=gt, up=up)
        )
        if layer < last:
            hidden = mixed + received_sum(sends)

    def finish(x):
        return features(gathered(x.astype(bf16), "tensor")).reshape(1, piece_len, width)

    last_sends = sends
    wide = shape((layers, half, local_width), f32)
    inner = shape((layers, half, w_gate.shape[2]), f32)
    results = list(
        unset(
            wide, wide, wide, wide, shape((layers, local_width, half), f32),
            inner, inner, shape((layers, w_down.shape[1], half), f32),
        )
    )
    small = [[None] * layers for _ in range(2)]
    gain_grads = [None] * (2 * layers)

    def ffn_theirs_of(layer, *tokens):
        s = saved[layer]
        values = ffn_theirs(s["b_rows"], s["g_rows"], layer, w3, t3, *tokens)
        s.update(values=values[:3], ffn_received=[other(x) for x in values[3:]])

    def ffn_mine_of(layer, *tokens):
        s = saved[layer]
        received = s["ffn_received"]
        results[5:] = ffn_mine(layer, s["b_rows"], s["g_rows"], s["values"], received, results[5:], *tokens)

    def attention_theirs_of(layer, *tokens):
        s = saved[layer]
        s["theirs"] = attention_grads(layer, *s["grads"], tokens=tokens)
        s["received"] = [other(x) for x in s["theirs"]]
        bias_grad = jnp.sum(s["grads"][2].astype(f32), axis=0)[:heads]
        small[1][layer] = bias_grad + other(bias_grad)

    def attention_mine_of(layer, *tokens):
        s = saved[layer]
        found = attention_grads(layer, *s["grads"], s["received"], results[:5], tokens)
        results[:5] = [*found[:4], found[5]]
        small[0][layer] = found[4][:, :heads]

    for layer in reversed(range(layers)):
        s = saved[layer]
        gain_one, gain_two = gains[layer], gains[layers + layer]
        tokens = ()
        if layer == last:
            g = cotangent_rows
            if shared_rows:
                s.update(b_rows=sequence_rows(s["b_shard"]), g_rows=g_last)
        else:
            g_shard = grad.astype(bf16)
            g = gathered(g_shard, "tensor")
            tokens = (saved[layer + 1]["theirs"][0],)
            if shared_rows:
                s.update(b_rows=sequence_rows(after(s["b_shard"], token)), g_rows=sequence_rows(g_shard))
        if not shared_rows:
            s.update(b_rows=s["b"], g_rows=g)
        sends = ffn_backward(g, s["gt"], s["up"], layer, w3, t3, *tokens)
        back, gain_grads[layers + layer] = norm_back(received_sum(sends), s["mixed"], s["inverse_two"], gain_two)
        grad_mixed = grad + back
        y_parts, y_far = all_rows(grad_mixed.astype(bf16), together=True)
        if layer == last:
            ffn_theirs_of(layer, *y_far)
            tokens = (s["values"][0],)
        else:
            if layer + 1 < last:
                ffn_theirs_of(layer + 1)
            attention_mine_of(layer + 1)
            ffn_mine_of(layer + 1)
            tokens = (results[0], results[5])
        kept = (*s["kept"][:-1], after(s["kept"][-1], *tokens))
        y, (dq, dk, dv, dg, u, dz), sends = attention_backward(
            place, y_parts, layer, w4, t4, w_attn_out, to, w_forget_full[layer], kept, doc_start, piece_len,
        )
        token = y_parts[-1]
        if layer == last:
            block_sum = own_block(last_sends).astype(f32) + s["mixed"]
            with_rows = lax.dynamic_update_slice_in_dim(last_sends, block_sum.astype(bf16), t * block, 0)
            output = lax.psum(after(with_rows, token), "tensor")
        s["grads"] = (s["a"], (dq, dk, dv, dg), dz, u, y)
        if layer > 0:
            attention_theirs_of(layer)
        back, gain_grads[layer] = norm_back(received_sum(sends), s["hidden"], s["inverse_one"], gain_one)
        grad = grad_mixed + back

    if layers > 1:
        ffn_theirs_of(0)
    attention_theirs_of(0, saved[0]["values"][0], grad)
    attention_mine_of(0, *saved[0]["ffn_received"])
    ffn_mine_of(0)
    if not shared_rows:
        results[5:] = [lax.psum(x, "context") for x in results[5:]]
    output = features(after(output, saved[0]["values"][0])).reshape(1, piece_len, width)
    grad_input = finish(grad)
    gain_total = jnp.stack(gain_grads).reshape(1, -1)
    for axis in (("context", "tensor"),) if shared_rows else ("context", "tensor"):
        gain_total = jnp.sum(gathered(gain_total, axis), axis=0, keepdims=True)
    gain_total = gain_total.reshape(2 * layers, width)
    gain_total = gain_total[:, :half] + other(gain_total[:, half:])
    return (
        output, grad_input, *results[:5], jnp.stack(small[0]), jnp.stack(small[1]),
        gain_total[:layers], gain_total[layers:], *results[5:],
    )


def solution(mesh):
    rows = P("fsdp", "context", None)
    wide, tall = P(None, "fsdp", "tensor"), P(None, "tensor", "fsdp")
    heads, gain = P(None, "tensor"), P(None, "fsdp")
    return jax.shard_map(
        local,
        mesh=mesh,
        in_specs=(
            rows, P("fsdp", "context"), wide, wide, wide, wide, tall, wide, heads, gain, gain, wide, wide, tall, rows,
        ),
        out_specs=(rows, rows, wide, wide, wide, wide, tall, wide, heads, gain, gain, wide, wide, tall),
        check_vma=False,
    )
```

```python
import functools

import jax
import jax.numpy as jnp
from jax import lax
from jax.experimental import pallas as pl
from jax.experimental.pallas import tpu as pltpu
from jax.sharding import PartitionSpec as P

epsilon = 1e-06
masked_value = -1e30
bf16 = jnp.bfloat16
f32 = jnp.float32
pair_lanes = 128
hidden_block = 256
chunk_rows = 256


def query_rows(seq_len):
    return 256 if seq_len <= 2048 else 128


def swap(x, axis, k):
    n = lax.axis_size(axis)
    return lax.ppermute(x, axis, [(i, i ^ k) for i in range(n)])


def pass_kernel(*refs):
    pass


def after(x, *tokens):
    if not tokens:
        return x
    anywhere = pl.BlockSpec(memory_space=pl.ANY)
    return pl.pallas_call(
        pass_kernel,
        in_specs=[anywhere] * (1 + len(tokens)),
        out_specs=anywhere,
        out_shape=jax.ShapeDtypeStruct(x.shape, x.dtype),
        input_output_aliases={0: 0},
    )(x, *tokens)


def gathered(block, axis):
    count = lax.axis_size(axis)
    copies = jnp.broadcast_to(block[None], (count,) + block.shape)
    return lax.all_to_all(copies, axis, 0, 0, tiled=True).reshape((-1,) + block.shape[1:])


def sequence_rows(shard):
    return lax.all_gather(shard, ("context", "tensor"), tiled=True)


def near_rows(own):
    return swap(own, "context", 1)


def far_blocks(shard):
    return swap(shard, "context", 2), swap(shard, "context", 3)


def all_rows(shard, own=None, token=None, together=False):
    if own is None:
        own = gathered(shard, "tensor")
    if lax.axis_size("context") != 4:
        return (lax.all_gather(own, "context", tiled=True),), ()
    second, third = far_blocks(shard)
    near = near_rows(own)
    if together:
        block, width = shard.shape
        far = gathered(jnp.concatenate([second, third], axis=0), "tensor")
        return (own, near, far.reshape(-1, 2, block, width)), (second, third)
    if token is not None:
        second = after(second, token)
    third = after(third, second)
    blocks = [second] + [swap(second, "tensor", k) for k in range(1, lax.axis_size("tensor"))]
    return (own, near, *blocks, gathered(third, "tensor")), (second, third)


def received_sum(sends):
    count = lax.axis_size("tensor")
    got = lax.all_to_all(sends.reshape(count, -1, sends.shape[1]), "tensor", 0, 0, tiled=True)
    return jnp.sum(got.astype(f32), axis=0)


def dot_nt(a, b):
    return lax.dot_general(a, b, (((1,), (1,)), ((), ())), preferred_element_type=f32)


def dot_tn(a, b):
    return lax.dot_general(a, b, (((0,), (0,)), ((), ())), preferred_element_type=f32)


def dot_nn(a, b):
    return jnp.dot(a, b, preferred_element_type=f32)


def each(count, body):
    if count <= 4:
        for i in range(count):
            body(i)
        return

    def one(i, carry):
        body(i)
        return carry

    lax.fori_loop(0, count, one, 0)


def rows_at(i, rows):
    start = i * rows
    return pl.ds(start if isinstance(start, int) else pl.multiple_of(start, rows), rows)


def assemble(parts, whole_ref, place_ref):
    z, t = place_ref[0], place_ref[1]
    piece, blocks_seen, piece_len = 0, 0, parts[0].shape[0]
    for part in parts:
        if len(part.shape) == 4:
            blocks, pieces, block = part.shape[:3]
            for p in range(pieces):
                for b in range(blocks):
                    at = pl.multiple_of((z ^ (piece + p)) * piece_len + b * block, block)
                    whole_ref[pl.ds(at, block), :] = part[b, p]
            piece += pieces
            continue
        rows = part.shape[0]
        if rows == piece_len:
            at = pl.multiple_of((z ^ piece) * piece_len, piece_len)
            piece += 1
        else:
            at = pl.multiple_of((z ^ piece) * piece_len + (t ^ blocks_seen) * rows, rows)
            blocks_seen += 1
            if blocks_seen * rows == piece_len:
                piece, blocks_seen = piece + 1, 0
        whole_ref[pl.ds(at, rows), :] = part[...]


def triangle(rows, reverse):
    row = lax.broadcasted_iota(jnp.int32, (rows, rows), 0)
    column = lax.broadcasted_iota(jnp.int32, (rows, rows), 1)
    return jnp.where((column >= row) if reverse else (column <= row), 1.0, 0.0).astype(bf16)


def running_sum(ref, reverse):
    rows = chunk_rows
    ones = triangle(rows, reverse)
    count = ref.shape[0] // rows
    edge = 0 if reverse else rows - 1

    def chunk(i, carry):
        here = pl.ds(pl.multiple_of((count - 1 - i if reverse else i) * rows, rows), rows)
        high, middle, lowest = three_parts(ref[here, :])
        total = dot_nn(ones, high) + dot_nn(ones, middle) + dot_nn(ones, lowest) + carry
        ref[here, :] = total
        return total[edge : edge + 1, :]

    lax.fori_loop(0, count, chunk, jnp.zeros((1, ref.shape[1]), f32), unroll=count <= 4)


def log_sigmoid(z):
    e = jnp.exp(-jnp.abs(z))
    small = e * (1.0 - e * (1 / 2 - e * (1 / 3 - e * (1 / 4 - e * (1 / 5 - e * (1 / 6 - e * (1 / 7)))))))
    return jnp.minimum(z, 0.0) - jnp.where(e < 0.0625, small, jnp.log(1.0 + e))


def three_parts(x):
    high = x.astype(bf16)
    middle = (x - high.astype(f32)).astype(bf16)
    return high, middle, (x - high.astype(f32) - middle.astype(f32)).astype(bf16)


def decay_side(terms, pair, key_side):
    row = lax.broadcasted_iota(jnp.int32, (pair_lanes, pair_lanes), 0)
    lane = lax.broadcasted_iota(jnp.int32, (pair_lanes, pair_lanes), 1)
    spot = lane & 63
    term = spot if key_side else spot - 3
    head = jnp.where(lane >= 64, 2 * pair, 2 * pair + 1)
    chosen = (term >= 0) & (term < 3) & (row == 8 * term + head)
    pick = jnp.where(chosen, -1.0 if key_side else 1.0, 0.0).astype(bf16)
    lanes_now = lax.broadcasted_iota(jnp.int32, (1, pair_lanes), 1) & 63
    other = lanes_now - 3 if key_side else lanes_now
    ones = jnp.where((other >= 0) & (other < 3), 1.0, 0.0)
    return (dot_nn(terms, pick) + ones).astype(bf16)


def mix_keys(k_ref, terms_ref, pair, ka, kb):
    def mix(i):
        here = rows_at(i, chunk_rows)
        lane = lax.broadcasted_iota(jnp.int32, (chunk_rows, pair_lanes), 1)
        k, side = k_ref[here, :], decay_side(terms_ref[here, :], pair, True)
        ka[here, :] = jnp.where(lane < 64, k, side)
        kb[here, :] = jnp.where(lane < 64, side, k)

    each(k_ref.shape[0] // chunk_rows, mix)


def mix_queries(q_ref, terms_ref, start, pair, qa, qb):
    def mix(i):
        here = rows_at(i, chunk_rows)
        lane = lax.broadcasted_iota(jnp.int32, (chunk_rows, pair_lanes), 1)
        q = (q_ref[here, :].astype(f32) * 0.125).astype(bf16)
        terms = terms_ref[pl.ds(pl.multiple_of(start + i * chunk_rows, chunk_rows), chunk_rows), :]
        side = decay_side(terms, pair, False)
        qa[here, :] = jnp.where(lane < 64, q, side)
        qb[here, :] = jnp.where(lane < 64, side, q)

    each(q_ref.shape[0] // chunk_rows, mix)


def live_mask(start_ref, start, first, width, rows):
    key_pos = first + lax.broadcasted_iota(jnp.int32, (rows, width), 1)
    query_pos = start + lax.broadcasted_iota(jnp.int32, (rows, width), 0)
    doc_start = start_ref[pl.ds(start, rows), :]
    return (key_pos <= query_pos) & (key_pos >= doc_start)


def over_query_blocks(seq_len, rows, body):
    before = seq_len // 2
    if seq_len // rows <= 4:
        for start in range(0, seq_len, rows):
            first = max(0, start - before)
            body(start, first, start + rows - first)
        return
    width = before + rows

    def one(i, carry):
        start = pl.multiple_of(i * rows, rows)
        first = pl.multiple_of(jnp.maximum(start - before, 0), rows)
        body(start, first, width)
        return carry

    lax.fori_loop(0, seq_len // rows, one, 0)


def probabilities(q_rows, k_rows, mask):
    s = jnp.where(mask, dot_nt(q_rows, k_rows), masked_value)
    e = jnp.exp(s - jnp.max(s, axis=1, keepdims=True))
    return e * (1.0 / jnp.sum(e, axis=1, keepdims=True))


def lane_blocks(refs):
    return jnp.concatenate([r[0] for r in refs], axis=1)


def forward_own_kernel(count_parts, piece_len, join, *refs):
    place_ref, parts, refs = refs[0], refs[1 : 1 + count_parts], list(refs[1 + count_parts :])
    (wq, wk, wv, wg), (tq, tk, tv, tg) = refs[:4], refs[4:8]
    wo, to, wf, bias, start_ref = refs[8:13]
    refs = refs[13:]
    a_ref = refs.pop(0) if join else parts[0]
    q_ref, k_ref, v_ref, gate_ref, z_ref, terms_ref, send_ref, qa, qb, ka, kb, decay, acc = refs
    pair = pl.program_id(0)
    seq_len, half = a_ref.shape[0], a_ref.shape[1] // 2
    piece_start = pl.multiple_of(place_ref[0] * piece_len, piece_len)

    @pl.when(pair == 0)
    def _():
        if join:
            assemble(parts, a_ref, place_ref)
        acc[...] = jnp.zeros_like(acc)

        def gates(i):
            here = rows_at(i, chunk_rows)
            z = dot_nn(a_ref[here, :], wf[...]) + bias[...]
            z_ref[here, :] = z
            decay[here, :] = log_sigmoid(z)

        each(seq_len // chunk_rows, gates)
        running_sum(decay, False)

        def split(i):
            here = rows_at(i, chunk_rows)
            lane = lax.broadcasted_iota(jnp.int32, (chunk_rows, pair_lanes), 1)
            high, middle, lowest = (x.astype(f32) for x in three_parts(decay[here, :]))
            later = jnp.where(lane < 16, pltpu.roll(middle, 8, 1), pltpu.roll(lowest, 16, 1))
            terms = jnp.where(lane < 8, high, later)
            terms_ref[here, :] = jnp.where(lane < 24, terms, 0.0).astype(bf16)

        each(seq_len // chunk_rows, split)

    w_mine, w_theirs = lane_blocks((wq, wk, wv, wg)), lane_blocks((tq, tk, tv, tg))

    def project(i):
        here = rows_at(i, chunk_rows)
        out = dot_nn(a_ref[here, :half], w_mine) + dot_nn(a_ref[here, half:], w_theirs)
        q_ref[here, :] = out[:, :128].astype(bf16)
        k_ref[here, :] = out[:, 128:256].astype(bf16)
        v_ref[here, :] = out[:, 256:384].astype(bf16)
        gate_ref[here, :] = out[:, 384:]

    each(seq_len // chunk_rows, project)
    piece = pl.ds(piece_start, piece_len)
    gate = jax.nn.sigmoid(gate_ref[piece, :])
    mix_keys(k_ref, terms_ref, pair, ka, kb)
    mix_queries(q_ref.at[piece, :], terms_ref, piece_start, pair, qa, qb)
    before = seq_len // 2
    for s in range(0, piece_len, query_rows(seq_len)):
        rows = query_rows(seq_len)
        width = before + rows
        start = pl.multiple_of(piece_start + s, rows)
        first = pl.multiple_of(jnp.maximum(start - before, 0), rows)
        mask = live_mask(start_ref, start, first, width, rows)
        keys = pl.ds(first, width)
        out = []
        for q_of, k_of in ((qa, ka), (qb, kb)):
            p = probabilities(q_of[s : s + rows, :], k_of[keys, :], mask).astype(bf16)
            out.append(dot_nn(p, v_ref[keys, :]))
        lane = lax.broadcasted_iota(jnp.int32, (rows, pair_lanes), 1)
        u = (jnp.where(lane < 64, out[0], out[1]) * gate[s : s + rows, :]).astype(bf16)
        acc[s : s + rows, :half] += dot_nn(u, wo[0])
        acc[s : s + rows, half:] += dot_nn(u, to[0])

    @pl.when(pair == pl.num_programs(0) - 1)
    def _():
        send_ref[...] = acc[...].astype(bf16)


def backward_kernel(count_parts, piece_len, join, *refs):
    place_ref, parts, refs = refs[0], refs[1 : 1 + count_parts], list(refs[1 + count_parts :])
    mine, theirs, (wo, to, wf) = refs[:4], refs[4:8], refs[8:11]
    q_ref, k_ref, v_ref, gate_ref, z_ref, terms_ref, start_ref = refs[11:18]
    refs = refs[18:]
    y_ref = refs.pop(0) if join else parts[0]
    dq_ref, dk_ref, dv_ref, dg_ref, u_ref, dz_ref, send_ref = refs[:7]
    qa, qb, ka, kb, dd, dus, dka, dkb, dva, dcs, acc = refs[7:]
    pair = pl.program_id(0)
    seq_len, half = y_ref.shape[0], y_ref.shape[1] // 2
    rows = query_rows(seq_len)
    piece = pl.ds(pl.multiple_of(place_ref[0] * piece_len, piece_len), piece_len)

    @pl.when(pair == 0)
    def _():
        if join:
            assemble(parts, y_ref, place_ref)
        acc[...] = jnp.zeros_like(acc)
        dcs[...] = jnp.zeros_like(dcs)

    def gates(i):
        here = rows_at(i, chunk_rows)
        du = dot_nt(y_ref[here, :half], wo[0]) + dot_nt(y_ref[here, half:], to[0])
        sig = jax.nn.sigmoid(gate_ref[here, :])
        dd[here, :] = (du * sig).astype(bf16)
        dus[here, :] = du * sig * (1.0 - sig)

    each(seq_len // chunk_rows, gates)
    mix_keys(k_ref, terms_ref, pair, ka, kb)
    mix_queries(q_ref, terms_ref, 0, pair, qa, qb)
    dka[...] = jnp.zeros_like(dka)
    dkb[...] = jnp.zeros_like(dkb)
    dva[...] = jnp.zeros_like(dva)
    lane = lax.broadcasted_iota(jnp.int32, (rows, pair_lanes), 1)

    def pick(column_a, column_b):
        at = lax.broadcasted_iota(jnp.int32, (column_a.shape[0], pair_lanes), 1)
        return jnp.where(at == 2 * pair, column_a, jnp.where(at == 2 * pair + 1, column_b, 0.0))

    def body(start, first, width):
        mask = live_mask(start_ref, start, first, width, rows)
        here, keys = pl.ds(start, rows), pl.ds(first, width)
        values = v_ref[keys, :]
        d_rows = dd[here, :]
        dq, o = [], []
        for head, (q_of, k_of, dk_of) in enumerate(((qa, ka, dka), (qb, kb, dkb))):
            own_lanes = (lane < 64) if head == 0 else (lane >= 64)
            p = probabilities(q_of[here, :], k_of[keys, :], mask)
            d_mine = jnp.where(own_lanes, d_rows, jnp.zeros_like(d_rows))
            dp = dot_nt(d_mine, values)
            delta = jnp.sum(p * dp, axis=1, keepdims=True)
            ds = (p * (dp - delta)).astype(bf16)
            dq.append(dot_nn(ds, k_of[keys, :]))
            dk_of[keys, :] += dot_tn(ds, q_of[here, :])
            low = p.astype(bf16)
            dva[keys, :] += dot_tn(low, d_mine)
            o.append(dot_nn(low, values))
        o = jnp.where(lane < 64, o[0], o[1])
        dg_ref[here, :] = (dus[here, :] * o).astype(bf16)
        u_ref[here, :] = (o * jax.nn.sigmoid(gate_ref[here, :])).astype(bf16)
        dq_ref[here, :] = (jnp.where(lane < 64, dq[0], dq[1]) * 0.125).astype(bf16)
        dcs[here, :] += pick(dq[0][:, 67:68], dq[1][:, 3:4])

    over_query_blocks(seq_len, rows, body)

    def finish(i):
        here = rows_at(i, chunk_rows)
        lanes_now = lax.broadcasted_iota(jnp.int32, (chunk_rows, pair_lanes), 1)
        ka_rows, kb_rows = dka[here, :], dkb[here, :]
        dk_ref[here, :] = jnp.where(lanes_now < 64, ka_rows, kb_rows).astype(bf16)
        dv_ref[here, :] = dva[here, :].astype(bf16)
        dcs[here, :] -= pick(ka_rows[:, 64:65], kb_rows[:, 0:1])

    each(seq_len // chunk_rows, finish)
    d_own = jnp.concatenate([r[piece, :] for r in (dq_ref, dk_ref, dv_ref, dg_ref)], axis=1)
    acc[:, :half] += dot_nt(d_own, lane_blocks(mine))
    acc[:, half:] += dot_nt(d_own, lane_blocks(theirs))

    @pl.when(pair == pl.num_programs(0) - 1)
    def _():
        running_sum(dcs, True)

        def last(i):
            here = rows_at(i, chunk_rows)
            dz_ref[here, :] = (dcs[here, :] * jax.nn.sigmoid(-z_ref[here, :])).astype(bf16)

        each(seq_len // chunk_rows, last)
        send_ref[...] = (acc[...] + dot_nt(dz_ref[piece, :], wf[...])).astype(bf16)


def ffn_forward_kernel(b_ref, wg, wu, wd, tg, tu, td, gt_ref, up_ref, send_ref, acc):
    half = b_ref.shape[1] // 2
    low, high = b_ref[:, :half], b_ref[:, half:]
    gt = dot_nn(low, wg[0]) + dot_nn(high, tg[0])
    up = dot_nn(low, wu[0]) + dot_nn(high, tu[0])
    gt_ref[...] = gt
    up_ref[...] = up
    m = (gt * jax.nn.sigmoid(gt) * up).astype(bf16)

    @pl.when(pl.program_id(0) == 0)
    def _():
        acc[...] = jnp.zeros_like(acc)

    acc[:, :half] += dot_nn(m, wd[0])
    acc[:, half:] += dot_nn(m, td[0])

    @pl.when(pl.program_id(0) == pl.num_programs(0) - 1)
    def _():
        send_ref[...] = acc[...].astype(bf16)


def inner_grads(dm, gt, up):
    sig = jax.nn.sigmoid(gt)
    d_gate = (dm * up * sig * (1.0 + gt * (1.0 - sig))).astype(bf16)
    return d_gate, (dm * (gt * sig)).astype(bf16)


def ffn_backward_kernel(g_ref, gt_ref, up_ref, wg, wu, wd, tg, tu, td, *refs):
    send_ref, acc = refs[-2:]
    half = g_ref.shape[1] // 2
    dm = dot_nt(g_ref[:, :half], wd[0]) + dot_nt(g_ref[:, half:], td[0])
    d_gate, d_up = inner_grads(dm, gt_ref[...], up_ref[...])

    @pl.when(pl.program_id(0) == 0)
    def _():
        acc[...] = jnp.zeros_like(acc)

    acc[:, :half] += dot_nt(d_gate, wg[0]) + dot_nt(d_up, wu[0])
    acc[:, half:] += dot_nt(d_gate, tg[0]) + dot_nt(d_up, tu[0])

    @pl.when(pl.program_id(0) == pl.num_programs(0) - 1)
    def _():
        send_ref[...] = acc[...].astype(bf16)


def ffn_theirs_kernel(b_ref, g_ref, wg, wu, wd, tg, tu, td, *refs):
    m_ref, dgate_ref, dup_ref, gate_out, up_out, down_out, turned = refs[-7:]
    half = b_ref.shape[1] // 2

    @pl.when(pl.program_id(0) == 0)
    def _():
        turned[...] = b_ref[:, half:].T

    def chunk(i):
        here = rows_at(i, chunk_rows)
        low, high = b_ref[here, :half], b_ref[here, half:]
        gt = dot_nn(low, wg[0]) + dot_nn(high, tg[0])
        up = dot_nn(low, wu[0]) + dot_nn(high, tu[0])
        dm = dot_nt(g_ref[here, :half], wd[0]) + dot_nt(g_ref[here, half:], td[0])
        m_ref[here, :] = (gt * jax.nn.sigmoid(gt) * up).astype(bf16)
        dgate_ref[here, :], dup_ref[here, :] = inner_grads(dm, gt, up)

    each(b_ref.shape[0] // chunk_rows, chunk)
    gate_out[...] = dot_nn(turned[...], dgate_ref[...]).astype(bf16)
    up_out[...] = dot_nn(turned[...], dup_ref[...]).astype(bf16)
    down_out[...] = dot_tn(m_ref[...], g_ref[:, half:]).astype(bf16)


def ffn_mine_kernel(b_ref, g_ref, m_ref, dgate_ref, dup_ref, gate_in, up_in, down_in, *refs):
    gate_out, up_out, down_out, turned = refs[-4:]

    @pl.when(pl.program_id(0) == 0)
    def _():
        turned[...] = b_ref[...].T

    gate_out[0] = dot_nn(turned[...], dgate_ref[...]) + gate_in[...].astype(f32)
    up_out[0] = dot_nn(turned[...], dup_ref[...]) + up_in[...].astype(f32)
    down_out[0] = dot_tn(m_ref[...], g_ref[...]) + down_in[...].astype(f32)


def attention_grads_kernel(steps, mine, *refs):
    a_ref, dq, dk, dv, dg, dz, u_ref, y_ref = refs[:8]
    received = refs[8:14] if mine else [None] * 6
    acc, acc_out = refs[-2:]
    outs = refs[-8:-2]
    turned = a_ref[...].T
    width = dq.shape[1]
    parts = [dot_nn(turned, d[...]) for d in (dq, dk, dv, dg, dz)]
    out = dot_tn(u_ref[...], y_ref[...])

    def give(values):
        for ref, value, more in zip(outs, values, received):
            total = value if more is None else value + more[...].astype(f32)
            if len(ref.shape) == 3:
                ref[0] = total.astype(ref.dtype)
            else:
                ref[...] = total.astype(ref.dtype)

    if steps == 1:
        give([*parts, out])
        return
    step = pl.program_id(0)

    @pl.when(step == 0)
    def _():
        acc[...] = jnp.zeros_like(acc)
        acc_out[...] = jnp.zeros_like(acc_out)

    for k, part in enumerate(parts):
        acc[:, k * width : k * width + part.shape[1]] += part
    acc_out[...] += out

    @pl.when(step == steps - 1)
    def _():
        found = [acc[:, k * width : k * width + p.shape[1]] for k, p in enumerate(parts)]
        give([*found, acc_out[...]])


def fixed(shape, single=True):
    zeros = (0,) * len(shape)
    if single:
        return pl.BlockSpec(shape, lambda *_: zeros, pipeline_mode=pl.Buffered(1))
    return pl.BlockSpec(shape, lambda *_: zeros)


def lanes(seq_len):
    return pl.BlockSpec((seq_len, pair_lanes), lambda p, *_: (0, p))


def lanes_read(seq_len):
    if seq_len <= 2048:
        return lanes(seq_len)
    return pl.BlockSpec((seq_len, pair_lanes), lambda p, *_: (0, p), pipeline_mode=pl.Buffered(1))


def columns_of(w, layer, width):
    return pl.BlockSpec((1, w.shape[1], width), lambda p, *_: (layer, 0, p))


def rows_of(w, layer, height):
    return pl.BlockSpec((1, height, w.shape[2]), lambda p, *_: (layer, p, 0))


def shape(dims, dtype):
    return jax.ShapeDtypeStruct(dims, dtype)


def attention_specs(parts, layer, w4, t4, wo, to, seq_len, join):
    specs = [fixed(p.shape) for p in parts]
    specs += [columns_of(w, layer, pair_lanes) for w in (*w4, *t4)]
    specs += [rows_of(wo, layer, pair_lanes), rows_of(to, layer, pair_lanes)]
    return specs


def cost(microseconds):
    return pl.CostEstimate(flops=int(microseconds * 1.1e9), bytes_accessed=0, transcendentals=0)


def token_specs(tokens):
    return [pl.BlockSpec((16, 128), lambda *_: (0, 0)) for _ in tokens]


def forward_own(place, parts, layer, w4, t4, wo, to, wf, bias, doc_start, piece_len):
    seq_len, width = doc_start.shape[0], parts[0].shape[1]
    local_width = wo.shape[1]
    join = len(parts) > 1
    terms = (seq_len, pair_lanes)
    outs = [shape((seq_len, local_width), bf16)] * 3 + [shape((seq_len, local_width), f32)]
    outs += [shape(terms, f32), shape(terms, bf16), shape((piece_len, width), bf16)]
    specs = [lanes(seq_len)] * 4 + [fixed(terms, False)] * 2 + [fixed((piece_len, width), False)]
    if join:
        outs, specs = [shape((seq_len, width), bf16)] + outs, [fixed((seq_len, width))] + specs
    low, piece = pltpu.VMEM((seq_len, pair_lanes), bf16), pltpu.VMEM((piece_len, pair_lanes), bf16)
    got = pl.pallas_call(
        functools.partial(forward_own_kernel, len(parts), piece_len, join),
        grid_spec=pltpu.PrefetchScalarGridSpec(
            num_scalar_prefetch=1,
            grid=(local_width // pair_lanes,),
            in_specs=attention_specs(parts, layer, w4, t4, wo, to, seq_len, join)
            + [fixed(wf.shape), fixed(bias.shape), fixed(doc_start.shape)],
            out_specs=specs,
            scratch_shapes=[piece] * 2 + [low] * 2 + [pltpu.VMEM(terms, f32), pltpu.VMEM((piece_len, width), f32)],
        ),
        out_shape=outs,
        cost_estimate=cost(19),
        compiler_params=pltpu.CompilerParams(vmem_limit_bytes=60 << 20),
    )(place, *parts, *w4, *t4, wo, to, wf, bias, doc_start)
    got = list(got)
    a = got.pop(0) if join else parts[0]
    return a, got[:6], got[6]


def attention_backward(place, parts, layer, w4, t4, wo, to, wf, saved, doc_start, piece_len):
    q, k, v, gate, z, terms = saved
    seq_len, width = doc_start.shape[0], parts[0].shape[1]
    local_width = wo.shape[1]
    join = len(parts) > 1
    outs = [shape((seq_len, local_width), bf16)] * 5 + [shape((seq_len, pair_lanes), bf16)]
    outs += [shape((piece_len, width), bf16)]
    specs = [lanes(seq_len)] * 5 + [fixed((seq_len, pair_lanes), False), fixed((piece_len, width), False)]
    if join:
        outs, specs = [shape((seq_len, width), bf16)] + outs, [fixed((seq_len, width))] + specs
    low, high = pltpu.VMEM((seq_len, pair_lanes), bf16), pltpu.VMEM((seq_len, pair_lanes), f32)
    got = pl.pallas_call(
        functools.partial(backward_kernel, len(parts), piece_len, join),
        grid_spec=pltpu.PrefetchScalarGridSpec(
            num_scalar_prefetch=1,
            grid=(local_width // pair_lanes,),
            in_specs=attention_specs(parts, layer, w4, t4, wo, to, seq_len, join)
            + [fixed(wf.shape)]
            + [lanes_read(seq_len)] * 4
            + [fixed(z.shape), fixed(terms.shape), fixed(doc_start.shape)],
            out_specs=specs,
            scratch_shapes=[low] * 5 + [high] * 5 + [pltpu.VMEM((piece_len, width), f32)],
        ),
        out_shape=outs,
        cost_estimate=cost(33),
        compiler_params=pltpu.CompilerParams(vmem_limit_bytes=60 << 20),
    )(place, *parts, *w4, *t4, wo, to, wf, q, k, v, gate, z, terms, doc_start)
    got = list(got)
    y = got.pop(0) if join else parts[0]
    return y, got[:6], got[6]


def ffn_weights(layer, w3, t3):
    specs = []
    for wg, wu, wd in (w3, t3):
        specs += [
            columns_of(wg, layer, hidden_block), columns_of(wu, layer, hidden_block), rows_of(wd, layer, hidden_block),
        ]
    return specs


def blocks_of(rows):
    return pl.BlockSpec((rows, hidden_block), lambda p, *_: (0, p))


def ffn_forward(b, layer, w3, t3):
    rows, width = b.shape
    inner = w3[2].shape[1]
    return pl.pallas_call(
        ffn_forward_kernel,
        grid=(inner // hidden_block,),
        in_specs=[fixed(b.shape)] + ffn_weights(layer, w3, t3),
        out_specs=[blocks_of(rows)] * 2 + [fixed((rows, width), False)],
        scratch_shapes=[pltpu.VMEM((rows, width), f32)],
        out_shape=[shape((rows, inner), f32)] * 2 + [shape((rows, width), bf16)],
        cost_estimate=cost(7),
        compiler_params=pltpu.CompilerParams(vmem_limit_bytes=60 << 20),
    )(b, *w3, *t3)


def ffn_backward(g, gt, up, layer, w3, t3, *tokens):
    rows, width = g.shape
    return pl.pallas_call(
        ffn_backward_kernel,
        grid=(gt.shape[1] // hidden_block,),
        in_specs=[fixed(g.shape)] + [blocks_of(rows)] * 2 + ffn_weights(layer, w3, t3) + token_specs(tokens),
        out_specs=fixed((rows, width), False),
        scratch_shapes=[pltpu.VMEM((rows, width), f32)],
        out_shape=shape((rows, width), bf16),
        cost_estimate=cost(8),
        compiler_params=pltpu.CompilerParams(vmem_limit_bytes=60 << 20),
    )(g, gt, up, *w3, *t3, *tokens)


def ffn_theirs(b, g, layer, w3, t3, *tokens):
    rows, width = b.shape
    half = width // 2
    inner = w3[2].shape[1]
    wide = pl.BlockSpec((half, hidden_block), lambda p: (0, p))
    return pl.pallas_call(
        ffn_theirs_kernel,
        grid=(inner // hidden_block,),
        in_specs=[fixed(b.shape), fixed(g.shape)] + ffn_weights(layer, w3, t3) + token_specs(tokens),
        out_specs=[blocks_of(rows)] * 3 + [wide, wide, pl.BlockSpec((hidden_block, half), lambda p: (p, 0))],
        scratch_shapes=[pltpu.VMEM((half, rows), bf16)],
        out_shape=[shape((rows, inner), bf16)] * 3
        + [shape((half, inner), bf16)] * 2
        + [shape((inner, half), bf16)],
        cost_estimate=cost(24),
        compiler_params=pltpu.CompilerParams(vmem_limit_bytes=60 << 20),
    )(b, g, *w3, *t3, *tokens)


def anywhere():
    return pl.BlockSpec(memory_space=pl.ANY)


def ffn_mine(layer, b, g, values, received, totals, *tokens):
    rows, width = b.shape
    half, inner = width // 2, values[0].shape[1]
    wide = pl.BlockSpec((half, hidden_block), lambda p: (0, p))
    tall = pl.BlockSpec((hidden_block, half), lambda p: (p, 0))
    wide_out = pl.BlockSpec((1, half, hidden_block), lambda p: (layer, 0, p))
    tall_out = pl.BlockSpec((1, hidden_block, half), lambda p: (layer, p, 0))
    return pl.pallas_call(
        ffn_mine_kernel,
        grid=(inner // hidden_block,),
        in_specs=[fixed((rows, half))] * 2
        + [blocks_of(rows)] * 3
        + [wide, wide, tall]
        + [anywhere()] * 3
        + token_specs(tokens),
        out_specs=[wide_out, wide_out, tall_out],
        out_shape=[shape(x.shape, x.dtype) for x in totals],
        scratch_shapes=[pltpu.VMEM((half, rows), bf16)],
        input_output_aliases={8: 0, 9: 1, 10: 2},
        cost_estimate=cost(9),
        compiler_params=pltpu.CompilerParams(vmem_limit_bytes=60 << 20),
    )(b, g, *values, *received, *totals, *tokens)


def attention_grads(layer, a, ds, dz, u, y, received=None, totals=None, tokens=()):
    rows, width = a.shape
    half, local_width = width // 2, u.shape[1]
    part = min(rows, 1024)
    steps = rows // part
    mine = received is not None
    side = 0 if mine else 1
    features = pl.BlockSpec((part, half), lambda p: (p, side))
    across = [pl.BlockSpec((part, x.shape[1]), lambda p: (p, 0)) for x in (*ds, dz, u)]
    specs = [features, *across, features]
    operands = [a, *ds, dz, u, y]
    flat = [(half, local_width)] * 4 + [(half, pair_lanes), (local_width, half)]
    if mine:
        specs += [fixed(x) for x in flat] + [anywhere()] * 5
        operands += [*received, *totals]
        outs = [shape(x.shape, f32) for x in totals[:4]] + [shape(flat[4], f32), shape(totals[4].shape, f32)]
        layered = pl.BlockSpec((1, half, local_width), lambda p: (layer, 0, 0))
        out_specs = [layered] * 4 + [fixed(flat[4], False)]
        out_specs += [pl.BlockSpec((1, local_width, half), lambda p: (layer, 0, 0))]
        aliases = {14: 0, 15: 1, 16: 2, 17: 3, 18: 5}
    else:
        outs, out_specs, aliases = [shape(x, bf16) for x in flat], [fixed(x, False) for x in flat], {}
    sizes = [(half, 4 * local_width + pair_lanes), (local_width, half)] if steps > 1 else [(8, 128)] * 2
    return pl.pallas_call(
        functools.partial(attention_grads_kernel, steps, mine),
        grid=(steps,),
        in_specs=specs + token_specs(tokens),
        out_specs=out_specs,
        out_shape=outs,
        scratch_shapes=[pltpu.VMEM(x, f32) for x in sizes],
        input_output_aliases=aliases,
        cost_estimate=cost(7),
        compiler_params=pltpu.CompilerParams(vmem_limit_bytes=60 << 20),
    )(*operands, *tokens)


def unset(*like):
    return pl.pallas_call(
        pass_kernel,
        out_specs=[pl.BlockSpec(memory_space=pl.ANY) for _ in like],
        out_shape=list(like),
    )()


def inverse_rms(h):
    return lax.rsqrt(jnp.mean(h * h, axis=-1, keepdims=True) + epsilon)


def norm_back(grad_normed, hidden, inverse, gain):
    scaled = hidden * inverse
    weighted = grad_normed * gain
    grad_gain = jnp.sum(grad_normed * scaled, axis=0)
    mean = jnp.mean(weighted * scaled, axis=-1, keepdims=True)
    return inverse * (weighted - scaled * mean), grad_gain


def local(
    hidden_in, segment_ids, w_query, w_key, w_value, w_gate_out, w_attn_out, w_forget, b_forget,
    gain_attn, gain_ffn, w_gate, w_up, w_down, cotangent,
):
    seq_count, piece_len, width = hidden_in.shape
    count_z, count_t = lax.axis_size("context"), lax.axis_size("tensor")
    core, z, t = lax.axis_index("fsdp"), lax.axis_index("context"), lax.axis_index("tensor")
    layers, half, local_width = w_query.shape
    heads = w_forget.shape[2]
    block = piece_len // count_t
    seq_len = piece_len * count_z
    shared_rows = count_z == 4
    place = jnp.stack([z, t]).astype(jnp.int32)

    def features(x):
        return jnp.where(core == 0, x, jnp.concatenate([x[..., half:], x[..., :half]], axis=-1))

    def own_block(x):
        return lax.dynamic_slice_in_dim(x, t * block, block, 0)

    def other(w):
        return swap(w, "fsdp", 1)

    def full(w, axis):
        return jnp.concatenate([w, other(w)], axis=axis)

    seg_all = gathered(segment_ids.reshape(1, piece_len), "context").reshape(seq_len)
    doc_start = jnp.sum((seg_all[None, :] < seg_all[:, None]).astype(jnp.int32), axis=1, keepdims=True)

    gains = full(jnp.concatenate([gain_attn, gain_ffn], axis=0), 1).astype(f32)
    hidden_rows = features(hidden_in.reshape(piece_len, width)).astype(f32)
    first_a = (hidden_rows * inverse_rms(hidden_rows) * gains[0]).astype(bf16)
    a_parts, _ = all_rows(own_block(first_a), first_a, seg_all)

    w_forget_full = jnp.pad(full(w_forget, 1), ((0, 0), (0, 0), (0, pair_lanes - heads)))
    bias = jnp.pad(b_forget, ((0, 0), (0, pair_lanes - heads)))
    w4 = (w_query, w_key, w_value, w_gate_out)
    t4 = tuple(other(w) for w in w4)
    to = other(w_attn_out)
    w3 = (w_gate, w_up, w_down)
    t3 = tuple(other(w) for w in w3)

    hidden = own_block(hidden_rows)
    saved = []
    cotangent_rows = features(cotangent.reshape(piece_len, width))
    last = layers - 1
    grad = own_block(cotangent_rows).astype(f32)
    for layer in range(layers):
        gain_one, gain_two = gains[layer], gains[layers + layer]
        inverse_one = inverse_rms(hidden)
        if layer > 0:
            a_parts, _ = all_rows((hidden * inverse_one * gain_one).astype(bf16))
        forget_weights = w_forget_full[layer]
        if shared_rows and layer == 1:
            forget_weights = after(forget_weights, g_last)
        a, (q, k, v, gate, forget, terms), sends = forward_own(
            place, a_parts, layer, w4, t4, w_attn_out, to, forget_weights,
            bias[layer : layer + 1], doc_start, piece_len,
        )
        if shared_rows and layer == 0:
            g_last = sequence_rows(after(own_block(cotangent_rows), a_parts[-1]))
        if shared_rows and layer > 0:
            saved[-1]["b_rows"] = sequence_rows(after(saved[-1]["b_shard"], a_parts[-1]))
        mixed = hidden + received_sum(sends)
        inverse_two = inverse_rms(mixed)
        b_shard = (mixed * inverse_two * gain_two).astype(bf16)
        b = gathered(b_shard, "tensor")
        gt, up, sends = ffn_forward(b, layer, w3, t3)
        saved.append(
            dict(hidden=hidden, inverse_one=inverse_one, a=a, kept=(q, k, v, gate, forget, terms), mixed=mixed,
                 inverse_two=inverse_two, b=b, b_shard=b_shard, gt=gt, up=up)
        )
        if layer < last:
            hidden = mixed + received_sum(sends)

    def finish(x):
        return features(gathered(x.astype(bf16), "tensor")).reshape(1, piece_len, width)

    last_sends = sends
    wide = shape((layers, half, local_width), f32)
    inner = shape((layers, half, w_gate.shape[2]), f32)
    results = list(
        unset(
            wide, wide, wide, wide, shape((layers, local_width, half), f32),
            inner, inner, shape((layers, w_down.shape[1], half), f32),
        )
    )
    small = [[None] * layers for _ in range(2)]
    gain_grads = [None] * (2 * layers)

    def ffn_theirs_of(layer, *tokens):
        s = saved[layer]
        values = ffn_theirs(s["b_rows"], s["g_rows"], layer, w3, t3, *tokens)
        s.update(values=values[:3], ffn_received=[other(x) for x in values[3:]])

    def ffn_mine_of(layer, *tokens):
        s = saved[layer]
        received = s["ffn_received"]
        results[5:] = ffn_mine(layer, s["b_rows"], s["g_rows"], s["values"], received, results[5:], *tokens)

    def attention_theirs_of(layer, *tokens):
        s = saved[layer]
        s["theirs"] = attention_grads(layer, *s["grads"], tokens=tokens)
        s["received"] = [other(x) for x in s["theirs"]]
        bias_grad = jnp.sum(s["grads"][2].astype(f32), axis=0)[:heads]
        small[1][layer] = bias_grad + other(bias_grad)

    def attention_mine_of(layer, *tokens):
        s = saved[layer]
        found = attention_grads(layer, *s["grads"], s["received"], results[:5], tokens)
        results[:5] = [*found[:4], found[5]]
        small[0][layer] = found[4][:, :heads]

    for layer in reversed(range(layers)):
        s = saved[layer]
        gain_one, gain_two = gains[layer], gains[layers + layer]
        tokens = ()
        if layer == last:
            g = cotangent_rows
        else:
            g_shard = grad.astype(bf16)
            g = gathered(g_shard, "tensor")
            tokens = (saved[layer + 1]["theirs"][0],)
            if shared_rows:
                s["g_rows"] = sequence_rows(g_shard)
        if not shared_rows:
            s.update(b_rows=s["b"], g_rows=g)
        sends = ffn_backward(g, s["gt"], s["up"], layer, w3, t3, *tokens)
        if layer < last:
            sends = after(sends, *saved[layer + 1]["received"])
        back, gain_grads[layers + layer] = norm_back(received_sum(sends), s["mixed"], s["inverse_two"], gain_two)
        grad_mixed = grad + back
        y_parts, y_far = all_rows(grad_mixed.astype(bf16), together=True)
        tokens = ()
        if layer < last:
            above = saved[layer + 1]
            attention_mine_of(layer + 1)
            ffn_theirs_of(layer + 1, *y_far)
            tokens = (results[0], above["values"][0])
        elif shared_rows:
            tokens = [x["b_rows"] for x in saved[:-1]]
        kept = (*s["kept"][:-1], after(s["kept"][-1], *tokens))
        y, (dq, dk, dv, dg, u, dz), sends = attention_backward(
            place, y_parts, layer, w4, t4, w_attn_out, to, w_forget_full[layer], kept, doc_start, piece_len,
        )
        token = y_parts[-1]
        if layer == last:
            block_sum = own_block(last_sends).astype(f32) + s["mixed"]
            with_rows = lax.dynamic_update_slice_in_dim(last_sends, block_sum.astype(bf16), t * block, 0)
            output = lax.psum(after(with_rows, token), "tensor")
        if layer < last:
            sends = after(sends, *above["ffn_received"])
        if shared_rows and layer == last:
            s.update(b_rows=sequence_rows(after(s["b_shard"], token)), g_rows=g_last)
        s["grads"] = (s["a"], (dq, dk, dv, dg), dz, u, y)
        if layer > 0:
            attention_theirs_of(layer)
        back, gain_grads[layer] = norm_back(received_sum(sends), s["hidden"], s["inverse_one"], gain_one)
        grad = grad_mixed + back

    for layer in reversed(range(1, layers)):
        ffn_mine_of(layer)
    ffn_theirs_of(0)
    attention_theirs_of(0, saved[0]["values"][0], grad)
    attention_mine_of(0, *saved[0]["ffn_received"])
    ffn_mine_of(0)
    if not shared_rows:
        results[5:] = [lax.psum(x, "context") for x in results[5:]]
    output = features(after(output, saved[0]["values"][0])).reshape(1, piece_len, width)
    grad_input = finish(grad)
    gain_total = jnp.stack(gain_grads).reshape(1, -1)
    for axis in (("context", "tensor"),) if shared_rows else ("context", "tensor"):
        gain_total = jnp.sum(gathered(gain_total, axis), axis=0, keepdims=True)
    gain_total = gain_total.reshape(2 * layers, width)
    gain_total = gain_total[:, :half] + other(gain_total[:, half:])
    return (
        output, grad_input, *results[:5], jnp.stack(small[0]), jnp.stack(small[1]),
        gain_total[:layers], gain_total[layers:], *results[5:],
    )


def solution(mesh):
    rows = P("fsdp", "context", None)
    wide, tall = P(None, "fsdp", "tensor"), P(None, "tensor", "fsdp")
    heads, gain = P(None, "tensor"), P(None, "fsdp")
    return jax.shard_map(
        local,
        mesh=mesh,
        in_specs=(
            rows, P("fsdp", "context"), wide, wide, wide, wide, tall, wide, heads, gain, gain, wide, wide, tall, rows,
        ),
        out_specs=(rows, rows, wide, wide, wide, wide, tall, wide, heads, gain, gain, wide, wide, tall),
        check_vma=False,
    )
```

```python
import functools

import jax
import jax.numpy as jnp
from jax import lax
from jax.experimental import pallas as pl
from jax.experimental.pallas import tpu as pltpu
from jax.sharding import PartitionSpec as P

epsilon = 1e-06
masked_value = -1e30
bf16 = jnp.bfloat16
f32 = jnp.float32
pair_lanes = 128
hidden_block = 256
chunk_rows = 256


def query_rows(seq_len):
    return 256 if seq_len <= 2048 else 128


def swap(x, axis, k):
    n = lax.axis_size(axis)
    return lax.ppermute(x, axis, [(i, i ^ k) for i in range(n)])


def pass_kernel(*refs):
    pass


def after(x, *tokens):
    if not tokens:
        return x
    anywhere = pl.BlockSpec(memory_space=pl.ANY)
    return pl.pallas_call(
        pass_kernel,
        in_specs=[anywhere] * (1 + len(tokens)),
        out_specs=anywhere,
        out_shape=jax.ShapeDtypeStruct(x.shape, x.dtype),
        input_output_aliases={0: 0},
    )(x, *tokens)


def gathered(block, axis):
    count = lax.axis_size(axis)
    copies = jnp.broadcast_to(block[None], (count,) + block.shape)
    return lax.all_to_all(copies, axis, 0, 0, tiled=True).reshape((-1,) + block.shape[1:])


def sequence_rows(shard):
    return lax.all_gather(shard, ("context", "tensor"), tiled=True)


def near_rows(own):
    return swap(own, "context", 1)


def far_blocks(shard):
    return swap(shard, "context", 2), swap(shard, "context", 3)


def all_rows(shard, own=None, token=None, together=False):
    if own is None:
        own = gathered(shard, "tensor")
    if lax.axis_size("context") != 4:
        return (lax.all_gather(own, "context", tiled=True),), ()
    second, third = far_blocks(shard)
    near = near_rows(own)
    if together:
        block, width = shard.shape
        far = gathered(jnp.concatenate([second, third], axis=0), "tensor")
        return (own, near, far.reshape(-1, 2, block, width)), (second, third)
    if token is not None:
        second = after(second, token)
    third = after(third, second)
    blocks = [second] + [swap(second, "tensor", k) for k in range(1, lax.axis_size("tensor"))]
    return (own, near, *blocks, gathered(third, "tensor")), (second, third)


def received_sum(sends):
    count = lax.axis_size("tensor")
    got = lax.all_to_all(sends.reshape(count, -1, sends.shape[1]), "tensor", 0, 0, tiled=True)
    return jnp.sum(got.astype(f32), axis=0)


def dot_nt(a, b):
    return lax.dot_general(a, b, (((1,), (1,)), ((), ())), preferred_element_type=f32)


def dot_tn(a, b):
    return lax.dot_general(a, b, (((0,), (0,)), ((), ())), preferred_element_type=f32)


def dot_nn(a, b):
    return jnp.dot(a, b, preferred_element_type=f32)


def each(count, body):
    if count <= 4:
        for i in range(count):
            body(i)
        return

    def one(i, carry):
        body(i)
        return carry

    lax.fori_loop(0, count, one, 0)


def rows_at(i, rows):
    start = i * rows
    return pl.ds(start if isinstance(start, int) else pl.multiple_of(start, rows), rows)


def assemble(parts, whole_ref, place_ref):
    z, t = place_ref[0], place_ref[1]
    piece, blocks_seen, piece_len = 0, 0, parts[0].shape[0]
    for part in parts:
        if len(part.shape) == 4:
            blocks, pieces, block = part.shape[:3]
            for p in range(pieces):
                for b in range(blocks):
                    at = pl.multiple_of((z ^ (piece + p)) * piece_len + b * block, block)
                    whole_ref[pl.ds(at, block), :] = part[b, p]
            piece += pieces
            continue
        rows = part.shape[0]
        if rows == piece_len:
            at = pl.multiple_of((z ^ piece) * piece_len, piece_len)
            piece += 1
        else:
            at = pl.multiple_of((z ^ piece) * piece_len + (t ^ blocks_seen) * rows, rows)
            blocks_seen += 1
            if blocks_seen * rows == piece_len:
                piece, blocks_seen = piece + 1, 0
        whole_ref[pl.ds(at, rows), :] = part[...]


def triangle(rows, reverse):
    row = lax.broadcasted_iota(jnp.int32, (rows, rows), 0)
    column = lax.broadcasted_iota(jnp.int32, (rows, rows), 1)
    return jnp.where((column >= row) if reverse else (column <= row), 1.0, 0.0).astype(bf16)


def running_sum(ref, reverse):
    rows = chunk_rows
    ones = triangle(rows, reverse)
    count = ref.shape[0] // rows
    edge = 0 if reverse else rows - 1

    def chunk(i, carry):
        here = pl.ds(pl.multiple_of((count - 1 - i if reverse else i) * rows, rows), rows)
        high, middle, lowest = three_parts(ref[here, :])
        total = dot_nn(ones, high) + dot_nn(ones, middle) + dot_nn(ones, lowest) + carry
        ref[here, :] = total
        return total[edge : edge + 1, :]

    lax.fori_loop(0, count, chunk, jnp.zeros((1, ref.shape[1]), f32), unroll=count <= 4)


def log_sigmoid(z):
    e = jnp.exp(-jnp.abs(z))
    small = e * (1.0 - e * (1 / 2 - e * (1 / 3 - e * (1 / 4 - e * (1 / 5 - e * (1 / 6 - e * (1 / 7)))))))
    return jnp.minimum(z, 0.0) - jnp.where(e < 0.0625, small, jnp.log(1.0 + e))


def three_parts(x):
    high = x.astype(bf16)
    middle = (x - high.astype(f32)).astype(bf16)
    return high, middle, (x - high.astype(f32) - middle.astype(f32)).astype(bf16)


def decay_side(terms, pair, key_side):
    row = lax.broadcasted_iota(jnp.int32, (pair_lanes, pair_lanes), 0)
    lane = lax.broadcasted_iota(jnp.int32, (pair_lanes, pair_lanes), 1)
    spot = lane & 63
    term = spot if key_side else spot - 3
    head = jnp.where(lane >= 64, 2 * pair, 2 * pair + 1)
    chosen = (term >= 0) & (term < 3) & (row == 8 * term + head)
    pick = jnp.where(chosen, -1.0 if key_side else 1.0, 0.0).astype(bf16)
    lanes_now = lax.broadcasted_iota(jnp.int32, (1, pair_lanes), 1) & 63
    other = lanes_now - 3 if key_side else lanes_now
    ones = jnp.where((other >= 0) & (other < 3), 1.0, 0.0)
    return (dot_nn(terms, pick) + ones).astype(bf16)


def mix_keys(k_ref, terms_ref, pair, ka, kb):
    def mix(i):
        here = rows_at(i, chunk_rows)
        lane = lax.broadcasted_iota(jnp.int32, (chunk_rows, pair_lanes), 1)
        k, side = k_ref[here, :], decay_side(terms_ref[here, :], pair, True)
        ka[here, :] = jnp.where(lane < 64, k, side)
        kb[here, :] = jnp.where(lane < 64, side, k)

    each(k_ref.shape[0] // chunk_rows, mix)


def mix_queries(q_ref, terms_ref, start, pair, qa, qb):
    def mix(i):
        here = rows_at(i, chunk_rows)
        lane = lax.broadcasted_iota(jnp.int32, (chunk_rows, pair_lanes), 1)
        q = (q_ref[here, :].astype(f32) * 0.125).astype(bf16)
        terms = terms_ref[pl.ds(pl.multiple_of(start + i * chunk_rows, chunk_rows), chunk_rows), :]
        side = decay_side(terms, pair, False)
        qa[here, :] = jnp.where(lane < 64, q, side)
        qb[here, :] = jnp.where(lane < 64, side, q)

    each(q_ref.shape[0] // chunk_rows, mix)


def live_mask(start_ref, start, first, width, rows):
    key_pos = first + lax.broadcasted_iota(jnp.int32, (rows, width), 1)
    query_pos = start + lax.broadcasted_iota(jnp.int32, (rows, width), 0)
    doc_start = start_ref[pl.ds(start, rows), :]
    return (key_pos <= query_pos) & (key_pos >= doc_start)


def over_query_blocks(seq_len, rows, body):
    before = seq_len // 2
    if seq_len // rows <= 4:
        for start in range(0, seq_len, rows):
            first = max(0, start - before)
            body(start, first, start + rows - first)
        return
    width = before + rows

    def one(i, carry):
        start = pl.multiple_of(i * rows, rows)
        first = pl.multiple_of(jnp.maximum(start - before, 0), rows)
        body(start, first, width)
        return carry

    lax.fori_loop(0, seq_len // rows, one, 0)


def probabilities(q_rows, k_rows, mask):
    s = jnp.where(mask, dot_nt(q_rows, k_rows), masked_value)
    e = jnp.exp(s - jnp.max(s, axis=1, keepdims=True))
    return e * (1.0 / jnp.sum(e, axis=1, keepdims=True))


def lane_blocks(refs):
    return jnp.concatenate([r[0] for r in refs], axis=1)


def forward_own_kernel(count_parts, piece_len, join, *refs):
    place_ref, parts, refs = refs[0], refs[1 : 1 + count_parts], list(refs[1 + count_parts :])
    (wq, wk, wv, wg), (tq, tk, tv, tg) = refs[:4], refs[4:8]
    wo, to, wf, bias, start_ref = refs[8:13]
    refs = refs[13:]
    a_ref = refs.pop(0) if join else parts[0]
    q_ref, k_ref, v_ref, gate_ref, z_ref, terms_ref, send_ref, qa, qb, ka, kb, decay, acc = refs
    pair = pl.program_id(0)
    seq_len, half = a_ref.shape[0], a_ref.shape[1] // 2
    piece_start = pl.multiple_of(place_ref[0] * piece_len, piece_len)

    @pl.when(pair == 0)
    def _():
        if join:
            assemble(parts, a_ref, place_ref)
        acc[...] = jnp.zeros_like(acc)

        def gates(i):
            here = rows_at(i, chunk_rows)
            z = dot_nn(a_ref[here, :], wf[...]) + bias[...]
            z_ref[here, :] = z
            decay[here, :] = log_sigmoid(z)

        each(seq_len // chunk_rows, gates)
        running_sum(decay, False)

        def split(i):
            here = rows_at(i, chunk_rows)
            lane = lax.broadcasted_iota(jnp.int32, (chunk_rows, pair_lanes), 1)
            high, middle, lowest = (x.astype(f32) for x in three_parts(decay[here, :]))
            later = jnp.where(lane < 16, pltpu.roll(middle, 8, 1), pltpu.roll(lowest, 16, 1))
            terms = jnp.where(lane < 8, high, later)
            terms_ref[here, :] = jnp.where(lane < 24, terms, 0.0).astype(bf16)

        each(seq_len // chunk_rows, split)

    w_mine, w_theirs = lane_blocks((wq, wk, wv, wg)), lane_blocks((tq, tk, tv, tg))

    def project(i):
        here = rows_at(i, chunk_rows)
        out = dot_nn(a_ref[here, :half], w_mine) + dot_nn(a_ref[here, half:], w_theirs)
        q_ref[here, :] = out[:, :128].astype(bf16)
        k_ref[here, :] = out[:, 128:256].astype(bf16)
        v_ref[here, :] = out[:, 256:384].astype(bf16)
        gate_ref[here, :] = out[:, 384:]

    each(seq_len // chunk_rows, project)
    piece = pl.ds(piece_start, piece_len)
    gate = jax.nn.sigmoid(gate_ref[piece, :])
    mix_keys(k_ref, terms_ref, pair, ka, kb)
    mix_queries(q_ref.at[piece, :], terms_ref, piece_start, pair, qa, qb)
    before = seq_len // 2
    for s in range(0, piece_len, query_rows(seq_len)):
        rows = query_rows(seq_len)
        width = before + rows
        start = pl.multiple_of(piece_start + s, rows)
        first = pl.multiple_of(jnp.maximum(start - before, 0), rows)
        mask = live_mask(start_ref, start, first, width, rows)
        keys = pl.ds(first, width)
        out = []
        for q_of, k_of in ((qa, ka), (qb, kb)):
            p = probabilities(q_of[s : s + rows, :], k_of[keys, :], mask).astype(bf16)
            out.append(dot_nn(p, v_ref[keys, :]))
        lane = lax.broadcasted_iota(jnp.int32, (rows, pair_lanes), 1)
        u = (jnp.where(lane < 64, out[0], out[1]) * gate[s : s + rows, :]).astype(bf16)
        acc[s : s + rows, :half] += dot_nn(u, wo[0])
        acc[s : s + rows, half:] += dot_nn(u, to[0])

    @pl.when(pair == pl.num_programs(0) - 1)
    def _():
        send_ref[...] = acc[...].astype(bf16)


def backward_kernel(count_parts, piece_len, join, *refs):
    place_ref, parts, refs = refs[0], refs[1 : 1 + count_parts], list(refs[1 + count_parts :])
    mine, theirs, (wo, to, wf) = refs[:4], refs[4:8], refs[8:11]
    q_ref, k_ref, v_ref, gate_ref, z_ref, terms_ref, start_ref = refs[11:18]
    refs = refs[18:]
    y_ref = refs.pop(0) if join else parts[0]
    dq_ref, dk_ref, dv_ref, dg_ref, u_ref, dz_ref, send_ref = refs[:7]
    qa, qb, ka, kb, dd, dus, dka, dkb, dva, dcs, acc = refs[7:]
    pair = pl.program_id(0)
    seq_len, half = y_ref.shape[0], y_ref.shape[1] // 2
    rows = query_rows(seq_len)
    piece = pl.ds(pl.multiple_of(place_ref[0] * piece_len, piece_len), piece_len)

    @pl.when(pair == 0)
    def _():
        if join:
            assemble(parts, y_ref, place_ref)
        acc[...] = jnp.zeros_like(acc)
        dcs[...] = jnp.zeros_like(dcs)

    def gates(i):
        here = rows_at(i, chunk_rows)
        du = dot_nt(y_ref[here, :half], wo[0]) + dot_nt(y_ref[here, half:], to[0])
        sig = jax.nn.sigmoid(gate_ref[here, :])
        dd[here, :] = (du * sig).astype(bf16)
        dus[here, :] = du * sig * (1.0 - sig)

    each(seq_len // chunk_rows, gates)
    mix_keys(k_ref, terms_ref, pair, ka, kb)
    mix_queries(q_ref, terms_ref, 0, pair, qa, qb)
    dka[...] = jnp.zeros_like(dka)
    dkb[...] = jnp.zeros_like(dkb)
    dva[...] = jnp.zeros_like(dva)
    lane = lax.broadcasted_iota(jnp.int32, (rows, pair_lanes), 1)

    def pick(column_a, column_b):
        at = lax.broadcasted_iota(jnp.int32, (column_a.shape[0], pair_lanes), 1)
        return jnp.where(at == 2 * pair, column_a, jnp.where(at == 2 * pair + 1, column_b, 0.0))

    def body(start, first, width):
        mask = live_mask(start_ref, start, first, width, rows)
        here, keys = pl.ds(start, rows), pl.ds(first, width)
        values = v_ref[keys, :]
        d_rows = dd[here, :]
        dq, o = [], []
        for head, (q_of, k_of, dk_of) in enumerate(((qa, ka, dka), (qb, kb, dkb))):
            own_lanes = (lane < 64) if head == 0 else (lane >= 64)
            p = probabilities(q_of[here, :], k_of[keys, :], mask)
            d_mine = jnp.where(own_lanes, d_rows, jnp.zeros_like(d_rows))
            dp = dot_nt(d_mine, values)
            delta = jnp.sum(p * dp, axis=1, keepdims=True)
            ds = (p * (dp - delta)).astype(bf16)
            dq.append(dot_nn(ds, k_of[keys, :]))
            dk_of[keys, :] += dot_tn(ds, q_of[here, :])
            low = p.astype(bf16)
            dva[keys, :] += dot_tn(low, d_mine)
            o.append(dot_nn(low, values))
        o = jnp.where(lane < 64, o[0], o[1])
        dg_ref[here, :] = (dus[here, :] * o).astype(bf16)
        u_ref[here, :] = (o * jax.nn.sigmoid(gate_ref[here, :])).astype(bf16)
        dq_ref[here, :] = (jnp.where(lane < 64, dq[0], dq[1]) * 0.125).astype(bf16)
        dcs[here, :] += pick(dq[0][:, 67:68], dq[1][:, 3:4])

    over_query_blocks(seq_len, rows, body)

    def finish(i):
        here = rows_at(i, chunk_rows)
        lanes_now = lax.broadcasted_iota(jnp.int32, (chunk_rows, pair_lanes), 1)
        ka_rows, kb_rows = dka[here, :], dkb[here, :]
        dk_ref[here, :] = jnp.where(lanes_now < 64, ka_rows, kb_rows).astype(bf16)
        dv_ref[here, :] = dva[here, :].astype(bf16)
        dcs[here, :] -= pick(ka_rows[:, 64:65], kb_rows[:, 0:1])

    each(seq_len // chunk_rows, finish)
    d_own = jnp.concatenate([r[piece, :] for r in (dq_ref, dk_ref, dv_ref, dg_ref)], axis=1)
    acc[:, :half] += dot_nt(d_own, lane_blocks(mine))
    acc[:, half:] += dot_nt(d_own, lane_blocks(theirs))

    @pl.when(pair == pl.num_programs(0) - 1)
    def _():
        running_sum(dcs, True)

        def last(i):
            here = rows_at(i, chunk_rows)
            dz_ref[here, :] = (dcs[here, :] * jax.nn.sigmoid(-z_ref[here, :])).astype(bf16)

        each(seq_len // chunk_rows, last)
        send_ref[...] = (acc[...] + dot_nt(dz_ref[piece, :], wf[...])).astype(bf16)


def ffn_forward_kernel(b_ref, wg, wu, wd, tg, tu, td, gt_ref, up_ref, send_ref, acc):
    half = b_ref.shape[1] // 2
    low, high = b_ref[:, :half], b_ref[:, half:]
    gt = dot_nn(low, wg[0]) + dot_nn(high, tg[0])
    up = dot_nn(low, wu[0]) + dot_nn(high, tu[0])
    gt_ref[...] = gt
    up_ref[...] = up
    m = (gt * jax.nn.sigmoid(gt) * up).astype(bf16)

    @pl.when(pl.program_id(0) == 0)
    def _():
        acc[...] = jnp.zeros_like(acc)

    acc[:, :half] += dot_nn(m, wd[0])
    acc[:, half:] += dot_nn(m, td[0])

    @pl.when(pl.program_id(0) == pl.num_programs(0) - 1)
    def _():
        send_ref[...] = acc[...].astype(bf16)


def inner_grads(dm, gt, up):
    sig = jax.nn.sigmoid(gt)
    d_gate = (dm * up * sig * (1.0 + gt * (1.0 - sig))).astype(bf16)
    return d_gate, (dm * (gt * sig)).astype(bf16)


def ffn_backward_kernel(g_ref, gt_ref, up_ref, wg, wu, wd, tg, tu, td, *refs):
    send_ref, acc = refs[-2:]
    half = g_ref.shape[1] // 2
    dm = dot_nt(g_ref[:, :half], wd[0]) + dot_nt(g_ref[:, half:], td[0])
    d_gate, d_up = inner_grads(dm, gt_ref[...], up_ref[...])

    @pl.when(pl.program_id(0) == 0)
    def _():
        acc[...] = jnp.zeros_like(acc)

    acc[:, :half] += dot_nt(d_gate, wg[0]) + dot_nt(d_up, wu[0])
    acc[:, half:] += dot_nt(d_gate, tg[0]) + dot_nt(d_up, tu[0])

    @pl.when(pl.program_id(0) == pl.num_programs(0) - 1)
    def _():
        send_ref[...] = acc[...].astype(bf16)


def ffn_theirs_kernel(b_ref, g_ref, wg, wu, wd, tg, tu, td, *refs):
    m_ref, dgate_ref, dup_ref, gate_out, up_out, down_out, turned = refs[-7:]
    half = b_ref.shape[1] // 2

    @pl.when(pl.program_id(0) == 0)
    def _():
        turned[...] = b_ref[:, half:].T

    def chunk(i):
        here = rows_at(i, chunk_rows)
        low, high = b_ref[here, :half], b_ref[here, half:]
        gt = dot_nn(low, wg[0]) + dot_nn(high, tg[0])
        up = dot_nn(low, wu[0]) + dot_nn(high, tu[0])
        dm = dot_nt(g_ref[here, :half], wd[0]) + dot_nt(g_ref[here, half:], td[0])
        m_ref[here, :] = (gt * jax.nn.sigmoid(gt) * up).astype(bf16)
        dgate_ref[here, :], dup_ref[here, :] = inner_grads(dm, gt, up)

    each(b_ref.shape[0] // chunk_rows, chunk)
    gate_out[...] = dot_nn(turned[...], dgate_ref[...]).astype(bf16)
    up_out[...] = dot_nn(turned[...], dup_ref[...]).astype(bf16)
    down_out[...] = dot_tn(m_ref[...], g_ref[:, half:]).astype(bf16)


def ffn_mine_kernel(b_ref, g_ref, m_ref, dgate_ref, dup_ref, gate_in, up_in, down_in, *refs):
    gate_out, up_out, down_out, turned = refs[-4:]

    @pl.when(pl.program_id(0) == 0)
    def _():
        turned[...] = b_ref[...].T

    gate_out[0] = dot_nn(turned[...], dgate_ref[...]) + gate_in[...].astype(f32)
    up_out[0] = dot_nn(turned[...], dup_ref[...]) + up_in[...].astype(f32)
    down_out[0] = dot_tn(m_ref[...], g_ref[...]) + down_in[...].astype(f32)


def attention_grads_kernel(steps, mine, *refs):
    a_ref, dq, dk, dv, dg, dz, u_ref, y_ref = refs[:8]
    received = refs[8:14] if mine else [None] * 6
    acc, acc_out = refs[-2:]
    outs = refs[-8:-2]
    turned = a_ref[...].T
    width = dq.shape[1]
    parts = [dot_nn(turned, d[...]) for d in (dq, dk, dv, dg, dz)]
    out = dot_tn(u_ref[...], y_ref[...])

    def give(values):
        for ref, value, more in zip(outs, values, received):
            total = value if more is None else value + more[...].astype(f32)
            if len(ref.shape) == 3:
                ref[0] = total.astype(ref.dtype)
            else:
                ref[...] = total.astype(ref.dtype)

    if steps == 1:
        give([*parts, out])
        return
    step = pl.program_id(0)

    @pl.when(step == 0)
    def _():
        acc[...] = jnp.zeros_like(acc)
        acc_out[...] = jnp.zeros_like(acc_out)

    for k, part in enumerate(parts):
        acc[:, k * width : k * width + part.shape[1]] += part
    acc_out[...] += out

    @pl.when(step == steps - 1)
    def _():
        found = [acc[:, k * width : k * width + p.shape[1]] for k, p in enumerate(parts)]
        give([*found, acc_out[...]])


def fixed(shape, single=True):
    zeros = (0,) * len(shape)
    if single:
        return pl.BlockSpec(shape, lambda *_: zeros, pipeline_mode=pl.Buffered(1))
    return pl.BlockSpec(shape, lambda *_: zeros)


def lanes(seq_len):
    return pl.BlockSpec((seq_len, pair_lanes), lambda p, *_: (0, p))


def lanes_read(seq_len):
    if seq_len <= 2048:
        return lanes(seq_len)
    return pl.BlockSpec((seq_len, pair_lanes), lambda p, *_: (0, p), pipeline_mode=pl.Buffered(1))


def columns_of(w, layer, width):
    return pl.BlockSpec((1, w.shape[1], width), lambda p, *_: (layer, 0, p))


def rows_of(w, layer, height):
    return pl.BlockSpec((1, height, w.shape[2]), lambda p, *_: (layer, p, 0))


def shape(dims, dtype):
    return jax.ShapeDtypeStruct(dims, dtype)


def attention_specs(parts, layer, w4, t4, wo, to, seq_len, join):
    specs = [fixed(p.shape) for p in parts]
    specs += [columns_of(w, layer, pair_lanes) for w in (*w4, *t4)]
    specs += [rows_of(wo, layer, pair_lanes), rows_of(to, layer, pair_lanes)]
    return specs


def cost(microseconds):
    return pl.CostEstimate(flops=int(microseconds * 1.1e9), bytes_accessed=0, transcendentals=0)


def token_specs(tokens):
    return [pl.BlockSpec(memory_space=pl.ANY) for _ in tokens]


def forward_own(place, parts, layer, w4, t4, wo, to, wf, bias, doc_start, piece_len):
    seq_len, width = doc_start.shape[0], parts[0].shape[1]
    local_width = wo.shape[1]
    join = len(parts) > 1
    terms = (seq_len, pair_lanes)
    outs = [shape((seq_len, local_width), bf16)] * 3 + [shape((seq_len, local_width), f32)]
    outs += [shape(terms, f32), shape(terms, bf16), shape((piece_len, width), bf16)]
    specs = [lanes(seq_len)] * 4 + [fixed(terms, False)] * 2 + [fixed((piece_len, width), False)]
    if join:
        outs, specs = [shape((seq_len, width), bf16)] + outs, [fixed((seq_len, width))] + specs
    low, piece = pltpu.VMEM((seq_len, pair_lanes), bf16), pltpu.VMEM((piece_len, pair_lanes), bf16)
    got = pl.pallas_call(
        functools.partial(forward_own_kernel, len(parts), piece_len, join),
        grid_spec=pltpu.PrefetchScalarGridSpec(
            num_scalar_prefetch=1,
            grid=(local_width // pair_lanes,),
            in_specs=attention_specs(parts, layer, w4, t4, wo, to, seq_len, join)
            + [fixed(wf.shape), fixed(bias.shape), fixed(doc_start.shape)],
            out_specs=specs,
            scratch_shapes=[piece] * 2 + [low] * 2 + [pltpu.VMEM(terms, f32), pltpu.VMEM((piece_len, width), f32)],
        ),
        out_shape=outs,
        cost_estimate=cost(19),
        compiler_params=pltpu.CompilerParams(vmem_limit_bytes=60 << 20),
    )(place, *parts, *w4, *t4, wo, to, wf, bias, doc_start)
    got = list(got)
    a = got.pop(0) if join else parts[0]
    return a, got[:6], got[6]


def attention_backward(place, parts, layer, w4, t4, wo, to, wf, saved, doc_start, piece_len):
    q, k, v, gate, z, terms = saved
    seq_len, width = doc_start.shape[0], parts[0].shape[1]
    local_width = wo.shape[1]
    join = len(parts) > 1
    outs = [shape((seq_len, local_width), bf16)] * 5 + [shape((seq_len, pair_lanes), bf16)]
    outs += [shape((piece_len, width), bf16)]
    specs = [lanes(seq_len)] * 5 + [fixed((seq_len, pair_lanes), False), fixed((piece_len, width), False)]
    if join:
        outs, specs = [shape((seq_len, width), bf16)] + outs, [fixed((seq_len, width))] + specs
    low, high = pltpu.VMEM((seq_len, pair_lanes), bf16), pltpu.VMEM((seq_len, pair_lanes), f32)
    got = pl.pallas_call(
        functools.partial(backward_kernel, len(parts), piece_len, join),
        grid_spec=pltpu.PrefetchScalarGridSpec(
            num_scalar_prefetch=1,
            grid=(local_width // pair_lanes,),
            in_specs=attention_specs(parts, layer, w4, t4, wo, to, seq_len, join)
            + [fixed(wf.shape)]
            + [lanes_read(seq_len)] * 4
            + [fixed(z.shape), fixed(terms.shape), fixed(doc_start.shape)],
            out_specs=specs,
            scratch_shapes=[low] * 5 + [high] * 5 + [pltpu.VMEM((piece_len, width), f32)],
        ),
        out_shape=outs,
        cost_estimate=cost(33),
        compiler_params=pltpu.CompilerParams(vmem_limit_bytes=60 << 20),
    )(place, *parts, *w4, *t4, wo, to, wf, q, k, v, gate, z, terms, doc_start)
    got = list(got)
    y = got.pop(0) if join else parts[0]
    return y, got[:6], got[6]


def ffn_weights(layer, w3, t3):
    specs = []
    for wg, wu, wd in (w3, t3):
        specs += [
            columns_of(wg, layer, hidden_block), columns_of(wu, layer, hidden_block), rows_of(wd, layer, hidden_block),
        ]
    return specs


def blocks_of(rows):
    return pl.BlockSpec((rows, hidden_block), lambda p, *_: (0, p))


def ffn_forward(b, layer, w3, t3):
    rows, width = b.shape
    inner = w3[2].shape[1]
    return pl.pallas_call(
        ffn_forward_kernel,
        grid=(inner // hidden_block,),
        in_specs=[fixed(b.shape)] + ffn_weights(layer, w3, t3),
        out_specs=[blocks_of(rows)] * 2 + [fixed((rows, width), False)],
        scratch_shapes=[pltpu.VMEM((rows, width), f32)],
        out_shape=[shape((rows, inner), f32)] * 2 + [shape((rows, width), bf16)],
        cost_estimate=cost(7),
        compiler_params=pltpu.CompilerParams(vmem_limit_bytes=60 << 20),
    )(b, *w3, *t3)


def ffn_backward(g, gt, up, layer, w3, t3, *tokens):
    rows, width = g.shape
    return pl.pallas_call(
        ffn_backward_kernel,
        grid=(gt.shape[1] // hidden_block,),
        in_specs=[fixed(g.shape)] + [blocks_of(rows)] * 2 + ffn_weights(layer, w3, t3) + token_specs(tokens),
        out_specs=fixed((rows, width), False),
        scratch_shapes=[pltpu.VMEM((rows, width), f32)],
        out_shape=shape((rows, width), bf16),
        cost_estimate=cost(8),
        compiler_params=pltpu.CompilerParams(vmem_limit_bytes=60 << 20),
    )(g, gt, up, *w3, *t3, *tokens)


def ffn_theirs(b, g, layer, w3, t3, *tokens):
    rows, width = b.shape
    half = width // 2
    inner = w3[2].shape[1]
    wide = pl.BlockSpec((half, hidden_block), lambda p: (0, p))
    return pl.pallas_call(
        ffn_theirs_kernel,
        grid=(inner // hidden_block,),
        in_specs=[fixed(b.shape), fixed(g.shape)] + ffn_weights(layer, w3, t3) + token_specs(tokens),
        out_specs=[blocks_of(rows)] * 3 + [wide, wide, pl.BlockSpec((hidden_block, half), lambda p: (p, 0))],
        scratch_shapes=[pltpu.VMEM((half, rows), bf16)],
        out_shape=[shape((rows, inner), bf16)] * 3
        + [shape((half, inner), bf16)] * 2
        + [shape((inner, half), bf16)],
        cost_estimate=cost(24),
        compiler_params=pltpu.CompilerParams(vmem_limit_bytes=60 << 20),
    )(b, g, *w3, *t3, *tokens)


def anywhere():
    return pl.BlockSpec(memory_space=pl.ANY)


def ffn_mine(layer, b, g, values, received, totals, *tokens):
    rows, width = b.shape
    half, inner = width // 2, values[0].shape[1]
    wide = pl.BlockSpec((half, hidden_block), lambda p: (0, p))
    tall = pl.BlockSpec((hidden_block, half), lambda p: (p, 0))
    wide_out = pl.BlockSpec((1, half, hidden_block), lambda p: (layer, 0, p))
    tall_out = pl.BlockSpec((1, hidden_block, half), lambda p: (layer, p, 0))
    return pl.pallas_call(
        ffn_mine_kernel,
        grid=(inner // hidden_block,),
        in_specs=[fixed((rows, half))] * 2
        + [blocks_of(rows)] * 3
        + [wide, wide, tall]
        + [anywhere()] * 3
        + token_specs(tokens),
        out_specs=[wide_out, wide_out, tall_out],
        out_shape=[shape(x.shape, x.dtype) for x in totals],
        scratch_shapes=[pltpu.VMEM((half, rows), bf16)],
        input_output_aliases={8: 0, 9: 1, 10: 2},
        cost_estimate=cost(9),
        compiler_params=pltpu.CompilerParams(vmem_limit_bytes=60 << 20),
    )(b, g, *values, *received, *totals, *tokens)


def attention_grads(layer, a, ds, dz, u, y, received=None, totals=None, tokens=()):
    rows, width = a.shape
    half, local_width = width // 2, u.shape[1]
    part = min(rows, 1024)
    steps = rows // part
    mine = received is not None
    side = 0 if mine else 1
    features = pl.BlockSpec((part, half), lambda p: (p, side))
    across = [pl.BlockSpec((part, x.shape[1]), lambda p: (p, 0)) for x in (*ds, dz, u)]
    specs = [features, *across, features]
    operands = [a, *ds, dz, u, y]
    flat = [(half, local_width)] * 4 + [(half, pair_lanes), (local_width, half)]
    if mine:
        specs += [fixed(x) for x in flat] + [anywhere()] * 5
        operands += [*received, *totals]
        outs = [shape(x.shape, f32) for x in totals[:4]] + [shape(flat[4], f32), shape(totals[4].shape, f32)]
        layered = pl.BlockSpec((1, half, local_width), lambda p: (layer, 0, 0))
        out_specs = [layered] * 4 + [fixed(flat[4], False)]
        out_specs += [pl.BlockSpec((1, local_width, half), lambda p: (layer, 0, 0))]
        aliases = {14: 0, 15: 1, 16: 2, 17: 3, 18: 5}
    else:
        outs, out_specs, aliases = [shape(x, bf16) for x in flat], [fixed(x, False) for x in flat], {}
    sizes = [(half, 4 * local_width + pair_lanes), (local_width, half)] if steps > 1 else [(8, 128)] * 2
    return pl.pallas_call(
        functools.partial(attention_grads_kernel, steps, mine),
        grid=(steps,),
        in_specs=specs + token_specs(tokens),
        out_specs=out_specs,
        out_shape=outs,
        scratch_shapes=[pltpu.VMEM(x, f32) for x in sizes],
        input_output_aliases=aliases,
        cost_estimate=cost(7),
        compiler_params=pltpu.CompilerParams(vmem_limit_bytes=60 << 20),
    )(*operands, *tokens)


def unset(*like):
    return pl.pallas_call(
        pass_kernel,
        out_specs=[pl.BlockSpec(memory_space=pl.ANY) for _ in like],
        out_shape=list(like),
    )()


def inverse_rms(h):
    return lax.rsqrt(jnp.mean(h * h, axis=-1, keepdims=True) + epsilon)


def norm_back(grad_normed, hidden, inverse, gain):
    scaled = hidden * inverse
    weighted = grad_normed * gain
    grad_gain = jnp.sum(grad_normed * scaled, axis=0)
    mean = jnp.mean(weighted * scaled, axis=-1, keepdims=True)
    return inverse * (weighted - scaled * mean), grad_gain


def local(
    hidden_in, segment_ids, w_query, w_key, w_value, w_gate_out, w_attn_out, w_forget, b_forget,
    gain_attn, gain_ffn, w_gate, w_up, w_down, cotangent,
):
    seq_count, piece_len, width = hidden_in.shape
    count_z, count_t = lax.axis_size("context"), lax.axis_size("tensor")
    core, z, t = lax.axis_index("fsdp"), lax.axis_index("context"), lax.axis_index("tensor")
    layers, half, local_width = w_query.shape
    heads = w_forget.shape[2]
    block = piece_len // count_t
    seq_len = piece_len * count_z
    shared_rows = count_z == 4
    place = jnp.stack([z, t]).astype(jnp.int32)

    def features(x):
        return jnp.where(core == 0, x, jnp.concatenate([x[..., half:], x[..., :half]], axis=-1))

    def own_block(x):
        return lax.dynamic_slice_in_dim(x, t * block, block, 0)

    def other(w):
        return swap(w, "fsdp", 1)

    def full(w, axis):
        return jnp.concatenate([w, other(w)], axis=axis)

    seg_all = gathered(segment_ids.reshape(1, piece_len), "context").reshape(seq_len)
    doc_start = jnp.sum((seg_all[None, :] < seg_all[:, None]).astype(jnp.int32), axis=1, keepdims=True)

    gains = full(jnp.concatenate([gain_attn, gain_ffn], axis=0), 1).astype(f32)
    hidden_rows = features(hidden_in.reshape(piece_len, width)).astype(f32)
    first_a = (hidden_rows * inverse_rms(hidden_rows) * gains[0]).astype(bf16)
    a_parts, _ = all_rows(own_block(first_a), first_a, seg_all)

    w_forget_full = jnp.pad(full(w_forget, 1), ((0, 0), (0, 0), (0, pair_lanes - heads)))
    bias = jnp.pad(b_forget, ((0, 0), (0, pair_lanes - heads)))
    w4 = (w_query, w_key, w_value, w_gate_out)
    t4 = tuple(other(w) for w in w4)
    to = other(w_attn_out)
    w3 = (w_gate, w_up, w_down)
    t3 = tuple(other(w) for w in w3)

    hidden = own_block(hidden_rows)
    saved = []
    cotangent_rows = features(cotangent.reshape(piece_len, width))
    last = layers - 1
    grad = own_block(cotangent_rows).astype(f32)
    for layer in range(layers):
        gain_one, gain_two = gains[layer], gains[layers + layer]
        inverse_one = inverse_rms(hidden)
        if layer > 0:
            a_parts, _ = all_rows((hidden * inverse_one * gain_one).astype(bf16))
        forget_weights = w_forget_full[layer]
        if shared_rows and layer == 1:
            forget_weights = after(forget_weights, g_last)
        a, (q, k, v, gate, forget, terms), sends = forward_own(
            place, a_parts, layer, w4, t4, w_attn_out, to, forget_weights,
            bias[layer : layer + 1], doc_start, piece_len,
        )
        if shared_rows and layer == 0:
            g_last = sequence_rows(after(own_block(cotangent_rows), a_parts[-1]))
        if shared_rows and layer > 0:
            saved[-1]["b_rows"] = sequence_rows(after(saved[-1]["b_shard"], a_parts[-1]))
        mixed = hidden + received_sum(sends)
        inverse_two = inverse_rms(mixed)
        b_shard = (mixed * inverse_two * gain_two).astype(bf16)
        b = gathered(b_shard, "tensor")
        gt, up, sends = ffn_forward(b, layer, w3, t3)
        saved.append(
            dict(hidden=hidden, inverse_one=inverse_one, a=a, kept=(q, k, v, gate, forget, terms), mixed=mixed,
                 inverse_two=inverse_two, b=b, b_shard=b_shard, gt=gt, up=up)
        )
        if layer < last:
            hidden = mixed + received_sum(sends)

    def finish(x):
        return features(gathered(x.astype(bf16), "tensor")).reshape(1, piece_len, width)

    last_sends = sends
    wide = shape((layers, half, local_width), f32)
    inner = shape((layers, half, w_gate.shape[2]), f32)
    results = list(
        unset(
            wide, wide, wide, wide, shape((layers, local_width, half), f32),
            inner, inner, shape((layers, w_down.shape[1], half), f32),
        )
    )
    small = [[None] * layers for _ in range(2)]
    gain_grads = [None] * (2 * layers)

    def ffn_theirs_of(layer, *tokens):
        s = saved[layer]
        values = ffn_theirs(s["b_rows"], s["g_rows"], layer, w3, t3, *tokens)
        s.update(values=values[:3], ffn_received=[other(x) for x in values[3:]])

    def ffn_mine_of(layer, *tokens):
        s = saved[layer]
        received = s["ffn_received"]
        results[5:] = ffn_mine(layer, s["b_rows"], s["g_rows"], s["values"], received, results[5:], *tokens)

    def attention_theirs_of(layer, *tokens):
        s = saved[layer]
        s["theirs"] = attention_grads(layer, *s["grads"], tokens=tokens)
        s["received"] = [other(x) for x in s["theirs"]]
        bias_grad = jnp.sum(s["grads"][2].astype(f32), axis=0)[:heads]
        small[1][layer] = bias_grad + other(bias_grad)

    def attention_mine_of(layer, *tokens):
        s = saved[layer]
        found = attention_grads(layer, *s["grads"], s["received"], results[:5], tokens)
        results[:5] = [*found[:4], found[5]]
        small[0][layer] = found[4][:, :heads]

    for layer in reversed(range(layers)):
        s = saved[layer]
        gain_one, gain_two = gains[layer], gains[layers + layer]
        tokens = ()
        if layer == last:
            g = cotangent_rows
        else:
            g_shard = grad.astype(bf16)
            g = gathered(g_shard, "tensor")
            tokens = (saved[layer + 1]["theirs"][0],)
            if shared_rows:
                s["g_rows"] = sequence_rows(g_shard)
        if not shared_rows:
            s.update(b_rows=s["b"], g_rows=g)
        sends = ffn_backward(g, s["gt"], s["up"], layer, w3, t3, *tokens)
        if layer < last:
            sends = after(sends, *saved[layer + 1]["received"])
        back, gain_grads[layers + layer] = norm_back(received_sum(sends), s["mixed"], s["inverse_two"], gain_two)
        grad_mixed = grad + back
        y_shard = grad_mixed.astype(bf16)
        if layer < last:
            attention_mine_of(layer + 1)
            y_shard = after(y_shard, results[0])
        y_parts, y_far = all_rows(y_shard, together=layer < last)
        tokens = ()
        if layer < last:
            above = saved[layer + 1]
            ffn_theirs_of(layer + 1, *y_far)
            tokens = (above["values"][0], s["g_rows"])
        elif shared_rows:
            tokens = [x["b_rows"] for x in saved[:-1]]
        kept = (*s["kept"][:-1], after(s["kept"][-1], *tokens))
        y, (dq, dk, dv, dg, u, dz), sends = attention_backward(
            place, y_parts, layer, w4, t4, w_attn_out, to, w_forget_full[layer], kept, doc_start, piece_len,
        )
        token = y_parts[-1]
        if layer == last:
            block_sum = own_block(last_sends).astype(f32) + s["mixed"]
            with_rows = lax.dynamic_update_slice_in_dim(last_sends, block_sum.astype(bf16), t * block, 0)
            output = lax.psum(after(with_rows, token), "tensor")
        if shared_rows and layer == last:
            s.update(b_rows=sequence_rows(after(s["b_shard"], token)), g_rows=g_last)
        s["grads"] = (s["a"], (dq, dk, dv, dg), dz, u, y)
        if layer > 0:
            attention_theirs_of(layer)
        back, gain_grads[layer] = norm_back(received_sum(sends), s["hidden"], s["inverse_one"], gain_one)
        grad = grad_mixed + back

    for layer in reversed(range(1, layers)):
        ffn_mine_of(layer)
    ffn_theirs_of(0)
    grad = after(grad, saved[0]["values"][0])
    attention_theirs_of(0, grad)
    gain_total = jnp.stack(gain_grads).reshape(1, -1)
    for axis in (("context", "tensor"),) if shared_rows else ("context", "tensor"):
        gain_total = jnp.sum(gathered(gain_total, axis), axis=0, keepdims=True)
    gain_total = gain_total.reshape(2 * layers, width)
    gain_total = gain_total[:, :half] + other(gain_total[:, half:])
    attention_mine_of(0, gain_total, *saved[0]["ffn_received"])
    ffn_mine_of(0)
    if not shared_rows:
        results[5:] = [lax.psum(x, "context") for x in results[5:]]
    output = features(after(output, saved[0]["values"][0])).reshape(1, piece_len, width)
    grad_input = finish(grad)
    return (
        output, grad_input, *results[:5], jnp.stack(small[0]), jnp.stack(small[1]),
        gain_total[:layers], gain_total[layers:], *results[5:],
    )


def solution(mesh):
    rows = P("fsdp", "context", None)
    wide, tall = P(None, "fsdp", "tensor"), P(None, "tensor", "fsdp")
    heads, gain = P(None, "tensor"), P(None, "fsdp")
    return jax.shard_map(
        local,
        mesh=mesh,
        in_specs=(
            rows, P("fsdp", "context"), wide, wide, wide, wide, tall, wide, heads, gain, gain, wide, wide, tall, rows,
        ),
        out_specs=(rows, rows, wide, wide, wide, wide, tall, wide, heads, gain, gain, wide, wide, tall),
        check_vma=False,
    )
```

```python
import functools

import jax
import jax.numpy as jnp
from jax import lax
from jax.experimental import pallas as pl
from jax.experimental.pallas import tpu as pltpu
from jax.sharding import PartitionSpec as P

epsilon = 1e-06
masked_value = -1e30
bf16 = jnp.bfloat16
f32 = jnp.float32
pair_lanes = 128
hidden_block = 256
chunk_rows = 256


def query_rows(seq_len):
    return 256 if seq_len <= 2048 else 128


def swap(x, axis, k):
    n = lax.axis_size(axis)
    return lax.ppermute(x, axis, [(i, i ^ k) for i in range(n)])


def pass_kernel(*refs):
    pass


def after(x, *tokens):
    if not tokens:
        return x
    anywhere = pl.BlockSpec(memory_space=pl.ANY)
    return pl.pallas_call(
        pass_kernel,
        in_specs=[anywhere] * (1 + len(tokens)),
        out_specs=anywhere,
        out_shape=jax.ShapeDtypeStruct(x.shape, x.dtype),
        input_output_aliases={0: 0},
    )(x, *tokens)


def gathered(block, axis):
    count = lax.axis_size(axis)
    copies = jnp.broadcast_to(block[None], (count,) + block.shape)
    return lax.all_to_all(copies, axis, 0, 0, tiled=True).reshape((-1,) + block.shape[1:])


def sequence_rows(shard):
    return lax.all_gather(shard, ("context", "tensor"), tiled=True)


def near_rows(own):
    return swap(own, "context", 1)


def far_blocks(shard):
    return swap(shard, "context", 2), swap(shard, "context", 3)


def all_rows(shard, own=None, token=None, together=False):
    if own is None:
        own = gathered(shard, "tensor")
    if lax.axis_size("context") != 4:
        return (lax.all_gather(own, "context", tiled=True),), ()
    second, third = far_blocks(shard)
    near = near_rows(own)
    if together:
        block, width = shard.shape
        far = gathered(after(jnp.concatenate([second, third], axis=0), own), "tensor")
        return (own, near, far.reshape(-1, 2, block, width)), (second, third)
    if token is not None:
        second = after(second, token)
    parts = [own, near]
    for far in (second, third):
        parts += [far] + [swap(far, "tensor", k) for k in range(1, lax.axis_size("tensor"))]
    return tuple(parts), (second, third)


def received_sum(sends):
    count = lax.axis_size("tensor")
    got = lax.all_to_all(sends.reshape(count, -1, sends.shape[1]), "tensor", 0, 0, tiled=True)
    return jnp.sum(got.astype(f32), axis=0)


def dot_nt(a, b):
    return lax.dot_general(a, b, (((1,), (1,)), ((), ())), preferred_element_type=f32)


def dot_tn(a, b):
    return lax.dot_general(a, b, (((0,), (0,)), ((), ())), preferred_element_type=f32)


def dot_nn(a, b):
    return jnp.dot(a, b, preferred_element_type=f32)


def each(count, body):
    if count <= 4:
        for i in range(count):
            body(i)
        return

    def one(i, carry):
        body(i)
        return carry

    lax.fori_loop(0, count, one, 0)


def rows_at(i, rows):
    start = i * rows
    return pl.ds(start if isinstance(start, int) else pl.multiple_of(start, rows), rows)


def assemble(parts, whole_ref, place_ref):
    z, t = place_ref[0], place_ref[1]
    piece, blocks_seen, piece_len = 0, 0, parts[0].shape[0]
    for part in parts:
        if len(part.shape) == 4:
            blocks, pieces, block = part.shape[:3]
            for p in range(pieces):
                for b in range(blocks):
                    at = pl.multiple_of((z ^ (piece + p)) * piece_len + b * block, block)
                    whole_ref[pl.ds(at, block), :] = part[b, p]
            piece += pieces
            continue
        rows = part.shape[0]
        if rows == piece_len:
            at = pl.multiple_of((z ^ piece) * piece_len, piece_len)
            piece += 1
        else:
            at = pl.multiple_of((z ^ piece) * piece_len + (t ^ blocks_seen) * rows, rows)
            blocks_seen += 1
            if blocks_seen * rows == piece_len:
                piece, blocks_seen = piece + 1, 0
        whole_ref[pl.ds(at, rows), :] = part[...]


def triangle(rows, reverse):
    row = lax.broadcasted_iota(jnp.int32, (rows, rows), 0)
    column = lax.broadcasted_iota(jnp.int32, (rows, rows), 1)
    return jnp.where((column >= row) if reverse else (column <= row), 1.0, 0.0).astype(bf16)


def running_sum(ref, reverse):
    rows = chunk_rows
    ones = triangle(rows, reverse)
    count = ref.shape[0] // rows
    edge = 0 if reverse else rows - 1

    def chunk(i, carry):
        here = pl.ds(pl.multiple_of((count - 1 - i if reverse else i) * rows, rows), rows)
        high, middle, lowest = three_parts(ref[here, :])
        total = dot_nn(ones, high) + dot_nn(ones, middle) + dot_nn(ones, lowest) + carry
        ref[here, :] = total
        return total[edge : edge + 1, :]

    lax.fori_loop(0, count, chunk, jnp.zeros((1, ref.shape[1]), f32), unroll=count <= 4)


def log_sigmoid(z):
    e = jnp.exp(-jnp.abs(z))
    small = e * (1.0 - e * (1 / 2 - e * (1 / 3 - e * (1 / 4 - e * (1 / 5 - e * (1 / 6 - e * (1 / 7)))))))
    return jnp.minimum(z, 0.0) - jnp.where(e < 0.0625, small, jnp.log(1.0 + e))


def three_parts(x):
    high = x.astype(bf16)
    middle = (x - high.astype(f32)).astype(bf16)
    return high, middle, (x - high.astype(f32) - middle.astype(f32)).astype(bf16)


def decay_side(terms, pair, key_side):
    row = lax.broadcasted_iota(jnp.int32, (pair_lanes, pair_lanes), 0)
    lane = lax.broadcasted_iota(jnp.int32, (pair_lanes, pair_lanes), 1)
    spot = lane & 63
    term = spot if key_side else spot - 3
    head = jnp.where(lane >= 64, 2 * pair, 2 * pair + 1)
    chosen = (term >= 0) & (term < 3) & (row == 8 * term + head)
    pick = jnp.where(chosen, -1.0 if key_side else 1.0, 0.0).astype(bf16)
    lanes_now = lax.broadcasted_iota(jnp.int32, (1, pair_lanes), 1) & 63
    other = lanes_now - 3 if key_side else lanes_now
    ones = jnp.where((other >= 0) & (other < 3), 1.0, 0.0)
    return (dot_nn(terms, pick) + ones).astype(bf16)


def mix_keys(k_ref, terms_ref, pair, ka, kb):
    def mix(i):
        here = rows_at(i, chunk_rows)
        lane = lax.broadcasted_iota(jnp.int32, (chunk_rows, pair_lanes), 1)
        k, side = k_ref[here, :], decay_side(terms_ref[here, :], pair, True)
        ka[here, :] = jnp.where(lane < 64, k, side)
        kb[here, :] = jnp.where(lane < 64, side, k)

    each(k_ref.shape[0] // chunk_rows, mix)


def mix_queries(q_ref, terms_ref, start, pair, qa, qb):
    def mix(i):
        here = rows_at(i, chunk_rows)
        lane = lax.broadcasted_iota(jnp.int32, (chunk_rows, pair_lanes), 1)
        q = (q_ref[here, :].astype(f32) * 0.125).astype(bf16)
        terms = terms_ref[pl.ds(pl.multiple_of(start + i * chunk_rows, chunk_rows), chunk_rows), :]
        side = decay_side(terms, pair, False)
        qa[here, :] = jnp.where(lane < 64, q, side)
        qb[here, :] = jnp.where(lane < 64, side, q)

    each(q_ref.shape[0] // chunk_rows, mix)


def live_mask(start_ref, start, first, width, rows):
    key_pos = first + lax.broadcasted_iota(jnp.int32, (rows, width), 1)
    query_pos = start + lax.broadcasted_iota(jnp.int32, (rows, width), 0)
    doc_start = start_ref[pl.ds(start, rows), :]
    return (key_pos <= query_pos) & (key_pos >= doc_start)


def over_query_blocks(seq_len, rows, body):
    before = seq_len // 2
    if seq_len // rows <= 4:
        for start in range(0, seq_len, rows):
            first = max(0, start - before)
            body(start, first, start + rows - first)
        return
    width = before + rows

    def one(i, carry):
        start = pl.multiple_of(i * rows, rows)
        first = pl.multiple_of(jnp.maximum(start - before, 0), rows)
        body(start, first, width)
        return carry

    lax.fori_loop(0, seq_len // rows, one, 0)


def probabilities(q_rows, k_rows, mask):
    s = jnp.where(mask, dot_nt(q_rows, k_rows), masked_value)
    e = jnp.exp(s - jnp.max(s, axis=1, keepdims=True))
    return e * (1.0 / jnp.sum(e, axis=1, keepdims=True))


def lane_blocks(refs):
    return jnp.concatenate([r[0] for r in refs], axis=1)


def forward_own_kernel(count_parts, piece_len, join, *refs):
    place_ref, parts, refs = refs[0], refs[1 : 1 + count_parts], list(refs[1 + count_parts :])
    (wq, wk, wv, wg), (tq, tk, tv, tg) = refs[:4], refs[4:8]
    wo, to, wf, bias, start_ref = refs[8:13]
    refs = refs[13:]
    a_ref = refs.pop(0) if join else parts[0]
    q_ref, k_ref, v_ref, gate_ref, z_ref, terms_ref, send_ref, qa, qb, ka, kb, decay, acc = refs
    pair = pl.program_id(0)
    seq_len, half = a_ref.shape[0], a_ref.shape[1] // 2
    piece_start = pl.multiple_of(place_ref[0] * piece_len, piece_len)

    @pl.when(pair == 0)
    def _():
        if join:
            assemble(parts, a_ref, place_ref)
        acc[...] = jnp.zeros_like(acc)

        def gates(i):
            here = rows_at(i, chunk_rows)
            z = dot_nn(a_ref[here, :], wf[...]) + bias[...]
            z_ref[here, :] = z
            decay[here, :] = log_sigmoid(z)

        each(seq_len // chunk_rows, gates)
        running_sum(decay, False)

        def split(i):
            here = rows_at(i, chunk_rows)
            lane = lax.broadcasted_iota(jnp.int32, (chunk_rows, pair_lanes), 1)
            high, middle, lowest = (x.astype(f32) for x in three_parts(decay[here, :]))
            later = jnp.where(lane < 16, pltpu.roll(middle, 8, 1), pltpu.roll(lowest, 16, 1))
            terms = jnp.where(lane < 8, high, later)
            terms_ref[here, :] = jnp.where(lane < 24, terms, 0.0).astype(bf16)

        each(seq_len // chunk_rows, split)

    w_mine, w_theirs = lane_blocks((wq, wk, wv, wg)), lane_blocks((tq, tk, tv, tg))

    def project(i):
        here = rows_at(i, chunk_rows)
        out = dot_nn(a_ref[here, :half], w_mine) + dot_nn(a_ref[here, half:], w_theirs)
        q_ref[here, :] = out[:, :128].astype(bf16)
        k_ref[here, :] = out[:, 128:256].astype(bf16)
        v_ref[here, :] = out[:, 256:384].astype(bf16)
        gate_ref[here, :] = out[:, 384:]

    each(seq_len // chunk_rows, project)
    piece = pl.ds(piece_start, piece_len)
    gate = jax.nn.sigmoid(gate_ref[piece, :])
    mix_keys(k_ref, terms_ref, pair, ka, kb)
    mix_queries(q_ref.at[piece, :], terms_ref, piece_start, pair, qa, qb)
    before = seq_len // 2
    for s in range(0, piece_len, query_rows(seq_len)):
        rows = query_rows(seq_len)
        width = before + rows
        start = pl.multiple_of(piece_start + s, rows)
        first = pl.multiple_of(jnp.maximum(start - before, 0), rows)
        mask = live_mask(start_ref, start, first, width, rows)
        keys = pl.ds(first, width)
        out = []
        for q_of, k_of in ((qa, ka), (qb, kb)):
            p = probabilities(q_of[s : s + rows, :], k_of[keys, :], mask).astype(bf16)
            out.append(dot_nn(p, v_ref[keys, :]))
        lane = lax.broadcasted_iota(jnp.int32, (rows, pair_lanes), 1)
        u = (jnp.where(lane < 64, out[0], out[1]) * gate[s : s + rows, :]).astype(bf16)
        acc[s : s + rows, :half] += dot_nn(u, wo[0])
        acc[s : s + rows, half:] += dot_nn(u, to[0])

    @pl.when(pair == pl.num_programs(0) - 1)
    def _():
        send_ref[...] = acc[...].astype(bf16)


def backward_kernel(count_parts, piece_len, join, *refs):
    place_ref, parts, refs = refs[0], refs[1 : 1 + count_parts], list(refs[1 + count_parts :])
    mine, theirs, (wo, to, wf) = refs[:4], refs[4:8], refs[8:11]
    q_ref, k_ref, v_ref, gate_ref, z_ref, terms_ref, start_ref = refs[11:18]
    refs = refs[18:]
    y_ref = refs.pop(0) if join else parts[0]
    dq_ref, dk_ref, dv_ref, dg_ref, u_ref, dz_ref, send_ref = refs[:7]
    qa, qb, ka, kb, dd, dus, dka, dkb, dva, dcs, acc = refs[7:]
    pair = pl.program_id(0)
    seq_len, half = y_ref.shape[0], y_ref.shape[1] // 2
    rows = query_rows(seq_len)
    piece = pl.ds(pl.multiple_of(place_ref[0] * piece_len, piece_len), piece_len)

    @pl.when(pair == 0)
    def _():
        if join:
            assemble(parts, y_ref, place_ref)
        acc[...] = jnp.zeros_like(acc)
        dcs[...] = jnp.zeros_like(dcs)

    def gates(i):
        here = rows_at(i, chunk_rows)
        du = dot_nt(y_ref[here, :half], wo[0]) + dot_nt(y_ref[here, half:], to[0])
        sig = jax.nn.sigmoid(gate_ref[here, :])
        dd[here, :] = (du * sig).astype(bf16)
        dus[here, :] = du * sig * (1.0 - sig)

    each(seq_len // chunk_rows, gates)
    mix_keys(k_ref, terms_ref, pair, ka, kb)
    mix_queries(q_ref, terms_ref, 0, pair, qa, qb)
    dka[...] = jnp.zeros_like(dka)
    dkb[...] = jnp.zeros_like(dkb)
    dva[...] = jnp.zeros_like(dva)
    lane = lax.broadcasted_iota(jnp.int32, (rows, pair_lanes), 1)

    def pick(column_a, column_b):
        at = lax.broadcasted_iota(jnp.int32, (column_a.shape[0], pair_lanes), 1)
        return jnp.where(at == 2 * pair, column_a, jnp.where(at == 2 * pair + 1, column_b, 0.0))

    def body(start, first, width):
        mask = live_mask(start_ref, start, first, width, rows)
        here, keys = pl.ds(start, rows), pl.ds(first, width)
        values = v_ref[keys, :]
        d_rows = dd[here, :]
        dq, o = [], []
        for head, (q_of, k_of, dk_of) in enumerate(((qa, ka, dka), (qb, kb, dkb))):
            own_lanes = (lane < 64) if head == 0 else (lane >= 64)
            p = probabilities(q_of[here, :], k_of[keys, :], mask)
            d_mine = jnp.where(own_lanes, d_rows, jnp.zeros_like(d_rows))
            dp = dot_nt(d_mine, values)
            delta = jnp.sum(p * dp, axis=1, keepdims=True)
            ds = (p * (dp - delta)).astype(bf16)
            dq.append(dot_nn(ds, k_of[keys, :]))
            dk_of[keys, :] += dot_tn(ds, q_of[here, :])
            low = p.astype(bf16)
            dva[keys, :] += dot_tn(low, d_mine)
            o.append(dot_nn(low, values))
        o = jnp.where(lane < 64, o[0], o[1])
        dg_ref[here, :] = (dus[here, :] * o).astype(bf16)
        u_ref[here, :] = (o * jax.nn.sigmoid(gate_ref[here, :])).astype(bf16)
        dq_ref[here, :] = (jnp.where(lane < 64, dq[0], dq[1]) * 0.125).astype(bf16)
        dcs[here, :] += pick(dq[0][:, 67:68], dq[1][:, 3:4])

    over_query_blocks(seq_len, rows, body)

    def finish(i):
        here = rows_at(i, chunk_rows)
        lanes_now = lax.broadcasted_iota(jnp.int32, (chunk_rows, pair_lanes), 1)
        ka_rows, kb_rows = dka[here, :], dkb[here, :]
        dk_ref[here, :] = jnp.where(lanes_now < 64, ka_rows, kb_rows).astype(bf16)
        dv_ref[here, :] = dva[here, :].astype(bf16)
        dcs[here, :] -= pick(ka_rows[:, 64:65], kb_rows[:, 0:1])

    each(seq_len // chunk_rows, finish)
    d_own = jnp.concatenate([r[piece, :] for r in (dq_ref, dk_ref, dv_ref, dg_ref)], axis=1)
    acc[:, :half] += dot_nt(d_own, lane_blocks(mine))
    acc[:, half:] += dot_nt(d_own, lane_blocks(theirs))

    @pl.when(pair == pl.num_programs(0) - 1)
    def _():
        running_sum(dcs, True)

        def last(i):
            here = rows_at(i, chunk_rows)
            dz_ref[here, :] = (dcs[here, :] * jax.nn.sigmoid(-z_ref[here, :])).astype(bf16)

        each(seq_len // chunk_rows, last)
        send_ref[...] = (acc[...] + dot_nt(dz_ref[piece, :], wf[...])).astype(bf16)


def ffn_forward_kernel(b_ref, wg, wu, wd, tg, tu, td, gt_ref, up_ref, send_ref, acc):
    half = b_ref.shape[1] // 2
    low, high = b_ref[:, :half], b_ref[:, half:]
    gt = dot_nn(low, wg[0]) + dot_nn(high, tg[0])
    up = dot_nn(low, wu[0]) + dot_nn(high, tu[0])
    gt_ref[...] = gt
    up_ref[...] = up
    m = (gt * jax.nn.sigmoid(gt) * up).astype(bf16)

    @pl.when(pl.program_id(0) == 0)
    def _():
        acc[...] = jnp.zeros_like(acc)

    acc[:, :half] += dot_nn(m, wd[0])
    acc[:, half:] += dot_nn(m, td[0])

    @pl.when(pl.program_id(0) == pl.num_programs(0) - 1)
    def _():
        send_ref[...] = acc[...].astype(bf16)


def inner_grads(dm, gt, up):
    sig = jax.nn.sigmoid(gt)
    d_gate = (dm * up * sig * (1.0 + gt * (1.0 - sig))).astype(bf16)
    return d_gate, (dm * (gt * sig)).astype(bf16)


def ffn_backward_kernel(g_ref, gt_ref, up_ref, wg, wu, wd, tg, tu, td, *refs):
    send_ref, acc = refs[-2:]
    half = g_ref.shape[1] // 2
    dm = dot_nt(g_ref[:, :half], wd[0]) + dot_nt(g_ref[:, half:], td[0])
    d_gate, d_up = inner_grads(dm, gt_ref[...], up_ref[...])

    @pl.when(pl.program_id(0) == 0)
    def _():
        acc[...] = jnp.zeros_like(acc)

    acc[:, :half] += dot_nt(d_gate, wg[0]) + dot_nt(d_up, wu[0])
    acc[:, half:] += dot_nt(d_gate, tg[0]) + dot_nt(d_up, tu[0])

    @pl.when(pl.program_id(0) == pl.num_programs(0) - 1)
    def _():
        send_ref[...] = acc[...].astype(bf16)


def ffn_theirs_kernel(b_ref, g_ref, wg, wu, wd, tg, tu, td, *refs):
    m_ref, dgate_ref, dup_ref, gate_out, up_out, down_out, turned = refs[-7:]
    half = b_ref.shape[1] // 2

    @pl.when(pl.program_id(0) == 0)
    def _():
        turned[...] = b_ref[:, half:].T

    def chunk(i):
        here = rows_at(i, chunk_rows)
        low, high = b_ref[here, :half], b_ref[here, half:]
        gt = dot_nn(low, wg[0]) + dot_nn(high, tg[0])
        up = dot_nn(low, wu[0]) + dot_nn(high, tu[0])
        dm = dot_nt(g_ref[here, :half], wd[0]) + dot_nt(g_ref[here, half:], td[0])
        m_ref[here, :] = (gt * jax.nn.sigmoid(gt) * up).astype(bf16)
        dgate_ref[here, :], dup_ref[here, :] = inner_grads(dm, gt, up)

    each(b_ref.shape[0] // chunk_rows, chunk)
    gate_out[...] = dot_nn(turned[...], dgate_ref[...]).astype(bf16)
    up_out[...] = dot_nn(turned[...], dup_ref[...]).astype(bf16)
    down_out[...] = dot_tn(m_ref[...], g_ref[:, half:]).astype(bf16)


def ffn_mine_kernel(b_ref, g_ref, m_ref, dgate_ref, dup_ref, gate_in, up_in, down_in, *refs):
    gate_out, up_out, down_out, turned = refs[-4:]

    @pl.when(pl.program_id(0) == 0)
    def _():
        turned[...] = b_ref[...].T

    gate_out[0] = dot_nn(turned[...], dgate_ref[...]) + gate_in[...].astype(f32)
    up_out[0] = dot_nn(turned[...], dup_ref[...]) + up_in[...].astype(f32)
    down_out[0] = dot_tn(m_ref[...], g_ref[...]) + down_in[...].astype(f32)


def attention_grads_kernel(steps, mine, *refs):
    a_ref, dq, dk, dv, dg, dz, u_ref, y_ref = refs[:8]
    received = refs[8:14] if mine else [None] * 6
    acc, acc_out = refs[-2:]
    outs = refs[-8:-2]
    turned = a_ref[...].T
    width = dq.shape[1]
    parts = [dot_nn(turned, d[...]) for d in (dq, dk, dv, dg, dz)]
    out = dot_tn(u_ref[...], y_ref[...])

    def give(values):
        for ref, value, more in zip(outs, values, received):
            total = value if more is None else value + more[...].astype(f32)
            if len(ref.shape) == 3:
                ref[0] = total.astype(ref.dtype)
            else:
                ref[...] = total.astype(ref.dtype)

    if steps == 1:
        give([*parts, out])
        return
    step = pl.program_id(0)

    @pl.when(step == 0)
    def _():
        acc[...] = jnp.zeros_like(acc)
        acc_out[...] = jnp.zeros_like(acc_out)

    for k, part in enumerate(parts):
        acc[:, k * width : k * width + part.shape[1]] += part
    acc_out[...] += out

    @pl.when(step == steps - 1)
    def _():
        found = [acc[:, k * width : k * width + p.shape[1]] for k, p in enumerate(parts)]
        give([*found, acc_out[...]])


def fixed(shape, single=True):
    zeros = (0,) * len(shape)
    if single:
        return pl.BlockSpec(shape, lambda *_: zeros, pipeline_mode=pl.Buffered(1))
    return pl.BlockSpec(shape, lambda *_: zeros)


def lanes(seq_len):
    return pl.BlockSpec((seq_len, pair_lanes), lambda p, *_: (0, p))


def lanes_read(seq_len):
    if seq_len <= 2048:
        return lanes(seq_len)
    return pl.BlockSpec((seq_len, pair_lanes), lambda p, *_: (0, p), pipeline_mode=pl.Buffered(1))


def columns_of(w, layer, width):
    return pl.BlockSpec((1, w.shape[1], width), lambda p, *_: (layer, 0, p))


def rows_of(w, layer, height):
    return pl.BlockSpec((1, height, w.shape[2]), lambda p, *_: (layer, p, 0))


def shape(dims, dtype):
    return jax.ShapeDtypeStruct(dims, dtype)


def attention_specs(parts, layer, w4, t4, wo, to, seq_len, join):
    specs = [fixed(p.shape) for p in parts]
    specs += [columns_of(w, layer, pair_lanes) for w in (*w4, *t4)]
    specs += [rows_of(wo, layer, pair_lanes), rows_of(to, layer, pair_lanes)]
    return specs


def cost(microseconds):
    return pl.CostEstimate(flops=int(microseconds * 1.1e9), bytes_accessed=0, transcendentals=0)


def token_specs(tokens):
    return [pl.BlockSpec(memory_space=pl.ANY) for _ in tokens]


def forward_own(place, parts, layer, w4, t4, wo, to, wf, bias, doc_start, piece_len):
    seq_len, width = doc_start.shape[0], parts[0].shape[1]
    local_width = wo.shape[1]
    join = len(parts) > 1
    terms = (seq_len, pair_lanes)
    outs = [shape((seq_len, local_width), bf16)] * 3 + [shape((seq_len, local_width), f32)]
    outs += [shape(terms, f32), shape(terms, bf16), shape((piece_len, width), bf16)]
    specs = [lanes(seq_len)] * 4 + [fixed(terms, False)] * 2 + [fixed((piece_len, width), False)]
    if join:
        outs, specs = [shape((seq_len, width), bf16)] + outs, [fixed((seq_len, width))] + specs
    low, piece = pltpu.VMEM((seq_len, pair_lanes), bf16), pltpu.VMEM((piece_len, pair_lanes), bf16)
    got = pl.pallas_call(
        functools.partial(forward_own_kernel, len(parts), piece_len, join),
        grid_spec=pltpu.PrefetchScalarGridSpec(
            num_scalar_prefetch=1,
            grid=(local_width // pair_lanes,),
            in_specs=attention_specs(parts, layer, w4, t4, wo, to, seq_len, join)
            + [fixed(wf.shape), fixed(bias.shape), fixed(doc_start.shape)],
            out_specs=specs,
            scratch_shapes=[piece] * 2 + [low] * 2 + [pltpu.VMEM(terms, f32), pltpu.VMEM((piece_len, width), f32)],
        ),
        out_shape=outs,
        cost_estimate=cost(19),
        compiler_params=pltpu.CompilerParams(vmem_limit_bytes=60 << 20),
    )(place, *parts, *w4, *t4, wo, to, wf, bias, doc_start)
    got = list(got)
    a = got.pop(0) if join else parts[0]
    return a, got[:6], got[6]


def attention_backward(place, parts, layer, w4, t4, wo, to, wf, saved, doc_start, piece_len):
    q, k, v, gate, z, terms = saved
    seq_len, width = doc_start.shape[0], parts[0].shape[1]
    local_width = wo.shape[1]
    join = len(parts) > 1
    outs = [shape((seq_len, local_width), bf16)] * 5 + [shape((seq_len, pair_lanes), bf16)]
    outs += [shape((piece_len, width), bf16)]
    specs = [lanes(seq_len)] * 5 + [fixed((seq_len, pair_lanes), False), fixed((piece_len, width), False)]
    if join:
        outs, specs = [shape((seq_len, width), bf16)] + outs, [fixed((seq_len, width))] + specs
    low, high = pltpu.VMEM((seq_len, pair_lanes), bf16), pltpu.VMEM((seq_len, pair_lanes), f32)
    got = pl.pallas_call(
        functools.partial(backward_kernel, len(parts), piece_len, join),
        grid_spec=pltpu.PrefetchScalarGridSpec(
            num_scalar_prefetch=1,
            grid=(local_width // pair_lanes,),
            in_specs=attention_specs(parts, layer, w4, t4, wo, to, seq_len, join)
            + [fixed(wf.shape)]
            + [lanes_read(seq_len)] * 4
            + [fixed(z.shape), fixed(terms.shape), fixed(doc_start.shape)],
            out_specs=specs,
            scratch_shapes=[low] * 5 + [high] * 5 + [pltpu.VMEM((piece_len, width), f32)],
        ),
        out_shape=outs,
        cost_estimate=cost(33),
        compiler_params=pltpu.CompilerParams(vmem_limit_bytes=60 << 20),
    )(place, *parts, *w4, *t4, wo, to, wf, q, k, v, gate, z, terms, doc_start)
    got = list(got)
    y = got.pop(0) if join else parts[0]
    return y, got[:6], got[6]


def ffn_weights(layer, w3, t3):
    specs = []
    for wg, wu, wd in (w3, t3):
        specs += [
            columns_of(wg, layer, hidden_block), columns_of(wu, layer, hidden_block), rows_of(wd, layer, hidden_block),
        ]
    return specs


def blocks_of(rows):
    return pl.BlockSpec((rows, hidden_block), lambda p, *_: (0, p))


def ffn_forward(b, layer, w3, t3):
    rows, width = b.shape
    inner = w3[2].shape[1]
    return pl.pallas_call(
        ffn_forward_kernel,
        grid=(inner // hidden_block,),
        in_specs=[fixed(b.shape)] + ffn_weights(layer, w3, t3),
        out_specs=[blocks_of(rows)] * 2 + [fixed((rows, width), False)],
        scratch_shapes=[pltpu.VMEM((rows, width), f32)],
        out_shape=[shape((rows, inner), f32)] * 2 + [shape((rows, width), bf16)],
        cost_estimate=cost(7),
        compiler_params=pltpu.CompilerParams(vmem_limit_bytes=60 << 20),
    )(b, *w3, *t3)


def ffn_backward(g, gt, up, layer, w3, t3, *tokens):
    rows, width = g.shape
    return pl.pallas_call(
        ffn_backward_kernel,
        grid=(gt.shape[1] // hidden_block,),
        in_specs=[fixed(g.shape)] + [blocks_of(rows)] * 2 + ffn_weights(layer, w3, t3) + token_specs(tokens),
        out_specs=fixed((rows, width), False),
        scratch_shapes=[pltpu.VMEM((rows, width), f32)],
        out_shape=shape((rows, width), bf16),
        cost_estimate=cost(8),
        compiler_params=pltpu.CompilerParams(vmem_limit_bytes=60 << 20),
    )(g, gt, up, *w3, *t3, *tokens)


def ffn_theirs(b, g, layer, w3, t3, *tokens):
    rows, width = b.shape
    half = width // 2
    inner = w3[2].shape[1]
    wide = pl.BlockSpec((half, hidden_block), lambda p: (0, p))
    return pl.pallas_call(
        ffn_theirs_kernel,
        grid=(inner // hidden_block,),
        in_specs=[fixed(b.shape), fixed(g.shape)] + ffn_weights(layer, w3, t3) + token_specs(tokens),
        out_specs=[blocks_of(rows)] * 3 + [wide, wide, pl.BlockSpec((hidden_block, half), lambda p: (p, 0))],
        scratch_shapes=[pltpu.VMEM((half, rows), bf16)],
        out_shape=[shape((rows, inner), bf16)] * 3
        + [shape((half, inner), bf16)] * 2
        + [shape((inner, half), bf16)],
        cost_estimate=cost(24),
        compiler_params=pltpu.CompilerParams(vmem_limit_bytes=60 << 20),
    )(b, g, *w3, *t3, *tokens)


def anywhere():
    return pl.BlockSpec(memory_space=pl.ANY)


def ffn_mine(layer, b, g, values, received, totals, *tokens):
    rows, width = b.shape
    half, inner = width // 2, values[0].shape[1]
    wide = pl.BlockSpec((half, hidden_block), lambda p: (0, p))
    tall = pl.BlockSpec((hidden_block, half), lambda p: (p, 0))
    wide_out = pl.BlockSpec((1, half, hidden_block), lambda p: (layer, 0, p))
    tall_out = pl.BlockSpec((1, hidden_block, half), lambda p: (layer, p, 0))
    return pl.pallas_call(
        ffn_mine_kernel,
        grid=(inner // hidden_block,),
        in_specs=[fixed((rows, half))] * 2
        + [blocks_of(rows)] * 3
        + [wide, wide, tall]
        + [anywhere()] * 3
        + token_specs(tokens),
        out_specs=[wide_out, wide_out, tall_out],
        out_shape=[shape(x.shape, x.dtype) for x in totals],
        scratch_shapes=[pltpu.VMEM((half, rows), bf16)],
        input_output_aliases={8: 0, 9: 1, 10: 2},
        cost_estimate=cost(9),
        compiler_params=pltpu.CompilerParams(vmem_limit_bytes=60 << 20),
    )(b, g, *values, *received, *totals, *tokens)


def attention_grads(layer, a, ds, dz, u, y, received=None, totals=None, tokens=()):
    rows, width = a.shape
    half, local_width = width // 2, u.shape[1]
    part = min(rows, 1024)
    steps = rows // part
    mine = received is not None
    side = 0 if mine else 1
    features = pl.BlockSpec((part, half), lambda p: (p, side))
    across = [pl.BlockSpec((part, x.shape[1]), lambda p: (p, 0)) for x in (*ds, dz, u)]
    specs = [features, *across, features]
    operands = [a, *ds, dz, u, y]
    flat = [(half, local_width)] * 4 + [(half, pair_lanes), (local_width, half)]
    if mine:
        specs += [fixed(x) for x in flat] + [anywhere()] * 5
        operands += [*received, *totals]
        outs = [shape(x.shape, f32) for x in totals[:4]] + [shape(flat[4], f32), shape(totals[4].shape, f32)]
        layered = pl.BlockSpec((1, half, local_width), lambda p: (layer, 0, 0))
        out_specs = [layered] * 4 + [fixed(flat[4], False)]
        out_specs += [pl.BlockSpec((1, local_width, half), lambda p: (layer, 0, 0))]
        aliases = {14: 0, 15: 1, 16: 2, 17: 3, 18: 5}
    else:
        outs, out_specs, aliases = [shape(x, bf16) for x in flat], [fixed(x, False) for x in flat], {}
    sizes = [(half, 4 * local_width + pair_lanes), (local_width, half)] if steps > 1 else [(8, 128)] * 2
    return pl.pallas_call(
        functools.partial(attention_grads_kernel, steps, mine),
        grid=(steps,),
        in_specs=specs + token_specs(tokens),
        out_specs=out_specs,
        out_shape=outs,
        scratch_shapes=[pltpu.VMEM(x, f32) for x in sizes],
        input_output_aliases=aliases,
        cost_estimate=cost(7),
        compiler_params=pltpu.CompilerParams(vmem_limit_bytes=60 << 20),
    )(*operands, *tokens)


def unset(*like):
    return pl.pallas_call(
        pass_kernel,
        out_specs=[pl.BlockSpec(memory_space=pl.ANY) for _ in like],
        out_shape=list(like),
    )()


def inverse_rms(h):
    return lax.rsqrt(jnp.mean(h * h, axis=-1, keepdims=True) + epsilon)


def norm_back(grad_normed, hidden, inverse, gain):
    scaled = hidden * inverse
    weighted = grad_normed * gain
    grad_gain = jnp.sum(grad_normed * scaled, axis=0)
    mean = jnp.mean(weighted * scaled, axis=-1, keepdims=True)
    return inverse * (weighted - scaled * mean), grad_gain


def local(
    hidden_in, segment_ids, w_query, w_key, w_value, w_gate_out, w_attn_out, w_forget, b_forget,
    gain_attn, gain_ffn, w_gate, w_up, w_down, cotangent,
):
    seq_count, piece_len, width = hidden_in.shape
    count_z, count_t = lax.axis_size("context"), lax.axis_size("tensor")
    core, z, t = lax.axis_index("fsdp"), lax.axis_index("context"), lax.axis_index("tensor")
    layers, half, local_width = w_query.shape
    heads = w_forget.shape[2]
    block = piece_len // count_t
    seq_len = piece_len * count_z
    shared_rows = count_z == 4
    place = jnp.stack([z, t]).astype(jnp.int32)

    def features(x):
        return jnp.where(core == 0, x, jnp.concatenate([x[..., half:], x[..., :half]], axis=-1))

    def own_block(x):
        return lax.dynamic_slice_in_dim(x, t * block, block, 0)

    def other(w):
        return swap(w, "fsdp", 1)

    def full(w, axis):
        return jnp.concatenate([w, other(w)], axis=axis)

    seg_all = gathered(segment_ids.reshape(1, piece_len), "context").reshape(seq_len)
    doc_start = jnp.sum((seg_all[None, :] < seg_all[:, None]).astype(jnp.int32), axis=1, keepdims=True)

    gains = full(jnp.concatenate([gain_attn, gain_ffn], axis=0), 1).astype(f32)
    hidden_rows = features(hidden_in.reshape(piece_len, width)).astype(f32)
    first_a = (hidden_rows * inverse_rms(hidden_rows) * gains[0]).astype(bf16)
    a_parts, _ = all_rows(own_block(first_a), first_a, seg_all)

    w_forget_full = jnp.pad(full(w_forget, 1), ((0, 0), (0, 0), (0, pair_lanes - heads)))
    bias = jnp.pad(b_forget, ((0, 0), (0, pair_lanes - heads)))
    w4 = (w_query, w_key, w_value, w_gate_out)
    t4 = tuple(other(w) for w in w4)
    to = other(w_attn_out)
    w3 = (w_gate, w_up, w_down)
    t3 = tuple(other(w) for w in w3)

    hidden = own_block(hidden_rows)
    saved = []
    cotangent_rows = features(cotangent.reshape(piece_len, width))
    last = layers - 1
    grad = own_block(cotangent_rows).astype(f32)
    for layer in range(layers):
        gain_one, gain_two = gains[layer], gains[layers + layer]
        inverse_one = inverse_rms(hidden)
        if layer > 0:
            a_parts, _ = all_rows((hidden * inverse_one * gain_one).astype(bf16))
        forget_weights = w_forget_full[layer]
        if shared_rows and layer > 0:
            b_sent = after(saved[-1]["b_shard"], a_parts[-1])
            saved[-1]["b_rows"] = sequence_rows(b_sent)
            forget_weights = after(forget_weights, *([g_last] if layer == 1 else []), b_sent)
        a, (q, k, v, gate, forget, terms), sends = forward_own(
            place, a_parts, layer, w4, t4, w_attn_out, to, forget_weights,
            bias[layer : layer + 1], doc_start, piece_len,
        )
        if shared_rows and layer == 0:
            g_last = sequence_rows(after(own_block(cotangent_rows), a_parts[-1]))
        mixed = hidden + received_sum(sends)
        inverse_two = inverse_rms(mixed)
        b_shard = (mixed * inverse_two * gain_two).astype(bf16)
        b = gathered(b_shard, "tensor")
        gt, up, sends = ffn_forward(b, layer, w3, t3)
        saved.append(
            dict(hidden=hidden, inverse_one=inverse_one, a=a, kept=(q, k, v, gate, forget, terms), mixed=mixed,
                 inverse_two=inverse_two, b=b, b_shard=b_shard, gt=gt, up=up)
        )
        if layer < last:
            hidden = mixed + received_sum(sends)

    def finish(x):
        return features(gathered(x.astype(bf16), "tensor")).reshape(1, piece_len, width)

    last_sends = sends
    wide = shape((layers, half, local_width), f32)
    inner = shape((layers, half, w_gate.shape[2]), f32)
    results = list(
        unset(
            wide, wide, wide, wide, shape((layers, local_width, half), f32),
            inner, inner, shape((layers, w_down.shape[1], half), f32),
        )
    )
    small = [[None] * layers for _ in range(2)]
    gain_grads = [None] * (2 * layers)

    def ffn_theirs_of(layer, *tokens):
        s = saved[layer]
        values = ffn_theirs(s["b_rows"], s["g_rows"], layer, w3, t3, *tokens)
        s.update(values=values[:3], ffn_received=[other(x) for x in values[3:]])

    def ffn_mine_of(layer, *tokens):
        s = saved[layer]
        received = s["ffn_received"]
        results[5:] = ffn_mine(layer, s["b_rows"], s["g_rows"], s["values"], received, results[5:], *tokens)

    def attention_theirs_of(layer, *tokens):
        s = saved[layer]
        s["theirs"] = attention_grads(layer, *s["grads"], tokens=tokens)
        s["received"] = [other(x) for x in s["theirs"]]
        bias_grad = jnp.sum(s["grads"][2].astype(f32), axis=0)[:heads]
        small[1][layer] = bias_grad + other(bias_grad)

    def attention_mine_of(layer, *tokens):
        s = saved[layer]
        found = attention_grads(layer, *s["grads"], s["received"], results[:5], tokens)
        results[:5] = [*found[:4], found[5]]
        small[0][layer] = found[4][:, :heads]

    for layer in reversed(range(layers)):
        s = saved[layer]
        gain_one, gain_two = gains[layer], gains[layers + layer]
        tokens = ()
        if layer == last:
            g = cotangent_rows
        else:
            g_shard = grad.astype(bf16)
            g = gathered(g_shard, "tensor")
            tokens = (saved[layer + 1]["theirs"][0],)
            if shared_rows:
                s["g_rows"] = sequence_rows(g_shard)
        if not shared_rows:
            s.update(b_rows=s["b"], g_rows=g)
        sends = ffn_backward(g, s["gt"], s["up"], layer, w3, t3, *tokens)
        if layer < last:
            sends = after(sends, *saved[layer + 1]["received"])
        back, gain_grads[layers + layer] = norm_back(received_sum(sends), s["mixed"], s["inverse_two"], gain_two)
        grad_mixed = grad + back
        y_shard = grad_mixed.astype(bf16)
        if layer < last:
            attention_mine_of(layer + 1)
            y_shard = after(y_shard, results[0])
        elif shared_rows:
            y_shard = after(y_shard, *[x["b_rows"] for x in saved[:-1]])
        y_parts, y_far = all_rows(y_shard, together=layer < last)
        tokens = ()
        if layer < last:
            above = saved[layer + 1]
            ffn_theirs_of(layer + 1, *y_far, y_parts[0])
            tokens = (above["values"][0], *([s["g_rows"]] if shared_rows else []))
        kept = (*s["kept"][:-1], after(s["kept"][-1], *tokens))
        y, (dq, dk, dv, dg, u, dz), sends = attention_backward(
            place, y_parts, layer, w4, t4, w_attn_out, to, w_forget_full[layer], kept, doc_start, piece_len,
        )
        token = y_parts[-1]
        if layer == last:
            block_sum = own_block(last_sends).astype(f32) + s["mixed"]
            with_rows = lax.dynamic_update_slice_in_dim(last_sends, block_sum.astype(bf16), t * block, 0)
            output = lax.psum(after(with_rows, token), "tensor")
        if shared_rows and layer == last:
            s.update(b_rows=sequence_rows(after(s["b_shard"], token)), g_rows=g_last)
        s["grads"] = (s["a"], (dq, dk, dv, dg), dz, u, y)
        if layer > 0:
            attention_theirs_of(layer)
        back, gain_grads[layer] = norm_back(received_sum(sends), s["hidden"], s["inverse_one"], gain_one)
        grad = grad_mixed + back

    ffn_theirs_of(0)
    for layer in reversed(range(1, layers)):
        ffn_mine_of(layer, grad)
    attention_theirs_of(0, grad)
    gain_total = jnp.stack(gain_grads).reshape(1, -1)
    for axis in (("context", "tensor"),) if shared_rows else ("context", "tensor"):
        gain_total = jnp.sum(gathered(gain_total, axis), axis=0, keepdims=True)
    gain_total = gain_total.reshape(2 * layers, width)
    gain_total = gain_total[:, :half] + other(gain_total[:, half:])
    attention_mine_of(0, gain_total, *saved[0]["ffn_received"])
    ffn_mine_of(0)
    if not shared_rows:
        results[5:] = [lax.psum(x, "context") for x in results[5:]]
    output = features(after(output, saved[0]["values"][0])).reshape(1, piece_len, width)
    grad_input = finish(grad)
    return (
        output, grad_input, *results[:5], jnp.stack(small[0]), jnp.stack(small[1]),
        gain_total[:layers], gain_total[layers:], *results[5:],
    )


def solution(mesh):
    rows = P("fsdp", "context", None)
    wide, tall = P(None, "fsdp", "tensor"), P(None, "tensor", "fsdp")
    heads, gain = P(None, "tensor"), P(None, "fsdp")
    return jax.shard_map(
        local,
        mesh=mesh,
        in_specs=(
            rows, P("fsdp", "context"), wide, wide, wide, wide, tall, wide, heads, gain, gain, wide, wide, tall, rows,
        ),
        out_specs=(rows, rows, wide, wide, wide, wide, tall, wide, heads, gain, gain, wide, wide, tall),
        check_vma=False,
    )
```

```python
import functools

import jax
import jax.numpy as jnp
from jax import lax
from jax.experimental import pallas as pl
from jax.experimental.pallas import tpu as pltpu
from jax.sharding import PartitionSpec as P

epsilon = 1e-06
masked_value = -1e30
bf16 = jnp.bfloat16
f32 = jnp.float32
pair_lanes = 128
hidden_block = 256
chunk_rows = 256


def query_rows(seq_len):
    return 256 if seq_len <= 2048 else 128


def swap(x, axis, k):
    n = lax.axis_size(axis)
    return lax.ppermute(x, axis, [(i, i ^ k) for i in range(n)])


def pass_kernel(*refs):
    pass


def after(x, *tokens):
    if not tokens:
        return x
    anywhere = pl.BlockSpec(memory_space=pl.ANY)
    return pl.pallas_call(
        pass_kernel,
        in_specs=[anywhere] * (1 + len(tokens)),
        out_specs=anywhere,
        out_shape=jax.ShapeDtypeStruct(x.shape, x.dtype),
        input_output_aliases={0: 0},
    )(x, *tokens)


def gathered(block, axis):
    count = lax.axis_size(axis)
    copies = jnp.broadcast_to(block[None], (count,) + block.shape)
    return lax.all_to_all(copies, axis, 0, 0, tiled=True).reshape((-1,) + block.shape[1:])


def sequence_rows(shard):
    return lax.all_gather(shard, ("context", "tensor"), tiled=True)


def near_rows(own):
    return swap(own, "context", 1)


def far_blocks(shard):
    return swap(shard, "context", 2), swap(shard, "context", 3)


def all_rows(shard, own=None, token=None, together=False):
    if own is None:
        own = gathered(shard, "tensor")
    if lax.axis_size("context") != 4:
        return (lax.all_gather(own, "context", tiled=True),), ()
    second, third = far_blocks(shard)
    near = near_rows(own)
    if together:
        block, width = shard.shape
        far = gathered(after(jnp.concatenate([second, third], axis=0), own), "tensor")
        return (own, near, far.reshape(-1, 2, block, width)), (second, third)
    if token is not None:
        second = after(second, token)
    parts = [own, near]
    for far in (second, third):
        parts += [far] + [swap(far, "tensor", k) for k in range(1, lax.axis_size("tensor"))]
    return tuple(parts), (second, third)


def received_sum(sends):
    count = lax.axis_size("tensor")
    got = lax.all_to_all(sends.reshape(count, -1, sends.shape[1]), "tensor", 0, 0, tiled=True)
    return jnp.sum(got.astype(f32), axis=0)


def dot_nt(a, b):
    return lax.dot_general(a, b, (((1,), (1,)), ((), ())), preferred_element_type=f32)


def dot_tn(a, b):
    return lax.dot_general(a, b, (((0,), (0,)), ((), ())), preferred_element_type=f32)


def dot_nn(a, b):
    return jnp.dot(a, b, preferred_element_type=f32)


def each(count, body):
    if count <= 4:
        for i in range(count):
            body(i)
        return

    def one(i, carry):
        body(i)
        return carry

    lax.fori_loop(0, count, one, 0)


def rows_at(i, rows):
    start = i * rows
    return pl.ds(start if isinstance(start, int) else pl.multiple_of(start, rows), rows)


def assemble(parts, whole_ref, place_ref):
    z, t = place_ref[0], place_ref[1]
    piece, blocks_seen, piece_len = 0, 0, parts[0].shape[0]
    for part in parts:
        if len(part.shape) == 4:
            blocks, pieces, block = part.shape[:3]
            for p in range(pieces):
                for b in range(blocks):
                    at = pl.multiple_of((z ^ (piece + p)) * piece_len + b * block, block)
                    whole_ref[pl.ds(at, block), :] = part[b, p]
            piece += pieces
            continue
        rows = part.shape[0]
        if rows == piece_len:
            at = pl.multiple_of((z ^ piece) * piece_len, piece_len)
            piece += 1
        else:
            at = pl.multiple_of((z ^ piece) * piece_len + (t ^ blocks_seen) * rows, rows)
            blocks_seen += 1
            if blocks_seen * rows == piece_len:
                piece, blocks_seen = piece + 1, 0
        whole_ref[pl.ds(at, rows), :] = part[...]


def triangle(rows, reverse):
    row = lax.broadcasted_iota(jnp.int32, (rows, rows), 0)
    column = lax.broadcasted_iota(jnp.int32, (rows, rows), 1)
    return jnp.where((column >= row) if reverse else (column <= row), 1.0, 0.0).astype(bf16)


def running_sum(ref, reverse):
    rows = chunk_rows
    ones = triangle(rows, reverse)
    count = ref.shape[0] // rows
    edge = 0 if reverse else rows - 1

    def chunk(i, carry):
        here = pl.ds(pl.multiple_of((count - 1 - i if reverse else i) * rows, rows), rows)
        high, middle, lowest = three_parts(ref[here, :])
        total = dot_nn(ones, high) + dot_nn(ones, middle) + dot_nn(ones, lowest) + carry
        ref[here, :] = total
        return total[edge : edge + 1, :]

    lax.fori_loop(0, count, chunk, jnp.zeros((1, ref.shape[1]), f32), unroll=count <= 4)


def log_sigmoid(z):
    e = jnp.exp(-jnp.abs(z))
    small = e * (1.0 - e * (1 / 2 - e * (1 / 3 - e * (1 / 4 - e * (1 / 5 - e * (1 / 6 - e * (1 / 7)))))))
    return jnp.minimum(z, 0.0) - jnp.where(e < 0.0625, small, jnp.log(1.0 + e))


def three_parts(x):
    high = x.astype(bf16)
    middle = (x - high.astype(f32)).astype(bf16)
    return high, middle, (x - high.astype(f32) - middle.astype(f32)).astype(bf16)


def decay_side(terms, pair, key_side):
    row = lax.broadcasted_iota(jnp.int32, (pair_lanes, pair_lanes), 0)
    lane = lax.broadcasted_iota(jnp.int32, (pair_lanes, pair_lanes), 1)
    spot = lane & 63
    term = spot if key_side else spot - 3
    head = jnp.where(lane >= 64, 2 * pair, 2 * pair + 1)
    chosen = (term >= 0) & (term < 3) & (row == 8 * term + head)
    pick = jnp.where(chosen, -1.0 if key_side else 1.0, 0.0).astype(bf16)
    lanes_now = lax.broadcasted_iota(jnp.int32, (1, pair_lanes), 1) & 63
    other = lanes_now - 3 if key_side else lanes_now
    ones = jnp.where((other >= 0) & (other < 3), 1.0, 0.0)
    return (dot_nn(terms, pick) + ones).astype(bf16)


def mix_keys(k_ref, terms_ref, pair, ka, kb):
    def mix(i):
        here = rows_at(i, chunk_rows)
        lane = lax.broadcasted_iota(jnp.int32, (chunk_rows, pair_lanes), 1)
        k, side = k_ref[here, :], decay_side(terms_ref[here, :], pair, True)
        ka[here, :] = jnp.where(lane < 64, k, side)
        kb[here, :] = jnp.where(lane < 64, side, k)

    each(k_ref.shape[0] // chunk_rows, mix)


def mix_queries(q_ref, terms_ref, start, pair, qa, qb):
    def mix(i):
        here = rows_at(i, chunk_rows)
        lane = lax.broadcasted_iota(jnp.int32, (chunk_rows, pair_lanes), 1)
        q = (q_ref[here, :].astype(f32) * 0.125).astype(bf16)
        terms = terms_ref[pl.ds(pl.multiple_of(start + i * chunk_rows, chunk_rows), chunk_rows), :]
        side = decay_side(terms, pair, False)
        qa[here, :] = jnp.where(lane < 64, q, side)
        qb[here, :] = jnp.where(lane < 64, side, q)

    each(q_ref.shape[0] // chunk_rows, mix)


def live_mask(start_ref, start, first, width, rows):
    key_pos = first + lax.broadcasted_iota(jnp.int32, (rows, width), 1)
    query_pos = start + lax.broadcasted_iota(jnp.int32, (rows, width), 0)
    doc_start = start_ref[pl.ds(start, rows), :]
    return (key_pos <= query_pos) & (key_pos >= doc_start)


def over_query_blocks(seq_len, rows, body):
    before = seq_len // 2
    if seq_len // rows <= 4:
        for start in range(0, seq_len, rows):
            first = max(0, start - before)
            body(start, first, start + rows - first)
        return
    width = before + rows

    def one(i, carry):
        start = pl.multiple_of(i * rows, rows)
        first = pl.multiple_of(jnp.maximum(start - before, 0), rows)
        body(start, first, width)
        return carry

    lax.fori_loop(0, seq_len // rows, one, 0)


def probabilities(q_rows, k_rows, mask):
    s = jnp.where(mask, dot_nt(q_rows, k_rows), masked_value)
    e = jnp.exp(s - jnp.max(s, axis=1, keepdims=True))
    return e * (1.0 / jnp.sum(e, axis=1, keepdims=True))


def lane_blocks(refs):
    return jnp.concatenate([r[0] for r in refs], axis=1)


def forward_own_kernel(count_parts, piece_len, join, *refs):
    place_ref, parts, refs = refs[0], refs[1 : 1 + count_parts], list(refs[1 + count_parts :])
    (wq, wk, wv, wg), (tq, tk, tv, tg) = refs[:4], refs[4:8]
    wo, to, wf, bias, start_ref = refs[8:13]
    refs = refs[13:]
    a_ref = refs.pop(0) if join else parts[0]
    q_ref, k_ref, v_ref, gate_ref, z_ref, terms_ref, send_ref, qa, qb, ka, kb, decay, acc = refs
    pair = pl.program_id(0)
    seq_len, half = a_ref.shape[0], a_ref.shape[1] // 2
    piece_start = pl.multiple_of(place_ref[0] * piece_len, piece_len)

    @pl.when(pair == 0)
    def _():
        if join:
            assemble(parts, a_ref, place_ref)
        acc[...] = jnp.zeros_like(acc)

        def gates(i):
            here = rows_at(i, chunk_rows)
            z = dot_nn(a_ref[here, :], wf[...]) + bias[...]
            z_ref[here, :] = z
            decay[here, :] = log_sigmoid(z)

        each(seq_len // chunk_rows, gates)
        running_sum(decay, False)

        def split(i):
            here = rows_at(i, chunk_rows)
            lane = lax.broadcasted_iota(jnp.int32, (chunk_rows, pair_lanes), 1)
            high, middle, lowest = (x.astype(f32) for x in three_parts(decay[here, :]))
            later = jnp.where(lane < 16, pltpu.roll(middle, 8, 1), pltpu.roll(lowest, 16, 1))
            terms = jnp.where(lane < 8, high, later)
            terms_ref[here, :] = jnp.where(lane < 24, terms, 0.0).astype(bf16)

        each(seq_len // chunk_rows, split)

    w_mine, w_theirs = lane_blocks((wq, wk, wv, wg)), lane_blocks((tq, tk, tv, tg))

    def project(i):
        here = rows_at(i, chunk_rows)
        out = dot_nn(a_ref[here, :half], w_mine) + dot_nn(a_ref[here, half:], w_theirs)
        q_ref[here, :] = out[:, :128].astype(bf16)
        k_ref[here, :] = out[:, 128:256].astype(bf16)
        v_ref[here, :] = out[:, 256:384].astype(bf16)
        gate_ref[here, :] = out[:, 384:]

    each(seq_len // chunk_rows, project)
    piece = pl.ds(piece_start, piece_len)
    gate = jax.nn.sigmoid(gate_ref[piece, :])
    mix_keys(k_ref, terms_ref, pair, ka, kb)
    mix_queries(q_ref.at[piece, :], terms_ref, piece_start, pair, qa, qb)
    before = seq_len // 2
    for s in range(0, piece_len, query_rows(seq_len)):
        rows = query_rows(seq_len)
        width = before + rows
        start = pl.multiple_of(piece_start + s, rows)
        first = pl.multiple_of(jnp.maximum(start - before, 0), rows)
        mask = live_mask(start_ref, start, first, width, rows)
        keys = pl.ds(first, width)
        out = []
        for q_of, k_of in ((qa, ka), (qb, kb)):
            p = probabilities(q_of[s : s + rows, :], k_of[keys, :], mask).astype(bf16)
            out.append(dot_nn(p, v_ref[keys, :]))
        lane = lax.broadcasted_iota(jnp.int32, (rows, pair_lanes), 1)
        u = (jnp.where(lane < 64, out[0], out[1]) * gate[s : s + rows, :]).astype(bf16)
        acc[s : s + rows, :half] += dot_nn(u, wo[0])
        acc[s : s + rows, half:] += dot_nn(u, to[0])

    @pl.when(pair == pl.num_programs(0) - 1)
    def _():
        send_ref[...] = acc[...].astype(bf16)


def backward_kernel(count_parts, piece_len, join, *refs):
    place_ref, parts, refs = refs[0], refs[1 : 1 + count_parts], list(refs[1 + count_parts :])
    mine, theirs, (wo, to, wf) = refs[:4], refs[4:8], refs[8:11]
    q_ref, k_ref, v_ref, gate_ref, z_ref, terms_ref, start_ref = refs[11:18]
    refs = refs[18:]
    y_ref = refs.pop(0) if join else parts[0]
    dq_ref, dk_ref, dv_ref, dg_ref, u_ref, dz_ref, send_ref = refs[:7]
    qa, qb, ka, kb, dd, dus, dka, dkb, dva, dcs, acc = refs[7:]
    pair = pl.program_id(0)
    seq_len, half = y_ref.shape[0], y_ref.shape[1] // 2
    rows = query_rows(seq_len)
    piece = pl.ds(pl.multiple_of(place_ref[0] * piece_len, piece_len), piece_len)

    @pl.when(pair == 0)
    def _():
        if join:
            assemble(parts, y_ref, place_ref)
        acc[...] = jnp.zeros_like(acc)
        dcs[...] = jnp.zeros_like(dcs)

    def gates(i):
        here = rows_at(i, chunk_rows)
        du = dot_nt(y_ref[here, :half], wo[0]) + dot_nt(y_ref[here, half:], to[0])
        sig = jax.nn.sigmoid(gate_ref[here, :])
        dd[here, :] = (du * sig).astype(bf16)
        dus[here, :] = du * sig * (1.0 - sig)

    each(seq_len // chunk_rows, gates)
    mix_keys(k_ref, terms_ref, pair, ka, kb)
    mix_queries(q_ref, terms_ref, 0, pair, qa, qb)
    dka[...] = jnp.zeros_like(dka)
    dkb[...] = jnp.zeros_like(dkb)
    dva[...] = jnp.zeros_like(dva)
    lane = lax.broadcasted_iota(jnp.int32, (rows, pair_lanes), 1)

    def pick(column_a, column_b):
        at = lax.broadcasted_iota(jnp.int32, (column_a.shape[0], pair_lanes), 1)
        return jnp.where(at == 2 * pair, column_a, jnp.where(at == 2 * pair + 1, column_b, 0.0))

    def body(start, first, width):
        mask = live_mask(start_ref, start, first, width, rows)
        here, keys = pl.ds(start, rows), pl.ds(first, width)
        values = v_ref[keys, :]
        d_rows = dd[here, :]
        dq, o = [], []
        for head, (q_of, k_of, dk_of) in enumerate(((qa, ka, dka), (qb, kb, dkb))):
            own_lanes = (lane < 64) if head == 0 else (lane >= 64)
            p = probabilities(q_of[here, :], k_of[keys, :], mask)
            d_mine = jnp.where(own_lanes, d_rows, jnp.zeros_like(d_rows))
            dp = dot_nt(d_mine, values)
            delta = jnp.sum(p * dp, axis=1, keepdims=True)
            ds = (p * (dp - delta)).astype(bf16)
            dq.append(dot_nn(ds, k_of[keys, :]))
            dk_of[keys, :] += dot_tn(ds, q_of[here, :])
            low = p.astype(bf16)
            dva[keys, :] += dot_tn(low, d_mine)
            o.append(dot_nn(low, values))
        o = jnp.where(lane < 64, o[0], o[1])
        dg_ref[here, :] = (dus[here, :] * o).astype(bf16)
        u_ref[here, :] = (o * jax.nn.sigmoid(gate_ref[here, :])).astype(bf16)
        dq_ref[here, :] = (jnp.where(lane < 64, dq[0], dq[1]) * 0.125).astype(bf16)
        dcs[here, :] += pick(dq[0][:, 67:68], dq[1][:, 3:4])

    over_query_blocks(seq_len, rows, body)

    def finish(i):
        here = rows_at(i, chunk_rows)
        lanes_now = lax.broadcasted_iota(jnp.int32, (chunk_rows, pair_lanes), 1)
        ka_rows, kb_rows = dka[here, :], dkb[here, :]
        dk_ref[here, :] = jnp.where(lanes_now < 64, ka_rows, kb_rows).astype(bf16)
        dv_ref[here, :] = dva[here, :].astype(bf16)
        dcs[here, :] -= pick(ka_rows[:, 64:65], kb_rows[:, 0:1])

    each(seq_len // chunk_rows, finish)
    d_own = jnp.concatenate([r[piece, :] for r in (dq_ref, dk_ref, dv_ref, dg_ref)], axis=1)
    acc[:, :half] += dot_nt(d_own, lane_blocks(mine))
    acc[:, half:] += dot_nt(d_own, lane_blocks(theirs))

    @pl.when(pair == pl.num_programs(0) - 1)
    def _():
        running_sum(dcs, True)

        def last(i):
            here = rows_at(i, chunk_rows)
            dz_ref[here, :] = (dcs[here, :] * jax.nn.sigmoid(-z_ref[here, :])).astype(bf16)

        each(seq_len // chunk_rows, last)
        send_ref[...] = (acc[...] + dot_nt(dz_ref[piece, :], wf[...])).astype(bf16)


def ffn_forward_kernel(b_ref, wg, wu, wd, tg, tu, td, gt_ref, up_ref, send_ref, acc):
    half = b_ref.shape[1] // 2
    low, high = b_ref[:, :half], b_ref[:, half:]
    gt = dot_nn(low, wg[0]) + dot_nn(high, tg[0])
    up = dot_nn(low, wu[0]) + dot_nn(high, tu[0])
    gt_ref[...] = gt
    up_ref[...] = up
    m = (gt * jax.nn.sigmoid(gt) * up).astype(bf16)

    @pl.when(pl.program_id(0) == 0)
    def _():
        acc[...] = jnp.zeros_like(acc)

    acc[:, :half] += dot_nn(m, wd[0])
    acc[:, half:] += dot_nn(m, td[0])

    @pl.when(pl.program_id(0) == pl.num_programs(0) - 1)
    def _():
        send_ref[...] = acc[...].astype(bf16)


def inner_grads(dm, gt, up):
    sig = jax.nn.sigmoid(gt)
    d_gate = (dm * up * sig * (1.0 + gt * (1.0 - sig))).astype(bf16)
    return d_gate, (dm * (gt * sig)).astype(bf16)


def ffn_backward_kernel(g_ref, gt_ref, up_ref, wg, wu, wd, tg, tu, td, *refs):
    send_ref, acc = refs[-2:]
    half = g_ref.shape[1] // 2
    dm = dot_nt(g_ref[:, :half], wd[0]) + dot_nt(g_ref[:, half:], td[0])
    d_gate, d_up = inner_grads(dm, gt_ref[...], up_ref[...])

    @pl.when(pl.program_id(0) == 0)
    def _():
        acc[...] = jnp.zeros_like(acc)

    acc[:, :half] += dot_nt(d_gate, wg[0]) + dot_nt(d_up, wu[0])
    acc[:, half:] += dot_nt(d_gate, tg[0]) + dot_nt(d_up, tu[0])

    @pl.when(pl.program_id(0) == pl.num_programs(0) - 1)
    def _():
        send_ref[...] = acc[...].astype(bf16)


def ffn_theirs_kernel(b_ref, g_ref, wg, wu, wd, tg, tu, td, *refs):
    m_ref, dgate_ref, dup_ref, gate_out, up_out, down_out, turned = refs[-7:]
    half = b_ref.shape[1] // 2

    @pl.when(pl.program_id(0) == 0)
    def _():
        turned[...] = b_ref[:, half:].T

    def chunk(i):
        here = rows_at(i, chunk_rows)
        low, high = b_ref[here, :half], b_ref[here, half:]
        gt = dot_nn(low, wg[0]) + dot_nn(high, tg[0])
        up = dot_nn(low, wu[0]) + dot_nn(high, tu[0])
        dm = dot_nt(g_ref[here, :half], wd[0]) + dot_nt(g_ref[here, half:], td[0])
        m_ref[here, :] = (gt * jax.nn.sigmoid(gt) * up).astype(bf16)
        dgate_ref[here, :], dup_ref[here, :] = inner_grads(dm, gt, up)

    each(b_ref.shape[0] // chunk_rows, chunk)
    gate_out[...] = dot_nn(turned[...], dgate_ref[...]).astype(bf16)
    up_out[...] = dot_nn(turned[...], dup_ref[...]).astype(bf16)
    down_out[...] = dot_tn(m_ref[...], g_ref[:, half:]).astype(bf16)


def ffn_mine_kernel(b_ref, g_ref, m_ref, dgate_ref, dup_ref, gate_in, up_in, down_in, *refs):
    gate_out, up_out, down_out, turned = refs[-4:]

    @pl.when(pl.program_id(0) == 0)
    def _():
        turned[...] = b_ref[...].T

    gate_out[0] = dot_nn(turned[...], dgate_ref[...]) + gate_in[...].astype(f32)
    up_out[0] = dot_nn(turned[...], dup_ref[...]) + up_in[...].astype(f32)
    down_out[0] = dot_tn(m_ref[...], g_ref[...]) + down_in[...].astype(f32)


def attention_grads_kernel(steps, mine, *refs):
    a_ref, dq, dk, dv, dg, dz, u_ref, y_ref = refs[:8]
    received = refs[8:14] if mine else [None] * 6
    acc, acc_out = refs[-2:]
    outs = refs[-8:-2]
    turned = a_ref[...].T
    width = dq.shape[1]
    parts = [dot_nn(turned, d[...]) for d in (dq, dk, dv, dg, dz)]
    out = dot_tn(u_ref[...], y_ref[...])

    def give(values):
        for ref, value, more in zip(outs, values, received):
            total = value if more is None else value + more[...].astype(f32)
            if len(ref.shape) == 3:
                ref[0] = total.astype(ref.dtype)
            else:
                ref[...] = total.astype(ref.dtype)

    if steps == 1:
        give([*parts, out])
        return
    step = pl.program_id(0)

    @pl.when(step == 0)
    def _():
        acc[...] = jnp.zeros_like(acc)
        acc_out[...] = jnp.zeros_like(acc_out)

    for k, part in enumerate(parts):
        acc[:, k * width : k * width + part.shape[1]] += part
    acc_out[...] += out

    @pl.when(step == steps - 1)
    def _():
        found = [acc[:, k * width : k * width + p.shape[1]] for k, p in enumerate(parts)]
        give([*found, acc_out[...]])


def fixed(shape, single=True):
    zeros = (0,) * len(shape)
    if single:
        return pl.BlockSpec(shape, lambda *_: zeros, pipeline_mode=pl.Buffered(1))
    return pl.BlockSpec(shape, lambda *_: zeros)


def lanes(seq_len):
    return pl.BlockSpec((seq_len, pair_lanes), lambda p, *_: (0, p))


def lanes_read(seq_len):
    if seq_len <= 2048:
        return lanes(seq_len)
    return pl.BlockSpec((seq_len, pair_lanes), lambda p, *_: (0, p), pipeline_mode=pl.Buffered(1))


def columns_of(w, layer, width):
    return pl.BlockSpec((1, w.shape[1], width), lambda p, *_: (layer, 0, p))


def rows_of(w, layer, height):
    return pl.BlockSpec((1, height, w.shape[2]), lambda p, *_: (layer, p, 0))


def shape(dims, dtype):
    return jax.ShapeDtypeStruct(dims, dtype)


def attention_specs(parts, layer, w4, t4, wo, to, seq_len, join):
    specs = [fixed(p.shape) for p in parts]
    specs += [columns_of(w, layer, pair_lanes) for w in (*w4, *t4)]
    specs += [rows_of(wo, layer, pair_lanes), rows_of(to, layer, pair_lanes)]
    return specs


def cost(microseconds):
    return pl.CostEstimate(flops=int(microseconds * 1.1e9), bytes_accessed=0, transcendentals=0)


def token_specs(tokens):
    return [pl.BlockSpec(memory_space=pl.ANY) for _ in tokens]


def forward_own(place, parts, layer, w4, t4, wo, to, wf, bias, doc_start, piece_len):
    seq_len, width = doc_start.shape[0], parts[0].shape[1]
    local_width = wo.shape[1]
    join = len(parts) > 1
    terms = (seq_len, pair_lanes)
    outs = [shape((seq_len, local_width), bf16)] * 3 + [shape((seq_len, local_width), f32)]
    outs += [shape(terms, f32), shape(terms, bf16), shape((piece_len, width), bf16)]
    specs = [lanes(seq_len)] * 4 + [fixed(terms, False)] * 2 + [fixed((piece_len, width), False)]
    if join:
        outs, specs = [shape((seq_len, width), bf16)] + outs, [fixed((seq_len, width))] + specs
    low, piece = pltpu.VMEM((seq_len, pair_lanes), bf16), pltpu.VMEM((piece_len, pair_lanes), bf16)
    got = pl.pallas_call(
        functools.partial(forward_own_kernel, len(parts), piece_len, join),
        grid_spec=pltpu.PrefetchScalarGridSpec(
            num_scalar_prefetch=1,
            grid=(local_width // pair_lanes,),
            in_specs=attention_specs(parts, layer, w4, t4, wo, to, seq_len, join)
            + [fixed(wf.shape), fixed(bias.shape), fixed(doc_start.shape)],
            out_specs=specs,
            scratch_shapes=[piece] * 2 + [low] * 2 + [pltpu.VMEM(terms, f32), pltpu.VMEM((piece_len, width), f32)],
        ),
        out_shape=outs,
        cost_estimate=cost(19),
        compiler_params=pltpu.CompilerParams(vmem_limit_bytes=60 << 20),
    )(place, *parts, *w4, *t4, wo, to, wf, bias, doc_start)
    got = list(got)
    a = got.pop(0) if join else parts[0]
    return a, got[:6], got[6]


def attention_backward(place, parts, layer, w4, t4, wo, to, wf, saved, doc_start, piece_len):
    q, k, v, gate, z, terms = saved
    seq_len, width = doc_start.shape[0], parts[0].shape[1]
    local_width = wo.shape[1]
    join = len(parts) > 1
    outs = [shape((seq_len, local_width), bf16)] * 5 + [shape((seq_len, pair_lanes), bf16)]
    outs += [shape((piece_len, width), bf16)]
    specs = [lanes(seq_len)] * 5 + [fixed((seq_len, pair_lanes), False), fixed((piece_len, width), False)]
    if join:
        outs, specs = [shape((seq_len, width), bf16)] + outs, [fixed((seq_len, width))] + specs
    low, high = pltpu.VMEM((seq_len, pair_lanes), bf16), pltpu.VMEM((seq_len, pair_lanes), f32)
    got = pl.pallas_call(
        functools.partial(backward_kernel, len(parts), piece_len, join),
        grid_spec=pltpu.PrefetchScalarGridSpec(
            num_scalar_prefetch=1,
            grid=(local_width // pair_lanes,),
            in_specs=attention_specs(parts, layer, w4, t4, wo, to, seq_len, join)
            + [fixed(wf.shape)]
            + [lanes_read(seq_len)] * 4
            + [fixed(z.shape), fixed(terms.shape), fixed(doc_start.shape)],
            out_specs=specs,
            scratch_shapes=[low] * 5 + [high] * 5 + [pltpu.VMEM((piece_len, width), f32)],
        ),
        out_shape=outs,
        cost_estimate=cost(33),
        compiler_params=pltpu.CompilerParams(vmem_limit_bytes=60 << 20),
    )(place, *parts, *w4, *t4, wo, to, wf, q, k, v, gate, z, terms, doc_start)
    got = list(got)
    y = got.pop(0) if join else parts[0]
    return y, got[:6], got[6]


def ffn_weights(layer, w3, t3):
    specs = []
    for wg, wu, wd in (w3, t3):
        specs += [
            columns_of(wg, layer, hidden_block), columns_of(wu, layer, hidden_block), rows_of(wd, layer, hidden_block),
        ]
    return specs


def blocks_of(rows):
    return pl.BlockSpec((rows, hidden_block), lambda p, *_: (0, p))


def ffn_forward(b, layer, w3, t3):
    rows, width = b.shape
    inner = w3[2].shape[1]
    return pl.pallas_call(
        ffn_forward_kernel,
        grid=(inner // hidden_block,),
        in_specs=[fixed(b.shape)] + ffn_weights(layer, w3, t3),
        out_specs=[blocks_of(rows)] * 2 + [fixed((rows, width), False)],
        scratch_shapes=[pltpu.VMEM((rows, width), f32)],
        out_shape=[shape((rows, inner), f32)] * 2 + [shape((rows, width), bf16)],
        cost_estimate=cost(7),
        compiler_params=pltpu.CompilerParams(vmem_limit_bytes=60 << 20),
    )(b, *w3, *t3)


def ffn_backward(g, gt, up, layer, w3, t3, *tokens):
    rows, width = g.shape
    return pl.pallas_call(
        ffn_backward_kernel,
        grid=(gt.shape[1] // hidden_block,),
        in_specs=[fixed(g.shape)] + [blocks_of(rows)] * 2 + ffn_weights(layer, w3, t3) + token_specs(tokens),
        out_specs=fixed((rows, width), False),
        scratch_shapes=[pltpu.VMEM((rows, width), f32)],
        out_shape=shape((rows, width), bf16),
        cost_estimate=cost(8),
        compiler_params=pltpu.CompilerParams(vmem_limit_bytes=60 << 20),
    )(g, gt, up, *w3, *t3, *tokens)


def ffn_theirs(b, g, layer, w3, t3, *tokens):
    rows, width = b.shape
    half = width // 2
    inner = w3[2].shape[1]
    wide = pl.BlockSpec((half, hidden_block), lambda p: (0, p))
    return pl.pallas_call(
        ffn_theirs_kernel,
        grid=(inner // hidden_block,),
        in_specs=[fixed(b.shape), fixed(g.shape)] + ffn_weights(layer, w3, t3) + token_specs(tokens),
        out_specs=[blocks_of(rows)] * 3 + [wide, wide, pl.BlockSpec((hidden_block, half), lambda p: (p, 0))],
        scratch_shapes=[pltpu.VMEM((half, rows), bf16)],
        out_shape=[shape((rows, inner), bf16)] * 3
        + [shape((half, inner), bf16)] * 2
        + [shape((inner, half), bf16)],
        cost_estimate=cost(24),
        compiler_params=pltpu.CompilerParams(vmem_limit_bytes=60 << 20),
    )(b, g, *w3, *t3, *tokens)


def anywhere():
    return pl.BlockSpec(memory_space=pl.ANY)


def ffn_mine(layer, b, g, values, received, totals, *tokens):
    rows, width = b.shape
    half, inner = width // 2, values[0].shape[1]
    wide = pl.BlockSpec((half, hidden_block), lambda p: (0, p))
    tall = pl.BlockSpec((hidden_block, half), lambda p: (p, 0))
    wide_out = pl.BlockSpec((1, half, hidden_block), lambda p: (layer, 0, p))
    tall_out = pl.BlockSpec((1, hidden_block, half), lambda p: (layer, p, 0))
    return pl.pallas_call(
        ffn_mine_kernel,
        grid=(inner // hidden_block,),
        in_specs=[fixed((rows, half))] * 2
        + [blocks_of(rows)] * 3
        + [wide, wide, tall]
        + [anywhere()] * 3
        + token_specs(tokens),
        out_specs=[wide_out, wide_out, tall_out],
        out_shape=[shape(x.shape, x.dtype) for x in totals],
        scratch_shapes=[pltpu.VMEM((half, rows), bf16)],
        input_output_aliases={8: 0, 9: 1, 10: 2},
        cost_estimate=cost(9),
        compiler_params=pltpu.CompilerParams(vmem_limit_bytes=60 << 20),
    )(b, g, *values, *received, *totals, *tokens)


def attention_grads(layer, a, ds, dz, u, y, received=None, totals=None, tokens=()):
    rows, width = a.shape
    half, local_width = width // 2, u.shape[1]
    part = min(rows, 1024)
    steps = rows // part
    mine = received is not None
    side = 0 if mine else 1
    features = pl.BlockSpec((part, half), lambda p: (p, side))
    across = [pl.BlockSpec((part, x.shape[1]), lambda p: (p, 0)) for x in (*ds, dz, u)]
    specs = [features, *across, features]
    operands = [a, *ds, dz, u, y]
    flat = [(half, local_width)] * 4 + [(half, pair_lanes), (local_width, half)]
    if mine:
        specs += [fixed(x) for x in flat] + [anywhere()] * 5
        operands += [*received, *totals]
        outs = [shape(x.shape, f32) for x in totals[:4]] + [shape(flat[4], f32), shape(totals[4].shape, f32)]
        layered = pl.BlockSpec((1, half, local_width), lambda p: (layer, 0, 0))
        out_specs = [layered] * 4 + [fixed(flat[4], False)]
        out_specs += [pl.BlockSpec((1, local_width, half), lambda p: (layer, 0, 0))]
        aliases = {14: 0, 15: 1, 16: 2, 17: 3, 18: 5}
    else:
        outs, out_specs, aliases = [shape(x, bf16) for x in flat], [fixed(x, False) for x in flat], {}
    sizes = [(half, 4 * local_width + pair_lanes), (local_width, half)] if steps > 1 else [(8, 128)] * 2
    return pl.pallas_call(
        functools.partial(attention_grads_kernel, steps, mine),
        grid=(steps,),
        in_specs=specs + token_specs(tokens),
        out_specs=out_specs,
        out_shape=outs,
        scratch_shapes=[pltpu.VMEM(x, f32) for x in sizes],
        input_output_aliases=aliases,
        cost_estimate=cost(7),
        compiler_params=pltpu.CompilerParams(vmem_limit_bytes=60 << 20),
    )(*operands, *tokens)


def unset(*like):
    return pl.pallas_call(
        pass_kernel,
        out_specs=[pl.BlockSpec(memory_space=pl.ANY) for _ in like],
        out_shape=list(like),
    )()


def inverse_rms(h):
    return lax.rsqrt(jnp.mean(h * h, axis=-1, keepdims=True) + epsilon)


def norm_back(grad_normed, hidden, inverse, gain):
    scaled = hidden * inverse
    weighted = grad_normed * gain
    grad_gain = jnp.sum(grad_normed * scaled, axis=0)
    mean = jnp.mean(weighted * scaled, axis=-1, keepdims=True)
    return inverse * (weighted - scaled * mean), grad_gain


def local(
    hidden_in, segment_ids, w_query, w_key, w_value, w_gate_out, w_attn_out, w_forget, b_forget,
    gain_attn, gain_ffn, w_gate, w_up, w_down, cotangent,
):
    seq_count, piece_len, width = hidden_in.shape
    count_z, count_t = lax.axis_size("context"), lax.axis_size("tensor")
    core, z, t = lax.axis_index("fsdp"), lax.axis_index("context"), lax.axis_index("tensor")
    layers, half, local_width = w_query.shape
    heads = w_forget.shape[2]
    block = piece_len // count_t
    seq_len = piece_len * count_z
    shared_rows = count_z == 4
    place = jnp.stack([z, t]).astype(jnp.int32)

    def features(x):
        return jnp.where(core == 0, x, jnp.concatenate([x[..., half:], x[..., :half]], axis=-1))

    def own_block(x):
        return lax.dynamic_slice_in_dim(x, t * block, block, 0)

    def other(w):
        return swap(w, "fsdp", 1)

    def full(w, axis):
        return jnp.concatenate([w, other(w)], axis=axis)

    seg_all = gathered(segment_ids.reshape(1, piece_len), "context").reshape(seq_len)
    doc_start = jnp.sum((seg_all[None, :] < seg_all[:, None]).astype(jnp.int32), axis=1, keepdims=True)

    gains = full(jnp.concatenate([gain_attn, gain_ffn], axis=0), 1).astype(f32)
    hidden_rows = features(hidden_in.reshape(piece_len, width)).astype(f32)
    first_a = (hidden_rows * inverse_rms(hidden_rows) * gains[0]).astype(bf16)
    a_parts, a_far = all_rows(own_block(first_a), first_a, seg_all)

    w_forget_full = jnp.pad(full(w_forget, 1), ((0, 0), (0, 0), (0, pair_lanes - heads)))
    bias = jnp.pad(b_forget, ((0, 0), (0, pair_lanes - heads)))
    w4 = (w_query, w_key, w_value, w_gate_out)
    t4 = tuple(other(w) for w in w4)
    to = other(w_attn_out)
    w3 = (w_gate, w_up, w_down)
    t3 = tuple(other(w) for w in w3)

    hidden = own_block(hidden_rows)
    saved = []
    cotangent_rows = features(cotangent.reshape(piece_len, width))
    last = layers - 1
    grad = own_block(cotangent_rows).astype(f32)
    for layer in range(layers):
        gain_one, gain_two = gains[layer], gains[layers + layer]
        inverse_one = inverse_rms(hidden)
        if layer > 0:
            a_shard = (hidden * inverse_one * gain_one).astype(bf16)
            if shared_rows and layer == 1:
                a_shard = after(a_shard, g_last)
            a_parts, _ = all_rows(a_shard)
        forget_weights = w_forget_full[layer]
        if shared_rows and layer > 0:
            b_sent = after(saved[-1]["b_shard"], a_parts[-1])
            saved[-1]["b_rows"] = sequence_rows(b_sent)
            forget_weights = after(forget_weights, b_sent)
        a, (q, k, v, gate, forget, terms), sends = forward_own(
            place, a_parts, layer, w4, t4, w_attn_out, to, forget_weights,
            bias[layer : layer + 1], doc_start, piece_len,
        )
        if shared_rows and layer == 0:
            g_last = lax.all_gather(after(cotangent_rows, *a_far), "context", tiled=True)
        mixed = hidden + received_sum(sends)
        inverse_two = inverse_rms(mixed)
        b_shard = (mixed * inverse_two * gain_two).astype(bf16)
        b = gathered(b_shard, "tensor")
        gt, up, sends = ffn_forward(b, layer, w3, t3)
        saved.append(
            dict(hidden=hidden, inverse_one=inverse_one, a=a, kept=(q, k, v, gate, forget, terms), mixed=mixed,
                 inverse_two=inverse_two, b=b, b_shard=b_shard, gt=gt, up=up)
        )
        if layer < last:
            hidden = mixed + received_sum(sends)

    def finish(x):
        return features(gathered(x.astype(bf16), "tensor")).reshape(1, piece_len, width)

    last_sends = sends
    wide = shape((layers, half, local_width), f32)
    inner = shape((layers, half, w_gate.shape[2]), f32)
    results = list(
        unset(
            wide, wide, wide, wide, shape((layers, local_width, half), f32),
            inner, inner, shape((layers, w_down.shape[1], half), f32),
        )
    )
    small = [[None] * layers for _ in range(2)]
    gain_grads = [None] * (2 * layers)

    def ffn_theirs_of(layer, *tokens):
        s = saved[layer]
        values = ffn_theirs(s["b_rows"], s["g_rows"], layer, w3, t3, *tokens)
        s.update(values=values[:3], ffn_received=[other(x) for x in values[3:]])

    def ffn_mine_of(layer, *tokens):
        s = saved[layer]
        received = s["ffn_received"]
        results[5:] = ffn_mine(layer, s["b_rows"], s["g_rows"], s["values"], received, results[5:], *tokens)

    def attention_theirs_of(layer, *tokens):
        s = saved[layer]
        s["theirs"] = attention_grads(layer, *s["grads"], tokens=tokens)
        s["received"] = [other(x) for x in s["theirs"]]
        bias_grad = jnp.sum(s["grads"][2].astype(f32), axis=0)[:heads]
        small[1][layer] = bias_grad + other(bias_grad)

    def attention_mine_of(layer, *tokens):
        s = saved[layer]
        found = attention_grads(layer, *s["grads"], s["received"], results[:5], tokens)
        results[:5] = [*found[:4], found[5]]
        small[0][layer] = found[4][:, :heads]

    for layer in reversed(range(layers)):
        s = saved[layer]
        gain_one, gain_two = gains[layer], gains[layers + layer]
        tokens = ()
        if layer == last:
            g = cotangent_rows
        else:
            g_shard = grad.astype(bf16)
            g = gathered(g_shard, "tensor")
            tokens = (saved[layer + 1]["theirs"][0],)
        if not shared_rows:
            s.update(b_rows=s["b"], g_rows=g)
        sends = ffn_backward(g, s["gt"], s["up"], layer, w3, t3, *tokens)
        if layer < last:
            sends = after(sends, *saved[layer + 1]["received"])
        back, gain_grads[layers + layer] = norm_back(received_sum(sends), s["mixed"], s["inverse_two"], gain_two)
        grad_mixed = grad + back
        y_shard = grad_mixed.astype(bf16)
        if layer < last:
            attention_mine_of(layer + 1)
            y_shard = after(y_shard, results[0])
        elif shared_rows:
            y_shard = after(y_shard, *[x["b_rows"] for x in saved[:-1]])
        y_parts, y_far = all_rows(y_shard, together=layer < last)
        tokens = ()
        if layer < last:
            above = saved[layer + 1]
            ffn_theirs_of(layer + 1, *y_far, y_parts[0])
            tokens = (above["values"][0],)
        kept = (*s["kept"][:-1], after(s["kept"][-1], *tokens))
        y, (dq, dk, dv, dg, u, dz), sends = attention_backward(
            place, y_parts, layer, w4, t4, w_attn_out, to, w_forget_full[layer], kept, doc_start, piece_len,
        )
        token = y_parts[-1]
        if shared_rows and layer == last:
            s.update(b_rows=sequence_rows(after(s["b_shard"], *y_parts)), g_rows=g_last)
        elif shared_rows:
            s["g_rows"] = sequence_rows(after(g_shard, above["values"][0]))
        s["grads"] = (s["a"], (dq, dk, dv, dg), dz, u, y)
        if layer > 0:
            attention_theirs_of(layer)
        back, gain_grads[layer] = norm_back(received_sum(sends), s["hidden"], s["inverse_one"], gain_one)
        grad = grad_mixed + back

    block_sum = own_block(last_sends).astype(f32) + saved[last]["mixed"]
    with_rows = lax.dynamic_update_slice_in_dim(last_sends, block_sum.astype(bf16), t * block, 0)
    output = lax.psum(after(with_rows, sends), "tensor")
    ffn_theirs_of(0)
    for layer in reversed(range(1, layers)):
        ffn_mine_of(layer, sends)
    attention_theirs_of(0, sends)
    gain_total = jnp.stack(gain_grads).reshape(1, -1)
    for axis in (("context", "tensor"),) if shared_rows else ("context", "tensor"):
        gain_total = jnp.sum(gathered(gain_total, axis), axis=0, keepdims=True)
    gain_total = gain_total.reshape(2 * layers, width)
    gain_total = gain_total[:, :half] + other(gain_total[:, half:])
    attention_mine_of(0, gain_total)
    ffn_mine_of(0)
    if not shared_rows:
        results[5:] = [lax.psum(x, "context") for x in results[5:]]
    output = features(after(output, saved[0]["values"][0])).reshape(1, piece_len, width)
    grad_input = finish(grad)
    return (
        output, grad_input, *results[:5], jnp.stack(small[0]), jnp.stack(small[1]),
        gain_total[:layers], gain_total[layers:], *results[5:],
    )


def solution(mesh):
    rows = P("fsdp", "context", None)
    wide, tall = P(None, "fsdp", "tensor"), P(None, "tensor", "fsdp")
    heads, gain = P(None, "tensor"), P(None, "fsdp")
    return jax.shard_map(
        local,
        mesh=mesh,
        in_specs=(
            rows, P("fsdp", "context"), wide, wide, wide, wide, tall, wide, heads, gain, gain, wide, wide, tall, rows,
        ),
        out_specs=(rows, rows, wide, wide, wide, wide, tall, wide, heads, gain, gain, wide, wide, tall),
        check_vma=False,
    )
```

```python
import functools

import jax
import jax.numpy as jnp
from jax import lax
from jax.experimental import pallas as pl
from jax.experimental.pallas import tpu as pltpu
from jax.sharding import PartitionSpec as P

epsilon = 1e-06
masked_value = -1e30
bf16 = jnp.bfloat16
f32 = jnp.float32
pair_lanes = 128
hidden_block = 256
chunk_rows = 256


def query_rows(seq_len):
    return 256 if seq_len <= 2048 else 128


def swap(x, axis, k):
    n = lax.axis_size(axis)
    return lax.ppermute(x, axis, [(i, i ^ k) for i in range(n)])


def pass_kernel(*refs):
    pass


def after(x, *tokens):
    if not tokens:
        return x
    anywhere = pl.BlockSpec(memory_space=pl.ANY)
    return pl.pallas_call(
        pass_kernel,
        in_specs=[anywhere] * (1 + len(tokens)),
        out_specs=anywhere,
        out_shape=jax.ShapeDtypeStruct(x.shape, x.dtype),
        input_output_aliases={0: 0},
    )(x, *tokens)


def gathered(block, axis):
    count = lax.axis_size(axis)
    copies = jnp.broadcast_to(block[None], (count,) + block.shape)
    return lax.all_to_all(copies, axis, 0, 0, tiled=True).reshape((-1,) + block.shape[1:])


def sequence_rows(shard):
    return lax.all_gather(shard, ("context", "tensor"), tiled=True)


def near_rows(own):
    return swap(own, "context", 1)


def far_blocks(shard):
    return swap(shard, "context", 2), swap(shard, "context", 3)


def all_rows(shard, own=None, token=None, together=False):
    if own is None:
        own = gathered(shard, "tensor")
    if lax.axis_size("context") != 4:
        return (lax.all_gather(own, "context", tiled=True),), ()
    second, third = far_blocks(shard)
    near = near_rows(own)
    if together:
        block, width = shard.shape
        far = gathered(after(jnp.concatenate([second, third], axis=0), own), "tensor")
        return (own, near, far.reshape(-1, 2, block, width)), (second, third)
    if token is not None:
        second = after(second, token)
    parts = [own, near]
    for far in (second, third):
        parts += [far] + [swap(far, "tensor", k) for k in range(1, lax.axis_size("tensor"))]
    return tuple(parts), (second, third)


def received_sum(sends):
    count = lax.axis_size("tensor")
    got = lax.all_to_all(sends.reshape(count, -1, sends.shape[1]), "tensor", 0, 0, tiled=True)
    return jnp.sum(got.astype(f32), axis=0)


def dot_nt(a, b):
    return lax.dot_general(a, b, (((1,), (1,)), ((), ())), preferred_element_type=f32)


def dot_tn(a, b):
    return lax.dot_general(a, b, (((0,), (0,)), ((), ())), preferred_element_type=f32)


def dot_nn(a, b):
    return jnp.dot(a, b, preferred_element_type=f32)


def each(count, body):
    if count <= 4:
        for i in range(count):
            body(i)
        return

    def one(i, carry):
        body(i)
        return carry

    lax.fori_loop(0, count, one, 0)


def rows_at(i, rows):
    start = i * rows
    return pl.ds(start if isinstance(start, int) else pl.multiple_of(start, rows), rows)


def assemble(parts, whole_ref, place_ref):
    z, t = place_ref[0], place_ref[1]
    piece, blocks_seen, piece_len = 0, 0, parts[0].shape[0]
    for part in parts:
        if len(part.shape) == 4:
            blocks, pieces, block = part.shape[:3]
            for p in range(pieces):
                for b in range(blocks):
                    at = pl.multiple_of((z ^ (piece + p)) * piece_len + b * block, block)
                    whole_ref[pl.ds(at, block), :] = part[b, p]
            piece += pieces
            continue
        rows = part.shape[0]
        if rows == piece_len:
            at = pl.multiple_of((z ^ piece) * piece_len, piece_len)
            piece += 1
        else:
            at = pl.multiple_of((z ^ piece) * piece_len + (t ^ blocks_seen) * rows, rows)
            blocks_seen += 1
            if blocks_seen * rows == piece_len:
                piece, blocks_seen = piece + 1, 0
        whole_ref[pl.ds(at, rows), :] = part[...]


def triangle(rows, reverse):
    row = lax.broadcasted_iota(jnp.int32, (rows, rows), 0)
    column = lax.broadcasted_iota(jnp.int32, (rows, rows), 1)
    return jnp.where((column >= row) if reverse else (column <= row), 1.0, 0.0).astype(bf16)


def running_sum(ref, reverse):
    rows = chunk_rows
    ones = triangle(rows, reverse)
    count = ref.shape[0] // rows
    edge = 0 if reverse else rows - 1

    def chunk(i, carry):
        here = pl.ds(pl.multiple_of((count - 1 - i if reverse else i) * rows, rows), rows)
        high, middle, lowest = three_parts(ref[here, :])
        total = dot_nn(ones, high) + dot_nn(ones, middle) + dot_nn(ones, lowest) + carry
        ref[here, :] = total
        return total[edge : edge + 1, :]

    lax.fori_loop(0, count, chunk, jnp.zeros((1, ref.shape[1]), f32), unroll=count <= 4)


def log_sigmoid(z):
    e = jnp.exp(-jnp.abs(z))
    small = e * (1.0 - e * (1 / 2 - e * (1 / 3 - e * (1 / 4 - e * (1 / 5 - e * (1 / 6 - e * (1 / 7)))))))
    return jnp.minimum(z, 0.0) - jnp.where(e < 0.0625, small, jnp.log(1.0 + e))


def three_parts(x):
    high = x.astype(bf16)
    middle = (x - high.astype(f32)).astype(bf16)
    return high, middle, (x - high.astype(f32) - middle.astype(f32)).astype(bf16)


def decay_side(terms, pair, key_side):
    row = lax.broadcasted_iota(jnp.int32, (pair_lanes, pair_lanes), 0)
    lane = lax.broadcasted_iota(jnp.int32, (pair_lanes, pair_lanes), 1)
    spot = lane & 63
    term = spot if key_side else spot - 3
    head = jnp.where(lane >= 64, 2 * pair, 2 * pair + 1)
    chosen = (term >= 0) & (term < 3) & (row == 8 * term + head)
    pick = jnp.where(chosen, -1.0 if key_side else 1.0, 0.0).astype(bf16)
    lanes_now = lax.broadcasted_iota(jnp.int32, (1, pair_lanes), 1) & 63
    other = lanes_now - 3 if key_side else lanes_now
    ones = jnp.where((other >= 0) & (other < 3), 1.0, 0.0)
    return (dot_nn(terms, pick) + ones).astype(bf16)


def mix_keys(k_ref, terms_ref, pair, ka, kb):
    def mix(i):
        here = rows_at(i, chunk_rows)
        lane = lax.broadcasted_iota(jnp.int32, (chunk_rows, pair_lanes), 1)
        k, side = k_ref[here, :], decay_side(terms_ref[here, :], pair, True)
        ka[here, :] = jnp.where(lane < 64, k, side)
        kb[here, :] = jnp.where(lane < 64, side, k)

    each(k_ref.shape[0] // chunk_rows, mix)


def mix_queries(q_ref, terms_ref, start, pair, qa, qb):
    def mix(i):
        here = rows_at(i, chunk_rows)
        lane = lax.broadcasted_iota(jnp.int32, (chunk_rows, pair_lanes), 1)
        q = (q_ref[here, :].astype(f32) * 0.125).astype(bf16)
        terms = terms_ref[pl.ds(pl.multiple_of(start + i * chunk_rows, chunk_rows), chunk_rows), :]
        side = decay_side(terms, pair, False)
        qa[here, :] = jnp.where(lane < 64, q, side)
        qb[here, :] = jnp.where(lane < 64, side, q)

    each(q_ref.shape[0] // chunk_rows, mix)


def live_mask(start_ref, start, first, width, rows):
    key_pos = first + lax.broadcasted_iota(jnp.int32, (rows, width), 1)
    query_pos = start + lax.broadcasted_iota(jnp.int32, (rows, width), 0)
    doc_start = start_ref[pl.ds(start, rows), :]
    return (key_pos <= query_pos) & (key_pos >= doc_start)


def over_query_blocks(seq_len, rows, body):
    before = seq_len // 2
    if seq_len // rows <= 4:
        for start in range(0, seq_len, rows):
            first = max(0, start - before)
            body(start, first, start + rows - first)
        return
    width = before + rows

    def one(i, carry):
        start = pl.multiple_of(i * rows, rows)
        first = pl.multiple_of(jnp.maximum(start - before, 0), rows)
        body(start, first, width)
        return carry

    lax.fori_loop(0, seq_len // rows, one, 0)


def probabilities(q_rows, k_rows, mask):
    s = jnp.where(mask, dot_nt(q_rows, k_rows), masked_value)
    e = jnp.exp(s - jnp.max(s, axis=1, keepdims=True))
    return e * (1.0 / jnp.sum(e, axis=1, keepdims=True))


def lane_blocks(refs):
    return jnp.concatenate([r[0] for r in refs], axis=1)


def forward_own_kernel(count_parts, piece_len, join, *refs):
    place_ref, parts, refs = refs[0], refs[1 : 1 + count_parts], list(refs[1 + count_parts :])
    (wq, wk, wv, wg), (tq, tk, tv, tg) = refs[:4], refs[4:8]
    wo, to, wf, bias, start_ref = refs[8:13]
    refs = refs[13:]
    a_ref = refs.pop(0) if join else parts[0]
    q_ref, k_ref, v_ref, gate_ref, z_ref, terms_ref, send_ref, qa, qb, ka, kb, decay, acc = refs
    pair = pl.program_id(0)
    seq_len, half = a_ref.shape[0], a_ref.shape[1] // 2
    piece_start = pl.multiple_of(place_ref[0] * piece_len, piece_len)

    @pl.when(pair == 0)
    def _():
        if join:
            assemble(parts, a_ref, place_ref)
        acc[...] = jnp.zeros_like(acc)

        def gates(i):
            here = rows_at(i, chunk_rows)
            z = dot_nn(a_ref[here, :], wf[...]) + bias[...]
            z_ref[here, :] = z
            decay[here, :] = log_sigmoid(z)

        each(seq_len // chunk_rows, gates)
        running_sum(decay, False)

        def split(i):
            here = rows_at(i, chunk_rows)
            lane = lax.broadcasted_iota(jnp.int32, (chunk_rows, pair_lanes), 1)
            high, middle, lowest = (x.astype(f32) for x in three_parts(decay[here, :]))
            later = jnp.where(lane < 16, pltpu.roll(middle, 8, 1), pltpu.roll(lowest, 16, 1))
            terms = jnp.where(lane < 8, high, later)
            terms_ref[here, :] = jnp.where(lane < 24, terms, 0.0).astype(bf16)

        each(seq_len // chunk_rows, split)

    w_mine, w_theirs = lane_blocks((wq, wk, wv, wg)), lane_blocks((tq, tk, tv, tg))

    def project(i):
        here = rows_at(i, chunk_rows)
        out = dot_nn(a_ref[here, :half], w_mine) + dot_nn(a_ref[here, half:], w_theirs)
        q_ref[here, :] = out[:, :128].astype(bf16)
        k_ref[here, :] = out[:, 128:256].astype(bf16)
        v_ref[here, :] = out[:, 256:384].astype(bf16)
        gate_ref[here, :] = out[:, 384:]

    each(seq_len // chunk_rows, project)
    piece = pl.ds(piece_start, piece_len)
    gate = jax.nn.sigmoid(gate_ref[piece, :])
    mix_keys(k_ref, terms_ref, pair, ka, kb)
    mix_queries(q_ref.at[piece, :], terms_ref, piece_start, pair, qa, qb)
    before = seq_len // 2
    for s in range(0, piece_len, query_rows(seq_len)):
        rows = query_rows(seq_len)
        width = before + rows
        start = pl.multiple_of(piece_start + s, rows)
        first = pl.multiple_of(jnp.maximum(start - before, 0), rows)
        mask = live_mask(start_ref, start, first, width, rows)
        keys = pl.ds(first, width)
        out = []
        for q_of, k_of in ((qa, ka), (qb, kb)):
            p = probabilities(q_of[s : s + rows, :], k_of[keys, :], mask).astype(bf16)
            out.append(dot_nn(p, v_ref[keys, :]))
        lane = lax.broadcasted_iota(jnp.int32, (rows, pair_lanes), 1)
        u = (jnp.where(lane < 64, out[0], out[1]) * gate[s : s + rows, :]).astype(bf16)
        acc[s : s + rows, :half] += dot_nn(u, wo[0])
        acc[s : s + rows, half:] += dot_nn(u, to[0])

    @pl.when(pair == pl.num_programs(0) - 1)
    def _():
        send_ref[...] = acc[...].astype(bf16)


def backward_kernel(count_parts, piece_len, join, *refs):
    place_ref, parts, refs = refs[0], refs[1 : 1 + count_parts], list(refs[1 + count_parts :])
    mine, theirs, (wo, to, wf) = refs[:4], refs[4:8], refs[8:11]
    q_ref, k_ref, v_ref, gate_ref, z_ref, terms_ref, start_ref = refs[11:18]
    refs = refs[18:]
    y_ref = refs.pop(0) if join else parts[0]
    dq_ref, dk_ref, dv_ref, dg_ref, u_ref, dz_ref, send_ref = refs[:7]
    qa, qb, ka, kb, dd, dus, dka, dkb, dva, dcs, acc = refs[7:]
    pair = pl.program_id(0)
    seq_len, half = y_ref.shape[0], y_ref.shape[1] // 2
    rows = query_rows(seq_len)
    piece = pl.ds(pl.multiple_of(place_ref[0] * piece_len, piece_len), piece_len)

    @pl.when(pair == 0)
    def _():
        if join:
            assemble(parts, y_ref, place_ref)
        acc[...] = jnp.zeros_like(acc)
        dcs[...] = jnp.zeros_like(dcs)

    def gates(i):
        here = rows_at(i, chunk_rows)
        du = dot_nt(y_ref[here, :half], wo[0]) + dot_nt(y_ref[here, half:], to[0])
        sig = jax.nn.sigmoid(gate_ref[here, :])
        dd[here, :] = (du * sig).astype(bf16)
        dus[here, :] = du * sig * (1.0 - sig)

    each(seq_len // chunk_rows, gates)
    mix_keys(k_ref, terms_ref, pair, ka, kb)
    mix_queries(q_ref, terms_ref, 0, pair, qa, qb)
    dka[...] = jnp.zeros_like(dka)
    dkb[...] = jnp.zeros_like(dkb)
    dva[...] = jnp.zeros_like(dva)
    lane = lax.broadcasted_iota(jnp.int32, (rows, pair_lanes), 1)

    def pick(column_a, column_b):
        at = lax.broadcasted_iota(jnp.int32, (column_a.shape[0], pair_lanes), 1)
        return jnp.where(at == 2 * pair, column_a, jnp.where(at == 2 * pair + 1, column_b, 0.0))

    def body(start, first, width):
        mask = live_mask(start_ref, start, first, width, rows)
        here, keys = pl.ds(start, rows), pl.ds(first, width)
        values = v_ref[keys, :]
        d_rows = dd[here, :]
        dq, o = [], []
        for head, (q_of, k_of, dk_of) in enumerate(((qa, ka, dka), (qb, kb, dkb))):
            own_lanes = (lane < 64) if head == 0 else (lane >= 64)
            p = probabilities(q_of[here, :], k_of[keys, :], mask)
            d_mine = jnp.where(own_lanes, d_rows, jnp.zeros_like(d_rows))
            dp = dot_nt(d_mine, values)
            delta = jnp.sum(p * dp, axis=1, keepdims=True)
            ds = (p * (dp - delta)).astype(bf16)
            dq.append(dot_nn(ds, k_of[keys, :]))
            dk_of[keys, :] += dot_tn(ds, q_of[here, :])
            low = p.astype(bf16)
            dva[keys, :] += dot_tn(low, d_mine)
            o.append(dot_nn(low, values))
        o = jnp.where(lane < 64, o[0], o[1])
        dg_ref[here, :] = (dus[here, :] * o).astype(bf16)
        u_ref[here, :] = (o * jax.nn.sigmoid(gate_ref[here, :])).astype(bf16)
        dq_ref[here, :] = (jnp.where(lane < 64, dq[0], dq[1]) * 0.125).astype(bf16)
        dcs[here, :] += pick(dq[0][:, 67:68], dq[1][:, 3:4])

    over_query_blocks(seq_len, rows, body)

    def finish(i):
        here = rows_at(i, chunk_rows)
        lanes_now = lax.broadcasted_iota(jnp.int32, (chunk_rows, pair_lanes), 1)
        ka_rows, kb_rows = dka[here, :], dkb[here, :]
        dk_ref[here, :] = jnp.where(lanes_now < 64, ka_rows, kb_rows).astype(bf16)
        dv_ref[here, :] = dva[here, :].astype(bf16)
        dcs[here, :] -= pick(ka_rows[:, 64:65], kb_rows[:, 0:1])

    each(seq_len // chunk_rows, finish)
    d_own = jnp.concatenate([r[piece, :] for r in (dq_ref, dk_ref, dv_ref, dg_ref)], axis=1)
    acc[:, :half] += dot_nt(d_own, lane_blocks(mine))
    acc[:, half:] += dot_nt(d_own, lane_blocks(theirs))

    @pl.when(pair == pl.num_programs(0) - 1)
    def _():
        running_sum(dcs, True)

        def last(i):
            here = rows_at(i, chunk_rows)
            dz_ref[here, :] = (dcs[here, :] * jax.nn.sigmoid(-z_ref[here, :])).astype(bf16)

        each(seq_len // chunk_rows, last)
        send_ref[...] = (acc[...] + dot_nt(dz_ref[piece, :], wf[...])).astype(bf16)


def ffn_forward_kernel(b_ref, wg, wu, wd, tg, tu, td, gt_ref, up_ref, send_ref, acc):
    half = b_ref.shape[1] // 2
    low, high = b_ref[:, :half], b_ref[:, half:]
    gt = dot_nn(low, wg[0]) + dot_nn(high, tg[0])
    up = dot_nn(low, wu[0]) + dot_nn(high, tu[0])
    gt_ref[...] = gt
    up_ref[...] = up
    m = (gt * jax.nn.sigmoid(gt) * up).astype(bf16)

    @pl.when(pl.program_id(0) == 0)
    def _():
        acc[...] = jnp.zeros_like(acc)

    acc[:, :half] += dot_nn(m, wd[0])
    acc[:, half:] += dot_nn(m, td[0])

    @pl.when(pl.program_id(0) == pl.num_programs(0) - 1)
    def _():
        send_ref[...] = acc[...].astype(bf16)


def inner_grads(dm, gt, up):
    sig = jax.nn.sigmoid(gt)
    d_gate = (dm * up * sig * (1.0 + gt * (1.0 - sig))).astype(bf16)
    return d_gate, (dm * (gt * sig)).astype(bf16)


def ffn_backward_kernel(g_ref, gt_ref, up_ref, wg, wu, wd, tg, tu, td, *refs):
    send_ref, acc = refs[-2:]
    half = g_ref.shape[1] // 2
    dm = dot_nt(g_ref[:, :half], wd[0]) + dot_nt(g_ref[:, half:], td[0])
    d_gate, d_up = inner_grads(dm, gt_ref[...], up_ref[...])

    @pl.when(pl.program_id(0) == 0)
    def _():
        acc[...] = jnp.zeros_like(acc)

    acc[:, :half] += dot_nt(d_gate, wg[0]) + dot_nt(d_up, wu[0])
    acc[:, half:] += dot_nt(d_gate, tg[0]) + dot_nt(d_up, tu[0])

    @pl.when(pl.program_id(0) == pl.num_programs(0) - 1)
    def _():
        send_ref[...] = acc[...].astype(bf16)


def ffn_theirs_kernel(b_ref, g_ref, wg, wu, wd, tg, tu, td, *refs):
    m_ref, dgate_ref, dup_ref, gate_out, up_out, down_out, turned = refs[-7:]
    half = b_ref.shape[1] // 2

    @pl.when(pl.program_id(0) == 0)
    def _():
        turned[...] = b_ref[:, half:].T

    def chunk(i):
        here = rows_at(i, chunk_rows)
        low, high = b_ref[here, :half], b_ref[here, half:]
        gt = dot_nn(low, wg[0]) + dot_nn(high, tg[0])
        up = dot_nn(low, wu[0]) + dot_nn(high, tu[0])
        dm = dot_nt(g_ref[here, :half], wd[0]) + dot_nt(g_ref[here, half:], td[0])
        m_ref[here, :] = (gt * jax.nn.sigmoid(gt) * up).astype(bf16)
        dgate_ref[here, :], dup_ref[here, :] = inner_grads(dm, gt, up)

    each(b_ref.shape[0] // chunk_rows, chunk)
    gate_out[...] = dot_nn(turned[...], dgate_ref[...]).astype(bf16)
    up_out[...] = dot_nn(turned[...], dup_ref[...]).astype(bf16)
    down_out[...] = dot_tn(m_ref[...], g_ref[:, half:]).astype(bf16)


def ffn_mine_kernel(b_ref, g_ref, m_ref, dgate_ref, dup_ref, gate_in, up_in, down_in, *refs):
    gate_out, up_out, down_out, turned = refs[-4:]

    @pl.when(pl.program_id(0) == 0)
    def _():
        turned[...] = b_ref[...].T

    gate_out[0] = dot_nn(turned[...], dgate_ref[...]) + gate_in[...].astype(f32)
    up_out[0] = dot_nn(turned[...], dup_ref[...]) + up_in[...].astype(f32)
    down_out[0] = dot_tn(m_ref[...], g_ref[...]) + down_in[...].astype(f32)


def attention_grads_kernel(steps, mine, *refs):
    a_ref, dq, dk, dv, dg, dz, u_ref, y_ref = refs[:8]
    received = refs[8:14] if mine else [None] * 6
    acc, acc_out = refs[-2:]
    outs = refs[-8:-2]
    turned = a_ref[...].T
    width = dq.shape[1]
    parts = [dot_nn(turned, d[...]) for d in (dq, dk, dv, dg, dz)]
    out = dot_tn(u_ref[...], y_ref[...])

    def give(values):
        for ref, value, more in zip(outs, values, received):
            total = value if more is None else value + more[...].astype(f32)
            if len(ref.shape) == 3:
                ref[0] = total.astype(ref.dtype)
            else:
                ref[...] = total.astype(ref.dtype)

    if steps == 1:
        give([*parts, out])
        return
    step = pl.program_id(0)

    @pl.when(step == 0)
    def _():
        acc[...] = jnp.zeros_like(acc)
        acc_out[...] = jnp.zeros_like(acc_out)

    for k, part in enumerate(parts):
        acc[:, k * width : k * width + part.shape[1]] += part
    acc_out[...] += out

    @pl.when(step == steps - 1)
    def _():
        found = [acc[:, k * width : k * width + p.shape[1]] for k, p in enumerate(parts)]
        give([*found, acc_out[...]])


def fixed(shape, single=True):
    zeros = (0,) * len(shape)
    if single:
        return pl.BlockSpec(shape, lambda *_: zeros, pipeline_mode=pl.Buffered(1))
    return pl.BlockSpec(shape, lambda *_: zeros)


def lanes(seq_len):
    return pl.BlockSpec((seq_len, pair_lanes), lambda p, *_: (0, p))


def lanes_read(seq_len):
    if seq_len <= 2048:
        return lanes(seq_len)
    return pl.BlockSpec((seq_len, pair_lanes), lambda p, *_: (0, p), pipeline_mode=pl.Buffered(1))


def columns_of(w, layer, width):
    return pl.BlockSpec((1, w.shape[1], width), lambda p, *_: (layer, 0, p))


def rows_of(w, layer, height):
    return pl.BlockSpec((1, height, w.shape[2]), lambda p, *_: (layer, p, 0))


def shape(dims, dtype):
    return jax.ShapeDtypeStruct(dims, dtype)


def attention_specs(parts, layer, w4, t4, wo, to, seq_len, join):
    specs = [fixed(p.shape) for p in parts]
    specs += [columns_of(w, layer, pair_lanes) for w in (*w4, *t4)]
    specs += [rows_of(wo, layer, pair_lanes), rows_of(to, layer, pair_lanes)]
    return specs


def cost(microseconds):
    return pl.CostEstimate(flops=int(microseconds * 1.1e9), bytes_accessed=0, transcendentals=0)


def token_specs(tokens):
    return [pl.BlockSpec(memory_space=pl.ANY) for _ in tokens]


def forward_own(place, parts, layer, w4, t4, wo, to, wf, bias, doc_start, piece_len):
    seq_len, width = doc_start.shape[0], parts[0].shape[1]
    local_width = wo.shape[1]
    join = len(parts) > 1
    terms = (seq_len, pair_lanes)
    outs = [shape((seq_len, local_width), bf16)] * 3 + [shape((seq_len, local_width), f32)]
    outs += [shape(terms, f32), shape(terms, bf16), shape((piece_len, width), bf16)]
    specs = [lanes(seq_len)] * 4 + [fixed(terms, False)] * 2 + [fixed((piece_len, width), False)]
    if join:
        outs, specs = [shape((seq_len, width), bf16)] + outs, [fixed((seq_len, width))] + specs
    low, piece = pltpu.VMEM((seq_len, pair_lanes), bf16), pltpu.VMEM((piece_len, pair_lanes), bf16)
    got = pl.pallas_call(
        functools.partial(forward_own_kernel, len(parts), piece_len, join),
        grid_spec=pltpu.PrefetchScalarGridSpec(
            num_scalar_prefetch=1,
            grid=(local_width // pair_lanes,),
            in_specs=attention_specs(parts, layer, w4, t4, wo, to, seq_len, join)
            + [fixed(wf.shape), fixed(bias.shape), fixed(doc_start.shape)],
            out_specs=specs,
            scratch_shapes=[piece] * 2 + [low] * 2 + [pltpu.VMEM(terms, f32), pltpu.VMEM((piece_len, width), f32)],
        ),
        out_shape=outs,
        cost_estimate=cost(19),
        compiler_params=pltpu.CompilerParams(vmem_limit_bytes=60 << 20),
    )(place, *parts, *w4, *t4, wo, to, wf, bias, doc_start)
    got = list(got)
    a = got.pop(0) if join else parts[0]
    return a, got[:6], got[6]


def attention_backward(place, parts, layer, w4, t4, wo, to, wf, saved, doc_start, piece_len):
    q, k, v, gate, z, terms = saved
    seq_len, width = doc_start.shape[0], parts[0].shape[1]
    local_width = wo.shape[1]
    join = len(parts) > 1
    outs = [shape((seq_len, local_width), bf16)] * 5 + [shape((seq_len, pair_lanes), bf16)]
    outs += [shape((piece_len, width), bf16)]
    specs = [lanes(seq_len)] * 5 + [fixed((seq_len, pair_lanes), False), fixed((piece_len, width), False)]
    if join:
        outs, specs = [shape((seq_len, width), bf16)] + outs, [fixed((seq_len, width))] + specs
    low, high = pltpu.VMEM((seq_len, pair_lanes), bf16), pltpu.VMEM((seq_len, pair_lanes), f32)
    got = pl.pallas_call(
        functools.partial(backward_kernel, len(parts), piece_len, join),
        grid_spec=pltpu.PrefetchScalarGridSpec(
            num_scalar_prefetch=1,
            grid=(local_width // pair_lanes,),
            in_specs=attention_specs(parts, layer, w4, t4, wo, to, seq_len, join)
            + [fixed(wf.shape)]
            + [lanes_read(seq_len)] * 4
            + [fixed(z.shape), fixed(terms.shape), fixed(doc_start.shape)],
            out_specs=specs,
            scratch_shapes=[low] * 5 + [high] * 5 + [pltpu.VMEM((piece_len, width), f32)],
        ),
        out_shape=outs,
        cost_estimate=cost(33),
        compiler_params=pltpu.CompilerParams(vmem_limit_bytes=60 << 20),
    )(place, *parts, *w4, *t4, wo, to, wf, q, k, v, gate, z, terms, doc_start)
    got = list(got)
    y = got.pop(0) if join else parts[0]
    return y, got[:6], got[6]


def ffn_weights(layer, w3, t3):
    specs = []
    for wg, wu, wd in (w3, t3):
        specs += [
            columns_of(wg, layer, hidden_block), columns_of(wu, layer, hidden_block), rows_of(wd, layer, hidden_block),
        ]
    return specs


def blocks_of(rows):
    return pl.BlockSpec((rows, hidden_block), lambda p, *_: (0, p))


def ffn_forward(b, layer, w3, t3):
    rows, width = b.shape
    inner = w3[2].shape[1]
    return pl.pallas_call(
        ffn_forward_kernel,
        grid=(inner // hidden_block,),
        in_specs=[fixed(b.shape)] + ffn_weights(layer, w3, t3),
        out_specs=[blocks_of(rows)] * 2 + [fixed((rows, width), False)],
        scratch_shapes=[pltpu.VMEM((rows, width), f32)],
        out_shape=[shape((rows, inner), f32)] * 2 + [shape((rows, width), bf16)],
        cost_estimate=cost(7),
        compiler_params=pltpu.CompilerParams(vmem_limit_bytes=60 << 20),
    )(b, *w3, *t3)


def ffn_backward(g, gt, up, layer, w3, t3, *tokens):
    rows, width = g.shape
    return pl.pallas_call(
        ffn_backward_kernel,
        grid=(gt.shape[1] // hidden_block,),
        in_specs=[fixed(g.shape)] + [blocks_of(rows)] * 2 + ffn_weights(layer, w3, t3) + token_specs(tokens),
        out_specs=fixed((rows, width), False),
        scratch_shapes=[pltpu.VMEM((rows, width), f32)],
        out_shape=shape((rows, width), bf16),
        cost_estimate=cost(8),
        compiler_params=pltpu.CompilerParams(vmem_limit_bytes=60 << 20),
    )(g, gt, up, *w3, *t3, *tokens)


def ffn_theirs(b, g, layer, w3, t3, *tokens):
    rows, width = b.shape
    half = width // 2
    inner = w3[2].shape[1]
    wide = pl.BlockSpec((half, hidden_block), lambda p: (0, p))
    return pl.pallas_call(
        ffn_theirs_kernel,
        grid=(inner // hidden_block,),
        in_specs=[fixed(b.shape), fixed(g.shape)] + ffn_weights(layer, w3, t3) + token_specs(tokens),
        out_specs=[blocks_of(rows)] * 3 + [wide, wide, pl.BlockSpec((hidden_block, half), lambda p: (p, 0))],
        scratch_shapes=[pltpu.VMEM((half, rows), bf16)],
        out_shape=[shape((rows, inner), bf16)] * 3
        + [shape((half, inner), bf16)] * 2
        + [shape((inner, half), bf16)],
        cost_estimate=cost(24),
        compiler_params=pltpu.CompilerParams(vmem_limit_bytes=60 << 20),
    )(b, g, *w3, *t3, *tokens)


def anywhere():
    return pl.BlockSpec(memory_space=pl.ANY)


def ffn_mine(layer, b, g, values, received, totals, *tokens):
    rows, width = b.shape
    half, inner = width // 2, values[0].shape[1]
    wide = pl.BlockSpec((half, hidden_block), lambda p: (0, p))
    tall = pl.BlockSpec((hidden_block, half), lambda p: (p, 0))
    wide_out = pl.BlockSpec((1, half, hidden_block), lambda p: (layer, 0, p))
    tall_out = pl.BlockSpec((1, hidden_block, half), lambda p: (layer, p, 0))
    return pl.pallas_call(
        ffn_mine_kernel,
        grid=(inner // hidden_block,),
        in_specs=[fixed((rows, half))] * 2
        + [blocks_of(rows)] * 3
        + [wide, wide, tall]
        + [anywhere()] * 3
        + token_specs(tokens),
        out_specs=[wide_out, wide_out, tall_out],
        out_shape=[shape(x.shape, x.dtype) for x in totals],
        scratch_shapes=[pltpu.VMEM((half, rows), bf16)],
        input_output_aliases={8: 0, 9: 1, 10: 2},
        cost_estimate=cost(9),
        compiler_params=pltpu.CompilerParams(vmem_limit_bytes=60 << 20),
    )(b, g, *values, *received, *totals, *tokens)


def attention_grads(layer, a, ds, dz, u, y, received=None, totals=None, tokens=()):
    rows, width = a.shape
    half, local_width = width // 2, u.shape[1]
    part = min(rows, 1024)
    steps = rows // part
    mine = received is not None
    side = 0 if mine else 1
    features = pl.BlockSpec((part, half), lambda p: (p, side))
    across = [pl.BlockSpec((part, x.shape[1]), lambda p: (p, 0)) for x in (*ds, dz, u)]
    specs = [features, *across, features]
    operands = [a, *ds, dz, u, y]
    flat = [(half, local_width)] * 4 + [(half, pair_lanes), (local_width, half)]
    if mine:
        specs += [fixed(x) for x in flat] + [anywhere()] * 5
        operands += [*received, *totals]
        outs = [shape(x.shape, f32) for x in totals[:4]] + [shape(flat[4], f32), shape(totals[4].shape, f32)]
        layered = pl.BlockSpec((1, half, local_width), lambda p: (layer, 0, 0))
        out_specs = [layered] * 4 + [fixed(flat[4], False)]
        out_specs += [pl.BlockSpec((1, local_width, half), lambda p: (layer, 0, 0))]
        aliases = {14: 0, 15: 1, 16: 2, 17: 3, 18: 5}
    else:
        outs, out_specs, aliases = [shape(x, bf16) for x in flat], [fixed(x, False) for x in flat], {}
    sizes = [(half, 4 * local_width + pair_lanes), (local_width, half)] if steps > 1 else [(8, 128)] * 2
    return pl.pallas_call(
        functools.partial(attention_grads_kernel, steps, mine),
        grid=(steps,),
        in_specs=specs + token_specs(tokens),
        out_specs=out_specs,
        out_shape=outs,
        scratch_shapes=[pltpu.VMEM(x, f32) for x in sizes],
        input_output_aliases=aliases,
        cost_estimate=cost(7),
        compiler_params=pltpu.CompilerParams(vmem_limit_bytes=60 << 20),
    )(*operands, *tokens)


def unset(*like):
    return pl.pallas_call(
        pass_kernel,
        out_specs=[pl.BlockSpec(memory_space=pl.ANY) for _ in like],
        out_shape=list(like),
    )()


def inverse_rms(h):
    return lax.rsqrt(jnp.mean(h * h, axis=-1, keepdims=True) + epsilon)


def norm_back(grad_normed, hidden, inverse, gain):
    scaled = hidden * inverse
    weighted = grad_normed * gain
    grad_gain = jnp.sum(grad_normed * scaled, axis=0)
    mean = jnp.mean(weighted * scaled, axis=-1, keepdims=True)
    return inverse * (weighted - scaled * mean), grad_gain


def local(
    hidden_in, segment_ids, w_query, w_key, w_value, w_gate_out, w_attn_out, w_forget, b_forget,
    gain_attn, gain_ffn, w_gate, w_up, w_down, cotangent,
):
    seq_count, piece_len, width = hidden_in.shape
    count_z, count_t = lax.axis_size("context"), lax.axis_size("tensor")
    core, z, t = lax.axis_index("fsdp"), lax.axis_index("context"), lax.axis_index("tensor")
    layers, half, local_width = w_query.shape
    heads = w_forget.shape[2]
    block = piece_len // count_t
    seq_len = piece_len * count_z
    shared_rows = count_z == 4
    place = jnp.stack([z, t]).astype(jnp.int32)

    def features(x):
        return jnp.where(core == 0, x, jnp.concatenate([x[..., half:], x[..., :half]], axis=-1))

    def own_block(x):
        return lax.dynamic_slice_in_dim(x, t * block, block, 0)

    def other(w):
        return swap(w, "fsdp", 1)

    def full(w, axis):
        return jnp.concatenate([w, other(w)], axis=axis)

    seg_all = gathered(segment_ids.reshape(1, piece_len), "context").reshape(seq_len)
    doc_start = jnp.sum((seg_all[None, :] < seg_all[:, None]).astype(jnp.int32), axis=1, keepdims=True)

    gains = full(jnp.concatenate([gain_attn, gain_ffn], axis=0), 1).astype(f32)
    hidden_rows = features(hidden_in.reshape(piece_len, width)).astype(f32)
    first_a = (hidden_rows * inverse_rms(hidden_rows) * gains[0]).astype(bf16)
    a_parts, a_far = all_rows(own_block(first_a), first_a, seg_all)

    w_forget_full = jnp.pad(full(w_forget, 1), ((0, 0), (0, 0), (0, pair_lanes - heads)))
    bias = jnp.pad(b_forget, ((0, 0), (0, pair_lanes - heads)))
    w4 = (w_query, w_key, w_value, w_gate_out)
    t4 = tuple(other(w) for w in w4)
    to = other(w_attn_out)
    w3 = (w_gate, w_up, w_down)
    t3 = tuple(other(w) for w in w3)

    hidden = own_block(hidden_rows)
    saved = []
    cotangent_rows = features(cotangent.reshape(piece_len, width))
    last = layers - 1
    grad = own_block(cotangent_rows).astype(f32)
    for layer in range(layers):
        gain_one, gain_two = gains[layer], gains[layers + layer]
        inverse_one = inverse_rms(hidden)
        if layer > 0:
            a_shard = (hidden * inverse_one * gain_one).astype(bf16)
            if shared_rows and layer == 1:
                a_shard = after(a_shard, g_last)
            a_parts, _ = all_rows(a_shard)
        forget_weights = w_forget_full[layer]
        if shared_rows and layer > 0:
            b_sent = after(saved[-1]["b_shard"], a_parts[-1])
            saved[-1]["b_rows"] = sequence_rows(b_sent)
            forget_weights = after(forget_weights, b_sent)
        a, (q, k, v, gate, forget, terms), sends = forward_own(
            place, a_parts, layer, w4, t4, w_attn_out, to, forget_weights,
            bias[layer : layer + 1], doc_start, piece_len,
        )
        if shared_rows and layer == 0:
            g_last = lax.all_gather(after(cotangent_rows, *a_far), "context", tiled=True)
        mixed = hidden + received_sum(sends)
        inverse_two = inverse_rms(mixed)
        b_shard = (mixed * inverse_two * gain_two).astype(bf16)
        b = gathered(b_shard, "tensor")
        gt, up, sends = ffn_forward(b, layer, w3, t3)
        saved.append(
            dict(hidden=hidden, inverse_one=inverse_one, a=a, kept=(q, k, v, gate, forget, terms), mixed=mixed,
                 inverse_two=inverse_two, b=b, b_shard=b_shard, gt=gt, up=up)
        )
        if layer < last:
            hidden = mixed + received_sum(sends)

    def finish(x):
        return features(gathered(x.astype(bf16), "tensor")).reshape(1, piece_len, width)

    last_sends = sends
    wide = shape((layers, half, local_width), f32)
    inner = shape((layers, half, w_gate.shape[2]), f32)
    results = list(
        unset(
            wide, wide, wide, wide, shape((layers, local_width, half), f32),
            inner, inner, shape((layers, w_down.shape[1], half), f32),
        )
    )
    small = [[None] * layers for _ in range(2)]
    gain_grads = [None] * (2 * layers)

    def ffn_theirs_of(layer, *tokens):
        s = saved[layer]
        values = ffn_theirs(s["b_rows"], s["g_rows"], layer, w3, t3, *tokens)
        s.update(values=values[:3], ffn_received=[other(x) for x in values[3:]])

    def ffn_mine_of(layer, *tokens):
        s = saved[layer]
        received = s["ffn_received"]
        results[5:] = ffn_mine(layer, s["b_rows"], s["g_rows"], s["values"], received, results[5:], *tokens)

    def attention_theirs_of(layer, *tokens):
        s = saved[layer]
        s["theirs"] = attention_grads(layer, *s["grads"], tokens=tokens)
        s["received"] = [other(x) for x in s["theirs"]]
        bias_grad = jnp.sum(s["grads"][2].astype(f32), axis=0)[:heads]
        small[1][layer] = bias_grad + other(bias_grad)

    def attention_mine_of(layer, *tokens):
        s = saved[layer]
        found = attention_grads(layer, *s["grads"], s["received"], results[:5], tokens)
        results[:5] = [*found[:4], found[5]]
        small[0][layer] = found[4][:, :heads]

    for layer in reversed(range(layers)):
        s = saved[layer]
        gain_one, gain_two = gains[layer], gains[layers + layer]
        tokens = ()
        if layer == last:
            g = cotangent_rows
        else:
            g_shard = grad.astype(bf16)
            g = gathered(g_shard, "tensor")
            tokens = (saved[layer + 1]["theirs"][0],)
        if not shared_rows:
            s.update(b_rows=s["b"], g_rows=g)
        sends = ffn_backward(g, s["gt"], s["up"], layer, w3, t3, *tokens)
        if layer < last:
            sends = after(sends, *saved[layer + 1]["received"])
        back, gain_grads[layers + layer] = norm_back(received_sum(sends), s["mixed"], s["inverse_two"], gain_two)
        grad_mixed = grad + back
        y_shard = grad_mixed.astype(bf16)
        if layer < last:
            attention_mine_of(layer + 1)
            y_shard = after(y_shard, results[0])
        elif shared_rows:
            y_shard = after(y_shard, *[x["b_rows"] for x in saved[:-1]])
        y_parts, y_far = all_rows(y_shard, together=layer < last)
        tokens = ()
        if layer < last:
            above = saved[layer + 1]
            ffn_theirs_of(layer + 1, *y_far, y_parts[0])
            tokens = (above["values"][0],)
        kept = (*s["kept"][:-1], after(s["kept"][-1], *tokens))
        y, (dq, dk, dv, dg, u, dz), sends = attention_backward(
            place, y_parts, layer, w4, t4, w_attn_out, to, w_forget_full[layer], kept, doc_start, piece_len,
        )
        token = y_parts[-1]
        if shared_rows and layer == last:
            s.update(b_rows=sequence_rows(after(s["b_shard"], *y_parts)), g_rows=g_last)
        elif shared_rows:
            s["g_rows"] = sequence_rows(after(g_shard, above["values"][0]))
        s["grads"] = (s["a"], (dq, dk, dv, dg), dz, u, y)
        if layer > 0:
            attention_theirs_of(layer)
        back, gain_grads[layer] = norm_back(received_sum(sends), s["hidden"], s["inverse_one"], gain_one)
        grad = grad_mixed + back

    block_sum = own_block(last_sends).astype(f32) + saved[last]["mixed"]
    with_rows = lax.dynamic_update_slice_in_dim(last_sends, block_sum.astype(bf16), t * block, 0)
    output = lax.psum(after(with_rows, sends), "tensor")
    for layer in reversed(range(1, layers)):
        ffn_mine_of(layer, sends)
    attention_theirs_of(0, sends)
    gain_total = after(jnp.stack(gain_grads).reshape(1, -1), *([results[5]] if layers > 1 else []))
    for axis in (("context", "tensor"),) if shared_rows else ("context", "tensor"):
        gain_total = jnp.sum(gathered(gain_total, axis), axis=0, keepdims=True)
    gain_total = gain_total.reshape(2 * layers, width)
    gain_total = gain_total[:, :half] + other(gain_total[:, half:])
    grad_input = finish(after(grad, saved[0]["theirs"][0]))
    ffn_theirs_of(0)
    attention_mine_of(0, gain_total, saved[0]["values"][0])
    ffn_mine_of(0)
    if not shared_rows:
        results[5:] = [lax.psum(x, "context") for x in results[5:]]
    output = features(after(output, saved[0]["values"][0])).reshape(1, piece_len, width)
    return (
        output, grad_input, *results[:5], jnp.stack(small[0]), jnp.stack(small[1]),
        gain_total[:layers], gain_total[layers:], *results[5:],
    )


def solution(mesh):
    rows = P("fsdp", "context", None)
    wide, tall = P(None, "fsdp", "tensor"), P(None, "tensor", "fsdp")
    heads, gain = P(None, "tensor"), P(None, "fsdp")
    return jax.shard_map(
        local,
        mesh=mesh,
        in_specs=(
            rows, P("fsdp", "context"), wide, wide, wide, wide, tall, wide, heads, gain, gain, wide, wide, tall, rows,
        ),
        out_specs=(rows, rows, wide, wide, wide, wide, tall, wide, heads, gain, gain, wide, wide, tall),
        check_vma=False,
    )
```

```python
import functools

import jax
import jax.numpy as jnp
from jax import lax
from jax.experimental import pallas as pl
from jax.experimental.pallas import tpu as pltpu
from jax.sharding import PartitionSpec as P

epsilon = 1e-06
masked_value = -1e30
bf16 = jnp.bfloat16
f32 = jnp.float32
pair_lanes = 128
hidden_block = 256
chunk_rows = 256


def query_rows(seq_len):
    return 256 if seq_len <= 2048 else 128


def swap(x, axis, k):
    n = lax.axis_size(axis)
    return lax.ppermute(x, axis, [(i, i ^ k) for i in range(n)])


def pass_kernel(*refs):
    pass


def after(x, *tokens):
    if not tokens:
        return x
    anywhere = pl.BlockSpec(memory_space=pl.ANY)
    return pl.pallas_call(
        pass_kernel,
        in_specs=[anywhere] * (1 + len(tokens)),
        out_specs=anywhere,
        out_shape=jax.ShapeDtypeStruct(x.shape, x.dtype),
        input_output_aliases={0: 0},
    )(x, *tokens)


def gathered(block, axis):
    count = lax.axis_size(axis)
    copies = jnp.broadcast_to(block[None], (count,) + block.shape)
    return lax.all_to_all(copies, axis, 0, 0, tiled=True).reshape((-1,) + block.shape[1:])


def sequence_rows(shard):
    return lax.all_gather(shard, ("context", "tensor"), tiled=True)


def near_rows(own):
    return swap(own, "context", 1)


def far_blocks(shard, *tokens):
    shard = after(shard, *tokens)
    return swap(shard, "context", 2), swap(shard, "context", 3)


def all_rows(shard, own=None, first=(), second_stage=(), together=False):
    if own is None:
        own = gathered(shard, "tensor")
    if lax.axis_size("context") != 4:
        return (lax.all_gather(own, "context", tiled=True),), ()
    second, third = far_blocks(shard, *first)
    near = near_rows(own)
    if together:
        block, width = shard.shape
        far = gathered(after(jnp.concatenate([second, third], axis=0), own), "tensor")
        return (own, near, far.reshape(-1, 2, block, width)), (second, third)
    second = after(second, *second_stage)
    parts = [own, near]
    for far in (second, third):
        parts += [far] + [swap(far, "tensor", k) for k in range(1, lax.axis_size("tensor"))]
    return tuple(parts), (second, third)


def received_sum(sends):
    count = lax.axis_size("tensor")
    got = lax.all_to_all(sends.reshape(count, -1, sends.shape[1]), "tensor", 0, 0, tiled=True)
    return jnp.sum(got.astype(f32), axis=0)


def dot_nt(a, b):
    return lax.dot_general(a, b, (((1,), (1,)), ((), ())), preferred_element_type=f32)


def dot_tn(a, b):
    return lax.dot_general(a, b, (((0,), (0,)), ((), ())), preferred_element_type=f32)


def dot_nn(a, b):
    return jnp.dot(a, b, preferred_element_type=f32)


def each(count, body):
    if count <= 4:
        for i in range(count):
            body(i)
        return

    def one(i, carry):
        body(i)
        return carry

    lax.fori_loop(0, count, one, 0)


def rows_at(i, rows):
    start = i * rows
    return pl.ds(start if isinstance(start, int) else pl.multiple_of(start, rows), rows)


def assemble(parts, whole_ref, place_ref):
    z, t = place_ref[0], place_ref[1]
    piece, blocks_seen, piece_len = 0, 0, parts[0].shape[0]
    for part in parts:
        if len(part.shape) == 4:
            blocks, pieces, block = part.shape[:3]
            for p in range(pieces):
                for b in range(blocks):
                    at = pl.multiple_of((z ^ (piece + p)) * piece_len + b * block, block)
                    whole_ref[pl.ds(at, block), :] = part[b, p]
            piece += pieces
            continue
        rows = part.shape[0]
        if rows == piece_len:
            at = pl.multiple_of((z ^ piece) * piece_len, piece_len)
            piece += 1
        else:
            at = pl.multiple_of((z ^ piece) * piece_len + (t ^ blocks_seen) * rows, rows)
            blocks_seen += 1
            if blocks_seen * rows == piece_len:
                piece, blocks_seen = piece + 1, 0
        whole_ref[pl.ds(at, rows), :] = part[...]


def triangle(rows, reverse):
    row = lax.broadcasted_iota(jnp.int32, (rows, rows), 0)
    column = lax.broadcasted_iota(jnp.int32, (rows, rows), 1)
    return jnp.where((column >= row) if reverse else (column <= row), 1.0, 0.0).astype(bf16)


def running_sum(ref, reverse):
    rows = chunk_rows
    ones = triangle(rows, reverse)
    count = ref.shape[0] // rows
    edge = 0 if reverse else rows - 1

    def chunk(i, carry):
        here = pl.ds(pl.multiple_of((count - 1 - i if reverse else i) * rows, rows), rows)
        high, middle, lowest = three_parts(ref[here, :])
        total = dot_nn(ones, high) + dot_nn(ones, middle) + dot_nn(ones, lowest) + carry
        ref[here, :] = total
        return total[edge : edge + 1, :]

    lax.fori_loop(0, count, chunk, jnp.zeros((1, ref.shape[1]), f32), unroll=count <= 4)


def log_sigmoid(z):
    e = jnp.exp(-jnp.abs(z))
    small = e * (1.0 - e * (1 / 2 - e * (1 / 3 - e * (1 / 4 - e * (1 / 5 - e * (1 / 6 - e * (1 / 7)))))))
    return jnp.minimum(z, 0.0) - jnp.where(e < 0.0625, small, jnp.log(1.0 + e))


def three_parts(x):
    high = x.astype(bf16)
    middle = (x - high.astype(f32)).astype(bf16)
    return high, middle, (x - high.astype(f32) - middle.astype(f32)).astype(bf16)


def decay_side(terms, pair, key_side):
    row = lax.broadcasted_iota(jnp.int32, (pair_lanes, pair_lanes), 0)
    lane = lax.broadcasted_iota(jnp.int32, (pair_lanes, pair_lanes), 1)
    spot = lane & 63
    term = spot if key_side else spot - 3
    head = jnp.where(lane >= 64, 2 * pair, 2 * pair + 1)
    chosen = (term >= 0) & (term < 3) & (row == 8 * term + head)
    pick = jnp.where(chosen, -1.0 if key_side else 1.0, 0.0).astype(bf16)
    lanes_now = lax.broadcasted_iota(jnp.int32, (1, pair_lanes), 1) & 63
    other = lanes_now - 3 if key_side else lanes_now
    ones = jnp.where((other >= 0) & (other < 3), 1.0, 0.0)
    return (dot_nn(terms, pick) + ones).astype(bf16)


def mix_keys(k_ref, terms_ref, pair, ka, kb):
    def mix(i):
        here = rows_at(i, chunk_rows)
        lane = lax.broadcasted_iota(jnp.int32, (chunk_rows, pair_lanes), 1)
        k, side = k_ref[here, :], decay_side(terms_ref[here, :], pair, True)
        ka[here, :] = jnp.where(lane < 64, k, side)
        kb[here, :] = jnp.where(lane < 64, side, k)

    each(k_ref.shape[0] // chunk_rows, mix)


def mix_queries(q_ref, terms_ref, start, pair, qa, qb):
    def mix(i):
        here = rows_at(i, chunk_rows)
        lane = lax.broadcasted_iota(jnp.int32, (chunk_rows, pair_lanes), 1)
        q = (q_ref[here, :].astype(f32) * 0.125).astype(bf16)
        terms = terms_ref[pl.ds(pl.multiple_of(start + i * chunk_rows, chunk_rows), chunk_rows), :]
        side = decay_side(terms, pair, False)
        qa[here, :] = jnp.where(lane < 64, q, side)
        qb[here, :] = jnp.where(lane < 64, side, q)

    each(q_ref.shape[0] // chunk_rows, mix)


def live_mask(start_ref, start, first, width, rows):
    key_pos = first + lax.broadcasted_iota(jnp.int32, (rows, width), 1)
    query_pos = start + lax.broadcasted_iota(jnp.int32, (rows, width), 0)
    doc_start = start_ref[pl.ds(start, rows), :]
    return (key_pos <= query_pos) & (key_pos >= doc_start)


def over_query_blocks(seq_len, rows, body):
    before = seq_len // 2
    if seq_len // rows <= 4:
        for start in range(0, seq_len, rows):
            first = max(0, start - before)
            body(start, first, start + rows - first)
        return
    width = before + rows

    def one(i, carry):
        start = pl.multiple_of(i * rows, rows)
        first = pl.multiple_of(jnp.maximum(start - before, 0), rows)
        body(start, first, width)
        return carry

    lax.fori_loop(0, seq_len // rows, one, 0)


def probabilities(q_rows, k_rows, mask):
    s = jnp.where(mask, dot_nt(q_rows, k_rows), masked_value)
    e = jnp.exp(s - jnp.max(s, axis=1, keepdims=True))
    return e * (1.0 / jnp.sum(e, axis=1, keepdims=True))


def lane_blocks(refs):
    return jnp.concatenate([r[0] for r in refs], axis=1)


def forward_own_kernel(count_parts, piece_len, join, *refs):
    place_ref, parts, refs = refs[0], refs[1 : 1 + count_parts], list(refs[1 + count_parts :])
    (wq, wk, wv, wg), (tq, tk, tv, tg) = refs[:4], refs[4:8]
    wo, to, wf, bias, start_ref = refs[8:13]
    refs = refs[13:]
    a_ref = refs.pop(0) if join else parts[0]
    q_ref, k_ref, v_ref, gate_ref, z_ref, terms_ref, send_ref, qa, qb, ka, kb, decay, acc = refs
    pair = pl.program_id(0)
    seq_len, half = a_ref.shape[0], a_ref.shape[1] // 2
    piece_start = pl.multiple_of(place_ref[0] * piece_len, piece_len)

    @pl.when(pair == 0)
    def _():
        if join:
            assemble(parts, a_ref, place_ref)
        acc[...] = jnp.zeros_like(acc)

        def gates(i):
            here = rows_at(i, chunk_rows)
            z = dot_nn(a_ref[here, :], wf[...]) + bias[...]
            z_ref[here, :] = z
            decay[here, :] = log_sigmoid(z)

        each(seq_len // chunk_rows, gates)
        running_sum(decay, False)

        def split(i):
            here = rows_at(i, chunk_rows)
            lane = lax.broadcasted_iota(jnp.int32, (chunk_rows, pair_lanes), 1)
            high, middle, lowest = (x.astype(f32) for x in three_parts(decay[here, :]))
            later = jnp.where(lane < 16, pltpu.roll(middle, 8, 1), pltpu.roll(lowest, 16, 1))
            terms = jnp.where(lane < 8, high, later)
            terms_ref[here, :] = jnp.where(lane < 24, terms, 0.0).astype(bf16)

        each(seq_len // chunk_rows, split)

    w_mine, w_theirs = lane_blocks((wq, wk, wv, wg)), lane_blocks((tq, tk, tv, tg))

    def project(i):
        here = rows_at(i, chunk_rows)
        out = dot_nn(a_ref[here, :half], w_mine) + dot_nn(a_ref[here, half:], w_theirs)
        q_ref[here, :] = out[:, :128].astype(bf16)
        k_ref[here, :] = out[:, 128:256].astype(bf16)
        v_ref[here, :] = out[:, 256:384].astype(bf16)
        gate_ref[here, :] = out[:, 384:]

    each(seq_len // chunk_rows, project)
    piece = pl.ds(piece_start, piece_len)
    gate = jax.nn.sigmoid(gate_ref[piece, :])
    mix_keys(k_ref, terms_ref, pair, ka, kb)
    mix_queries(q_ref.at[piece, :], terms_ref, piece_start, pair, qa, qb)
    before = seq_len // 2
    for s in range(0, piece_len, query_rows(seq_len)):
        rows = query_rows(seq_len)
        width = before + rows
        start = pl.multiple_of(piece_start + s, rows)
        first = pl.multiple_of(jnp.maximum(start - before, 0), rows)
        mask = live_mask(start_ref, start, first, width, rows)
        keys = pl.ds(first, width)
        out = []
        for q_of, k_of in ((qa, ka), (qb, kb)):
            p = probabilities(q_of[s : s + rows, :], k_of[keys, :], mask).astype(bf16)
            out.append(dot_nn(p, v_ref[keys, :]))
        lane = lax.broadcasted_iota(jnp.int32, (rows, pair_lanes), 1)
        u = (jnp.where(lane < 64, out[0], out[1]) * gate[s : s + rows, :]).astype(bf16)
        acc[s : s + rows, :half] += dot_nn(u, wo[0])
        acc[s : s + rows, half:] += dot_nn(u, to[0])

    @pl.when(pair == pl.num_programs(0) - 1)
    def _():
        send_ref[...] = acc[...].astype(bf16)


def backward_kernel(count_parts, piece_len, join, *refs):
    place_ref, parts, refs = refs[0], refs[1 : 1 + count_parts], list(refs[1 + count_parts :])
    mine, theirs, (wo, to, wf) = refs[:4], refs[4:8], refs[8:11]
    q_ref, k_ref, v_ref, gate_ref, z_ref, terms_ref, start_ref = refs[11:18]
    refs = refs[18:]
    y_ref = refs.pop(0) if join else parts[0]
    dq_ref, dk_ref, dv_ref, dg_ref, u_ref, dz_ref, send_ref = refs[:7]
    qa, qb, ka, kb, dd, dus, dka, dkb, dva, dcs, acc = refs[7:]
    pair = pl.program_id(0)
    seq_len, half = y_ref.shape[0], y_ref.shape[1] // 2
    rows = query_rows(seq_len)
    piece = pl.ds(pl.multiple_of(place_ref[0] * piece_len, piece_len), piece_len)

    @pl.when(pair == 0)
    def _():
        if join:
            assemble(parts, y_ref, place_ref)
        acc[...] = jnp.zeros_like(acc)
        dcs[...] = jnp.zeros_like(dcs)

    def gates(i):
        here = rows_at(i, chunk_rows)
        du = dot_nt(y_ref[here, :half], wo[0]) + dot_nt(y_ref[here, half:], to[0])
        sig = jax.nn.sigmoid(gate_ref[here, :])
        dd[here, :] = (du * sig).astype(bf16)
        dus[here, :] = du * sig * (1.0 - sig)

    each(seq_len // chunk_rows, gates)
    mix_keys(k_ref, terms_ref, pair, ka, kb)
    mix_queries(q_ref, terms_ref, 0, pair, qa, qb)
    dka[...] = jnp.zeros_like(dka)
    dkb[...] = jnp.zeros_like(dkb)
    dva[...] = jnp.zeros_like(dva)
    lane = lax.broadcasted_iota(jnp.int32, (rows, pair_lanes), 1)

    def pick(column_a, column_b):
        at = lax.broadcasted_iota(jnp.int32, (column_a.shape[0], pair_lanes), 1)
        return jnp.where(at == 2 * pair, column_a, jnp.where(at == 2 * pair + 1, column_b, 0.0))

    def body(start, first, width):
        mask = live_mask(start_ref, start, first, width, rows)
        here, keys = pl.ds(start, rows), pl.ds(first, width)
        values = v_ref[keys, :]
        d_rows = dd[here, :]
        dq, o = [], []
        for head, (q_of, k_of, dk_of) in enumerate(((qa, ka, dka), (qb, kb, dkb))):
            own_lanes = (lane < 64) if head == 0 else (lane >= 64)
            p = probabilities(q_of[here, :], k_of[keys, :], mask)
            d_mine = jnp.where(own_lanes, d_rows, jnp.zeros_like(d_rows))
            dp = dot_nt(d_mine, values)
            delta = jnp.sum(p * dp, axis=1, keepdims=True)
            ds = (p * (dp - delta)).astype(bf16)
            dq.append(dot_nn(ds, k_of[keys, :]))
            dk_of[keys, :] += dot_tn(ds, q_of[here, :])
            low = p.astype(bf16)
            dva[keys, :] += dot_tn(low, d_mine)
            o.append(dot_nn(low, values))
        o = jnp.where(lane < 64, o[0], o[1])
        dg_ref[here, :] = (dus[here, :] * o).astype(bf16)
        u_ref[here, :] = (o * jax.nn.sigmoid(gate_ref[here, :])).astype(bf16)
        dq_ref[here, :] = (jnp.where(lane < 64, dq[0], dq[1]) * 0.125).astype(bf16)
        dcs[here, :] += pick(dq[0][:, 67:68], dq[1][:, 3:4])

    over_query_blocks(seq_len, rows, body)

    def finish(i):
        here = rows_at(i, chunk_rows)
        lanes_now = lax.broadcasted_iota(jnp.int32, (chunk_rows, pair_lanes), 1)
        ka_rows, kb_rows = dka[here, :], dkb[here, :]
        dk_ref[here, :] = jnp.where(lanes_now < 64, ka_rows, kb_rows).astype(bf16)
        dv_ref[here, :] = dva[here, :].astype(bf16)
        dcs[here, :] -= pick(ka_rows[:, 64:65], kb_rows[:, 0:1])

    each(seq_len // chunk_rows, finish)
    d_own = jnp.concatenate([r[piece, :] for r in (dq_ref, dk_ref, dv_ref, dg_ref)], axis=1)
    acc[:, :half] += dot_nt(d_own, lane_blocks(mine))
    acc[:, half:] += dot_nt(d_own, lane_blocks(theirs))

    @pl.when(pair == pl.num_programs(0) - 1)
    def _():
        running_sum(dcs, True)

        def last(i):
            here = rows_at(i, chunk_rows)
            dz_ref[here, :] = (dcs[here, :] * jax.nn.sigmoid(-z_ref[here, :])).astype(bf16)

        each(seq_len // chunk_rows, last)
        send_ref[...] = (acc[...] + dot_nt(dz_ref[piece, :], wf[...])).astype(bf16)


def ffn_forward_kernel(b_ref, wg, wu, wd, tg, tu, td, gt_ref, up_ref, send_ref, acc):
    half = b_ref.shape[1] // 2
    low, high = b_ref[:, :half], b_ref[:, half:]
    gt = dot_nn(low, wg[0]) + dot_nn(high, tg[0])
    up = dot_nn(low, wu[0]) + dot_nn(high, tu[0])
    gt_ref[...] = gt
    up_ref[...] = up
    m = (gt * jax.nn.sigmoid(gt) * up).astype(bf16)

    @pl.when(pl.program_id(0) == 0)
    def _():
        acc[...] = jnp.zeros_like(acc)

    acc[:, :half] += dot_nn(m, wd[0])
    acc[:, half:] += dot_nn(m, td[0])

    @pl.when(pl.program_id(0) == pl.num_programs(0) - 1)
    def _():
        send_ref[...] = acc[...].astype(bf16)


def inner_grads(dm, gt, up):
    sig = jax.nn.sigmoid(gt)
    d_gate = (dm * up * sig * (1.0 + gt * (1.0 - sig))).astype(bf16)
    return d_gate, (dm * (gt * sig)).astype(bf16)


def ffn_backward_kernel(g_ref, gt_ref, up_ref, wg, wu, wd, tg, tu, td, *refs):
    send_ref, acc = refs[-2:]
    half = g_ref.shape[1] // 2
    dm = dot_nt(g_ref[:, :half], wd[0]) + dot_nt(g_ref[:, half:], td[0])
    d_gate, d_up = inner_grads(dm, gt_ref[...], up_ref[...])

    @pl.when(pl.program_id(0) == 0)
    def _():
        acc[...] = jnp.zeros_like(acc)

    acc[:, :half] += dot_nt(d_gate, wg[0]) + dot_nt(d_up, wu[0])
    acc[:, half:] += dot_nt(d_gate, tg[0]) + dot_nt(d_up, tu[0])

    @pl.when(pl.program_id(0) == pl.num_programs(0) - 1)
    def _():
        send_ref[...] = acc[...].astype(bf16)


def ffn_theirs_kernel(b_ref, g_ref, wg, wu, wd, tg, tu, td, *refs):
    m_ref, dgate_ref, dup_ref, gate_out, up_out, down_out, turned = refs[-7:]
    half = b_ref.shape[1] // 2

    @pl.when(pl.program_id(0) == 0)
    def _():
        turned[...] = b_ref[:, half:].T

    def chunk(i):
        here = rows_at(i, chunk_rows)
        low, high = b_ref[here, :half], b_ref[here, half:]
        gt = dot_nn(low, wg[0]) + dot_nn(high, tg[0])
        up = dot_nn(low, wu[0]) + dot_nn(high, tu[0])
        dm = dot_nt(g_ref[here, :half], wd[0]) + dot_nt(g_ref[here, half:], td[0])
        m_ref[here, :] = (gt * jax.nn.sigmoid(gt) * up).astype(bf16)
        dgate_ref[here, :], dup_ref[here, :] = inner_grads(dm, gt, up)

    each(b_ref.shape[0] // chunk_rows, chunk)
    gate_out[...] = dot_nn(turned[...], dgate_ref[...]).astype(bf16)
    up_out[...] = dot_nn(turned[...], dup_ref[...]).astype(bf16)
    down_out[...] = dot_tn(m_ref[...], g_ref[:, half:]).astype(bf16)


def ffn_mine_kernel(b_ref, g_ref, m_ref, dgate_ref, dup_ref, gate_in, up_in, down_in, *refs):
    gate_out, up_out, down_out, turned = refs[-4:]

    @pl.when(pl.program_id(0) == 0)
    def _():
        turned[...] = b_ref[...].T

    gate_out[0] = dot_nn(turned[...], dgate_ref[...]) + gate_in[...].astype(f32)
    up_out[0] = dot_nn(turned[...], dup_ref[...]) + up_in[...].astype(f32)
    down_out[0] = dot_tn(m_ref[...], g_ref[...]) + down_in[...].astype(f32)


def attention_grads_kernel(steps, mine, *refs):
    a_ref, dq, dk, dv, dg, dz, u_ref, y_ref = refs[:8]
    received = refs[8:14] if mine else [None] * 6
    acc, acc_out = refs[-2:]
    outs = refs[-8:-2]
    turned = a_ref[...].T
    width = dq.shape[1]
    parts = [dot_nn(turned, d[...]) for d in (dq, dk, dv, dg, dz)]
    out = dot_tn(u_ref[...], y_ref[...])

    def give(values):
        for ref, value, more in zip(outs, values, received):
            total = value if more is None else value + more[...].astype(f32)
            if len(ref.shape) == 3:
                ref[0] = total.astype(ref.dtype)
            else:
                ref[...] = total.astype(ref.dtype)

    if steps == 1:
        give([*parts, out])
        return
    step = pl.program_id(0)

    @pl.when(step == 0)
    def _():
        acc[...] = jnp.zeros_like(acc)
        acc_out[...] = jnp.zeros_like(acc_out)

    for k, part in enumerate(parts):
        acc[:, k * width : k * width + part.shape[1]] += part
    acc_out[...] += out

    @pl.when(step == steps - 1)
    def _():
        found = [acc[:, k * width : k * width + p.shape[1]] for k, p in enumerate(parts)]
        give([*found, acc_out[...]])


def fixed(shape, single=True):
    zeros = (0,) * len(shape)
    if single:
        return pl.BlockSpec(shape, lambda *_: zeros, pipeline_mode=pl.Buffered(1))
    return pl.BlockSpec(shape, lambda *_: zeros)


def lanes(seq_len):
    return pl.BlockSpec((seq_len, pair_lanes), lambda p, *_: (0, p))


def lanes_read(seq_len):
    if seq_len <= 2048:
        return lanes(seq_len)
    return pl.BlockSpec((seq_len, pair_lanes), lambda p, *_: (0, p), pipeline_mode=pl.Buffered(1))


def columns_of(w, layer, width):
    return pl.BlockSpec((1, w.shape[1], width), lambda p, *_: (layer, 0, p))


def rows_of(w, layer, height):
    return pl.BlockSpec((1, height, w.shape[2]), lambda p, *_: (layer, p, 0))


def shape(dims, dtype):
    return jax.ShapeDtypeStruct(dims, dtype)


def attention_specs(parts, layer, w4, t4, wo, to, seq_len, join):
    specs = [fixed(p.shape) for p in parts]
    specs += [columns_of(w, layer, pair_lanes) for w in (*w4, *t4)]
    specs += [rows_of(wo, layer, pair_lanes), rows_of(to, layer, pair_lanes)]
    return specs


def cost(microseconds):
    return pl.CostEstimate(flops=int(microseconds * 1.1e9), bytes_accessed=0, transcendentals=0)


def token_specs(tokens):
    return [pl.BlockSpec(memory_space=pl.ANY) for _ in tokens]


def forward_own(place, parts, layer, w4, t4, wo, to, wf, bias, doc_start, piece_len):
    seq_len, width = doc_start.shape[0], parts[0].shape[1]
    local_width = wo.shape[1]
    join = len(parts) > 1
    terms = (seq_len, pair_lanes)
    outs = [shape((seq_len, local_width), bf16)] * 3 + [shape((seq_len, local_width), f32)]
    outs += [shape(terms, f32), shape(terms, bf16), shape((piece_len, width), bf16)]
    specs = [lanes(seq_len)] * 4 + [fixed(terms, False)] * 2 + [fixed((piece_len, width), False)]
    if join:
        outs, specs = [shape((seq_len, width), bf16)] + outs, [fixed((seq_len, width))] + specs
    low, piece = pltpu.VMEM((seq_len, pair_lanes), bf16), pltpu.VMEM((piece_len, pair_lanes), bf16)
    got = pl.pallas_call(
        functools.partial(forward_own_kernel, len(parts), piece_len, join),
        grid_spec=pltpu.PrefetchScalarGridSpec(
            num_scalar_prefetch=1,
            grid=(local_width // pair_lanes,),
            in_specs=attention_specs(parts, layer, w4, t4, wo, to, seq_len, join)
            + [fixed(wf.shape), fixed(bias.shape), fixed(doc_start.shape)],
            out_specs=specs,
            scratch_shapes=[piece] * 2 + [low] * 2 + [pltpu.VMEM(terms, f32), pltpu.VMEM((piece_len, width), f32)],
        ),
        out_shape=outs,
        cost_estimate=cost(19),
        compiler_params=pltpu.CompilerParams(vmem_limit_bytes=60 << 20),
    )(place, *parts, *w4, *t4, wo, to, wf, bias, doc_start)
    got = list(got)
    a = got.pop(0) if join else parts[0]
    return a, got[:6], got[6]


def attention_backward(place, parts, layer, w4, t4, wo, to, wf, saved, doc_start, piece_len):
    q, k, v, gate, z, terms = saved
    seq_len, width = doc_start.shape[0], parts[0].shape[1]
    local_width = wo.shape[1]
    join = len(parts) > 1
    outs = [shape((seq_len, local_width), bf16)] * 5 + [shape((seq_len, pair_lanes), bf16)]
    outs += [shape((piece_len, width), bf16)]
    specs = [lanes(seq_len)] * 5 + [fixed((seq_len, pair_lanes), False), fixed((piece_len, width), False)]
    if join:
        outs, specs = [shape((seq_len, width), bf16)] + outs, [fixed((seq_len, width))] + specs
    low, high = pltpu.VMEM((seq_len, pair_lanes), bf16), pltpu.VMEM((seq_len, pair_lanes), f32)
    got = pl.pallas_call(
        functools.partial(backward_kernel, len(parts), piece_len, join),
        grid_spec=pltpu.PrefetchScalarGridSpec(
            num_scalar_prefetch=1,
            grid=(local_width // pair_lanes,),
            in_specs=attention_specs(parts, layer, w4, t4, wo, to, seq_len, join)
            + [fixed(wf.shape)]
            + [lanes_read(seq_len)] * 4
            + [fixed(z.shape), fixed(terms.shape), fixed(doc_start.shape)],
            out_specs=specs,
            scratch_shapes=[low] * 5 + [high] * 5 + [pltpu.VMEM((piece_len, width), f32)],
        ),
        out_shape=outs,
        cost_estimate=cost(33),
        compiler_params=pltpu.CompilerParams(vmem_limit_bytes=60 << 20),
    )(place, *parts, *w4, *t4, wo, to, wf, q, k, v, gate, z, terms, doc_start)
    got = list(got)
    y = got.pop(0) if join else parts[0]
    return y, got[:6], got[6]


def ffn_weights(layer, w3, t3):
    specs = []
    for wg, wu, wd in (w3, t3):
        specs += [
            columns_of(wg, layer, hidden_block), columns_of(wu, layer, hidden_block), rows_of(wd, layer, hidden_block),
        ]
    return specs


def blocks_of(rows):
    return pl.BlockSpec((rows, hidden_block), lambda p, *_: (0, p))


def ffn_forward(b, layer, w3, t3):
    rows, width = b.shape
    inner = w3[2].shape[1]
    return pl.pallas_call(
        ffn_forward_kernel,
        grid=(inner // hidden_block,),
        in_specs=[fixed(b.shape)] + ffn_weights(layer, w3, t3),
        out_specs=[blocks_of(rows)] * 2 + [fixed((rows, width), False)],
        scratch_shapes=[pltpu.VMEM((rows, width), f32)],
        out_shape=[shape((rows, inner), f32)] * 2 + [shape((rows, width), bf16)],
        cost_estimate=cost(7),
        compiler_params=pltpu.CompilerParams(vmem_limit_bytes=60 << 20),
    )(b, *w3, *t3)


def ffn_backward(g, gt, up, layer, w3, t3, *tokens):
    rows, width = g.shape
    return pl.pallas_call(
        ffn_backward_kernel,
        grid=(gt.shape[1] // hidden_block,),
        in_specs=[fixed(g.shape)] + [blocks_of(rows)] * 2 + ffn_weights(layer, w3, t3) + token_specs(tokens),
        out_specs=fixed((rows, width), False),
        scratch_shapes=[pltpu.VMEM((rows, width), f32)],
        out_shape=shape((rows, width), bf16),
        cost_estimate=cost(8),
        compiler_params=pltpu.CompilerParams(vmem_limit_bytes=60 << 20),
    )(g, gt, up, *w3, *t3, *tokens)


def ffn_theirs(b, g, layer, w3, t3, *tokens):
    rows, width = b.shape
    half = width // 2
    inner = w3[2].shape[1]
    wide = pl.BlockSpec((half, hidden_block), lambda p: (0, p))
    return pl.pallas_call(
        ffn_theirs_kernel,
        grid=(inner // hidden_block,),
        in_specs=[fixed(b.shape), fixed(g.shape)] + ffn_weights(layer, w3, t3) + token_specs(tokens),
        out_specs=[blocks_of(rows)] * 3 + [wide, wide, pl.BlockSpec((hidden_block, half), lambda p: (p, 0))],
        scratch_shapes=[pltpu.VMEM((half, rows), bf16)],
        out_shape=[shape((rows, inner), bf16)] * 3
        + [shape((half, inner), bf16)] * 2
        + [shape((inner, half), bf16)],
        cost_estimate=cost(24),
        compiler_params=pltpu.CompilerParams(vmem_limit_bytes=60 << 20),
    )(b, g, *w3, *t3, *tokens)


def anywhere():
    return pl.BlockSpec(memory_space=pl.ANY)


def ffn_mine(layer, b, g, values, received, totals, *tokens):
    rows, width = b.shape
    half, inner = width // 2, values[0].shape[1]
    wide = pl.BlockSpec((half, hidden_block), lambda p: (0, p))
    tall = pl.BlockSpec((hidden_block, half), lambda p: (p, 0))
    wide_out = pl.BlockSpec((1, half, hidden_block), lambda p: (layer, 0, p))
    tall_out = pl.BlockSpec((1, hidden_block, half), lambda p: (layer, p, 0))
    return pl.pallas_call(
        ffn_mine_kernel,
        grid=(inner // hidden_block,),
        in_specs=[fixed((rows, half))] * 2
        + [blocks_of(rows)] * 3
        + [wide, wide, tall]
        + [anywhere()] * 3
        + token_specs(tokens),
        out_specs=[wide_out, wide_out, tall_out],
        out_shape=[shape(x.shape, x.dtype) for x in totals],
        scratch_shapes=[pltpu.VMEM((half, rows), bf16)],
        input_output_aliases={8: 0, 9: 1, 10: 2},
        cost_estimate=cost(9),
        compiler_params=pltpu.CompilerParams(vmem_limit_bytes=60 << 20),
    )(b, g, *values, *received, *totals, *tokens)


def attention_grads(layer, a, ds, dz, u, y, received=None, totals=None, tokens=()):
    rows, width = a.shape
    half, local_width = width // 2, u.shape[1]
    part = min(rows, 1024)
    steps = rows // part
    mine = received is not None
    side = 0 if mine else 1
    features = pl.BlockSpec((part, half), lambda p: (p, side))
    across = [pl.BlockSpec((part, x.shape[1]), lambda p: (p, 0)) for x in (*ds, dz, u)]
    specs = [features, *across, features]
    operands = [a, *ds, dz, u, y]
    flat = [(half, local_width)] * 4 + [(half, pair_lanes), (local_width, half)]
    if mine:
        specs += [fixed(x) for x in flat] + [anywhere()] * 5
        operands += [*received, *totals]
        outs = [shape(x.shape, f32) for x in totals[:4]] + [shape(flat[4], f32), shape(totals[4].shape, f32)]
        layered = pl.BlockSpec((1, half, local_width), lambda p: (layer, 0, 0))
        out_specs = [layered] * 4 + [fixed(flat[4], False)]
        out_specs += [pl.BlockSpec((1, local_width, half), lambda p: (layer, 0, 0))]
        aliases = {14: 0, 15: 1, 16: 2, 17: 3, 18: 5}
    else:
        outs, out_specs, aliases = [shape(x, bf16) for x in flat], [fixed(x, False) for x in flat], {}
    sizes = [(half, 4 * local_width + pair_lanes), (local_width, half)] if steps > 1 else [(8, 128)] * 2
    return pl.pallas_call(
        functools.partial(attention_grads_kernel, steps, mine),
        grid=(steps,),
        in_specs=specs + token_specs(tokens),
        out_specs=out_specs,
        out_shape=outs,
        scratch_shapes=[pltpu.VMEM(x, f32) for x in sizes],
        input_output_aliases=aliases,
        cost_estimate=cost(7),
        compiler_params=pltpu.CompilerParams(vmem_limit_bytes=60 << 20),
    )(*operands, *tokens)


def unset(*like):
    return pl.pallas_call(
        pass_kernel,
        out_specs=[pl.BlockSpec(memory_space=pl.ANY) for _ in like],
        out_shape=list(like),
    )()


def inverse_rms(h):
    return lax.rsqrt(jnp.mean(h * h, axis=-1, keepdims=True) + epsilon)


def norm_back(grad_normed, hidden, inverse, gain):
    scaled = hidden * inverse
    weighted = grad_normed * gain
    grad_gain = jnp.sum(grad_normed * scaled, axis=0)
    mean = jnp.mean(weighted * scaled, axis=-1, keepdims=True)
    return inverse * (weighted - scaled * mean), grad_gain


def local(
    hidden_in, segment_ids, w_query, w_key, w_value, w_gate_out, w_attn_out, w_forget, b_forget,
    gain_attn, gain_ffn, w_gate, w_up, w_down, cotangent,
):
    seq_count, piece_len, width = hidden_in.shape
    count_z, count_t = lax.axis_size("context"), lax.axis_size("tensor")
    core, z, t = lax.axis_index("fsdp"), lax.axis_index("context"), lax.axis_index("tensor")
    layers, half, local_width = w_query.shape
    heads = w_forget.shape[2]
    block = piece_len // count_t
    seq_len = piece_len * count_z
    shared_rows = count_z == 4
    place = jnp.stack([z, t]).astype(jnp.int32)

    def features(x):
        return jnp.where(core == 0, x, jnp.concatenate([x[..., half:], x[..., :half]], axis=-1))

    def own_block(x):
        return lax.dynamic_slice_in_dim(x, t * block, block, 0)

    def other(w):
        return swap(w, "fsdp", 1)

    def full(w, axis):
        return jnp.concatenate([w, other(w)], axis=axis)

    seg_all = gathered(segment_ids.reshape(1, piece_len), "context").reshape(seq_len)
    doc_start = jnp.sum((seg_all[None, :] < seg_all[:, None]).astype(jnp.int32), axis=1, keepdims=True)

    gains = full(jnp.concatenate([gain_attn, gain_ffn], axis=0), 1).astype(f32)
    hidden_rows = features(hidden_in.reshape(piece_len, width)).astype(f32)
    first_a = (hidden_rows * inverse_rms(hidden_rows) * gains[0]).astype(bf16)
    w_forget_full = jnp.pad(full(w_forget, 1), ((0, 0), (0, 0), (0, pair_lanes - heads)))
    w_forget_full = [w_forget_full[layer] for layer in range(layers)]
    bias = jnp.pad(b_forget, ((0, 0), (0, pair_lanes - heads)))
    bias = [bias[layer : layer + 1] for layer in range(layers)]
    a_parts, a_far = all_rows(
        own_block(first_a), first_a, (seg_all,), (doc_start, w_forget_full[0], bias[0], place)
    )
    w4 = (w_query, w_key, w_value, w_gate_out)
    t4 = tuple(other(w) for w in w4)
    to = other(w_attn_out)
    w3 = (w_gate, w_up, w_down)
    t3 = tuple(other(w) for w in w3)

    hidden = own_block(hidden_rows)
    saved = []
    cotangent_rows = features(cotangent.reshape(piece_len, width))
    last = layers - 1
    grad = own_block(cotangent_rows).astype(f32)
    for layer in range(layers):
        gain_one, gain_two = gains[layer], gains[layers + layer]
        inverse_one = inverse_rms(hidden)
        if layer > 0:
            a_shard = (hidden * inverse_one * gain_one).astype(bf16)
            if shared_rows and layer == 1:
                a_shard = after(a_shard, g_last)
            a_parts, _ = all_rows(a_shard)
        forget_weights = w_forget_full[layer]
        if shared_rows and layer > 0:
            b_sent = after(saved[-1]["b_shard"], a_parts[-1])
            saved[-1]["b_rows"] = sequence_rows(b_sent)
            forget_weights = after(forget_weights, b_sent)
        a, (q, k, v, gate, forget, terms), sends = forward_own(
            place, a_parts, layer, w4, t4, w_attn_out, to, forget_weights,
            bias[layer], doc_start, piece_len,
        )
        if shared_rows and layer == 0:
            g_last = lax.all_gather(after(cotangent_rows, *a_far), "context", tiled=True)
        mixed = hidden + received_sum(sends)
        inverse_two = inverse_rms(mixed)
        b_shard = (mixed * inverse_two * gain_two).astype(bf16)
        b = gathered(b_shard, "tensor")
        gt, up, sends = ffn_forward(b, layer, w3, t3)
        saved.append(
            dict(hidden=hidden, inverse_one=inverse_one, a=a, kept=(q, k, v, gate, forget, terms), mixed=mixed,
                 inverse_two=inverse_two, b=b, b_shard=b_shard, gt=gt, up=up)
        )
        if layer < last:
            hidden = mixed + received_sum(sends)

    def finish(x):
        return features(gathered(x.astype(bf16), "tensor")).reshape(1, piece_len, width)

    last_sends = sends
    wide = shape((layers, half, local_width), f32)
    inner = shape((layers, half, w_gate.shape[2]), f32)
    results = list(
        unset(
            wide, wide, wide, wide, shape((layers, local_width, half), f32),
            inner, inner, shape((layers, w_down.shape[1], half), f32),
        )
    )
    small = [[None] * layers for _ in range(2)]
    gain_grads = [None] * (2 * layers)

    def ffn_theirs_of(layer, *tokens):
        s = saved[layer]
        values = ffn_theirs(s["b_rows"], s["g_rows"], layer, w3, t3, *tokens)
        s.update(values=values[:3], ffn_received=[other(x) for x in values[3:]])

    def ffn_mine_of(layer, *tokens):
        s = saved[layer]
        received = s["ffn_received"]
        results[5:] = ffn_mine(layer, s["b_rows"], s["g_rows"], s["values"], received, results[5:], *tokens)

    def attention_theirs_of(layer, *tokens):
        s = saved[layer]
        s["theirs"] = attention_grads(layer, *s["grads"], tokens=tokens)
        s["received"] = [other(x) for x in s["theirs"]]
        bias_grad = jnp.sum(s["grads"][2].astype(f32), axis=0)[:heads]
        small[1][layer] = bias_grad + other(bias_grad)

    def attention_mine_of(layer, *tokens):
        s = saved[layer]
        found = attention_grads(layer, *s["grads"], s["received"], results[:5], tokens)
        results[:5] = [*found[:4], found[5]]
        small[0][layer] = found[4][:, :heads]

    for layer in reversed(range(layers)):
        s = saved[layer]
        gain_one, gain_two = gains[layer], gains[layers + layer]
        tokens = ()
        if layer == last:
            g = cotangent_rows
        else:
            g_shard = grad.astype(bf16)
            g = gathered(g_shard, "tensor")
            tokens = (saved[layer + 1]["theirs"][0],)
        if not shared_rows:
            s.update(b_rows=s["b"], g_rows=g)
        sends = ffn_backward(g, s["gt"], s["up"], layer, w3, t3, *tokens)
        if layer < last:
            sends = after(sends, *saved[layer + 1]["received"])
        back, gain_grads[layers + layer] = norm_back(received_sum(sends), s["mixed"], s["inverse_two"], gain_two)
        grad_mixed = grad + back
        y_shard = grad_mixed.astype(bf16)
        if layer < last:
            attention_mine_of(layer + 1)
            y_shard = after(y_shard, results[0])
        elif shared_rows:
            y_shard = after(y_shard, *[x["b_rows"] for x in saved[:-1]])
        y_parts, y_far = all_rows(y_shard, together=layer < last)
        tokens = ()
        if layer < last:
            above = saved[layer + 1]
            ffn_theirs_of(layer + 1, *y_far, y_parts[0])
            tokens = (above["values"][0],)
        kept = (*s["kept"][:-1], after(s["kept"][-1], *tokens))
        y, (dq, dk, dv, dg, u, dz), sends = attention_backward(
            place, y_parts, layer, w4, t4, w_attn_out, to, w_forget_full[layer], kept, doc_start, piece_len,
        )
        token = y_parts[-1]
        if shared_rows and layer == last:
            s.update(b_rows=sequence_rows(after(s["b_shard"], *y_parts)), g_rows=g_last)
        elif shared_rows:
            s["g_rows"] = sequence_rows(after(g_shard, above["values"][0]))
        s["grads"] = (s["a"], (dq, dk, dv, dg), dz, u, y)
        if layer > 0:
            attention_theirs_of(layer)
        back, gain_grads[layer] = norm_back(received_sum(sends), s["hidden"], s["inverse_one"], gain_one)
        grad = grad_mixed + back

    block_sum = own_block(last_sends).astype(f32) + saved[last]["mixed"]
    with_rows = lax.dynamic_update_slice_in_dim(last_sends, block_sum.astype(bf16), t * block, 0)
    output = lax.psum(after(with_rows, sends), "tensor")
    for layer in reversed(range(1, layers)):
        ffn_mine_of(layer, sends)
    attention_theirs_of(0, sends)
    gain_total = after(jnp.stack(gain_grads).reshape(1, -1), *([results[5]] if layers > 1 else []))
    for axis in (("context", "tensor"),) if shared_rows else ("context", "tensor"):
        gain_total = jnp.sum(gathered(gain_total, axis), axis=0, keepdims=True)
    gain_total = gain_total.reshape(2 * layers, width)
    gain_total = gain_total[:, :half] + other(gain_total[:, half:])
    grad_input = finish(after(grad, saved[0]["theirs"][0]))
    ffn_theirs_of(0)
    attention_mine_of(0, gain_total, saved[0]["values"][0])
    ffn_mine_of(0)
    if not shared_rows:
        results[5:] = [lax.psum(x, "context") for x in results[5:]]
    output = features(after(output, saved[0]["values"][0])).reshape(1, piece_len, width)
    return (
        output, grad_input, *results[:5], jnp.stack(small[0]), jnp.stack(small[1]),
        gain_total[:layers], gain_total[layers:], *results[5:],
    )


def solution(mesh):
    rows = P("fsdp", "context", None)
    wide, tall = P(None, "fsdp", "tensor"), P(None, "tensor", "fsdp")
    heads, gain = P(None, "tensor"), P(None, "fsdp")
    return jax.shard_map(
        local,
        mesh=mesh,
        in_specs=(
            rows, P("fsdp", "context"), wide, wide, wide, wide, tall, wide, heads, gain, gain, wide, wide, tall, rows,
        ),
        out_specs=(rows, rows, wide, wide, wide, wide, tall, wide, heads, gain, gain, wide, wide, tall),
        check_vma=False,
    )
```

```python
import functools

import jax
import jax.numpy as jnp
from jax import lax
from jax.experimental import pallas as pl
from jax.experimental.pallas import tpu as pltpu
from jax.sharding import PartitionSpec as P

epsilon = 1e-06
masked_value = -1e30
bf16 = jnp.bfloat16
f32 = jnp.float32
pair_lanes = 128
hidden_block = 256
chunk_rows = 256


def query_rows(seq_len):
    return 256 if seq_len <= 2048 else 128


def swap(x, axis, k):
    n = lax.axis_size(axis)
    return lax.ppermute(x, axis, [(i, i ^ k) for i in range(n)])


def pass_kernel(*refs):
    pass


def after(x, *tokens):
    if not tokens:
        return x
    anywhere = pl.BlockSpec(memory_space=pl.ANY)
    return pl.pallas_call(
        pass_kernel,
        in_specs=[anywhere] * (1 + len(tokens)),
        out_specs=anywhere,
        out_shape=jax.ShapeDtypeStruct(x.shape, x.dtype),
        input_output_aliases={0: 0},
    )(x, *tokens)


def gathered(block, axis):
    count = lax.axis_size(axis)
    copies = jnp.broadcast_to(block[None], (count,) + block.shape)
    return lax.all_to_all(copies, axis, 0, 0, tiled=True).reshape((-1,) + block.shape[1:])


def sequence_rows(shard):
    return lax.all_gather(shard, ("context", "tensor"), tiled=True)


def near_rows(own):
    return swap(own, "context", 1)


def far_blocks(shard, *tokens):
    shard = after(shard, *tokens)
    return swap(shard, "context", 2), swap(shard, "context", 3)


def all_rows(shard, own=None, first=(), second_stage=(), together=False):
    if own is None:
        own = gathered(shard, "tensor")
    if lax.axis_size("context") != 4:
        return (lax.all_gather(own, "context", tiled=True),), ()
    second, third = far_blocks(shard, *first)
    near = near_rows(own)
    if together:
        block, width = shard.shape
        far = gathered(after(jnp.concatenate([second, third], axis=0), own), "tensor")
        return (own, near, far.reshape(-1, 2, block, width)), (second, third)
    second = after(second, *second_stage)
    parts = [own, near]
    for far in (second, third):
        parts += [far] + [swap(far, "tensor", k) for k in range(1, lax.axis_size("tensor"))]
    return tuple(parts), (second, third)


def received_sum(sends):
    count = lax.axis_size("tensor")
    got = lax.all_to_all(sends.reshape(count, -1, sends.shape[1]), "tensor", 0, 0, tiled=True)
    return jnp.sum(got.astype(f32), axis=0)


def dot_nt(a, b):
    return lax.dot_general(a, b, (((1,), (1,)), ((), ())), preferred_element_type=f32)


def dot_tn(a, b):
    return lax.dot_general(a, b, (((0,), (0,)), ((), ())), preferred_element_type=f32)


def dot_nn(a, b):
    return jnp.dot(a, b, preferred_element_type=f32)


def each(count, body):
    if count <= 4:
        for i in range(count):
            body(i)
        return

    def one(i, carry):
        body(i)
        return carry

    lax.fori_loop(0, count, one, 0)


def rows_at(i, rows):
    start = i * rows
    return pl.ds(start if isinstance(start, int) else pl.multiple_of(start, rows), rows)


def assemble(parts, whole_ref, place_ref):
    z, t = place_ref[0], place_ref[1]
    piece, blocks_seen, piece_len = 0, 0, parts[0].shape[0]
    for part in parts:
        if len(part.shape) == 4:
            blocks, pieces, block = part.shape[:3]
            for p in range(pieces):
                for b in range(blocks):
                    at = pl.multiple_of((z ^ (piece + p)) * piece_len + b * block, block)
                    whole_ref[pl.ds(at, block), :] = part[b, p]
            piece += pieces
            continue
        rows = part.shape[0]
        if rows == piece_len:
            at = pl.multiple_of((z ^ piece) * piece_len, piece_len)
            piece += 1
        else:
            at = pl.multiple_of((z ^ piece) * piece_len + (t ^ blocks_seen) * rows, rows)
            blocks_seen += 1
            if blocks_seen * rows == piece_len:
                piece, blocks_seen = piece + 1, 0
        whole_ref[pl.ds(at, rows), :] = part[...]


def triangle(rows, reverse):
    row = lax.broadcasted_iota(jnp.int32, (rows, rows), 0)
    column = lax.broadcasted_iota(jnp.int32, (rows, rows), 1)
    return jnp.where((column >= row) if reverse else (column <= row), 1.0, 0.0).astype(bf16)


def running_sum(ref, reverse):
    rows = chunk_rows
    ones = triangle(rows, reverse)
    count = ref.shape[0] // rows
    edge = 0 if reverse else rows - 1

    def chunk(i, carry):
        here = pl.ds(pl.multiple_of((count - 1 - i if reverse else i) * rows, rows), rows)
        high, middle, lowest = three_parts(ref[here, :])
        total = dot_nn(ones, high) + dot_nn(ones, middle) + dot_nn(ones, lowest) + carry
        ref[here, :] = total
        return total[edge : edge + 1, :]

    lax.fori_loop(0, count, chunk, jnp.zeros((1, ref.shape[1]), f32), unroll=count <= 4)


def log_sigmoid(z):
    e = jnp.exp(-jnp.abs(z))
    small = e * (1.0 - e * (1 / 2 - e * (1 / 3 - e * (1 / 4 - e * (1 / 5 - e * (1 / 6 - e * (1 / 7)))))))
    return jnp.minimum(z, 0.0) - jnp.where(e < 0.0625, small, jnp.log(1.0 + e))


def three_parts(x):
    high = x.astype(bf16)
    middle = (x - high.astype(f32)).astype(bf16)
    return high, middle, (x - high.astype(f32) - middle.astype(f32)).astype(bf16)


def decay_side(terms, pair, key_side):
    row = lax.broadcasted_iota(jnp.int32, (pair_lanes, pair_lanes), 0)
    lane = lax.broadcasted_iota(jnp.int32, (pair_lanes, pair_lanes), 1)
    spot = lane & 63
    term = spot if key_side else spot - 3
    head = jnp.where(lane >= 64, 2 * pair, 2 * pair + 1)
    chosen = (term >= 0) & (term < 3) & (row == 8 * term + head)
    pick = jnp.where(chosen, -1.0 if key_side else 1.0, 0.0).astype(bf16)
    lanes_now = lax.broadcasted_iota(jnp.int32, (1, pair_lanes), 1) & 63
    other = lanes_now - 3 if key_side else lanes_now
    ones = jnp.where((other >= 0) & (other < 3), 1.0, 0.0)
    return (dot_nn(terms, pick) + ones).astype(bf16)


def mix_keys(k_ref, terms_ref, pair, ka, kb):
    def mix(i):
        here = rows_at(i, chunk_rows)
        lane = lax.broadcasted_iota(jnp.int32, (chunk_rows, pair_lanes), 1)
        k, side = k_ref[here, :], decay_side(terms_ref[here, :], pair, True)
        ka[here, :] = jnp.where(lane < 64, k, side)
        kb[here, :] = jnp.where(lane < 64, side, k)

    each(k_ref.shape[0] // chunk_rows, mix)


def mix_queries(q_ref, terms_ref, start, pair, qa, qb):
    def mix(i):
        here = rows_at(i, chunk_rows)
        lane = lax.broadcasted_iota(jnp.int32, (chunk_rows, pair_lanes), 1)
        q = (q_ref[here, :].astype(f32) * 0.125).astype(bf16)
        terms = terms_ref[pl.ds(pl.multiple_of(start + i * chunk_rows, chunk_rows), chunk_rows), :]
        side = decay_side(terms, pair, False)
        qa[here, :] = jnp.where(lane < 64, q, side)
        qb[here, :] = jnp.where(lane < 64, side, q)

    each(q_ref.shape[0] // chunk_rows, mix)


def live_mask(start_ref, start, first, width, rows):
    key_pos = first + lax.broadcasted_iota(jnp.int32, (rows, width), 1)
    query_pos = start + lax.broadcasted_iota(jnp.int32, (rows, width), 0)
    doc_start = start_ref[pl.ds(start, rows), :]
    return (key_pos <= query_pos) & (key_pos >= doc_start)


def over_query_blocks(seq_len, rows, body):
    before = seq_len // 2
    if seq_len // rows <= 4:
        for start in range(0, seq_len, rows):
            first = max(0, start - before)
            body(start, first, start + rows - first)
        return
    width = before + rows

    def one(i, carry):
        start = pl.multiple_of(i * rows, rows)
        first = pl.multiple_of(jnp.maximum(start - before, 0), rows)
        body(start, first, width)
        return carry

    lax.fori_loop(0, seq_len // rows, one, 0)


def probabilities(q_rows, k_rows, mask):
    s = jnp.where(mask, dot_nt(q_rows, k_rows), masked_value)
    e = jnp.exp(s - jnp.max(s, axis=1, keepdims=True))
    return e * (1.0 / jnp.sum(e, axis=1, keepdims=True))


def lane_blocks(refs):
    return jnp.concatenate([r[0] for r in refs], axis=1)


def forward_own_kernel(count_parts, piece_len, join, *refs):
    place_ref, parts, refs = refs[0], refs[1 : 1 + count_parts], list(refs[1 + count_parts :])
    (wq, wk, wv, wg), (tq, tk, tv, tg) = refs[:4], refs[4:8]
    wo, to, wf, bias, start_ref = refs[8:13]
    refs = refs[13:]
    a_ref = refs.pop(0) if join else parts[0]
    q_ref, k_ref, v_ref, gate_ref, z_ref, terms_ref, send_ref, qa, qb, ka, kb, decay, acc = refs
    pair = pl.program_id(0)
    seq_len, half = a_ref.shape[0], a_ref.shape[1] // 2
    piece_start = pl.multiple_of(place_ref[0] * piece_len, piece_len)

    @pl.when(pair == 0)
    def _():
        if join:
            assemble(parts, a_ref, place_ref)
        acc[...] = jnp.zeros_like(acc)

        def gates(i):
            here = rows_at(i, chunk_rows)
            z = dot_nn(a_ref[here, :], wf[...]) + bias[...]
            z_ref[here, :] = z
            decay[here, :] = log_sigmoid(z)

        each(seq_len // chunk_rows, gates)
        running_sum(decay, False)

        def split(i):
            here = rows_at(i, chunk_rows)
            lane = lax.broadcasted_iota(jnp.int32, (chunk_rows, pair_lanes), 1)
            high, middle, lowest = (x.astype(f32) for x in three_parts(decay[here, :]))
            later = jnp.where(lane < 16, pltpu.roll(middle, 8, 1), pltpu.roll(lowest, 16, 1))
            terms = jnp.where(lane < 8, high, later)
            terms_ref[here, :] = jnp.where(lane < 24, terms, 0.0).astype(bf16)

        each(seq_len // chunk_rows, split)

    w_mine, w_theirs = lane_blocks((wq, wk, wv, wg)), lane_blocks((tq, tk, tv, tg))

    def project(i):
        here = rows_at(i, chunk_rows)
        out = dot_nn(a_ref[here, :half], w_mine) + dot_nn(a_ref[here, half:], w_theirs)
        q_ref[here, :] = out[:, :128].astype(bf16)
        k_ref[here, :] = out[:, 128:256].astype(bf16)
        v_ref[here, :] = out[:, 256:384].astype(bf16)
        gate_ref[here, :] = out[:, 384:]

    each(seq_len // chunk_rows, project)
    piece = pl.ds(piece_start, piece_len)
    gate = jax.nn.sigmoid(gate_ref[piece, :])
    mix_keys(k_ref, terms_ref, pair, ka, kb)
    mix_queries(q_ref.at[piece, :], terms_ref, piece_start, pair, qa, qb)
    before = seq_len // 2
    for s in range(0, piece_len, query_rows(seq_len)):
        rows = query_rows(seq_len)
        width = before + rows
        start = pl.multiple_of(piece_start + s, rows)
        first = pl.multiple_of(jnp.maximum(start - before, 0), rows)
        mask = live_mask(start_ref, start, first, width, rows)
        keys = pl.ds(first, width)
        out = []
        for q_of, k_of in ((qa, ka), (qb, kb)):
            p = probabilities(q_of[s : s + rows, :], k_of[keys, :], mask).astype(bf16)
            out.append(dot_nn(p, v_ref[keys, :]))
        lane = lax.broadcasted_iota(jnp.int32, (rows, pair_lanes), 1)
        u = (jnp.where(lane < 64, out[0], out[1]) * gate[s : s + rows, :]).astype(bf16)
        acc[s : s + rows, :half] += dot_nn(u, wo[0])
        acc[s : s + rows, half:] += dot_nn(u, to[0])

    @pl.when(pair == pl.num_programs(0) - 1)
    def _():
        send_ref[...] = acc[...].astype(bf16)


def backward_kernel(count_parts, piece_len, join, *refs):
    place_ref, parts, refs = refs[0], refs[1 : 1 + count_parts], list(refs[1 + count_parts :])
    mine, theirs, (wo, to, wf) = refs[:4], refs[4:8], refs[8:11]
    q_ref, k_ref, v_ref, gate_ref, z_ref, terms_ref, start_ref = refs[11:18]
    refs = refs[18:]
    y_ref = refs.pop(0) if join else parts[0]
    dq_ref, dk_ref, dv_ref, dg_ref, u_ref, dz_ref, send_ref = refs[:7]
    qa, qb, ka, kb, dd, dus, dka, dkb, dva, dcs, acc = refs[7:]
    pair = pl.program_id(0)
    seq_len, half = y_ref.shape[0], y_ref.shape[1] // 2
    rows = query_rows(seq_len)
    piece = pl.ds(pl.multiple_of(place_ref[0] * piece_len, piece_len), piece_len)

    @pl.when(pair == 0)
    def _():
        if join:
            assemble(parts, y_ref, place_ref)
        acc[...] = jnp.zeros_like(acc)
        dcs[...] = jnp.zeros_like(dcs)

    def gates(i):
        here = rows_at(i, chunk_rows)
        du = dot_nt(y_ref[here, :half], wo[0]) + dot_nt(y_ref[here, half:], to[0])
        sig = jax.nn.sigmoid(gate_ref[here, :])
        dd[here, :] = (du * sig).astype(bf16)
        dus[here, :] = du * sig * (1.0 - sig)

    each(seq_len // chunk_rows, gates)
    mix_keys(k_ref, terms_ref, pair, ka, kb)
    mix_queries(q_ref, terms_ref, 0, pair, qa, qb)
    dka[...] = jnp.zeros_like(dka)
    dkb[...] = jnp.zeros_like(dkb)
    dva[...] = jnp.zeros_like(dva)
    lane = lax.broadcasted_iota(jnp.int32, (rows, pair_lanes), 1)

    def pick(column_a, column_b):
        at = lax.broadcasted_iota(jnp.int32, (column_a.shape[0], pair_lanes), 1)
        return jnp.where(at == 2 * pair, column_a, jnp.where(at == 2 * pair + 1, column_b, 0.0))

    def body(start, first, width):
        mask = live_mask(start_ref, start, first, width, rows)
        here, keys = pl.ds(start, rows), pl.ds(first, width)
        values = v_ref[keys, :]
        d_rows = dd[here, :]
        dq, o = [], []
        for head, (q_of, k_of, dk_of) in enumerate(((qa, ka, dka), (qb, kb, dkb))):
            own_lanes = (lane < 64) if head == 0 else (lane >= 64)
            p = probabilities(q_of[here, :], k_of[keys, :], mask)
            d_mine = jnp.where(own_lanes, d_rows, jnp.zeros_like(d_rows))
            dp = dot_nt(d_mine, values)
            delta = jnp.sum(p * dp, axis=1, keepdims=True)
            ds = (p * (dp - delta)).astype(bf16)
            dq.append(dot_nn(ds, k_of[keys, :]))
            dk_of[keys, :] += dot_tn(ds, q_of[here, :])
            low = p.astype(bf16)
            dva[keys, :] += dot_tn(low, d_mine)
            o.append(dot_nn(low, values))
        o = jnp.where(lane < 64, o[0], o[1])
        dg_ref[here, :] = (dus[here, :] * o).astype(bf16)
        u_ref[here, :] = (o * jax.nn.sigmoid(gate_ref[here, :])).astype(bf16)
        dq_ref[here, :] = (jnp.where(lane < 64, dq[0], dq[1]) * 0.125).astype(bf16)
        dcs[here, :] += pick(dq[0][:, 67:68], dq[1][:, 3:4])

    over_query_blocks(seq_len, rows, body)

    def finish(i):
        here = rows_at(i, chunk_rows)
        lanes_now = lax.broadcasted_iota(jnp.int32, (chunk_rows, pair_lanes), 1)
        ka_rows, kb_rows = dka[here, :], dkb[here, :]
        dk_ref[here, :] = jnp.where(lanes_now < 64, ka_rows, kb_rows).astype(bf16)
        dv_ref[here, :] = dva[here, :].astype(bf16)
        dcs[here, :] -= pick(ka_rows[:, 64:65], kb_rows[:, 0:1])

    each(seq_len // chunk_rows, finish)
    d_own = jnp.concatenate([r[piece, :] for r in (dq_ref, dk_ref, dv_ref, dg_ref)], axis=1)
    acc[:, :half] += dot_nt(d_own, lane_blocks(mine))
    acc[:, half:] += dot_nt(d_own, lane_blocks(theirs))

    @pl.when(pair == pl.num_programs(0) - 1)
    def _():
        running_sum(dcs, True)

        def last(i):
            here = rows_at(i, chunk_rows)
            dz_ref[here, :] = (dcs[here, :] * jax.nn.sigmoid(-z_ref[here, :])).astype(bf16)

        each(seq_len // chunk_rows, last)
        send_ref[...] = (acc[...] + dot_nt(dz_ref[piece, :], wf[...])).astype(bf16)


def ffn_forward_kernel(b_ref, wg, wu, wd, tg, tu, td, gt_ref, up_ref, send_ref, acc):
    half = b_ref.shape[1] // 2
    low, high = b_ref[:, :half], b_ref[:, half:]
    gt = dot_nn(low, wg[0]) + dot_nn(high, tg[0])
    up = dot_nn(low, wu[0]) + dot_nn(high, tu[0])
    gt_ref[...] = gt
    up_ref[...] = up
    m = (gt * jax.nn.sigmoid(gt) * up).astype(bf16)

    @pl.when(pl.program_id(0) == 0)
    def _():
        acc[...] = jnp.zeros_like(acc)

    acc[:, :half] += dot_nn(m, wd[0])
    acc[:, half:] += dot_nn(m, td[0])

    @pl.when(pl.program_id(0) == pl.num_programs(0) - 1)
    def _():
        send_ref[...] = acc[...].astype(bf16)


def inner_grads(dm, gt, up):
    sig = jax.nn.sigmoid(gt)
    d_gate = (dm * up * sig * (1.0 + gt * (1.0 - sig))).astype(bf16)
    return d_gate, (dm * (gt * sig)).astype(bf16)


def ffn_backward_kernel(g_ref, gt_ref, up_ref, wg, wu, wd, tg, tu, td, *refs):
    send_ref, acc = refs[-2:]
    half = g_ref.shape[1] // 2
    dm = dot_nt(g_ref[:, :half], wd[0]) + dot_nt(g_ref[:, half:], td[0])
    d_gate, d_up = inner_grads(dm, gt_ref[...], up_ref[...])

    @pl.when(pl.program_id(0) == 0)
    def _():
        acc[...] = jnp.zeros_like(acc)

    acc[:, :half] += dot_nt(d_gate, wg[0]) + dot_nt(d_up, wu[0])
    acc[:, half:] += dot_nt(d_gate, tg[0]) + dot_nt(d_up, tu[0])

    @pl.when(pl.program_id(0) == pl.num_programs(0) - 1)
    def _():
        send_ref[...] = acc[...].astype(bf16)


def ffn_theirs_kernel(b_ref, g_ref, wg, wu, wd, tg, tu, td, *refs):
    m_ref, dgate_ref, dup_ref, gate_out, up_out, down_out, turned = refs[-7:]
    half = b_ref.shape[1] // 2

    @pl.when(pl.program_id(0) == 0)
    def _():
        turned[...] = b_ref[:, half:].T

    def chunk(i):
        here = rows_at(i, chunk_rows)
        low, high = b_ref[here, :half], b_ref[here, half:]
        gt = dot_nn(low, wg[0]) + dot_nn(high, tg[0])
        up = dot_nn(low, wu[0]) + dot_nn(high, tu[0])
        dm = dot_nt(g_ref[here, :half], wd[0]) + dot_nt(g_ref[here, half:], td[0])
        m_ref[here, :] = (gt * jax.nn.sigmoid(gt) * up).astype(bf16)
        dgate_ref[here, :], dup_ref[here, :] = inner_grads(dm, gt, up)

    each(b_ref.shape[0] // chunk_rows, chunk)
    gate_out[...] = dot_nn(turned[...], dgate_ref[...]).astype(bf16)
    up_out[...] = dot_nn(turned[...], dup_ref[...]).astype(bf16)
    down_out[...] = dot_tn(m_ref[...], g_ref[:, half:]).astype(bf16)


def ffn_mine_kernel(b_ref, g_ref, m_ref, dgate_ref, dup_ref, gate_in, up_in, down_in, *refs):
    gate_out, up_out, down_out, turned = refs[-4:]

    @pl.when(pl.program_id(0) == 0)
    def _():
        turned[...] = b_ref[...].T

    gate_out[0] = dot_nn(turned[...], dgate_ref[...]) + gate_in[...].astype(f32)
    up_out[0] = dot_nn(turned[...], dup_ref[...]) + up_in[...].astype(f32)
    down_out[0] = dot_tn(m_ref[...], g_ref[...]) + down_in[...].astype(f32)


def attention_grads_kernel(steps, mine, *refs):
    a_ref, dq, dk, dv, dg, dz, u_ref, y_ref = refs[:8]
    received = refs[8:14] if mine else [None] * 6
    acc, acc_out = refs[-2:]
    outs = refs[-8:-2]
    turned = a_ref[...].T
    width = dq.shape[1]
    parts = [dot_nn(turned, d[...]) for d in (dq, dk, dv, dg, dz)]
    out = dot_tn(u_ref[...], y_ref[...])

    def give(values):
        for ref, value, more in zip(outs, values, received):
            total = value if more is None else value + more[...].astype(f32)
            if len(ref.shape) == 3:
                ref[0] = total.astype(ref.dtype)
            else:
                ref[...] = total.astype(ref.dtype)

    if steps == 1:
        give([*parts, out])
        return
    step = pl.program_id(0)

    @pl.when(step == 0)
    def _():
        acc[...] = jnp.zeros_like(acc)
        acc_out[...] = jnp.zeros_like(acc_out)

    for k, part in enumerate(parts):
        acc[:, k * width : k * width + part.shape[1]] += part
    acc_out[...] += out

    @pl.when(step == steps - 1)
    def _():
        found = [acc[:, k * width : k * width + p.shape[1]] for k, p in enumerate(parts)]
        give([*found, acc_out[...]])


def fixed(shape, single=True):
    zeros = (0,) * len(shape)
    if single:
        return pl.BlockSpec(shape, lambda *_: zeros, pipeline_mode=pl.Buffered(1))
    return pl.BlockSpec(shape, lambda *_: zeros)


def lanes(seq_len):
    return pl.BlockSpec((seq_len, pair_lanes), lambda p, *_: (0, p))


def lanes_read(seq_len):
    if seq_len <= 2048:
        return lanes(seq_len)
    return pl.BlockSpec((seq_len, pair_lanes), lambda p, *_: (0, p), pipeline_mode=pl.Buffered(1))


def columns_of(w, layer, width):
    return pl.BlockSpec((1, w.shape[1], width), lambda p, *_: (layer, 0, p))


def rows_of(w, layer, height):
    return pl.BlockSpec((1, height, w.shape[2]), lambda p, *_: (layer, p, 0))


def shape(dims, dtype):
    return jax.ShapeDtypeStruct(dims, dtype)


def attention_specs(parts, layer, w4, t4, wo, to, seq_len, join):
    specs = [fixed(p.shape) for p in parts]
    specs += [columns_of(w, layer, pair_lanes) for w in (*w4, *t4)]
    specs += [rows_of(wo, layer, pair_lanes), rows_of(to, layer, pair_lanes)]
    return specs


def cost(microseconds):
    return pl.CostEstimate(flops=int(microseconds * 1.1e9), bytes_accessed=0, transcendentals=0)


def token_specs(tokens):
    return [pl.BlockSpec(memory_space=pl.ANY) for _ in tokens]


def forward_own(place, parts, layer, w4, t4, wo, to, wf, bias, doc_start, piece_len):
    seq_len, width = doc_start.shape[0], parts[0].shape[1]
    local_width = wo.shape[1]
    join = len(parts) > 1
    terms = (seq_len, pair_lanes)
    outs = [shape((seq_len, local_width), bf16)] * 3 + [shape((seq_len, local_width), f32)]
    outs += [shape(terms, f32), shape(terms, bf16), shape((piece_len, width), bf16)]
    specs = [lanes(seq_len)] * 4 + [fixed(terms, False)] * 2 + [fixed((piece_len, width), False)]
    if join:
        outs, specs = [shape((seq_len, width), bf16)] + outs, [fixed((seq_len, width))] + specs
    low, piece = pltpu.VMEM((seq_len, pair_lanes), bf16), pltpu.VMEM((piece_len, pair_lanes), bf16)
    got = pl.pallas_call(
        functools.partial(forward_own_kernel, len(parts), piece_len, join),
        grid_spec=pltpu.PrefetchScalarGridSpec(
            num_scalar_prefetch=1,
            grid=(local_width // pair_lanes,),
            in_specs=attention_specs(parts, layer, w4, t4, wo, to, seq_len, join)
            + [fixed(wf.shape), fixed(bias.shape), fixed(doc_start.shape)],
            out_specs=specs,
            scratch_shapes=[piece] * 2 + [low] * 2 + [pltpu.VMEM(terms, f32), pltpu.VMEM((piece_len, width), f32)],
        ),
        out_shape=outs,
        cost_estimate=cost(19),
        compiler_params=pltpu.CompilerParams(vmem_limit_bytes=60 << 20),
    )(place, *parts, *w4, *t4, wo, to, wf, bias, doc_start)
    got = list(got)
    a = got.pop(0) if join else parts[0]
    return a, got[:6], got[6]


def attention_backward(place, parts, layer, w4, t4, wo, to, wf, saved, doc_start, piece_len):
    q, k, v, gate, z, terms = saved
    seq_len, width = doc_start.shape[0], parts[0].shape[1]
    local_width = wo.shape[1]
    join = len(parts) > 1
    outs = [shape((seq_len, local_width), bf16)] * 5 + [shape((seq_len, pair_lanes), bf16)]
    outs += [shape((piece_len, width), bf16)]
    specs = [lanes(seq_len)] * 5 + [fixed((seq_len, pair_lanes), False), fixed((piece_len, width), False)]
    if join:
        outs, specs = [shape((seq_len, width), bf16)] + outs, [fixed((seq_len, width))] + specs
    low, high = pltpu.VMEM((seq_len, pair_lanes), bf16), pltpu.VMEM((seq_len, pair_lanes), f32)
    got = pl.pallas_call(
        functools.partial(backward_kernel, len(parts), piece_len, join),
        grid_spec=pltpu.PrefetchScalarGridSpec(
            num_scalar_prefetch=1,
            grid=(local_width // pair_lanes,),
            in_specs=attention_specs(parts, layer, w4, t4, wo, to, seq_len, join)
            + [fixed(wf.shape)]
            + [lanes_read(seq_len)] * 4
            + [fixed(z.shape), fixed(terms.shape), fixed(doc_start.shape)],
            out_specs=specs,
            scratch_shapes=[low] * 5 + [high] * 5 + [pltpu.VMEM((piece_len, width), f32)],
        ),
        out_shape=outs,
        cost_estimate=cost(33),
        compiler_params=pltpu.CompilerParams(vmem_limit_bytes=60 << 20),
    )(place, *parts, *w4, *t4, wo, to, wf, q, k, v, gate, z, terms, doc_start)
    got = list(got)
    y = got.pop(0) if join else parts[0]
    return y, got[:6], got[6]


def ffn_weights(layer, w3, t3):
    specs = []
    for wg, wu, wd in (w3, t3):
        specs += [
            columns_of(wg, layer, hidden_block), columns_of(wu, layer, hidden_block), rows_of(wd, layer, hidden_block),
        ]
    return specs


def blocks_of(rows):
    return pl.BlockSpec((rows, hidden_block), lambda p, *_: (0, p))


def ffn_forward(b, layer, w3, t3):
    rows, width = b.shape
    inner = w3[2].shape[1]
    return pl.pallas_call(
        ffn_forward_kernel,
        grid=(inner // hidden_block,),
        in_specs=[fixed(b.shape)] + ffn_weights(layer, w3, t3),
        out_specs=[blocks_of(rows)] * 2 + [fixed((rows, width), False)],
        scratch_shapes=[pltpu.VMEM((rows, width), f32)],
        out_shape=[shape((rows, inner), f32)] * 2 + [shape((rows, width), bf16)],
        cost_estimate=cost(7),
        compiler_params=pltpu.CompilerParams(vmem_limit_bytes=60 << 20),
    )(b, *w3, *t3)


def ffn_backward(g, gt, up, layer, w3, t3, *tokens):
    rows, width = g.shape
    return pl.pallas_call(
        ffn_backward_kernel,
        grid=(gt.shape[1] // hidden_block,),
        in_specs=[fixed(g.shape)] + [blocks_of(rows)] * 2 + ffn_weights(layer, w3, t3) + token_specs(tokens),
        out_specs=fixed((rows, width), False),
        scratch_shapes=[pltpu.VMEM((rows, width), f32)],
        out_shape=shape((rows, width), bf16),
        cost_estimate=cost(8),
        compiler_params=pltpu.CompilerParams(vmem_limit_bytes=60 << 20),
    )(g, gt, up, *w3, *t3, *tokens)


def ffn_theirs(b, g, layer, w3, t3, *tokens):
    rows, width = b.shape
    half = width // 2
    inner = w3[2].shape[1]
    wide = pl.BlockSpec((half, hidden_block), lambda p: (0, p))
    return pl.pallas_call(
        ffn_theirs_kernel,
        grid=(inner // hidden_block,),
        in_specs=[fixed(b.shape), fixed(g.shape)] + ffn_weights(layer, w3, t3) + token_specs(tokens),
        out_specs=[blocks_of(rows)] * 3 + [wide, wide, pl.BlockSpec((hidden_block, half), lambda p: (p, 0))],
        scratch_shapes=[pltpu.VMEM((half, rows), bf16)],
        out_shape=[shape((rows, inner), bf16)] * 3
        + [shape((half, inner), bf16)] * 2
        + [shape((inner, half), bf16)],
        cost_estimate=cost(24),
        compiler_params=pltpu.CompilerParams(vmem_limit_bytes=60 << 20),
    )(b, g, *w3, *t3, *tokens)


def anywhere():
    return pl.BlockSpec(memory_space=pl.ANY)


def ffn_mine(layer, b, g, values, received, totals, *tokens):
    rows, width = b.shape
    half, inner = width // 2, values[0].shape[1]
    wide = pl.BlockSpec((half, hidden_block), lambda p: (0, p))
    tall = pl.BlockSpec((hidden_block, half), lambda p: (p, 0))
    wide_out = pl.BlockSpec((1, half, hidden_block), lambda p: (layer, 0, p))
    tall_out = pl.BlockSpec((1, hidden_block, half), lambda p: (layer, p, 0))
    return pl.pallas_call(
        ffn_mine_kernel,
        grid=(inner // hidden_block,),
        in_specs=[fixed((rows, half))] * 2
        + [blocks_of(rows)] * 3
        + [wide, wide, tall]
        + [anywhere()] * 3
        + token_specs(tokens),
        out_specs=[wide_out, wide_out, tall_out],
        out_shape=[shape(x.shape, x.dtype) for x in totals],
        scratch_shapes=[pltpu.VMEM((half, rows), bf16)],
        input_output_aliases={8: 0, 9: 1, 10: 2},
        cost_estimate=cost(9),
        compiler_params=pltpu.CompilerParams(vmem_limit_bytes=60 << 20),
    )(b, g, *values, *received, *totals, *tokens)


def attention_grads(layer, a, ds, dz, u, y, received=None, totals=None, tokens=()):
    rows, width = a.shape
    half, local_width = width // 2, u.shape[1]
    part = min(rows, 1024)
    steps = rows // part
    mine = received is not None
    side = 0 if mine else 1
    features = pl.BlockSpec((part, half), lambda p: (p, side))
    across = [pl.BlockSpec((part, x.shape[1]), lambda p: (p, 0)) for x in (*ds, dz, u)]
    specs = [features, *across, features]
    operands = [a, *ds, dz, u, y]
    flat = [(half, local_width)] * 4 + [(half, pair_lanes), (local_width, half)]
    if mine:
        specs += [fixed(x) for x in flat] + [anywhere()] * 5
        operands += [*received, *totals]
        outs = [shape(x.shape, f32) for x in totals[:4]] + [shape(flat[4], f32), shape(totals[4].shape, f32)]
        layered = pl.BlockSpec((1, half, local_width), lambda p: (layer, 0, 0))
        out_specs = [layered] * 4 + [fixed(flat[4], False)]
        out_specs += [pl.BlockSpec((1, local_width, half), lambda p: (layer, 0, 0))]
        aliases = {14: 0, 15: 1, 16: 2, 17: 3, 18: 5}
    else:
        outs, out_specs, aliases = [shape(x, bf16) for x in flat], [fixed(x, False) for x in flat], {}
    sizes = [(half, 4 * local_width + pair_lanes), (local_width, half)] if steps > 1 else [(8, 128)] * 2
    return pl.pallas_call(
        functools.partial(attention_grads_kernel, steps, mine),
        grid=(steps,),
        in_specs=specs + token_specs(tokens),
        out_specs=out_specs,
        out_shape=outs,
        scratch_shapes=[pltpu.VMEM(x, f32) for x in sizes],
        input_output_aliases=aliases,
        cost_estimate=cost(7),
        compiler_params=pltpu.CompilerParams(vmem_limit_bytes=60 << 20),
    )(*operands, *tokens)


def unset(*like):
    return pl.pallas_call(
        pass_kernel,
        out_specs=[pl.BlockSpec(memory_space=pl.ANY) for _ in like],
        out_shape=list(like),
    )()


def inverse_rms(h):
    return lax.rsqrt(jnp.mean(h * h, axis=-1, keepdims=True) + epsilon)


def norm_back(grad_normed, hidden, inverse, gain):
    scaled = hidden * inverse
    weighted = grad_normed * gain
    grad_gain = jnp.sum(grad_normed * scaled, axis=0)
    mean = jnp.mean(weighted * scaled, axis=-1, keepdims=True)
    return inverse * (weighted - scaled * mean), grad_gain


def local(
    hidden_in, segment_ids, w_query, w_key, w_value, w_gate_out, w_attn_out, w_forget, b_forget,
    gain_attn, gain_ffn, w_gate, w_up, w_down, cotangent,
):
    seq_count, piece_len, width = hidden_in.shape
    count_z, count_t = lax.axis_size("context"), lax.axis_size("tensor")
    core, z, t = lax.axis_index("fsdp"), lax.axis_index("context"), lax.axis_index("tensor")
    layers, half, local_width = w_query.shape
    heads = w_forget.shape[2]
    block = piece_len // count_t
    seq_len = piece_len * count_z
    shared_rows = count_z == 4
    place = jnp.stack([z, t]).astype(jnp.int32)

    def features(x):
        return jnp.where(core == 0, x, jnp.concatenate([x[..., half:], x[..., :half]], axis=-1))

    def own_block(x):
        return lax.dynamic_slice_in_dim(x, t * block, block, 0)

    def other(w):
        return swap(w, "fsdp", 1)

    def full(w, axis):
        return jnp.concatenate([w, other(w)], axis=axis)

    seg_all = gathered(segment_ids.reshape(1, piece_len), "context").reshape(seq_len)
    doc_start = jnp.sum((seg_all[None, :] < seg_all[:, None]).astype(jnp.int32), axis=1, keepdims=True)

    gains = full(jnp.concatenate([gain_attn, gain_ffn], axis=0), 1).astype(f32)
    hidden_rows = features(hidden_in.reshape(piece_len, width)).astype(f32)
    first_a = (hidden_rows * inverse_rms(hidden_rows) * gains[0]).astype(bf16)
    w_forget_full = jnp.pad(full(w_forget, 1), ((0, 0), (0, 0), (0, pair_lanes - heads)))
    w_forget_full = [w_forget_full[layer] for layer in range(layers)]
    bias = jnp.pad(b_forget, ((0, 0), (0, pair_lanes - heads)))
    bias = [bias[layer : layer + 1] for layer in range(layers)]
    a_parts, a_far = all_rows(
        own_block(first_a), first_a, (seg_all,), (doc_start, w_forget_full[0], bias[0], place)
    )
    w4 = (w_query, w_key, w_value, w_gate_out)
    t4 = tuple(other(w) for w in w4)
    to = other(w_attn_out)
    w3 = (w_gate, w_up, w_down)
    t3 = tuple(other(w) for w in w3)

    hidden = own_block(hidden_rows)
    saved = []
    cotangent_rows = features(cotangent.reshape(piece_len, width))
    last = layers - 1
    grad = own_block(cotangent_rows).astype(f32)
    for layer in range(layers):
        gain_one, gain_two = gains[layer], gains[layers + layer]
        inverse_one = inverse_rms(hidden)
        if layer > 0:
            a_shard = (hidden * inverse_one * gain_one).astype(bf16)
            if shared_rows and layer == 1:
                a_shard = after(a_shard, g_last)
            a_parts, _ = all_rows(a_shard)
        forget_weights = w_forget_full[layer]
        if shared_rows and layer > 0:
            b_sent = after(saved[-1]["b_shard"], a_parts[-1])
            saved[-1]["b_rows"] = sequence_rows(b_sent)
            forget_weights = after(forget_weights, b_sent)
        a, (q, k, v, gate, forget, terms), sends = forward_own(
            place, a_parts, layer, w4, t4, w_attn_out, to, forget_weights,
            bias[layer], doc_start, piece_len,
        )
        if shared_rows and layer == 0:
            g_last = lax.all_gather(after(cotangent_rows, *a_far), "context", tiled=True)
        mixed = hidden + received_sum(sends)
        inverse_two = inverse_rms(mixed)
        b_shard = (mixed * inverse_two * gain_two).astype(bf16)
        b = gathered(b_shard, "tensor")
        gt, up, sends = ffn_forward(b, layer, w3, t3)
        saved.append(
            dict(hidden=hidden, inverse_one=inverse_one, a=a, kept=(q, k, v, gate, forget, terms), mixed=mixed,
                 inverse_two=inverse_two, b=b, b_shard=b_shard, gt=gt, up=up)
        )
        if layer < last:
            hidden = mixed + received_sum(sends)

    def finish(x):
        return features(gathered(x.astype(bf16), "tensor")).reshape(1, piece_len, width)

    last_sends = sends
    wide = shape((layers, half, local_width), f32)
    inner = shape((layers, half, w_gate.shape[2]), f32)
    results = list(
        unset(
            wide, wide, wide, wide, shape((layers, local_width, half), f32),
            inner, inner, shape((layers, w_down.shape[1], half), f32),
        )
    )
    small = [[None] * layers for _ in range(2)]
    gain_grads = [None] * (2 * layers)

    def ffn_theirs_of(layer, *tokens):
        s = saved[layer]
        values = ffn_theirs(s["b_rows"], s["g_rows"], layer, w3, t3, *tokens)
        s.update(values=values[:3], ffn_received=[other(x) for x in values[3:]])

    def ffn_mine_of(layer, *tokens):
        s = saved[layer]
        received = s["ffn_received"]
        results[5:] = ffn_mine(layer, s["b_rows"], s["g_rows"], s["values"], received, results[5:], *tokens)

    def attention_theirs_of(layer, *tokens):
        s = saved[layer]
        s["theirs"] = attention_grads(layer, *s["grads"], tokens=tokens)
        s["received"] = [other(x) for x in s["theirs"]]
        bias_grad = jnp.sum(s["grads"][2].astype(f32), axis=0)[:heads]
        small[1][layer] = bias_grad + other(bias_grad)

    def attention_mine_of(layer, *tokens):
        s = saved[layer]
        found = attention_grads(layer, *s["grads"], s["received"], results[:5], tokens)
        results[:5] = [*found[:4], found[5]]
        small[0][layer] = found[4][:, :heads]

    for layer in reversed(range(layers)):
        s = saved[layer]
        gain_one, gain_two = gains[layer], gains[layers + layer]
        tokens = ()
        if layer == last:
            g = cotangent_rows
        else:
            g_shard = grad.astype(bf16)
            g = gathered(g_shard, "tensor")
            tokens = (saved[layer + 1]["theirs"][0], output)
        if not shared_rows:
            s.update(b_rows=s["b"], g_rows=g)
        sends = ffn_backward(g, s["gt"], s["up"], layer, w3, t3, *tokens)
        if layer < last:
            sends = after(sends, *saved[layer + 1]["received"])
        back, gain_grads[layers + layer] = norm_back(received_sum(sends), s["mixed"], s["inverse_two"], gain_two)
        grad_mixed = grad + back
        y_shard = grad_mixed.astype(bf16)
        if layer < last:
            attention_mine_of(layer + 1)
            y_shard = after(y_shard, results[0])
        elif shared_rows:
            y_shard = after(y_shard, *[x["b_rows"] for x in saved[:-1]])
        y_parts, y_far = all_rows(y_shard, together=layer < last)
        tokens = ()
        if layer < last:
            above = saved[layer + 1]
            ffn_theirs_of(layer + 1, *y_far, y_parts[0])
            tokens = (above["values"][0],)
        kept = (*s["kept"][:-1], after(s["kept"][-1], *tokens))
        y, (dq, dk, dv, dg, u, dz), sends = attention_backward(
            place, y_parts, layer, w4, t4, w_attn_out, to, w_forget_full[layer], kept, doc_start, piece_len,
        )
        token = y_parts[-1]
        if layer == last:
            block_sum = own_block(last_sends).astype(f32) + s["mixed"]
            with_rows = lax.dynamic_update_slice_in_dim(last_sends, block_sum.astype(bf16), t * block, 0)
            output = lax.psum(after(with_rows, *y_parts), "tensor")
        if shared_rows and layer == last:
            s.update(b_rows=sequence_rows(after(s["b_shard"], *y_parts)), g_rows=g_last)
        elif shared_rows:
            s["g_rows"] = sequence_rows(after(g_shard, above["values"][0]))
        s["grads"] = (s["a"], (dq, dk, dv, dg), dz, u, y)
        if layer > 0:
            attention_theirs_of(layer)
        back, gain_grads[layer] = norm_back(received_sum(sends), s["hidden"], s["inverse_one"], gain_one)
        grad = grad_mixed + back

    for layer in reversed(range(1, layers)):
        ffn_mine_of(layer, sends)
    attention_theirs_of(0, sends)
    gain_total = after(jnp.stack(gain_grads).reshape(1, -1), *([results[5]] if layers > 1 else []))
    for axis in (("context", "tensor"),) if shared_rows else ("context", "tensor"):
        gain_total = jnp.sum(gathered(gain_total, axis), axis=0, keepdims=True)
    gain_total = gain_total.reshape(2 * layers, width)
    gain_total = gain_total[:, :half] + other(gain_total[:, half:])
    grad_input = finish(after(grad, saved[0]["theirs"][0]))
    ffn_theirs_of(0)
    attention_mine_of(0, gain_total, saved[0]["values"][0])
    ffn_mine_of(0)
    if not shared_rows:
        results[5:] = [lax.psum(x, "context") for x in results[5:]]
    output = features(output).reshape(1, piece_len, width)
    return (
        output, grad_input, *results[:5], jnp.stack(small[0]), jnp.stack(small[1]),
        gain_total[:layers], gain_total[layers:], *results[5:],
    )


def solution(mesh):
    rows = P("fsdp", "context", None)
    wide, tall = P(None, "fsdp", "tensor"), P(None, "tensor", "fsdp")
    heads, gain = P(None, "tensor"), P(None, "fsdp")
    return jax.shard_map(
        local,
        mesh=mesh,
        in_specs=(
            rows, P("fsdp", "context"), wide, wide, wide, wide, tall, wide, heads, gain, gain, wide, wide, tall, rows,
        ),
        out_specs=(rows, rows, wide, wide, wide, wide, tall, wide, heads, gain, gain, wide, wide, tall),
        check_vma=False,
    )
```

```python
import functools

import jax
import jax.numpy as jnp
from jax import lax
from jax.experimental import pallas as pl
from jax.experimental.pallas import tpu as pltpu
from jax.sharding import PartitionSpec as P

epsilon = 1e-06
masked_value = -1e30
bf16 = jnp.bfloat16
f32 = jnp.float32
pair_lanes = 128
hidden_block = 256
chunk_rows = 256


def query_rows(seq_len):
    return 256 if seq_len <= 2048 else 128


def swap(x, axis, k):
    n = lax.axis_size(axis)
    return lax.ppermute(x, axis, [(i, i ^ k) for i in range(n)])


def pass_kernel(*refs):
    pass


def after(x, *tokens):
    if not tokens:
        return x
    anywhere = pl.BlockSpec(memory_space=pl.ANY)
    return pl.pallas_call(
        pass_kernel,
        in_specs=[anywhere] * (1 + len(tokens)),
        out_specs=anywhere,
        out_shape=jax.ShapeDtypeStruct(x.shape, x.dtype),
        input_output_aliases={0: 0},
    )(x, *tokens)


def gathered(block, axis):
    count = lax.axis_size(axis)
    copies = jnp.broadcast_to(block[None], (count,) + block.shape)
    return lax.all_to_all(copies, axis, 0, 0, tiled=True).reshape((-1,) + block.shape[1:])


def sequence_rows(shard):
    return lax.all_gather(shard, ("context", "tensor"), tiled=True)


def near_rows(own):
    return swap(own, "context", 1)


def far_blocks(shard, *tokens):
    shard = after(shard, *tokens)
    return swap(shard, "context", 2), swap(shard, "context", 3)


def all_rows(shard, own=None, first=(), second_stage=(), together=False):
    if own is None:
        own = gathered(shard, "tensor")
    if lax.axis_size("context") != 4:
        return (lax.all_gather(own, "context", tiled=True),), ()
    second, third = far_blocks(shard, *first)
    near = near_rows(own)
    if together:
        block, width = shard.shape
        far = gathered(after(jnp.concatenate([second, third], axis=0), own), "tensor")
        return (own, near, far.reshape(-1, 2, block, width)), (second, third)
    second = after(second, *second_stage)
    parts = [own, near]
    for far in (second, third):
        parts += [far] + [swap(far, "tensor", k) for k in range(1, lax.axis_size("tensor"))]
    return tuple(parts), (second, third)


def received_sum(sends):
    count = lax.axis_size("tensor")
    got = lax.all_to_all(sends.reshape(count, -1, sends.shape[1]), "tensor", 0, 0, tiled=True)
    return jnp.sum(got.astype(f32), axis=0)


def dot_nt(a, b):
    return lax.dot_general(a, b, (((1,), (1,)), ((), ())), preferred_element_type=f32)


def dot_tn(a, b):
    return lax.dot_general(a, b, (((0,), (0,)), ((), ())), preferred_element_type=f32)


def dot_nn(a, b):
    return jnp.dot(a, b, preferred_element_type=f32)


def each(count, body):
    if count <= 4:
        for i in range(count):
            body(i)
        return

    def one(i, carry):
        body(i)
        return carry

    lax.fori_loop(0, count, one, 0)


def rows_at(i, rows):
    start = i * rows
    return pl.ds(start if isinstance(start, int) else pl.multiple_of(start, rows), rows)


def assemble(parts, whole_ref, place_ref):
    z, t = place_ref[0], place_ref[1]
    piece, blocks_seen, piece_len = 0, 0, parts[0].shape[0]
    for part in parts:
        if len(part.shape) == 4:
            blocks, pieces, block = part.shape[:3]
            for p in range(pieces):
                for b in range(blocks):
                    at = pl.multiple_of((z ^ (piece + p)) * piece_len + b * block, block)
                    whole_ref[pl.ds(at, block), :] = part[b, p]
            piece += pieces
            continue
        rows = part.shape[0]
        if rows == piece_len:
            at = pl.multiple_of((z ^ piece) * piece_len, piece_len)
            piece += 1
        else:
            at = pl.multiple_of((z ^ piece) * piece_len + (t ^ blocks_seen) * rows, rows)
            blocks_seen += 1
            if blocks_seen * rows == piece_len:
                piece, blocks_seen = piece + 1, 0
        whole_ref[pl.ds(at, rows), :] = part[...]


def triangle(rows, reverse):
    row = lax.broadcasted_iota(jnp.int32, (rows, rows), 0)
    column = lax.broadcasted_iota(jnp.int32, (rows, rows), 1)
    return jnp.where((column >= row) if reverse else (column <= row), 1.0, 0.0).astype(bf16)


def running_sum(ref, reverse):
    rows = chunk_rows
    ones = triangle(rows, reverse)
    count = ref.shape[0] // rows
    edge = 0 if reverse else rows - 1

    def chunk(i, carry):
        here = pl.ds(pl.multiple_of((count - 1 - i if reverse else i) * rows, rows), rows)
        high, middle, lowest = three_parts(ref[here, :])
        total = dot_nn(ones, high) + dot_nn(ones, middle) + dot_nn(ones, lowest) + carry
        ref[here, :] = total
        return total[edge : edge + 1, :]

    lax.fori_loop(0, count, chunk, jnp.zeros((1, ref.shape[1]), f32), unroll=count <= 4)


def log_sigmoid(z):
    e = jnp.exp(-jnp.abs(z))
    small = e * (1.0 - e * (1 / 2 - e * (1 / 3 - e * (1 / 4 - e * (1 / 5 - e * (1 / 6 - e * (1 / 7)))))))
    return jnp.minimum(z, 0.0) - jnp.where(e < 0.0625, small, jnp.log(1.0 + e))


def three_parts(x):
    high = x.astype(bf16)
    middle = (x - high.astype(f32)).astype(bf16)
    return high, middle, (x - high.astype(f32) - middle.astype(f32)).astype(bf16)


def decay_side(terms, pair, key_side):
    row = lax.broadcasted_iota(jnp.int32, (pair_lanes, pair_lanes), 0)
    lane = lax.broadcasted_iota(jnp.int32, (pair_lanes, pair_lanes), 1)
    spot = lane & 63
    term = spot if key_side else spot - 3
    head = jnp.where(lane >= 64, 2 * pair, 2 * pair + 1)
    chosen = (term >= 0) & (term < 3) & (row == 8 * term + head)
    pick = jnp.where(chosen, -1.0 if key_side else 1.0, 0.0).astype(bf16)
    lanes_now = lax.broadcasted_iota(jnp.int32, (1, pair_lanes), 1) & 63
    other = lanes_now - 3 if key_side else lanes_now
    ones = jnp.where((other >= 0) & (other < 3), 1.0, 0.0)
    return (dot_nn(terms, pick) + ones).astype(bf16)


def mix_keys(k_ref, terms_ref, pair, ka, kb):
    def mix(i):
        here = rows_at(i, chunk_rows)
        lane = lax.broadcasted_iota(jnp.int32, (chunk_rows, pair_lanes), 1)
        k, side = k_ref[here, :], decay_side(terms_ref[here, :], pair, True)
        ka[here, :] = jnp.where(lane < 64, k, side)
        kb[here, :] = jnp.where(lane < 64, side, k)

    each(k_ref.shape[0] // chunk_rows, mix)


def mix_queries(q_ref, terms_ref, start, pair, qa, qb):
    def mix(i):
        here = rows_at(i, chunk_rows)
        lane = lax.broadcasted_iota(jnp.int32, (chunk_rows, pair_lanes), 1)
        q = (q_ref[here, :].astype(f32) * 0.125).astype(bf16)
        terms = terms_ref[pl.ds(pl.multiple_of(start + i * chunk_rows, chunk_rows), chunk_rows), :]
        side = decay_side(terms, pair, False)
        qa[here, :] = jnp.where(lane < 64, q, side)
        qb[here, :] = jnp.where(lane < 64, side, q)

    each(q_ref.shape[0] // chunk_rows, mix)


def live_mask(start_ref, start, first, width, rows):
    key_pos = first + lax.broadcasted_iota(jnp.int32, (rows, width), 1)
    query_pos = start + lax.broadcasted_iota(jnp.int32, (rows, width), 0)
    doc_start = start_ref[pl.ds(start, rows), :]
    return (key_pos <= query_pos) & (key_pos >= doc_start)


def over_query_blocks(seq_len, rows, body):
    before = seq_len // 2
    if seq_len // rows <= 4:
        for start in range(0, seq_len, rows):
            first = max(0, start - before)
            body(start, first, start + rows - first)
        return
    width = before + rows

    def one(i, carry):
        start = pl.multiple_of(i * rows, rows)
        first = pl.multiple_of(jnp.maximum(start - before, 0), rows)
        body(start, first, width)
        return carry

    lax.fori_loop(0, seq_len // rows, one, 0)


def probabilities(q_rows, k_rows, mask):
    s = jnp.where(mask, dot_nt(q_rows, k_rows), masked_value)
    e = jnp.exp(s - jnp.max(s, axis=1, keepdims=True))
    return e * (1.0 / jnp.sum(e, axis=1, keepdims=True))


def lane_blocks(refs):
    return jnp.concatenate([r[0] for r in refs], axis=1)


def forward_own_kernel(count_parts, piece_len, join, *refs):
    place_ref, parts, refs = refs[0], refs[1 : 1 + count_parts], list(refs[1 + count_parts :])
    (wq, wk, wv, wg), (tq, tk, tv, tg) = refs[:4], refs[4:8]
    wo, to, wf, bias, start_ref = refs[8:13]
    refs = refs[13:]
    a_ref = refs.pop(0) if join else parts[0]
    q_ref, k_ref, v_ref, gate_ref, z_ref, terms_ref, send_ref, qa, qb, ka, kb, decay, acc = refs
    pair = pl.program_id(0)
    seq_len, half = a_ref.shape[0], a_ref.shape[1] // 2
    piece_start = pl.multiple_of(place_ref[0] * piece_len, piece_len)

    @pl.when(pair == 0)
    def _():
        if join:
            assemble(parts, a_ref, place_ref)
        acc[...] = jnp.zeros_like(acc)

        def gates(i):
            here = rows_at(i, chunk_rows)
            z = dot_nn(a_ref[here, :], wf[...]) + bias[...]
            z_ref[here, :] = z
            decay[here, :] = log_sigmoid(z)

        each(seq_len // chunk_rows, gates)
        running_sum(decay, False)

        def split(i):
            here = rows_at(i, chunk_rows)
            lane = lax.broadcasted_iota(jnp.int32, (chunk_rows, pair_lanes), 1)
            high, middle, lowest = (x.astype(f32) for x in three_parts(decay[here, :]))
            later = jnp.where(lane < 16, pltpu.roll(middle, 8, 1), pltpu.roll(lowest, 16, 1))
            terms = jnp.where(lane < 8, high, later)
            terms_ref[here, :] = jnp.where(lane < 24, terms, 0.0).astype(bf16)

        each(seq_len // chunk_rows, split)

    w_mine, w_theirs = lane_blocks((wq, wk, wv, wg)), lane_blocks((tq, tk, tv, tg))

    def project(i):
        here = rows_at(i, chunk_rows)
        out = dot_nn(a_ref[here, :half], w_mine) + dot_nn(a_ref[here, half:], w_theirs)
        q_ref[here, :] = out[:, :128].astype(bf16)
        k_ref[here, :] = out[:, 128:256].astype(bf16)
        v_ref[here, :] = out[:, 256:384].astype(bf16)
        gate_ref[here, :] = out[:, 384:]

    each(seq_len // chunk_rows, project)
    piece = pl.ds(piece_start, piece_len)
    gate = jax.nn.sigmoid(gate_ref[piece, :])
    mix_keys(k_ref, terms_ref, pair, ka, kb)
    mix_queries(q_ref.at[piece, :], terms_ref, piece_start, pair, qa, qb)
    before = seq_len // 2
    for s in range(0, piece_len, query_rows(seq_len)):
        rows = query_rows(seq_len)
        width = before + rows
        start = pl.multiple_of(piece_start + s, rows)
        first = pl.multiple_of(jnp.maximum(start - before, 0), rows)
        mask = live_mask(start_ref, start, first, width, rows)
        keys = pl.ds(first, width)
        out = []
        for q_of, k_of in ((qa, ka), (qb, kb)):
            p = probabilities(q_of[s : s + rows, :], k_of[keys, :], mask).astype(bf16)
            out.append(dot_nn(p, v_ref[keys, :]))
        lane = lax.broadcasted_iota(jnp.int32, (rows, pair_lanes), 1)
        u = (jnp.where(lane < 64, out[0], out[1]) * gate[s : s + rows, :]).astype(bf16)
        acc[s : s + rows, :half] += dot_nn(u, wo[0])
        acc[s : s + rows, half:] += dot_nn(u, to[0])

    @pl.when(pair == pl.num_programs(0) - 1)
    def _():
        send_ref[...] = acc[...].astype(bf16)


def backward_kernel(count_parts, piece_len, join, *refs):
    place_ref, parts, refs = refs[0], refs[1 : 1 + count_parts], list(refs[1 + count_parts :])
    mine, theirs, (wo, to, wf) = refs[:4], refs[4:8], refs[8:11]
    q_ref, k_ref, v_ref, gate_ref, z_ref, terms_ref, start_ref = refs[11:18]
    refs = refs[18:]
    y_ref = refs.pop(0) if join else parts[0]
    dq_ref, dk_ref, dv_ref, dg_ref, u_ref, dz_ref, send_ref = refs[:7]
    qa, qb, ka, kb, dd, dus, dka, dkb, dva, dcs, acc = refs[7:]
    pair = pl.program_id(0)
    seq_len, half = y_ref.shape[0], y_ref.shape[1] // 2
    rows = query_rows(seq_len)
    piece = pl.ds(pl.multiple_of(place_ref[0] * piece_len, piece_len), piece_len)

    @pl.when(pair == 0)
    def _():
        if join:
            assemble(parts, y_ref, place_ref)
        acc[...] = jnp.zeros_like(acc)
        dcs[...] = jnp.zeros_like(dcs)

    def gates(i):
        here = rows_at(i, chunk_rows)
        du = dot_nt(y_ref[here, :half], wo[0]) + dot_nt(y_ref[here, half:], to[0])
        sig = jax.nn.sigmoid(gate_ref[here, :])
        dd[here, :] = (du * sig).astype(bf16)
        dus[here, :] = du * sig * (1.0 - sig)

    each(seq_len // chunk_rows, gates)
    mix_keys(k_ref, terms_ref, pair, ka, kb)
    mix_queries(q_ref, terms_ref, 0, pair, qa, qb)
    dka[...] = jnp.zeros_like(dka)
    dkb[...] = jnp.zeros_like(dkb)
    dva[...] = jnp.zeros_like(dva)
    lane = lax.broadcasted_iota(jnp.int32, (rows, pair_lanes), 1)

    def pick(column_a, column_b):
        at = lax.broadcasted_iota(jnp.int32, (column_a.shape[0], pair_lanes), 1)
        return jnp.where(at == 2 * pair, column_a, jnp.where(at == 2 * pair + 1, column_b, 0.0))

    def body(start, first, width):
        mask = live_mask(start_ref, start, first, width, rows)
        here, keys = pl.ds(start, rows), pl.ds(first, width)
        values = v_ref[keys, :]
        d_rows = dd[here, :]
        dq, o = [], []
        for head, (q_of, k_of, dk_of) in enumerate(((qa, ka, dka), (qb, kb, dkb))):
            own_lanes = (lane < 64) if head == 0 else (lane >= 64)
            p = probabilities(q_of[here, :], k_of[keys, :], mask)
            d_mine = jnp.where(own_lanes, d_rows, jnp.zeros_like(d_rows))
            dp = dot_nt(d_mine, values)
            delta = jnp.sum(p * dp, axis=1, keepdims=True)
            ds = (p * (dp - delta)).astype(bf16)
            dq.append(dot_nn(ds, k_of[keys, :]))
            dk_of[keys, :] += dot_tn(ds, q_of[here, :])
            low = p.astype(bf16)
            dva[keys, :] += dot_tn(low, d_mine)
            o.append(dot_nn(low, values))
        o = jnp.where(lane < 64, o[0], o[1])
        dg_ref[here, :] = (dus[here, :] * o).astype(bf16)
        u_ref[here, :] = (o * jax.nn.sigmoid(gate_ref[here, :])).astype(bf16)
        dq_ref[here, :] = (jnp.where(lane < 64, dq[0], dq[1]) * 0.125).astype(bf16)
        dcs[here, :] += pick(dq[0][:, 67:68], dq[1][:, 3:4])

    over_query_blocks(seq_len, rows, body)

    def finish(i):
        here = rows_at(i, chunk_rows)
        lanes_now = lax.broadcasted_iota(jnp.int32, (chunk_rows, pair_lanes), 1)
        ka_rows, kb_rows = dka[here, :], dkb[here, :]
        dk_ref[here, :] = jnp.where(lanes_now < 64, ka_rows, kb_rows).astype(bf16)
        dv_ref[here, :] = dva[here, :].astype(bf16)
        dcs[here, :] -= pick(ka_rows[:, 64:65], kb_rows[:, 0:1])

    each(seq_len // chunk_rows, finish)
    d_own = jnp.concatenate([r[piece, :] for r in (dq_ref, dk_ref, dv_ref, dg_ref)], axis=1)
    acc[:, :half] += dot_nt(d_own, lane_blocks(mine))
    acc[:, half:] += dot_nt(d_own, lane_blocks(theirs))

    @pl.when(pair == pl.num_programs(0) - 1)
    def _():
        running_sum(dcs, True)

        def last(i):
            here = rows_at(i, chunk_rows)
            dz_ref[here, :] = (dcs[here, :] * jax.nn.sigmoid(-z_ref[here, :])).astype(bf16)

        each(seq_len // chunk_rows, last)
        send_ref[...] = (acc[...] + dot_nt(dz_ref[piece, :], wf[...])).astype(bf16)


def ffn_forward_kernel(b_ref, wg, wu, wd, tg, tu, td, gt_ref, up_ref, send_ref, acc):
    half = b_ref.shape[1] // 2
    low, high = b_ref[:, :half], b_ref[:, half:]
    gt = dot_nn(low, wg[0]) + dot_nn(high, tg[0])
    up = dot_nn(low, wu[0]) + dot_nn(high, tu[0])
    gt_ref[...] = gt
    up_ref[...] = up
    m = (gt * jax.nn.sigmoid(gt) * up).astype(bf16)

    @pl.when(pl.program_id(0) == 0)
    def _():
        acc[...] = jnp.zeros_like(acc)

    acc[:, :half] += dot_nn(m, wd[0])
    acc[:, half:] += dot_nn(m, td[0])

    @pl.when(pl.program_id(0) == pl.num_programs(0) - 1)
    def _():
        send_ref[...] = acc[...].astype(bf16)


def inner_grads(dm, gt, up):
    sig = jax.nn.sigmoid(gt)
    d_gate = (dm * up * sig * (1.0 + gt * (1.0 - sig))).astype(bf16)
    return d_gate, (dm * (gt * sig)).astype(bf16)


def ffn_backward_kernel(g_ref, gt_ref, up_ref, wg, wu, wd, tg, tu, td, *refs):
    send_ref, acc = refs[-2:]
    half = g_ref.shape[1] // 2
    dm = dot_nt(g_ref[:, :half], wd[0]) + dot_nt(g_ref[:, half:], td[0])
    d_gate, d_up = inner_grads(dm, gt_ref[...], up_ref[...])

    @pl.when(pl.program_id(0) == 0)
    def _():
        acc[...] = jnp.zeros_like(acc)

    acc[:, :half] += dot_nt(d_gate, wg[0]) + dot_nt(d_up, wu[0])
    acc[:, half:] += dot_nt(d_gate, tg[0]) + dot_nt(d_up, tu[0])

    @pl.when(pl.program_id(0) == pl.num_programs(0) - 1)
    def _():
        send_ref[...] = acc[...].astype(bf16)


def ffn_theirs_kernel(b_ref, g_ref, wg, wu, wd, tg, tu, td, *refs):
    m_ref, dgate_ref, dup_ref, gate_out, up_out, down_out, turned = refs[-7:]
    half = b_ref.shape[1] // 2

    @pl.when(pl.program_id(0) == 0)
    def _():
        turned[...] = b_ref[:, half:].T

    def chunk(i):
        here = rows_at(i, chunk_rows)
        low, high = b_ref[here, :half], b_ref[here, half:]
        gt = dot_nn(low, wg[0]) + dot_nn(high, tg[0])
        up = dot_nn(low, wu[0]) + dot_nn(high, tu[0])
        dm = dot_nt(g_ref[here, :half], wd[0]) + dot_nt(g_ref[here, half:], td[0])
        m_ref[here, :] = (gt * jax.nn.sigmoid(gt) * up).astype(bf16)
        dgate_ref[here, :], dup_ref[here, :] = inner_grads(dm, gt, up)

    each(b_ref.shape[0] // chunk_rows, chunk)
    gate_out[...] = dot_nn(turned[...], dgate_ref[...]).astype(bf16)
    up_out[...] = dot_nn(turned[...], dup_ref[...]).astype(bf16)
    down_out[...] = dot_tn(m_ref[...], g_ref[:, half:]).astype(bf16)


def ffn_mine_kernel(b_ref, g_ref, m_ref, dgate_ref, dup_ref, gate_in, up_in, down_in, *refs):
    gate_out, up_out, down_out, turned = refs[-4:]

    @pl.when(pl.program_id(0) == 0)
    def _():
        turned[...] = b_ref[...].T

    gate_out[0] = dot_nn(turned[...], dgate_ref[...]) + gate_in[...].astype(f32)
    up_out[0] = dot_nn(turned[...], dup_ref[...]) + up_in[...].astype(f32)
    down_out[0] = dot_tn(m_ref[...], g_ref[...]) + down_in[...].astype(f32)


def attention_grads_kernel(steps, mine, *refs):
    a_ref, dq, dk, dv, dg, dz, u_ref, y_ref = refs[:8]
    received = refs[8:14] if mine else [None] * 6
    acc, acc_out = refs[-2:]
    outs = refs[-8:-2]
    turned = a_ref[...].T
    width = dq.shape[1]
    parts = [dot_nn(turned, d[...]) for d in (dq, dk, dv, dg, dz)]
    out = dot_tn(u_ref[...], y_ref[...])

    def give(values):
        for ref, value, more in zip(outs, values, received):
            total = value if more is None else value + more[...].astype(f32)
            if len(ref.shape) == 3:
                ref[0] = total.astype(ref.dtype)
            else:
                ref[...] = total.astype(ref.dtype)

    if steps == 1:
        give([*parts, out])
        return
    step = pl.program_id(0)

    @pl.when(step == 0)
    def _():
        acc[...] = jnp.zeros_like(acc)
        acc_out[...] = jnp.zeros_like(acc_out)

    for k, part in enumerate(parts):
        acc[:, k * width : k * width + part.shape[1]] += part
    acc_out[...] += out

    @pl.when(step == steps - 1)
    def _():
        found = [acc[:, k * width : k * width + p.shape[1]] for k, p in enumerate(parts)]
        give([*found, acc_out[...]])


def fixed(shape, single=True):
    zeros = (0,) * len(shape)
    if single:
        return pl.BlockSpec(shape, lambda *_: zeros, pipeline_mode=pl.Buffered(1))
    return pl.BlockSpec(shape, lambda *_: zeros)


def lanes(seq_len):
    return pl.BlockSpec((seq_len, pair_lanes), lambda p, *_: (0, p))


def lanes_read(seq_len):
    if seq_len <= 2048:
        return lanes(seq_len)
    return pl.BlockSpec((seq_len, pair_lanes), lambda p, *_: (0, p), pipeline_mode=pl.Buffered(1))


def columns_of(w, layer, width):
    return pl.BlockSpec((1, w.shape[1], width), lambda p, *_: (layer, 0, p))


def rows_of(w, layer, height):
    return pl.BlockSpec((1, height, w.shape[2]), lambda p, *_: (layer, p, 0))


def shape(dims, dtype):
    return jax.ShapeDtypeStruct(dims, dtype)


def attention_specs(parts, layer, w4, t4, wo, to, seq_len, join):
    specs = [fixed(p.shape) for p in parts]
    specs += [columns_of(w, layer, pair_lanes) for w in (*w4, *t4)]
    specs += [rows_of(wo, layer, pair_lanes), rows_of(to, layer, pair_lanes)]
    return specs


def cost(microseconds):
    return pl.CostEstimate(flops=int(microseconds * 1.1e9), bytes_accessed=0, transcendentals=0)


def token_specs(tokens):
    return [pl.BlockSpec(memory_space=pl.ANY) for _ in tokens]


def forward_own(place, parts, layer, w4, t4, wo, to, wf, bias, doc_start, piece_len):
    seq_len, width = doc_start.shape[0], parts[0].shape[1]
    local_width = wo.shape[1]
    join = len(parts) > 1
    terms = (seq_len, pair_lanes)
    outs = [shape((seq_len, local_width), bf16)] * 3 + [shape((seq_len, local_width), f32)]
    outs += [shape(terms, f32), shape(terms, bf16), shape((piece_len, width), bf16)]
    specs = [lanes(seq_len)] * 4 + [fixed(terms, False)] * 2 + [fixed((piece_len, width), False)]
    if join:
        outs, specs = [shape((seq_len, width), bf16)] + outs, [fixed((seq_len, width))] + specs
    low, piece = pltpu.VMEM((seq_len, pair_lanes), bf16), pltpu.VMEM((piece_len, pair_lanes), bf16)
    got = pl.pallas_call(
        functools.partial(forward_own_kernel, len(parts), piece_len, join),
        grid_spec=pltpu.PrefetchScalarGridSpec(
            num_scalar_prefetch=1,
            grid=(local_width // pair_lanes,),
            in_specs=attention_specs(parts, layer, w4, t4, wo, to, seq_len, join)
            + [fixed(wf.shape), fixed(bias.shape), fixed(doc_start.shape)],
            out_specs=specs,
            scratch_shapes=[piece] * 2 + [low] * 2 + [pltpu.VMEM(terms, f32), pltpu.VMEM((piece_len, width), f32)],
        ),
        out_shape=outs,
        cost_estimate=cost(19),
        compiler_params=pltpu.CompilerParams(vmem_limit_bytes=60 << 20),
    )(place, *parts, *w4, *t4, wo, to, wf, bias, doc_start)
    got = list(got)
    a = got.pop(0) if join else parts[0]
    return a, got[:6], got[6]


def attention_backward(place, parts, layer, w4, t4, wo, to, wf, saved, doc_start, piece_len):
    q, k, v, gate, z, terms = saved
    seq_len, width = doc_start.shape[0], parts[0].shape[1]
    local_width = wo.shape[1]
    join = len(parts) > 1
    outs = [shape((seq_len, local_width), bf16)] * 5 + [shape((seq_len, pair_lanes), bf16)]
    outs += [shape((piece_len, width), bf16)]
    specs = [lanes(seq_len)] * 5 + [fixed((seq_len, pair_lanes), False), fixed((piece_len, width), False)]
    if join:
        outs, specs = [shape((seq_len, width), bf16)] + outs, [fixed((seq_len, width))] + specs
    low, high = pltpu.VMEM((seq_len, pair_lanes), bf16), pltpu.VMEM((seq_len, pair_lanes), f32)
    got = pl.pallas_call(
        functools.partial(backward_kernel, len(parts), piece_len, join),
        grid_spec=pltpu.PrefetchScalarGridSpec(
            num_scalar_prefetch=1,
            grid=(local_width // pair_lanes,),
            in_specs=attention_specs(parts, layer, w4, t4, wo, to, seq_len, join)
            + [fixed(wf.shape)]
            + [lanes_read(seq_len)] * 4
            + [fixed(z.shape), fixed(terms.shape), fixed(doc_start.shape)],
            out_specs=specs,
            scratch_shapes=[low] * 5 + [high] * 5 + [pltpu.VMEM((piece_len, width), f32)],
        ),
        out_shape=outs,
        cost_estimate=cost(33),
        compiler_params=pltpu.CompilerParams(vmem_limit_bytes=60 << 20),
    )(place, *parts, *w4, *t4, wo, to, wf, q, k, v, gate, z, terms, doc_start)
    got = list(got)
    y = got.pop(0) if join else parts[0]
    return y, got[:6], got[6]


def ffn_weights(layer, w3, t3):
    specs = []
    for wg, wu, wd in (w3, t3):
        specs += [
            columns_of(wg, layer, hidden_block), columns_of(wu, layer, hidden_block), rows_of(wd, layer, hidden_block),
        ]
    return specs


def blocks_of(rows):
    return pl.BlockSpec((rows, hidden_block), lambda p, *_: (0, p))


def ffn_forward(b, layer, w3, t3):
    rows, width = b.shape
    inner = w3[2].shape[1]
    return pl.pallas_call(
        ffn_forward_kernel,
        grid=(inner // hidden_block,),
        in_specs=[fixed(b.shape)] + ffn_weights(layer, w3, t3),
        out_specs=[blocks_of(rows)] * 2 + [fixed((rows, width), False)],
        scratch_shapes=[pltpu.VMEM((rows, width), f32)],
        out_shape=[shape((rows, inner), f32)] * 2 + [shape((rows, width), bf16)],
        cost_estimate=cost(7),
        compiler_params=pltpu.CompilerParams(vmem_limit_bytes=60 << 20),
    )(b, *w3, *t3)


def ffn_backward(g, gt, up, layer, w3, t3, *tokens):
    rows, width = g.shape
    return pl.pallas_call(
        ffn_backward_kernel,
        grid=(gt.shape[1] // hidden_block,),
        in_specs=[fixed(g.shape)] + [blocks_of(rows)] * 2 + ffn_weights(layer, w3, t3) + token_specs(tokens),
        out_specs=fixed((rows, width), False),
        scratch_shapes=[pltpu.VMEM((rows, width), f32)],
        out_shape=shape((rows, width), bf16),
        cost_estimate=cost(8),
        compiler_params=pltpu.CompilerParams(vmem_limit_bytes=60 << 20),
    )(g, gt, up, *w3, *t3, *tokens)


def ffn_theirs(b, g, layer, w3, t3, *tokens):
    rows, width = b.shape
    half = width // 2
    inner = w3[2].shape[1]
    wide = pl.BlockSpec((half, hidden_block), lambda p: (0, p))
    return pl.pallas_call(
        ffn_theirs_kernel,
        grid=(inner // hidden_block,),
        in_specs=[fixed(b.shape), fixed(g.shape)] + ffn_weights(layer, w3, t3) + token_specs(tokens),
        out_specs=[blocks_of(rows)] * 3 + [wide, wide, pl.BlockSpec((hidden_block, half), lambda p: (p, 0))],
        scratch_shapes=[pltpu.VMEM((half, rows), bf16)],
        out_shape=[shape((rows, inner), bf16)] * 3
        + [shape((half, inner), bf16)] * 2
        + [shape((inner, half), bf16)],
        cost_estimate=cost(24),
        compiler_params=pltpu.CompilerParams(vmem_limit_bytes=60 << 20),
    )(b, g, *w3, *t3, *tokens)


def anywhere():
    return pl.BlockSpec(memory_space=pl.ANY)


def ffn_mine(layer, b, g, values, received, totals, *tokens):
    rows, width = b.shape
    half, inner = width // 2, values[0].shape[1]
    wide = pl.BlockSpec((half, hidden_block), lambda p: (0, p))
    tall = pl.BlockSpec((hidden_block, half), lambda p: (p, 0))
    wide_out = pl.BlockSpec((1, half, hidden_block), lambda p: (layer, 0, p))
    tall_out = pl.BlockSpec((1, hidden_block, half), lambda p: (layer, p, 0))
    return pl.pallas_call(
        ffn_mine_kernel,
        grid=(inner // hidden_block,),
        in_specs=[fixed((rows, half))] * 2
        + [blocks_of(rows)] * 3
        + [wide, wide, tall]
        + [anywhere()] * 3
        + token_specs(tokens),
        out_specs=[wide_out, wide_out, tall_out],
        out_shape=[shape(x.shape, x.dtype) for x in totals],
        scratch_shapes=[pltpu.VMEM((half, rows), bf16)],
        input_output_aliases={8: 0, 9: 1, 10: 2},
        cost_estimate=cost(9),
        compiler_params=pltpu.CompilerParams(vmem_limit_bytes=60 << 20),
    )(b, g, *values, *received, *totals, *tokens)


def attention_grads(layer, a, ds, dz, u, y, received=None, totals=None, tokens=()):
    rows, width = a.shape
    half, local_width = width // 2, u.shape[1]
    part = min(rows, 1024)
    steps = rows // part
    mine = received is not None
    side = 0 if mine else 1
    features = pl.BlockSpec((part, half), lambda p: (p, side))
    across = [pl.BlockSpec((part, x.shape[1]), lambda p: (p, 0)) for x in (*ds, dz, u)]
    specs = [features, *across, features]
    operands = [a, *ds, dz, u, y]
    flat = [(half, local_width)] * 4 + [(half, pair_lanes), (local_width, half)]
    if mine:
        specs += [fixed(x) for x in flat] + [anywhere()] * 5
        operands += [*received, *totals]
        outs = [shape(x.shape, f32) for x in totals[:4]] + [shape(flat[4], f32), shape(totals[4].shape, f32)]
        layered = pl.BlockSpec((1, half, local_width), lambda p: (layer, 0, 0))
        out_specs = [layered] * 4 + [fixed(flat[4], False)]
        out_specs += [pl.BlockSpec((1, local_width, half), lambda p: (layer, 0, 0))]
        aliases = {14: 0, 15: 1, 16: 2, 17: 3, 18: 5}
    else:
        outs, out_specs, aliases = [shape(x, bf16) for x in flat], [fixed(x, False) for x in flat], {}
    sizes = [(half, 4 * local_width + pair_lanes), (local_width, half)] if steps > 1 else [(8, 128)] * 2
    return pl.pallas_call(
        functools.partial(attention_grads_kernel, steps, mine),
        grid=(steps,),
        in_specs=specs + token_specs(tokens),
        out_specs=out_specs,
        out_shape=outs,
        scratch_shapes=[pltpu.VMEM(x, f32) for x in sizes],
        input_output_aliases=aliases,
        cost_estimate=cost(7),
        compiler_params=pltpu.CompilerParams(vmem_limit_bytes=60 << 20),
    )(*operands, *tokens)


def unset(*like):
    return pl.pallas_call(
        pass_kernel,
        out_specs=[pl.BlockSpec(memory_space=pl.ANY) for _ in like],
        out_shape=list(like),
    )()


def inverse_rms(h):
    return lax.rsqrt(jnp.mean(h * h, axis=-1, keepdims=True) + epsilon)


def norm_back(grad_normed, hidden, inverse, gain):
    scaled = hidden * inverse
    weighted = grad_normed * gain
    grad_gain = jnp.sum(grad_normed * scaled, axis=0)
    mean = jnp.mean(weighted * scaled, axis=-1, keepdims=True)
    return inverse * (weighted - scaled * mean), grad_gain


def local(
    hidden_in, segment_ids, w_query, w_key, w_value, w_gate_out, w_attn_out, w_forget, b_forget,
    gain_attn, gain_ffn, w_gate, w_up, w_down, cotangent,
):
    seq_count, piece_len, width = hidden_in.shape
    count_z, count_t = lax.axis_size("context"), lax.axis_size("tensor")
    core, z, t = lax.axis_index("fsdp"), lax.axis_index("context"), lax.axis_index("tensor")
    layers, half, local_width = w_query.shape
    heads = w_forget.shape[2]
    block = piece_len // count_t
    seq_len = piece_len * count_z
    shared_rows = count_z == 4
    place = jnp.stack([z, t]).astype(jnp.int32)

    def features(x):
        return jnp.where(core == 0, x, jnp.concatenate([x[..., half:], x[..., :half]], axis=-1))

    def own_block(x):
        return lax.dynamic_slice_in_dim(x, t * block, block, 0)

    def other(w):
        return swap(w, "fsdp", 1)

    def full(w, axis):
        return jnp.concatenate([w, other(w)], axis=axis)

    seg_all = gathered(segment_ids.reshape(1, piece_len), "context").reshape(seq_len)
    doc_start = jnp.sum((seg_all[None, :] < seg_all[:, None]).astype(jnp.int32), axis=1, keepdims=True)

    gains = full(jnp.concatenate([gain_attn, gain_ffn], axis=0), 1).astype(f32)
    hidden_rows = features(hidden_in.reshape(piece_len, width)).astype(f32)
    first_a = (hidden_rows * inverse_rms(hidden_rows) * gains[0]).astype(bf16)
    w_forget_full = jnp.pad(full(w_forget, 1), ((0, 0), (0, 0), (0, pair_lanes - heads)))
    w_forget_full = [w_forget_full[layer] for layer in range(layers)]
    bias = jnp.pad(b_forget, ((0, 0), (0, pair_lanes - heads)))
    bias = [bias[layer : layer + 1] for layer in range(layers)]
    a_parts, a_far = all_rows(
        own_block(first_a), first_a, (seg_all,), (doc_start, w_forget_full[0], bias[0], place)
    )
    w4 = (w_query, w_key, w_value, w_gate_out)
    t4 = tuple(other(w) for w in w4)
    to = other(w_attn_out)
    w3 = (w_gate, w_up, w_down)
    t3 = tuple(other(w) for w in w3)

    hidden = own_block(hidden_rows)
    saved = []
    cotangent_rows = features(cotangent.reshape(piece_len, width))
    last = layers - 1
    grad = own_block(cotangent_rows).astype(f32)
    for layer in range(layers):
        gain_one, gain_two = gains[layer], gains[layers + layer]
        inverse_one = inverse_rms(hidden)
        if layer > 0:
            a_shard = (hidden * inverse_one * gain_one).astype(bf16)
            if shared_rows and layer == 1:
                a_shard = after(a_shard, g_last)
            a_parts, _ = all_rows(a_shard)
        forget_weights = w_forget_full[layer]
        if shared_rows and layer > 0:
            b_sent = after(saved[-1]["b_shard"], a_parts[-1])
            saved[-1]["b_rows"] = sequence_rows(b_sent)
            forget_weights = after(forget_weights, b_sent)
        a, (q, k, v, gate, forget, terms), sends = forward_own(
            place, a_parts, layer, w4, t4, w_attn_out, to, forget_weights,
            bias[layer], doc_start, piece_len,
        )
        if shared_rows and layer == 0:
            g_last = lax.all_gather(after(cotangent_rows, *a_far), "context", tiled=True)
        mixed = hidden + received_sum(sends)
        inverse_two = inverse_rms(mixed)
        b_shard = (mixed * inverse_two * gain_two).astype(bf16)
        b = gathered(b_shard, "tensor")
        gt, up, sends = ffn_forward(b, layer, w3, t3)
        saved.append(
            dict(hidden=hidden, inverse_one=inverse_one, a=a, kept=(q, k, v, gate, forget, terms), mixed=mixed,
                 inverse_two=inverse_two, b=b, b_shard=b_shard, gt=gt, up=up)
        )
        if layer < last:
            hidden = mixed + received_sum(sends)

    def finish(x):
        return features(gathered(x.astype(bf16), "tensor")).reshape(1, piece_len, width)

    last_sends = sends
    wide = shape((layers, half, local_width), f32)
    inner = shape((layers, half, w_gate.shape[2]), f32)
    results = list(
        unset(
            wide, wide, wide, wide, shape((layers, local_width, half), f32),
            inner, inner, shape((layers, w_down.shape[1], half), f32),
        )
    )
    small = [[None] * layers for _ in range(2)]
    gain_grads = [None] * (2 * layers)

    def ffn_theirs_of(layer, *tokens):
        s = saved[layer]
        values = ffn_theirs(s["b_rows"], s["g_rows"], layer, w3, t3, *tokens)
        s.update(values=values[:3], ffn_received=[other(x) for x in values[3:]])

    def ffn_mine_of(layer, *tokens):
        s = saved[layer]
        received = s["ffn_received"]
        results[5:] = ffn_mine(layer, s["b_rows"], s["g_rows"], s["values"], received, results[5:], *tokens)

    def attention_theirs_of(layer, *tokens):
        s = saved[layer]
        s["theirs"] = attention_grads(layer, *s["grads"], tokens=tokens)
        s["received"] = [other(x) for x in s["theirs"]]
        bias_grad = jnp.sum(s["grads"][2].astype(f32), axis=0)[:heads]
        small[1][layer] = bias_grad + other(bias_grad)

    def attention_mine_of(layer, *tokens):
        s = saved[layer]
        found = attention_grads(layer, *s["grads"], s["received"], results[:5], tokens)
        results[:5] = [*found[:4], found[5]]
        small[0][layer] = found[4][:, :heads]

    for layer in reversed(range(layers)):
        s = saved[layer]
        gain_one, gain_two = gains[layer], gains[layers + layer]
        tokens = ()
        if layer == last:
            g = cotangent_rows
        else:
            g_shard = grad.astype(bf16)
            g = gathered(g_shard, "tensor")
            tokens = (saved[layer + 1]["theirs"][0],)
        if not shared_rows:
            s.update(b_rows=s["b"], g_rows=g)
        sends = ffn_backward(g, s["gt"], s["up"], layer, w3, t3, *tokens)
        if layer < last:
            sends = after(sends, *saved[layer + 1]["received"])
        back, gain_grads[layers + layer] = norm_back(received_sum(sends), s["mixed"], s["inverse_two"], gain_two)
        grad_mixed = grad + back
        y_shard = grad_mixed.astype(bf16)
        if layer < last:
            attention_mine_of(layer + 1)
            y_shard = after(y_shard, results[0])
        elif shared_rows:
            y_shard = after(y_shard, *[x["b_rows"] for x in saved[:-1]])
        y_parts, y_far = all_rows(y_shard, together=layer < last)
        tokens = ()
        if layer < last:
            above = saved[layer + 1]
            ffn_theirs_of(layer + 1, *y_far, y_parts[0])
            tokens = (above["values"][0],)
        kept = (*s["kept"][:-1], after(s["kept"][-1], *tokens))
        y, (dq, dk, dv, dg, u, dz), sends = attention_backward(
            place, y_parts, layer, w4, t4, w_attn_out, to, w_forget_full[layer], kept, doc_start, piece_len,
        )
        token = y_parts[-1]
        if shared_rows and layer == last:
            s.update(b_rows=sequence_rows(after(s["b_shard"], *y_parts)), g_rows=g_last)
        elif shared_rows:
            s["g_rows"] = sequence_rows(after(g_shard, above["values"][0]))
        s["grads"] = (s["a"], (dq, dk, dv, dg), dz, u, y)
        if layer > 0:
            attention_theirs_of(layer)
        back, gain_grads[layer] = norm_back(received_sum(sends), s["hidden"], s["inverse_one"], gain_one)
        grad = grad_mixed + back

    block_sum = own_block(last_sends).astype(f32) + saved[last]["mixed"]
    with_rows = lax.dynamic_update_slice_in_dim(last_sends, block_sum.astype(bf16), t * block, 0)
    output = lax.psum(after(with_rows, sends), "tensor")
    for layer in reversed(range(1, layers)):
        ffn_mine_of(layer, sends)
    attention_theirs_of(0, sends)
    ffn_theirs_of(0)
    gain_total = after(jnp.stack(gain_grads).reshape(1, -1), saved[0]["values"][0])
    for axis in (("context", "tensor"),) if shared_rows else ("context", "tensor"):
        gain_total = jnp.sum(gathered(gain_total, axis), axis=0, keepdims=True)
    gain_total = gain_total.reshape(2 * layers, width)
    gain_total = gain_total[:, :half] + other(gain_total[:, half:])
    grad_input = finish(after(grad, saved[0]["theirs"][0]))
    attention_mine_of(0, saved[0]["values"][0])
    ffn_mine_of(0)
    if not shared_rows:
        results[5:] = [lax.psum(x, "context") for x in results[5:]]
    output = features(after(output, saved[0]["values"][0])).reshape(1, piece_len, width)
    return (
        output, grad_input, *results[:5], jnp.stack(small[0]), jnp.stack(small[1]),
        gain_total[:layers], gain_total[layers:], *results[5:],
    )


def solution(mesh):
    rows = P("fsdp", "context", None)
    wide, tall = P(None, "fsdp", "tensor"), P(None, "tensor", "fsdp")
    heads, gain = P(None, "tensor"), P(None, "fsdp")
    return jax.shard_map(
        local,
        mesh=mesh,
        in_specs=(
            rows, P("fsdp", "context"), wide, wide, wide, wide, tall, wide, heads, gain, gain, wide, wide, tall, rows,
        ),
        out_specs=(rows, rows, wide, wide, wide, wide, tall, wide, heads, gain, gain, wide, wide, tall),
        check_vma=False,
    )
```
